32 devices in a mesh: seq: 4 (over x, core), frame: 8 (over z, y).
Axes of the slice: x: 2, y: 2, z: 4, core: 2. Of those that a mesh axis runs over, the one named last changes fastest.
Arguments:
- inputs: bfloat16 [4, 16, 64, 768], P('seq', 'frame'), may hold values from -6 to 6
- clip_id: int32 [4, 16], P('seq'), may hold values from 0 to 12, as said below
- ln_gains: float32 [3, 768], replicated, may hold values from 0.25 to 1.75
- ln_biases: float32 [3, 768], replicated, may hold values from -2 to 2
- w_qkv: bfloat16 [768, 2304], P('frame'), may hold values from -0.3125 to 0.3125
- w_out: bfloat16 [768, 768], P('frame'), may hold values from -0.625 to 0.625
- w_up: bfloat16 [768, 3072], P('frame'), may hold values from -0.21875 to 0.21875
- w_down: bfloat16 [3072, 768], P('frame'), may hold values from -0.109375 to 0.109375
- up_bias: float32 [3072], replicated, may hold values from -3 to 3
- down_bias: float32 [768], replicated, may hold values from -2 to 2
- conv_first: bfloat16 [768, 72], P('frame'), may hold values from -0.078125 to 0.078125
- conv_first_bias: float32 [8], replicated, may hold values from -3 to 3
- conv_mid: float32 [3, 8, 72], replicated, may hold values from -0.75 to 0.75
- conv_mid_bias: float32 [3, 8], replicated, may hold values from -3 to 3
- cotangent: bfloat16 [4, 16, 8, 768], P('seq', 'frame'), may hold values from -6 to 6
Outputs:
- learned: float32 [4, 16, 8, 768], P('seq', 'frame')
- grad_input: float32 [4, 16, 64, 768], P('seq', 'frame')
- grad_qkv: float32 [768, 2304], P('frame')
- grad_out: float32 [768, 768], P('frame')
- grad_up: float32 [768, 3072], P('frame')
- grad_down: float32 [3072, 768], P('frame')
- grad_conv_first: float32 [768, 72], P('frame')
- grad_ln_gains: float32 [3, 768], replicated
- grad_ln_biases: float32 [3, 768], replicated
- grad_up_bias: float32 [3072], replicated
- grad_down_bias: float32 [768], replicated
- grad_conv_first_bias: float32 [8], replicated
- grad_conv_mid: float32 [3, 8, 72], replicated
- grad_conv_mid_bias: float32 [3, 8], replicated
The draws below stay inside these ranges and needn't reach their ends.
Inputs may be any that keep to these rules, and one draw needn't show every extreme that they name: `clip_id`: A clip is a run of whole frames, and its number is the index of its first frame within the sequence, so numbers never fall from one frame to the next. In one sequence, chosen by the seed, a single clip covers all 16 frames; in each of the others, clips are 4 to 36 frames long and the last clip is exactly the last 4 frames.
All inputs are finite; a program needn't handle non-finite values.
Results may differ from the reference program's by a relative error of at most 0.018.
Values may be sent and summed in bfloat16 or wider, within the bound.
No kernel may reach another device: no remote copies, remote signals or barrier semaphores. Data moves between devices by JAX's collectives and lax.ppermute only.
A program may use at most 192 MiB of HBM per device.

```python
import jax
import jax.numpy as jnp
from jax import lax

D = 768
HEADS = 12
HEAD_DIM = 64
FF = 3072
CH = 8
GRID = 8
PATCHES = 64
FRAMES = 16
SEQS = 4


def draw_clip_id(key, part):
    key = jax.random.fold_in(key, 7)
    key_long, key_lengths = jax.random.split(key)
    long_seq = jax.random.randint(key_long, (), 0, SEQS)
    count = FRAMES // 4
    lengths = jax.random.randint(key_lengths, (SEQS, count), 4, 33)
    starts = jnp.cumsum(lengths, axis=1).astype(jnp.int32)
    frame = jnp.arange(FRAMES, dtype=jnp.int32)
    hits = (starts[:, :, None] == frame[None, None, :]) & (starts[:, :, None] <= FRAMES - 8)
    begins = jnp.any(hits, axis=1) | (frame[None, :] == FRAMES - 4)
    marks = jnp.where(begins, frame[None, :], 0).astype(jnp.int32)
    ids = lax.cummax(marks, axis=1)
    rows = jnp.arange(SEQS, dtype=jnp.int32)
    ids = jnp.where(rows[:, None] == long_seq, 0, ids)
    return ids.astype(jnp.int32)


def block_levels(stream_key, shape, shards, smallest, high):
    level = 1.0
    for position, blocks in shards:
        draws = jax.random.uniform(jax.random.fold_in(jax.random.fold_in(stream_key, 6), position), (blocks,), jnp.float32, smallest / len(shards), high / len(shards))
        level = level * jnp.repeat(jnp.exp(draws), shape[position] // blocks).reshape((-1,) + (1,) * (len(shape) - 1 - position))
    return level


def gaussian(stream_key, extent, deviation, limit, cuts=(), kind=jnp.bfloat16):
    result = deviation * jax.random.normal(stream_key, extent, jnp.float32)
    if cuts:
        result = result * block_levels(stream_key, extent, cuts, -0.22, 0.18)
    return jnp.clip(result, -limit, limit).astype(kind)


def setup_inputs(seed: int = 0) -> dict:
    streams_of = jax.random.split(jax.random.key(seed), 16)
    return {
        "inputs": gaussian(streams_of[0], (SEQS, FRAMES, PATCHES, D), 1.0, 6.0, ((0, 4), (1, 8))),
        "clip_id": draw_clip_id(jax.random.fold_in(streams_of[15], 71), 0),
        "ln_gains": jnp.clip(1.0 + 0.15 * jax.random.normal(streams_of[2], (3, D), jnp.float32), 0.25, 1.75),
        "ln_biases": gaussian(streams_of[3], (3, D), 0.3, 2.0, (), jnp.float32),
        "w_qkv": gaussian(streams_of[4], (D, 3 * D), (D // 2) ** -0.5, 0.3125, ((0, 8),)),
        "w_out": gaussian(streams_of[5], (D, D), (max(1, D * 128 // (FRAMES * PATCHES))) ** -0.5, 0.625, ((0, 8),)),
        "w_up": gaussian(streams_of[6], (D, FF), D ** -0.5, 0.21875, ((0, 8),)),
        "w_down": gaussian(streams_of[7], (FF, D), FF ** -0.5, 0.109375, ((0, 8),)),
        "up_bias": gaussian(streams_of[8], (FF,), 0.5, 3.0, (), jnp.float32),
        "down_bias": gaussian(streams_of[9], (D,), 0.3, 2.0, (), jnp.float32),
        "conv_first": gaussian(streams_of[10], (D, 9 * CH), (9 * D) ** -0.5, 0.078125, ((0, 8),)),
        "conv_first_bias": gaussian(streams_of[11], (CH,), 0.5, 3.0, (), jnp.float32),
        "conv_mid": gaussian(streams_of[12], (3, CH, 9 * CH), (9 * CH) ** -0.5, 0.75, (), jnp.float32),
        "conv_mid_bias": gaussian(streams_of[13], (3, CH), 0.5, 3.0, (), jnp.float32),
        "cotangent": gaussian(streams_of[14], (SEQS, FRAMES, CH, D), 1.0, 6.0, ((0, 4), (1, 8))),
    }


EPSILON = 1e-06
FLOOR_SCORE = -1e+30
HIGHEST = lax.Precision.HIGHEST

@jax.custom_vjp
def low(v):
    return lax.optimization_barrier(v.astype(jnp.bfloat16)).astype(jnp.float32)

@jax.custom_vjp
def low_back(v):
    return v

def low_keep(v):
    return (low(v), None)

def low_pass(kept, grad):
    return (grad,)

def back_keep(v):
    return (v, None)

def back_low(kept, grad):
    return (low(grad),)
low.defvjp(low_keep, low_pass)
low_back.defvjp(back_keep, back_low)

def layer_norm(values, gain, shift):
    centre = lax.optimization_barrier(jnp.mean(values, axis=-1, keepdims=True))
    centred = values - centre
    variance = lax.optimization_barrier(jnp.mean(centred * centred, axis=-1, keepdims=True))
    return centred * lax.rsqrt(variance + EPSILON) * gain + shift

def gelu(values):
    return jax.nn.gelu(values, approximate=False)

def conv_grid(taps):
    side = taps.shape[1]
    width = taps.shape[-1] // 9
    padded = jnp.pad(taps, ((0, 0), (1, 1), (1, 1), (0, 0)))
    total = jnp.zeros(taps.shape[:-1] + (width,), taps.dtype)
    for tap in range(9):
        offset_row = tap // 3
        offset_column = tap % 3
        total = total + padded[:, offset_row:offset_row + side, offset_column:offset_column + side, tap * width:(tap + 1) * width]
    return total

def token_maps(first, conv_mid, conv_mid_bias):
    hidden = gelu(first)
    for layer in range(3):
        frames = hidden.shape[0]
        side = hidden.shape[1]
        flat = hidden.reshape(-1, hidden.shape[-1])
        taps = jnp.dot(flat, conv_mid[layer], precision=HIGHEST).reshape(frames, side, side, -1)
        hidden = conv_grid(taps) + conv_mid_bias[layer]
        if layer < 2:
            hidden = gelu(hidden)
    return jax.nn.sigmoid(hidden)

def pool_tokens(maps, features):
    return jnp.einsum('fpk,fpd->fkd', maps, features, precision=HIGHEST) / maps.shape[1]

def head_attention(head_query, head_key, head_value, clip_tokens):
    count = head_query.shape[0]
    blocks = count // 256
    scale = HEAD_DIM ** (-0.5)

    def one_block(inputs_pair):
        block_query, block_clip = inputs_pair
        raw_scores = jnp.dot(block_query, head_key.T, precision=HIGHEST) * scale
        scores = low_back(raw_scores)
        masked = jnp.where(block_clip[:, None] == clip_tokens[None, :], scores, FLOOR_SCORE)
        row_max = lax.optimization_barrier(jnp.max(masked, axis=-1, keepdims=True))
        shifted = jnp.exp(masked - row_max)
        prob = shifted / lax.optimization_barrier(jnp.sum(shifted, axis=-1, keepdims=True))
        return jnp.dot(low(prob), head_value, precision=HIGHEST)
    mixed = lax.map(jax.checkpoint(one_block), (head_query.reshape(blocks, 256, -1), clip_tokens.reshape(blocks, 256)))
    return mixed.reshape(count, -1)

def forward(tokens, clip_tokens, ln_gains, ln_biases, w_qkv, w_out, w_up, w_down, up_bias, down_bias, conv_first, conv_first_bias, conv_mid, conv_mid_bias):
    count = tokens.shape[0]
    normed_one = low(layer_norm(tokens, ln_gains[0], ln_biases[0]))
    projected = low(low_back(jnp.dot(normed_one, w_qkv, precision=HIGHEST)))

    def split_heads(block):
        return block.reshape(count, HEADS, HEAD_DIM).transpose(1, 0, 2)
    queries = split_heads(projected[:, :D])
    keys = split_heads(projected[:, D:2 * D])
    values = split_heads(projected[:, 2 * D:])

    def one_head(triple):
        return head_attention(triple[0], triple[1], triple[2], clip_tokens)
    mixed = lax.map(one_head, (queries, keys, values))
    attended = low(low_back(mixed.transpose(1, 0, 2).reshape(count, D)))
    after_attention = tokens + low_back(jnp.dot(attended, w_out, precision=HIGHEST))
    normed_two = low(layer_norm(after_attention, ln_gains[1], ln_biases[1]))
    pre_act = low_back(jnp.dot(normed_two, w_up, precision=HIGHEST) + up_bias)
    act_low = low(gelu(pre_act))
    block_out = after_attention + low_back(jnp.dot(act_low, w_down, precision=HIGHEST) + down_bias)
    normed_three = low(layer_norm(block_out, ln_gains[2], ln_biases[2]))
    tap_rows = jnp.dot(normed_three, conv_first, precision=HIGHEST).reshape(FRAMES, GRID, GRID, 9 * CH)
    first = low_back(conv_grid(tap_rows) + conv_first_bias)
    maps = token_maps(first, conv_mid, conv_mid_bias).reshape(FRAMES, PATCHES, CH)
    return pool_tokens(maps, block_out.reshape(FRAMES, PATCHES, D))

def reference(inputs, clip_id, ln_gains, ln_biases, w_qkv, w_out, w_up, w_down, up_bias, down_bias, conv_first, conv_first_bias, conv_mid, conv_mid_bias, cotangent):
    weights = tuple((item.astype(jnp.float32) for item in (ln_gains, ln_biases, w_qkv, w_out, w_up, w_down, up_bias, down_bias, conv_first, conv_first_bias, conv_mid, conv_mid_bias)))

    def one_sequence(carry, item):
        tokens_in, clips, grad_learned = item
        clip_tokens = jnp.repeat(clips, PATCHES, total_repeat_length=FRAMES * PATCHES)

        def apply_layer(tokens_arg, *params):
            return forward(tokens_arg, clip_tokens, *params)
        learned, back = jax.vjp(apply_layer, tokens_in, *weights)
        gradients = back(grad_learned)
        summed = tuple((held + fresh for held, fresh in zip(carry, gradients[1:])))
        return (summed, (learned, gradients[0]))
    tokens_all = inputs.astype(jnp.float32).reshape(SEQS, FRAMES * PATCHES, D)
    start = tuple((jnp.zeros_like(item) for item in weights))
    sums, (learned, grad_tokens) = lax.scan(one_sequence, start, (tokens_all, clip_id, cotangent.astype(jnp.float32)))
    grad_input = grad_tokens.reshape(SEQS, FRAMES, PATCHES, D)
    return (learned, grad_input, sums[2], sums[3], sums[4], sums[5], sums[8], sums[0], sums[1], sums[6], sums[7], sums[9], sums[10], sums[11])
```

```python
import functools

import jax
import jax.numpy as jnp
from jax import lax
from jax.experimental import pallas as pl
from jax.experimental.pallas import tpu as pltpu
from jax.sharding import PartitionSpec as P

HEADS = 12
HEAD_DIM = 64
CH = 8
GRID = 8

EPSILON = 1e-06
FLOOR_SCORE = -1e30
HIGHEST = lax.Precision.HIGHEST
AXES = ("seq", "frame")
PLANE_OF = (0, 1, 2, 3)
RANK_OF = (0, 1, 2, 3)
VMEM_LIMIT = 56 * 1024 * 1024
BF = jnp.bfloat16
F32 = jnp.float32


def norm_stats(values):
    centre = jnp.mean(values, axis=-1, keepdims=True)
    centred = values - centre
    variance = jnp.mean(centred * centred, axis=-1, keepdims=True)
    inverse = lax.rsqrt(variance + EPSILON)
    return centred * inverse, inverse


def norm_back(normed, inverse, gain, grad):
    scaled = grad * gain
    mean_scaled = jnp.mean(scaled, axis=-1, keepdims=True)
    mean_cross = jnp.mean(scaled * normed, axis=-1, keepdims=True)
    grad_values = inverse * (scaled - mean_scaled - normed * mean_cross)
    return grad_values, jnp.sum(grad * normed, axis=0), jnp.sum(grad, axis=0)


def gelu(values):
    return jax.nn.gelu(values, approximate=False)


def conv_grid(taps):
    side = taps.shape[1]
    width = taps.shape[-1] // 9
    padded = jnp.pad(taps, ((0, 0), (1, 1), (1, 1), (0, 0)))
    total = jnp.zeros(taps.shape[:-1] + (width,), taps.dtype)
    for tap in range(9):
        offset_row = tap // 3
        offset_column = tap % 3
        total = (
            total
            + padded[
                :,
                offset_row : offset_row + side,
                offset_column : offset_column + side,
                tap * width : (tap + 1) * width,
            ]
        )
    return total


def token_maps(first, conv_mid, conv_mid_bias):
    hidden = gelu(first)
    for layer in range(3):
        frames = hidden.shape[0]
        side = hidden.shape[1]
        flat = hidden.reshape(-1, hidden.shape[-1])
        taps = jnp.dot(flat, conv_mid[layer], precision=HIGHEST).reshape(frames, side, side, -1)
        hidden = conv_grid(taps) + conv_mid_bias[layer]
        if layer < 2:
            hidden = gelu(hidden)
    return jax.nn.sigmoid(hidden)


def pool_tokens(maps, features):
    return jnp.einsum("fpk,fpd->fkd", maps, features, precision=HIGHEST) / maps.shape[1]


def dot(left, right, left_dim=1, right_dim=0):
    return lax.dot_general(
        left, right, (((left_dim,), (right_dim,)), ((), ())), preferred_element_type=F32
    )


def attend_kernel(heads, scale, q_ref, kv_ref, qclip_ref, kclip_ref, mixed_ref, log_ref):
    width = heads * HEAD_DIM
    same = kclip_ref[...] == qclip_ref[...]
    for head in range(heads):
        lanes = slice(head * HEAD_DIM, (head + 1) * HEAD_DIM)
        value_lanes = slice(width + head * HEAD_DIM, width + (head + 1) * HEAD_DIM)
        scores = dot(kv_ref[:, lanes], q_ref[:, lanes], 1, 1) * scale
        scores = jnp.where(same, scores, FLOOR_SCORE)
        top = jnp.max(scores, axis=0, keepdims=True)
        shifted = jnp.exp(scores - top)
        total = jnp.sum(shifted, axis=0, keepdims=True)
        prob = (shifted * (1.0 / total)).astype(BF)
        mixed = dot(kv_ref[:, value_lanes], prob, 0, 0)
        mixed_ref[head * HEAD_DIM : (head + 1) * HEAD_DIM, :] = mixed.astype(BF)
        log_ref[head : head + 1, :] = top + jnp.log(total)


def attend_back_kernel(
    heads, scale, q_ref, kv_ref, grad_ref, log_ref, qclip_ref, kclip_ref, dq_ref, dkv_ref
):
    width = heads * HEAD_DIM
    same = kclip_ref[...] == qclip_ref[...]

    @pl.when(pl.program_id(0) == 0)
    def _():
        dkv_ref[...] = jnp.zeros_like(dkv_ref)

    key_parts = []
    value_parts = []
    for head in range(heads):
        lanes = slice(head * HEAD_DIM, (head + 1) * HEAD_DIM)
        value_lanes = slice(width + head * HEAD_DIM, width + (head + 1) * HEAD_DIM)
        scores = dot(kv_ref[:, lanes], q_ref[:, lanes], 1, 1) * scale
        scores = jnp.where(same, scores, FLOOR_SCORE)
        prob = jnp.exp(scores - log_ref[head : head + 1, :])
        grad_prob = dot(kv_ref[:, value_lanes], grad_ref[:, lanes], 1, 1)
        delta = jnp.sum(prob * grad_prob, axis=0, keepdims=True)
        grad_score = (prob * (grad_prob - delta)).astype(BF)
        grad_query = dot(kv_ref[:, lanes], grad_score, 0, 0) * scale
        dq_ref[head * HEAD_DIM : (head + 1) * HEAD_DIM, :] = grad_query.astype(BF)
        key_parts.append(dot(grad_score, q_ref[:, lanes]) * scale)
        value_parts.append(dot(prob.astype(BF), grad_ref[:, lanes]))
    dkv_ref[...] += jnp.concatenate(key_parts + value_parts, axis=1)


def query_block(count, keys):
    return min(count, 256) if keys <= 1024 else 128


def attend(queries, keyvals, query_clip, key_clip):
    count, width = queries.shape
    keys = keyvals.shape[0]
    heads = width // HEAD_DIM
    block = query_block(count, keys)
    return pl.pallas_call(
        functools.partial(attend_kernel, heads, HEAD_DIM ** (-0.5)),
        grid=(count // block,),
        in_specs=[
            pl.BlockSpec((block, width), lambda i: (i, 0)),
            pl.BlockSpec((keys, 2 * width), lambda i: (0, 0)),
            pl.BlockSpec((1, block), lambda i: (0, i)),
            pl.BlockSpec((keys, 1), lambda i: (0, 0)),
        ],
        out_specs=[
            pl.BlockSpec((width, block), lambda i: (0, i)),
            pl.BlockSpec((8, block), lambda i: (0, i)),
        ],
        out_shape=[
            jax.ShapeDtypeStruct((width, count), BF),
            jax.ShapeDtypeStruct((8, count), F32),
        ],
        compiler_params=pltpu.CompilerParams(vmem_limit_bytes=VMEM_LIMIT),
        name="attend",
    )(queries, keyvals, query_clip, key_clip)


def attend_back(queries, keyvals, grads, logs, query_clip, key_clip):
    count, width = queries.shape
    keys = keyvals.shape[0]
    heads = width // HEAD_DIM
    block = query_block(count, keys)
    return pl.pallas_call(
        functools.partial(attend_back_kernel, heads, HEAD_DIM ** (-0.5)),
        grid=(count // block,),
        in_specs=[
            pl.BlockSpec((block, width), lambda i: (i, 0)),
            pl.BlockSpec((keys, 2 * width), lambda i: (0, 0)),
            pl.BlockSpec((block, width), lambda i: (i, 0)),
            pl.BlockSpec((8, block), lambda i: (0, i)),
            pl.BlockSpec((1, block), lambda i: (0, i)),
            pl.BlockSpec((keys, 1), lambda i: (0, 0)),
        ],
        out_specs=[
            pl.BlockSpec((width, block), lambda i: (0, i)),
            pl.BlockSpec((keys, 2 * width), lambda i: (0, 0)),
        ],
        out_shape=[
            jax.ShapeDtypeStruct((width, count), BF),
            jax.ShapeDtypeStruct((keys, 2 * width), F32),
        ],
        compiler_params=pltpu.CompilerParams(vmem_limit_bytes=VMEM_LIMIT),
        name="attend_back",
    )(queries, keyvals, grads, logs, query_clip, key_clip)


def shards(
    ranks,
    frame_size,
    inputs,
    clip_id,
    ln_gains,
    ln_biases,
    w_qkv,
    w_out,
    w_up,
    w_down,
    up_bias,
    down_bias,
    conv_first,
    conv_first_bias,
    conv_mid,
    conv_mid_bias,
    cotangent,
):
    lows = frame_size // ranks
    frames_dev = inputs.shape[1]
    patches = inputs.shape[2]
    width = inputs.shape[3]
    rows = frames_dev * patches
    hidden = up_bias.shape[0]
    quarter = width // ranks
    hidden_quarter = hidden // ranks
    row_shard = width // frame_size
    rank = lax.axis_index("seq")
    place = lax.axis_index("frame")
    high = place // lows
    low = place % lows

    def permute(array, target):
        pairs = []
        for seq in range(ranks):
            for hi in range(ranks):
                for lo in range(lows):
                    to_seq, to_hi, to_lo = target(seq, hi, lo)
                    pairs.append(
                        (
                            seq * frame_size + hi * lows + lo,
                            to_seq * frame_size + to_hi * lows + to_lo,
                        )
                    )
        return lax.ppermute(array, AXES, pairs)

    def across(array, bits):
        return permute(array, lambda seq, hi, lo: (seq ^ bits, hi, lo))

    def along_high(array, step):
        return permute(array, lambda seq, hi, lo: (seq, (hi + step) % ranks, lo))

    def along_low(array, step):
        return permute(array, lambda seq, hi, lo: (seq, hi, (lo + step) % lows))

    def to_planes(array):
        return permute(array, lambda seq, hi, lo: (RANK_OF[hi], PLANE_OF[seq], lo))

    def from_planes(array):
        return permute(
            array, lambda seq, hi, lo: (PLANE_OF.index(hi), RANK_OF.index(seq), lo)
        )

    def gather_tokens(block):
        far = across(block, 2)
        near = across(block, 1)
        both = across(far, 1)
        return jnp.concatenate([block, near, far, both], axis=0)

    def scatter_tokens(partial):
        blocks = partial.astype(BF).reshape(ranks, rows, partial.shape[1])
        arrived_far = across(blocks[3], 1)
        arrived_near = across(blocks[1], 1)
        far = partial[2 * rows : 3 * rows] + arrived_far.astype(F32)
        arrived = across(far.astype(BF), 2)
        return partial[:rows] + arrived_near.astype(F32) + arrived.astype(F32)

    def gather_rows(block):
        if lows != 2:
            return lax.all_gather(block, "frame", axis=0, tiled=True)
        found = [block] + [along_high(block, step) for step in range(1, ranks)]
        other = [along_low(item, 1) for item in found]
        stacked = jnp.stack(found)
        stacked_other = jnp.stack(other)
        pieces = []
        for hi in range(ranks):
            index = (high - hi) % ranks
            mine = lax.dynamic_index_in_dim(stacked, index, 0, False)
            theirs = lax.dynamic_index_in_dim(stacked_other, index, 0, False)
            pieces.append(jnp.where(low == 0, mine, theirs))
            pieces.append(jnp.where(low == 0, theirs, mine))
        return jnp.concatenate(pieces, axis=0)

    def scatter_rows(partial):
        if lows != 2:
            return lax.psum_scatter(
                partial.astype(BF), "frame", scatter_dimension=0, tiled=True
            ).astype(F32)
        count = partial.shape[0] // frame_size
        columns = partial.shape[1]
        split = partial.reshape(ranks, lows, count, columns)
        kept = lax.dynamic_index_in_dim(split, low, 1, False)
        sent = lax.dynamic_index_in_dim(split, 1 - low, 1, False).astype(BF)
        half = kept + along_low(sent, 1).astype(F32)
        total = lax.dynamic_index_in_dim(half, high, 0, False)
        half_low = half.astype(BF)
        for step in range(1, ranks):
            piece = lax.dynamic_index_in_dim(half_low, (high + step) % ranks, 0, False)
            total = total + along_high(piece, step).astype(F32)
        return total

    def in_rank_order(items):
        stacked = jnp.stack(items)
        return [
            lax.dynamic_index_in_dim(stacked, rank ^ index, 0, False) for index in range(ranks)
        ]

    def gather_ranks(block):
        far = across(block, 2)
        near = across(block, 1)
        both = across(far, 1)
        return in_rank_order([block, near, far, both])

    token_rows = inputs[0].reshape(rows, width)
    grad_rows = cotangent[0].reshape(frames_dev * CH, width)
    frame_count = clip_id.shape[1]
    clip_rows = jnp.pad(
        clip_id.astype(BF), ((0, 15), (0, width - frame_count))
    )
    moved = to_planes(jnp.concatenate([token_rows, grad_rows, clip_rows], axis=0))
    tokens = moved[:rows].astype(F32)
    grad_learned = moved[rows : rows + frames_dev * CH].astype(F32)
    clips = moved[rows + frames_dev * CH, :frame_count].astype(jnp.int32)

    own_qkv = lax.dynamic_index_in_dim(
        w_qkv.reshape(row_shard, 3, ranks, quarter), rank, 2, False
    ).reshape(row_shard, 3 * quarter)
    qkv_quarter = gather_rows(own_qkv)
    unit = hidden // (frame_size * ranks)
    columns = jnp.arange(hidden_quarter, dtype=jnp.int32)
    wanted = (columns // unit) * (unit * ranks) + rank * unit + columns % unit
    choose = (jnp.arange(hidden, dtype=jnp.int32)[:, None] == wanted[None, :]).astype(BF)
    own_up = dot(w_up, choose).astype(BF)
    own_down = lax.dynamic_slice_in_dim(w_down, rank * unit, unit, 0)
    own_out = lax.dynamic_slice_in_dim(w_out, rank * quarter, quarter, 1)
    packed = gather_rows(jnp.concatenate([own_up, own_down, own_out, conv_first], axis=1))
    up_quarter = packed[:, :hidden_quarter]
    down_quarter = packed[:, hidden_quarter : hidden_quarter + width]
    out_columns = packed[:, hidden_quarter + width : hidden_quarter + width + quarter]
    full_conv = packed[:, hidden_quarter + width + quarter :]

    def swap_ranks(array):
        split = array.reshape(ranks, quarter, array.shape[1])
        found = []
        for bits in range(ranks):
            piece = lax.dynamic_index_in_dim(split, rank ^ bits, 0, False)
            found.append(across(piece, bits) if bits else piece)
        return in_rank_order(found)

    out_quarter = jnp.concatenate(swap_ranks(out_columns), axis=1)
    up_bias_quarter = lax.dynamic_index_in_dim(
        up_bias.reshape(frame_size, ranks, unit), rank, 1, False
    ).reshape(1, hidden_quarter)

    frame_ids = jnp.arange(frame_count, dtype=jnp.int32)

    def clip_tokens(lo):
        blocks = []
        inverse = jnp.array([RANK_OF.index(item) for item in range(ranks)], jnp.int32)
        for bits in range(ranks):
            hi = lax.dynamic_index_in_dim(inverse, rank ^ bits, 0, False)
            for frame in range(frames_dev):
                blocks.append((hi * lows + lo) * frames_dev + frame)
        wanted_frames = jnp.stack(blocks)
        found = jnp.sum(
            jnp.where(wanted_frames[:, None] == frame_ids[None, :], clips[None, :], 0), axis=1
        )
        return jnp.broadcast_to(found[:, None], (found.shape[0], patches)).reshape(-1)

    query_clip = clip_tokens(low)
    key_clip = jnp.concatenate(
        [query_clip] + [clip_tokens((low - step) % lows) for step in range(1, lows)]
    )
    query_clip = query_clip[None, :]
    key_clip = key_clip[:, None]

    normed_one, inverse_one = norm_stats(tokens)
    all_one = gather_tokens((normed_one * ln_gains[0] + ln_biases[0]).astype(BF))
    projected = dot(all_one, qkv_quarter).astype(BF)
    queries = projected[:, :quarter]
    own_keyvals = projected[:, quarter:]
    keyvals = jnp.concatenate(
        [own_keyvals] + [along_low(own_keyvals, step) for step in range(1, lows)], axis=0
    )
    attended, logs = attend(queries, keyvals, query_clip, key_clip)
    after_attention = tokens + scatter_tokens(dot(attended, out_quarter, 0, 0))
    normed_two, inverse_two = norm_stats(after_attention)
    all_two = gather_tokens((normed_two * ln_gains[1] + ln_biases[1]).astype(BF))
    pre_act = dot(all_two, up_quarter) + up_bias_quarter
    act_low = gelu(pre_act).astype(BF)
    block_out = after_attention + scatter_tokens(dot(act_low, down_quarter)) + down_bias

    normed_three, inverse_three = norm_stats(block_out)
    normed_three_low = (normed_three * ln_gains[2] + ln_biases[2]).astype(BF)
    tap_rows = dot(normed_three_low, full_conv).reshape(frames_dev, GRID, GRID, 9 * CH)
    first = conv_grid(tap_rows) + conv_first_bias
    features = block_out.reshape(frames_dev, patches, width)

    def tail(first_arg, features_arg, mid_arg, mid_bias_arg):
        maps = token_maps(first_arg, mid_arg, mid_bias_arg).reshape(frames_dev, patches, CH)
        return pool_tokens(maps, features_arg)

    learned, tail_back = jax.vjp(tail, first, features, conv_mid, conv_mid_bias)
    grad_first, grad_pool, grad_mid, grad_mid_bias = tail_back(
        grad_learned.reshape(frames_dev, CH, width)
    )
    grad_first_low = grad_first.astype(BF)
    grad_first_bias = jnp.sum(grad_first_low.astype(F32), axis=(0, 1, 2))
    spread_unused, spread_back = jax.vjp(conv_grid, tap_rows)
    spread = spread_back(grad_first_low.astype(F32))[0].reshape(rows, 9 * CH).astype(BF)
    grad_conv = dot(normed_three_low, spread, 0, 0)
    grad_normed_three = dot(spread, full_conv, 1, 1)
    grad_block, grad_gain_three, grad_shift_three = norm_back(
        normed_three, inverse_three, ln_gains[2], grad_normed_three
    )
    grad_block = grad_block + grad_pool.reshape(rows, width)
    grad_mlp = grad_block.astype(BF)
    grad_down_bias = jnp.sum(grad_mlp.astype(F32), axis=0)

    all_mlp = gather_tokens(grad_mlp)
    grad_act = dot(all_mlp, down_quarter, 1, 1)
    gelu_unused, gelu_back = jax.vjp(gelu, pre_act)
    grad_pre = gelu_back(grad_act)[0].astype(BF)
    grad_up_bias = jnp.sum(grad_pre.astype(F32), axis=0)
    grad_normed_two = scatter_tokens(dot(grad_pre, up_quarter, 1, 1))
    grad_down = dot(act_low, all_mlp, 0, 0)
    grad_up = dot(all_two, grad_pre, 0, 0)
    mlp_share = scatter_rows(jnp.concatenate([grad_up, grad_down, grad_conv], axis=1))
    grad_after, grad_gain_two, grad_shift_two = norm_back(
        normed_two, inverse_two, ln_gains[1], grad_normed_two
    )
    grad_after = grad_after + grad_block

    all_branch = gather_tokens(grad_after.astype(BF))
    grad_attended = dot(all_branch, out_quarter, 1, 1).astype(BF)
    grad_out = dot(attended, all_branch)
    grad_queries, grad_keyvals = attend_back(
        queries, keyvals, grad_attended, logs, query_clip, key_clip
    )
    own_count = ranks * rows
    own_grads = grad_keyvals[:own_count]
    for step in range(1, lows):
        piece = grad_keyvals[step * own_count : (step + 1) * own_count].astype(BF)
        own_grads = own_grads + along_low(piece, -step).astype(F32)
    grad_projected = jnp.concatenate([grad_queries.T, own_grads.astype(BF)], axis=1)
    grad_qkv = dot(all_one, grad_projected, 0, 0)
    grad_normed_one = scatter_tokens(dot(grad_projected, qkv_quarter, 1, 1))
    grad_out_columns = jnp.concatenate(
        swap_ranks_rows(grad_out.astype(BF), ranks, quarter, rank, across), axis=0
    )
    qkv_share = scatter_rows(jnp.concatenate([grad_qkv, grad_out_columns.astype(F32)], axis=1))
    grad_tokens, grad_gain_one, grad_shift_one = norm_back(
        normed_one, inverse_one, ln_gains[0], grad_normed_one
    )
    grad_input = from_planes((grad_after + grad_tokens).astype(BF)).astype(F32)
    learned = from_planes(learned.astype(BF)).astype(F32)

    mlp_parts = gather_ranks(mlp_share.astype(BF))
    qkv_parts = gather_ranks(qkv_share.astype(BF))
    sum_up = (
        jnp.stack([part[:, :hidden_quarter] for part in mlp_parts])
        .reshape(ranks, row_shard, frame_size, unit)
        .transpose(1, 2, 0, 3)
        .reshape(row_shard, hidden)
        .astype(F32)
    )
    sum_down = jnp.concatenate(
        [part[:, hidden_quarter : hidden_quarter + width] for part in mlp_parts], axis=0
    ).astype(F32)
    sum_conv = sum(part[:, hidden_quarter + width :].astype(F32) for part in mlp_parts)
    sum_qkv = (
        jnp.stack([part[:, : 3 * quarter] for part in qkv_parts])
        .reshape(ranks, row_shard, 3, quarter)
        .transpose(1, 2, 0, 3)
        .reshape(row_shard, 3 * width)
        .astype(F32)
    )
    sum_out = jnp.concatenate([part[:, 3 * quarter :] for part in qkv_parts], axis=1).astype(F32)

    up_bias_terms = lax.dynamic_update_index_in_dim(
        jnp.zeros((frame_size, ranks, unit), F32),
        grad_up_bias.reshape(frame_size, unit),
        rank,
        1,
    )
    small = [
        jnp.stack([grad_gain_one, grad_gain_two, grad_gain_three]),
        jnp.stack([grad_shift_one, grad_shift_two, grad_shift_three]),
        up_bias_terms,
        grad_down_bias,
        grad_first_bias,
        grad_mid,
        grad_mid_bias,
    ]
    summed = lax.psum(jnp.concatenate([item.reshape(-1) for item in small]), AXES)
    results = []
    start = 0
    for item in small:
        results.append(summed[start : start + item.size].reshape(item.shape))
        start += item.size
    return (
        learned.reshape(1, frames_dev, CH, width),
        grad_input.reshape(1, frames_dev, patches, width),
        sum_qkv,
        sum_out,
        sum_up,
        sum_down,
        sum_conv,
        results[0],
        results[1],
        results[2].reshape(hidden),
        results[3],
        results[4],
        results[5],
        results[6],
    )


def swap_ranks_rows(array, ranks, quarter, rank, across):
    split = array.reshape(quarter, ranks, quarter).transpose(1, 0, 2)
    found = []
    for bits in range(ranks):
        piece = lax.dynamic_index_in_dim(split, rank ^ bits, 0, False)
        found.append(across(piece, bits) if bits else piece)
    stacked = jnp.stack(found)
    return [lax.dynamic_index_in_dim(stacked, rank ^ index, 0, False) for index in range(ranks)]


def solution(mesh):
    placed = (
        P("seq", "frame", None, None),
        P("seq", None),
        P(),
        P(),
        P("frame", None),
        P("frame", None),
        P("frame", None),
        P("frame", None),
        P(),
        P(),
        P("frame", None),
        P(),
        P(),
        P(),
        P("seq", "frame", None, None),
    )
    return jax.shard_map(
        functools.partial(shards, mesh.shape["seq"], mesh.shape["frame"]),
        mesh=mesh,
        in_specs=placed,
        out_specs=(
            P("seq", "frame", None, None),
            P("seq", "frame", None, None),
            P("frame", None),
            P("frame", None),
            P("frame", None),
            P("frame", None),
            P("frame", None),
            P(),
            P(),
            P(),
            P(),
            P(),
            P(),
            P(),
        ),
        check_vma=False,
    )
```

```python
import functools

import jax
import jax.numpy as jnp
from jax import lax
from jax.experimental import pallas as pl
from jax.experimental.pallas import tpu as pltpu
from jax.sharding import PartitionSpec as P

HEADS = 12
HEAD_DIM = 64
CH = 8
GRID = 8

EPSILON = 1e-06
FLOOR_SCORE = -1e30
HIGHEST = lax.Precision.HIGHEST
AXES = ("seq", "frame")
PLANE_OF = (0, 1, 2, 3)
RANK_OF = (0, 1, 2, 3)
VMEM_LIMIT = 56 * 1024 * 1024
BF = jnp.bfloat16
F32 = jnp.float32


def norm_stats(values):
    centre = jnp.mean(values, axis=-1, keepdims=True)
    centred = values - centre
    variance = jnp.mean(centred * centred, axis=-1, keepdims=True)
    inverse = lax.rsqrt(variance + EPSILON)
    return centred * inverse, inverse


def norm_back(normed, inverse, gain, grad):
    scaled = grad * gain
    mean_scaled = jnp.mean(scaled, axis=-1, keepdims=True)
    mean_cross = jnp.mean(scaled * normed, axis=-1, keepdims=True)
    grad_values = inverse * (scaled - mean_scaled - normed * mean_cross)
    return grad_values, jnp.sum(grad * normed, axis=0), jnp.sum(grad, axis=0)


def gelu(values):
    return jax.nn.gelu(values, approximate=False)


def conv_grid(taps):
    side = taps.shape[1]
    width = taps.shape[-1] // 9
    padded = jnp.pad(taps, ((0, 0), (1, 1), (1, 1), (0, 0)))
    total = jnp.zeros(taps.shape[:-1] + (width,), taps.dtype)
    for tap in range(9):
        offset_row = tap // 3
        offset_column = tap % 3
        total = (
            total
            + padded[
                :,
                offset_row : offset_row + side,
                offset_column : offset_column + side,
                tap * width : (tap + 1) * width,
            ]
        )
    return total


def token_maps(first, conv_mid, conv_mid_bias):
    hidden = gelu(first)
    for layer in range(3):
        frames = hidden.shape[0]
        side = hidden.shape[1]
        flat = hidden.reshape(-1, hidden.shape[-1])
        taps = jnp.dot(flat, conv_mid[layer], precision=HIGHEST).reshape(frames, side, side, -1)
        hidden = conv_grid(taps) + conv_mid_bias[layer]
        if layer < 2:
            hidden = gelu(hidden)
    return jax.nn.sigmoid(hidden)


def pool_tokens(maps, features):
    return jnp.einsum("fpk,fpd->fkd", maps, features, precision=HIGHEST) / maps.shape[1]


def dot(left, right, left_dim=1, right_dim=0):
    return lax.dot_general(
        left, right, (((left_dim,), (right_dim,)), ((), ())), preferred_element_type=F32
    )


def attend_kernel(heads, scale, q_ref, kv_ref, qclip_ref, kclip_ref, mixed_ref, log_ref):
    width = heads * HEAD_DIM
    same = kclip_ref[...] == qclip_ref[...]
    for head in range(heads):
        lanes = slice(head * HEAD_DIM, (head + 1) * HEAD_DIM)
        value_lanes = slice(width + head * HEAD_DIM, width + (head + 1) * HEAD_DIM)
        scores = dot(kv_ref[:, lanes], q_ref[:, lanes], 1, 1) * scale
        scores = jnp.where(same, scores, FLOOR_SCORE)
        top = jnp.max(scores, axis=0, keepdims=True)
        shifted = jnp.exp(scores - top)
        total = jnp.sum(shifted, axis=0, keepdims=True)
        prob = (shifted * (1.0 / total)).astype(BF)
        mixed = dot(kv_ref[:, value_lanes], prob, 0, 0)
        mixed_ref[head * HEAD_DIM : (head + 1) * HEAD_DIM, :] = mixed.astype(BF)
        log_ref[head : head + 1, :] = top + jnp.log(total)


def attend_back_kernel(
    heads, scale, q_ref, kv_ref, grad_ref, log_ref, qclip_ref, kclip_ref, dq_ref, dkv_ref
):
    width = heads * HEAD_DIM
    same = kclip_ref[...] == qclip_ref[...]

    @pl.when(pl.program_id(0) == 0)
    def _():
        dkv_ref[...] = jnp.zeros_like(dkv_ref)

    key_parts = []
    value_parts = []
    for head in range(heads):
        lanes = slice(head * HEAD_DIM, (head + 1) * HEAD_DIM)
        value_lanes = slice(width + head * HEAD_DIM, width + (head + 1) * HEAD_DIM)
        scores = dot(kv_ref[:, lanes], q_ref[:, lanes], 1, 1) * scale
        scores = jnp.where(same, scores, FLOOR_SCORE)
        prob = jnp.exp(scores - log_ref[head : head + 1, :])
        grad_prob = dot(kv_ref[:, value_lanes], grad_ref[:, lanes], 1, 1)
        delta = jnp.sum(prob * grad_prob, axis=0, keepdims=True)
        grad_score = (prob * (grad_prob - delta)).astype(BF)
        grad_query = dot(kv_ref[:, lanes], grad_score, 0, 0) * scale
        dq_ref[head * HEAD_DIM : (head + 1) * HEAD_DIM, :] = grad_query.astype(BF)
        key_parts.append(dot(grad_score, q_ref[:, lanes]) * scale)
        value_parts.append(dot(prob.astype(BF), grad_ref[:, lanes]))
    dkv_ref[...] += jnp.concatenate(key_parts + value_parts, axis=1)


def query_block(count, keys):
    return min(count, 256) if keys <= 1024 else 128


def attend(queries, keyvals, query_clip, key_clip):
    count, width = queries.shape
    keys = keyvals.shape[0]
    heads = width // HEAD_DIM
    block = query_block(count, keys)
    return pl.pallas_call(
        functools.partial(attend_kernel, heads, HEAD_DIM ** (-0.5)),
        grid=(count // block,),
        in_specs=[
            pl.BlockSpec((block, width), lambda i: (i, 0)),
            pl.BlockSpec((keys, 2 * width), lambda i: (0, 0)),
            pl.BlockSpec((1, block), lambda i: (0, i)),
            pl.BlockSpec((keys, 1), lambda i: (0, 0)),
        ],
        out_specs=[
            pl.BlockSpec((width, block), lambda i: (0, i)),
            pl.BlockSpec((8, block), lambda i: (0, i)),
        ],
        out_shape=[
            jax.ShapeDtypeStruct((width, count), BF),
            jax.ShapeDtypeStruct((8, count), F32),
        ],
        compiler_params=pltpu.CompilerParams(vmem_limit_bytes=VMEM_LIMIT),
        name="attend",
    )(queries, keyvals, query_clip, key_clip)


def attend_back(queries, keyvals, grads, logs, query_clip, key_clip):
    count, width = queries.shape
    keys = keyvals.shape[0]
    heads = width // HEAD_DIM
    block = query_block(count, keys)
    return pl.pallas_call(
        functools.partial(attend_back_kernel, heads, HEAD_DIM ** (-0.5)),
        grid=(count // block,),
        in_specs=[
            pl.BlockSpec((block, width), lambda i: (i, 0)),
            pl.BlockSpec((keys, 2 * width), lambda i: (0, 0)),
            pl.BlockSpec((block, width), lambda i: (i, 0)),
            pl.BlockSpec((8, block), lambda i: (0, i)),
            pl.BlockSpec((1, block), lambda i: (0, i)),
            pl.BlockSpec((keys, 1), lambda i: (0, 0)),
        ],
        out_specs=[
            pl.BlockSpec((width, block), lambda i: (0, i)),
            pl.BlockSpec((keys, 2 * width), lambda i: (0, 0)),
        ],
        out_shape=[
            jax.ShapeDtypeStruct((width, count), BF),
            jax.ShapeDtypeStruct((keys, 2 * width), F32),
        ],
        compiler_params=pltpu.CompilerParams(vmem_limit_bytes=VMEM_LIMIT),
        name="attend_back",
    )(queries, keyvals, grads, logs, query_clip, key_clip)


def place_kernel(size, place_ref, *refs):
    pieces, out_ref = refs[:-1], refs[-1]
    index = 0
    for piece in pieces:
        for start in range(0, piece.shape[0], size):
            place = pl.multiple_of(place_ref[index] * size, size)
            out_ref[pl.ds(place, size), :] = piece[start : start + size, :]
            index += 1


def place_rows(pieces, places, size):
    columns = pieces[0].shape[1]
    return pl.pallas_call(
        functools.partial(place_kernel, size),
        in_specs=[pl.BlockSpec(memory_space=pltpu.SMEM)]
        + [pl.BlockSpec(memory_space=pltpu.VMEM)] * len(pieces),
        out_specs=pl.BlockSpec(memory_space=pltpu.VMEM),
        out_shape=jax.ShapeDtypeStruct((len(places) * size, columns), pieces[0].dtype),
        name="place_rows",
    )(jnp.stack(places), *pieces)


def ordered(refs, rank, lanes):
    blocks = [ref[:, lanes].astype(F32) for ref in refs]
    result = []
    for index in range(len(refs)):
        found = blocks[0]
        for bits in range(1, len(refs)):
            found = jnp.where(rank == index ^ bits, blocks[bits], found)
        result.append(found)
    return result


def finish_mlp_kernel(ranks, hidden_quarter, width, unit, rank_ref, *refs):
    parts = refs[:ranks]
    up_ref, down_ref, conv_ref = refs[ranks:]
    rank = rank_ref[0]
    ups = ordered(parts, rank, slice(0, hidden_quarter))
    pieces = []
    for group in range(hidden_quarter // unit):
        for block in ups:
            pieces.append(block[:, group * unit : (group + 1) * unit])
    up_ref[...] = jnp.concatenate(pieces, axis=1)
    size = parts[0].shape[0]
    downs = ordered(parts, rank, slice(hidden_quarter, hidden_quarter + width))
    for index in range(ranks):
        down_ref[index * size : (index + 1) * size, :] = downs[index]
    convs = ordered(parts, rank, slice(hidden_quarter + width, parts[0].shape[1]))
    total = convs[0]
    for block in convs[1:]:
        total = total + block
    conv_ref[...] = total


def finish_qkv_kernel(ranks, quarter, rank_ref, *refs):
    parts = refs[:ranks]
    qkv_ref, out_ref = refs[ranks:]
    rank = rank_ref[0]
    blocks = ordered(parts, rank, slice(0, parts[0].shape[1]))
    pieces = []
    for part in range(3):
        for block in blocks:
            pieces.append(block[:, part * quarter : (part + 1) * quarter])
    qkv_ref[...] = jnp.concatenate(pieces, axis=1)
    out_ref[...] = jnp.concatenate([block[:, 3 * quarter :] for block in blocks], axis=1)


def finish(kernel, rank, parts, shapes, name):
    return pl.pallas_call(
        kernel,
        in_specs=[pl.BlockSpec(memory_space=pltpu.SMEM)]
        + [pl.BlockSpec(memory_space=pltpu.VMEM)] * len(parts),
        out_specs=[pl.BlockSpec(memory_space=pltpu.VMEM)] * len(shapes),
        out_shape=[jax.ShapeDtypeStruct(shape, F32) for shape in shapes],
        compiler_params=pltpu.CompilerParams(vmem_limit_bytes=VMEM_LIMIT),
        name=name,
    )(rank.reshape(1), *parts)


def shards_general(
    ranks,
    frame_size,
    inputs,
    clip_id,
    ln_gains,
    ln_biases,
    w_qkv,
    w_out,
    w_up,
    w_down,
    up_bias,
    down_bias,
    conv_first,
    conv_first_bias,
    conv_mid,
    conv_mid_bias,
    cotangent,
):
    lows = frame_size // ranks
    frames_dev = inputs.shape[1]
    patches = inputs.shape[2]
    width = inputs.shape[3]
    rows = frames_dev * patches
    hidden = up_bias.shape[0]
    quarter = width // ranks
    hidden_quarter = hidden // ranks
    row_shard = width // frame_size
    rank = lax.axis_index("seq")
    place = lax.axis_index("frame")
    high = place // lows
    low = place % lows

    def permute(array, target):
        pairs = []
        for seq in range(ranks):
            for hi in range(ranks):
                for lo in range(lows):
                    to_seq, to_hi, to_lo = target(seq, hi, lo)
                    pairs.append(
                        (
                            seq * frame_size + hi * lows + lo,
                            to_seq * frame_size + to_hi * lows + to_lo,
                        )
                    )
        return lax.ppermute(array, AXES, pairs)

    def across(array, bits):
        return permute(array, lambda seq, hi, lo: (seq ^ bits, hi, lo))

    def along_high(array, step):
        return permute(array, lambda seq, hi, lo: (seq, (hi + step) % ranks, lo))

    def along_low(array, step):
        return permute(array, lambda seq, hi, lo: (seq, hi, (lo + step) % lows))

    def to_planes(array):
        return permute(array, lambda seq, hi, lo: (RANK_OF[hi], PLANE_OF[seq], lo))

    def from_planes(array):
        return permute(
            array, lambda seq, hi, lo: (PLANE_OF.index(hi), RANK_OF.index(seq), lo)
        )

    def flip_high(array, bits):
        return permute(array, lambda seq, hi, lo: (seq, hi ^ bits, lo))

    def gather_tokens(block):
        far = across(block, 2)
        near = across(block, 1)
        both = across(far, 1)
        return jnp.concatenate([block, near, far, both], axis=0)

    def scatter_tokens(partial):
        blocks = partial.astype(BF).reshape(ranks, rows, partial.shape[1])
        arrived_far = across(blocks[3], 1)
        arrived_near = across(blocks[1], 1)
        far = partial[2 * rows : 3 * rows] + arrived_far.astype(F32)
        arrived = across(far.astype(BF), 2)
        return partial[:rows] + arrived_near.astype(F32) + arrived.astype(F32)

    half_rows = rows // 2

    def gather_plane(block):
        if lows != 2:
            own = gather_tokens(block)
            return jnp.concatenate(
                [own] + [along_low(own, step) for step in range(1, lows)], axis=0
            )
        far = across(block, 2)
        side = along_low(block, 1)
        near = across(block, 1)
        corner = jnp.concatenate(
            [along_low(far[:half_rows], 1), across(side[half_rows:], 2)], axis=0
        )
        return jnp.concatenate(
            [
                block,
                near,
                far,
                across(far, 1),
                side,
                across(side, 1),
                corner,
                across(corner, 1),
            ],
            axis=0,
        )

    def scatter_plane(partial):
        if lows != 2:
            count = ranks * rows
            own = partial[:count]
            for step in range(1, lows):
                piece = partial[step * count : (step + 1) * count].astype(BF)
                own = own + along_low(piece, -step).astype(F32)
            return scatter_tokens(own)
        blocks = [partial[index * rows : (index + 1) * rows] for index in range(2 * ranks)]
        sums = {}
        for index in (6, 4, 2, 0):
            sums[index] = blocks[index] + across(blocks[index + 1].astype(BF), 1).astype(F32)
        corner = sums[6].astype(BF)
        by_far = across(corner[:half_rows], 2).astype(F32)
        by_side = along_low(corner[half_rows:], 1).astype(F32)
        side = jnp.concatenate([sums[4][:half_rows] + by_far, sums[4][half_rows:]], axis=0)
        far = jnp.concatenate([sums[2][:half_rows], sums[2][half_rows:] + by_side], axis=0)
        return (
            sums[0]
            + across(far.astype(BF), 2).astype(F32)
            + along_low(side.astype(BF), 1).astype(F32)
        )

    places = [(high ^ bits) * lows + low for bits in (0, 2, 1, 3)] + [
        (high ^ bits) * lows + (low + 1) % lows for bits in (0, 2, 1, 3)
    ]

    def after(array, *others):
        return lax.optimization_barrier((array,) + others)[0]

    staged = lows == 2

    def gather_two(block):
        return jnp.concatenate([block, flip_high(block, 2)], axis=0) if staged else block

    def gather_four(two):
        return jnp.concatenate([two, flip_high(two, 1)], axis=0) if staged else two

    def gather_all(four):
        if not staged:
            return lax.all_gather(four, "frame", axis=0, tiled=True)
        return place_rows([four, along_low(four, 1)], places, four.shape[0] // ranks)

    def scatter_half(partials):
        if not staged:
            return jnp.concatenate([partial.astype(BF) for partial in partials], axis=1)
        columns = [partial.shape[1] for partial in partials]
        cuts = [sum(columns[:index]) for index in range(len(columns) + 1)]
        count = partials[0].shape[0] // frame_size
        splits = [
            partial.reshape(ranks, lows, count, partial.shape[1]) for partial in partials
        ]
        sent = jnp.concatenate(
            [lax.dynamic_index_in_dim(split.astype(BF), 1 - low, 1, False) for split in splits],
            axis=2,
        )
        arrived = along_low(sent, 1)
        return jnp.concatenate(
            [
                lax.dynamic_index_in_dim(split, low, 1, False)
                + arrived[:, :, cuts[index] : cuts[index + 1]].astype(F32)
                for index, split in enumerate(splits)
            ],
            axis=2,
        ).reshape(2, 2, count, cuts[-1])

    def scatter_rest(half):
        if not staged:
            return lax.psum_scatter(half, "frame", scatter_dimension=0, tiled=True)
        sent = lax.dynamic_index_in_dim(half, 1 - high % 2, 1, False).astype(BF)
        kept = lax.dynamic_index_in_dim(half, high % 2, 1, False)
        two = kept + flip_high(sent, 1).astype(F32)
        sent = lax.dynamic_index_in_dim(two, 1 - high // 2, 0, False).astype(BF)
        kept = lax.dynamic_index_in_dim(two, high // 2, 0, False)
        return (kept + flip_high(sent, 2).astype(F32)).astype(BF)

    def swap_ranks(blocks):
        split = blocks.reshape((2, 2) + blocks.shape[1:])
        kept = lax.dynamic_index_in_dim(split, rank // 2, 0, False)
        found = across(lax.dynamic_index_in_dim(split, 1 - rank // 2, 0, False), 2)
        own = lax.dynamic_index_in_dim(kept, rank % 2, 0, False)
        far = lax.dynamic_index_in_dim(found, rank % 2, 0, False)
        near = across(lax.dynamic_index_in_dim(kept, 1 - rank % 2, 0, False), 1)
        both = across(lax.dynamic_index_in_dim(found, 1 - rank % 2, 0, False), 1)
        return in_rank_order([own, near, far, both])

    def sum_everywhere(array):
        bits = 1
        while bits < ranks:
            array = array + across(array, bits)
            bits *= 2
        bits = 1
        while bits < frame_size:
            pairs = [
                (seq * frame_size + item, seq * frame_size + (item ^ bits))
                for seq in range(ranks)
                for item in range(frame_size)
            ]
            array = array + lax.ppermute(array, AXES, pairs)
            bits *= 2
        return array

    def in_rank_order(items):
        stacked = jnp.stack(items)
        return [
            lax.dynamic_index_in_dim(stacked, rank ^ index, 0, False) for index in range(ranks)
        ]

    def gather_ranks(block):
        far = across(block, 2)
        near = across(block, 1)
        both = across(far, 1)
        return [block, near, far, both]

    token_rows = inputs[0].reshape(rows, width)
    grad_rows = cotangent[0].reshape(frames_dev * CH, width)
    frame_count = clip_id.shape[1]
    clip_rows = jnp.pad(
        clip_id.astype(BF), ((0, 15), (0, width - frame_count))
    )
    moved = to_planes(jnp.concatenate([token_rows, grad_rows, clip_rows], axis=0))
    tokens = moved[:rows].astype(F32)
    grad_learned = moved[rows : rows + frames_dev * CH].astype(F32)
    clips = moved[rows + frames_dev * CH, :frame_count].astype(jnp.int32)

    own_qkv = jnp.concatenate(
        [
            lax.dynamic_slice_in_dim(w_qkv, part * width + rank * quarter, quarter, 1)
            for part in range(3)
        ],
        axis=1,
    )
    two_qkv = gather_two(own_qkv)
    unit = hidden // (frame_size * ranks)
    columns = jnp.arange(hidden_quarter, dtype=jnp.int32)
    wanted = (columns // unit) * (unit * ranks) + rank * unit + columns % unit
    choose = (jnp.arange(hidden, dtype=jnp.int32)[:, None] == wanted[None, :]).astype(BF)
    own_up = dot(w_up, choose).astype(BF)
    own_down = lax.dynamic_slice_in_dim(w_down, rank * unit, unit, 0)
    own_out = lax.dynamic_slice_in_dim(w_out, rank * quarter, quarter, 1)
    own_out = jnp.concatenate([own_out, conv_first], axis=1)
    two_out = gather_two(after(own_out, two_qkv))
    four_qkv = gather_four(two_qkv)
    two_up = gather_two(after(own_up, two_out))
    four_out = gather_four(after(two_out, four_qkv))
    qkv_quarter = gather_all(four_qkv)
    two_down = gather_two(after(own_down, two_up))
    four_up = gather_four(after(two_up, four_out))
    qkv_quarter = after(qkv_quarter, four_out, two_up)
    packed = gather_all(after(four_out, qkv_quarter))
    out_columns = packed[:, :quarter]
    full_conv = packed[:, quarter:]
    out_quarter = jnp.concatenate(
        swap_ranks(out_columns.reshape(ranks, quarter, quarter)), axis=1
    )
    up_bias_quarter = lax.dynamic_index_in_dim(
        up_bias.reshape(frame_size, ranks, unit), rank, 1, False
    ).reshape(1, hidden_quarter)

    frame_ids = jnp.arange(frame_count, dtype=jnp.int32)

    def clip_tokens(lo):
        blocks = []
        inverse = jnp.array([RANK_OF.index(item) for item in range(ranks)], jnp.int32)
        for bits in range(ranks):
            hi = lax.dynamic_index_in_dim(inverse, rank ^ bits, 0, False)
            for frame in range(frames_dev):
                blocks.append((hi * lows + lo) * frames_dev + frame)
        wanted_frames = jnp.stack(blocks)
        found = jnp.sum(
            jnp.where(wanted_frames[:, None] == frame_ids[None, :], clips[None, :], 0), axis=1
        )
        return jnp.broadcast_to(found[:, None], (found.shape[0], patches)).reshape(-1)

    query_clip = clip_tokens(low)
    key_clip = jnp.concatenate(
        [query_clip] + [clip_tokens((low - step) % lows) for step in range(1, lows)]
    )
    query_clip = query_clip[None, :]
    key_clip = key_clip[:, None]

    normed_one, inverse_one = norm_stats(tokens)
    own_count = ranks * rows
    all_one = gather_plane((normed_one * ln_gains[0] + ln_biases[0]).astype(BF))
    queries = dot(all_one[:own_count], qkv_quarter[:, :quarter]).astype(BF)
    keyvals = dot(all_one, qkv_quarter[:, quarter:]).astype(BF)
    queries = after(queries, packed, four_up, two_down)
    up_quarter = gather_all(after(four_up, packed))
    four_down = gather_four(two_down)
    attended, logs = attend(queries, keyvals, query_clip, key_clip)
    after_attention = tokens + scatter_tokens(dot(attended, out_quarter, 0, 0))
    after_attention = after(after_attention, four_down)
    down_quarter = gather_all(after(four_down, up_quarter))
    normed_two, inverse_two = norm_stats(after_attention)
    all_two = gather_tokens((normed_two * ln_gains[1] + ln_biases[1]).astype(BF))
    pre_act = dot(all_two, up_quarter) + up_bias_quarter
    act_low = gelu(pre_act).astype(BF)
    block_out = after_attention + scatter_tokens(dot(act_low, down_quarter)) + down_bias

    normed_three, inverse_three = norm_stats(block_out)
    normed_three_low = (normed_three * ln_gains[2] + ln_biases[2]).astype(BF)
    tap_rows = dot(normed_three_low, full_conv).reshape(frames_dev, GRID, GRID, 9 * CH)
    first = conv_grid(tap_rows) + conv_first_bias
    features = block_out.reshape(frames_dev, patches, width)

    def tail(first_arg, features_arg, mid_arg, mid_bias_arg):
        maps = token_maps(first_arg, mid_arg, mid_bias_arg).reshape(frames_dev, patches, CH)
        return pool_tokens(maps, features_arg)

    learned, tail_back = jax.vjp(tail, first, features, conv_mid, conv_mid_bias)
    grad_first, grad_pool, grad_mid, grad_mid_bias = tail_back(
        grad_learned.reshape(frames_dev, CH, width)
    )
    grad_first_low = grad_first.astype(BF)
    grad_first_bias = jnp.sum(grad_first_low.astype(F32), axis=(0, 1, 2))
    spread_unused, spread_back = jax.vjp(conv_grid, tap_rows)
    spread = spread_back(grad_first_low.astype(F32))[0].reshape(rows, 9 * CH).astype(BF)
    grad_conv = dot(normed_three_low, spread, 0, 0)
    grad_normed_three = dot(spread, full_conv, 1, 1)
    grad_block, grad_gain_three, grad_shift_three = norm_back(
        normed_three, inverse_three, ln_gains[2], grad_normed_three
    )
    grad_block = grad_block + grad_pool.reshape(rows, width)
    grad_mlp = grad_block.astype(BF)
    grad_down_bias = jnp.sum(grad_mlp.astype(F32), axis=0)

    all_mlp = gather_tokens(grad_mlp)
    grad_act = dot(all_mlp, down_quarter, 1, 1)
    gelu_unused, gelu_back = jax.vjp(gelu, pre_act)
    grad_pre = gelu_back(grad_act)[0].astype(BF)
    grad_up_bias = jnp.sum(grad_pre.astype(F32), axis=0)
    grad_normed_two = scatter_tokens(dot(grad_pre, up_quarter, 1, 1))
    grad_down = dot(act_low, all_mlp, 0, 0)
    grad_up = dot(all_two, grad_pre, 0, 0)
    mlp_half = scatter_half([grad_up, grad_down, grad_conv])
    grad_after, grad_gain_two, grad_shift_two = norm_back(
        normed_two, inverse_two, ln_gains[1], grad_normed_two
    )
    grad_after = grad_after + grad_block

    all_branch = gather_tokens(grad_after.astype(BF))
    grad_attended = dot(all_branch, out_quarter, 1, 1).astype(BF)
    grad_out = dot(attended, all_branch)
    grad_attended = after(grad_attended, mlp_half)
    mlp_share = scatter_rest(mlp_half)
    grad_queries, grad_keyvals = attend_back(
        queries, keyvals, grad_attended, logs, query_clip, key_clip
    )
    grad_queries = grad_queries.T
    grad_keyvals = grad_keyvals.astype(BF)
    grad_normed_own = dot(grad_keyvals, qkv_quarter[:, quarter:], 1, 1)
    grad_normed_own = jnp.concatenate(
        [
            grad_normed_own[:own_count] + dot(grad_queries, qkv_quarter[:, :quarter], 1, 1),
            grad_normed_own[own_count:],
        ],
        axis=0,
    )
    grad_normed_one = scatter_plane(grad_normed_own)
    grad_q = dot(all_one[:own_count], grad_queries, 0, 0)
    grad_kv = dot(all_one, grad_keyvals, 0, 0)
    grad_out_columns = jnp.concatenate(
        swap_ranks(grad_out.astype(BF).reshape(quarter, ranks, quarter).transpose(1, 0, 2)),
        axis=0,
    )
    qkv_share = scatter_rest(
        after(scatter_half([grad_q, grad_kv, grad_out_columns]), mlp_share)
    )
    grad_tokens, grad_gain_one, grad_shift_one = norm_back(
        normed_one, inverse_one, ln_gains[0], grad_normed_one
    )
    moved_back = from_planes(
        jnp.concatenate(
            [
                (grad_after + grad_tokens).astype(BF),
                learned.astype(BF).reshape(frames_dev * CH, width),
            ],
            axis=0,
        )
    ).astype(F32)
    grad_input = moved_back[:rows]
    learned = moved_back[rows:]

    sum_up, sum_down, sum_conv = finish(
        functools.partial(finish_mlp_kernel, ranks, hidden_quarter, width, unit),
        rank,
        gather_ranks(mlp_share),
        [(row_shard, hidden), (ranks * unit, width), (row_shard, 9 * CH)],
        "finish_mlp",
    )
    sum_qkv, sum_out = finish(
        functools.partial(finish_qkv_kernel, ranks, quarter),
        rank,
        gather_ranks(qkv_share),
        [(row_shard, 3 * width), (row_shard, width)],
        "finish_qkv",
    )

    conv_terms = jnp.concatenate(
        [grad_first_bias.reshape(-1), grad_mid.reshape(-1), grad_mid_bias.reshape(-1)]
    )
    conv_rows = -(-conv_terms.shape[0] // width)
    conv_terms = jnp.pad(conv_terms, (0, conv_rows * width - conv_terms.shape[0]))
    up_terms = jnp.where(
        jnp.arange(ranks, dtype=jnp.int32)[:, None] == rank,
        grad_up_bias.reshape(1, hidden_quarter),
        0.0,
    )
    early = sum_everywhere(
        jnp.concatenate(
            [
                jnp.stack(
                    [
                        grad_gain_one,
                        grad_gain_two,
                        grad_gain_three,
                        grad_shift_one,
                        grad_shift_two,
                        grad_shift_three,
                        grad_down_bias,
                    ]
                ),
                conv_terms.reshape(conv_rows, width),
                up_terms.reshape(-1, width),
            ],
            axis=0,
        )
    )
    sum_gains = early[0:3]
    sum_shifts = early[3:6]
    conv_sums = early[7 : 7 + conv_rows].reshape(-1)
    sum_up_bias = (
        early[7 + conv_rows :]
        .reshape(ranks, frame_size, unit)
        .transpose(1, 0, 2)
        .reshape(hidden)
    )
    mid_count = grad_mid.size
    sum_mid = conv_sums[CH : CH + mid_count].reshape(grad_mid.shape)
    sum_mid_bias = conv_sums[CH + mid_count : CH + mid_count + grad_mid_bias.size]
    return (
        learned.reshape(1, frames_dev, CH, width),
        grad_input.reshape(1, frames_dev, patches, width),
        sum_qkv,
        sum_out,
        sum_up,
        sum_down,
        sum_conv,
        sum_gains,
        sum_shifts,
        sum_up_bias,
        early[6],
        conv_sums[:CH],
        sum_mid,
        sum_mid_bias.reshape(grad_mid_bias.shape),
    )


PAD = 128


def run(kernel, name, scalars, arrays, outs, scratch=(), limit=24):
    vmem = pl.BlockSpec(memory_space=pltpu.VMEM)
    return pl.pallas_call(
        kernel,
        in_specs=[pl.BlockSpec(memory_space=pltpu.SMEM)] + [vmem] * len(arrays),
        out_specs=[vmem] * len(outs),
        out_shape=[jax.ShapeDtypeStruct(shape, kind) for shape, kind in outs],
        scratch_shapes=list(scratch),
        compiler_params=pltpu.CompilerParams(vmem_limit_bytes=limit * 1024 * 1024),
        name=name,
    )(scalars, *arrays)


def rows_at(start, size):
    return pl.ds(pl.multiple_of(start * size, size), size)


def stack_rows(refs):
    return jnp.concatenate([ref[...] for ref in refs], axis=0)


def exact(left, right, left_dim=1, right_dim=0):
    return lax.dot_general(
        left,
        right,
        (((left_dim,), (right_dim,)), ((), ())),
        precision=HIGHEST,
        preferred_element_type=F32,
    )


def column_sum(values):
    return jnp.sum(values, axis=0, keepdims=True)


def back_of_norm(values, gain, grad):
    normed, inverse = norm_stats(values)
    scaled = grad * gain
    mean_scaled = jnp.mean(scaled, axis=-1, keepdims=True)
    mean_cross = jnp.mean(scaled * normed, axis=-1, keepdims=True)
    result = inverse * (scaled - mean_scaled - normed * mean_cross)
    return result, column_sum(grad * normed), column_sum(grad)


def norm_one_kernel(unused_ref, moved_ref, gains_ref, shifts_ref, low_ref):
    count = low_ref.shape[0]
    normed, unused = norm_stats(moved_ref[:count, :].astype(F32))
    low_ref[...] = (normed * gains_ref[0:1, :] + shifts_ref[0:1, :]).astype(BF)


def place_out_kernel(quarter, place_ref, *refs):
    blocks = refs[:8]
    own_ref, near_ref, others_ref, all_ref = refs[8:]
    size = blocks[0].shape[0]
    for index in range(8):
        all_ref[rows_at(place_ref[index], size), :] = blocks[index][:, 3 * quarter :]
    rank = place_ref[8]
    own_ref[...] = all_ref[rows_at(rank, quarter), :]
    near_ref[...] = all_ref[rows_at(rank ^ 1, quarter), :]
    others_ref[0] = all_ref[rows_at(rank ^ 2, quarter), :]
    others_ref[1] = all_ref[rows_at(rank ^ 3, quarter), :]


def project_kernel(quarter, place_ref, *refs):
    tokens, blocks = refs[:8], refs[8:16]
    q_ref, kv_ref, w_ref = refs[16:]
    size = blocks[0].shape[0]
    for index in range(8):
        w_ref[rows_at(place_ref[index], size), :] = blocks[index][:, : 3 * quarter]
    own = dot(stack_rows(tokens[:4]), w_ref[...]).astype(BF)
    q_ref[...] = own[:, :quarter]
    half = own.shape[0]
    kv_ref[:half, :] = own[:, quarter:]
    kv_ref[half:, :] = dot(stack_rows(tokens[4:]), w_ref[:, quarter:]).astype(BF)


def scores_of(kv_ref, q_ref, queries, lanes, same, scale):
    raw = dot(kv_ref[:, lanes], q_ref[queries, lanes], 1, 1) * scale
    return jnp.where(same, raw, FLOOR_SCORE)


def attend_wide_kernel(heads, scale, unused_ref, *refs):
    q_ref, kv_ref, qclip_ref, kclip_ref, mixed_ref, log_ref = refs
    width = heads * HEAD_DIM
    count = q_ref.shape[0] // 2
    for part in range(2):
        queries = slice(part * count, (part + 1) * count)
        same = kclip_ref[...] == qclip_ref[:, queries]
        for head in range(heads):
            lanes = slice(head * HEAD_DIM, (head + 1) * HEAD_DIM)
            values = slice(width + head * HEAD_DIM, width + (head + 1) * HEAD_DIM)
            scores = scores_of(kv_ref, q_ref, queries, lanes, same, scale)
            top = jnp.max(scores, axis=0, keepdims=True)
            shifted = jnp.exp(scores - top)
            total = jnp.sum(shifted, axis=0, keepdims=True)
            prob = (shifted * (1.0 / total)).astype(BF)
            mixed_ref[lanes, queries] = dot(kv_ref[:, values], prob, 0, 0).astype(BF)
            log_ref[head : head + 1, queries] = top + jnp.log(total)


def split_blocks(values, even_ref, odd_ref):
    rows = even_ref.shape[1]
    for part in range(even_ref.shape[0]):
        even_ref[part] = values[2 * part * rows : (2 * part + 1) * rows]
        odd_ref[part] = values[(2 * part + 1) * rows : (2 * part + 2) * rows].astype(BF)


def out_kernel(rank_ref, *refs):
    mixed_ref, own_ref, near_ref, others_ref, both_ref = refs[:5]
    even_ref, odd_ref, w_ref = refs[5:]
    blocks = [own_ref[...], near_ref[...], others_ref[0], both_ref[...]]
    rank = rank_ref[0]
    width = own_ref.shape[0]
    for index in range(4):
        found = blocks[0]
        for bits in range(1, 4):
            found = jnp.where(rank == index ^ bits, blocks[bits], found)
        w_ref[:, index * width : (index + 1) * width] = found
    split_blocks(dot(mixed_ref[...], w_ref[...], 0, 0), even_ref, odd_ref)


def norm_two_kernel(unused_ref, *refs):
    moved_ref, even_ref, arrived_ref, far_ref, gains_ref, shifts_ref = refs[:6]
    sum_ref, low_ref = refs[6:]
    count = low_ref.shape[0]
    values = (
        moved_ref[:count, :].astype(F32)
        + even_ref[0]
        + arrived_ref[0].astype(F32)
        + far_ref[...].astype(F32)
    )
    sum_ref[...] = values
    normed, unused = norm_stats(values)
    low_ref[...] = (normed * gains_ref[1:2, :] + shifts_ref[1:2, :]).astype(BF)


def gelu_both(values):
    size = jnp.abs(values) * 0.7071067811865476
    ratio = 1.0 / (1.0 + 0.3275911 * size)
    bell = jnp.exp(-size * size)
    series = ratio * (
        0.254829592
        + ratio
        * (-0.284496736 + ratio * (1.421413741 + ratio * (-1.453152027 + ratio * 1.061405429)))
    )
    tail = 0.5 * series * bell
    below = jnp.where(values >= 0.0, 1.0 - tail, tail)
    return values * below, below + values * bell * 0.3989422804014327


def mlp_kernel(low_ref, *refs):
    tokens = refs[:4]
    own_ref, side_ref, bias_ref = refs[4:7]
    act_ref, slope_ref, up_ref, down_ref, conv_ref, even_ref, odd_ref = refs[7:]
    low = low_ref[0]
    size = own_ref.shape[0] // 4
    quarter = up_ref.shape[1]
    width = down_ref.shape[1]
    for hi in range(4):
        rows = slice(hi * size, (hi + 1) * size)
        for ref, place in ((own_ref, 2 * hi + low), (side_ref, 2 * hi + 1 - low)):
            where = rows_at(place, size)
            up_ref[where, :] = ref[rows, :quarter]
            down_ref[where, :] = ref[rows, quarter : quarter + width]
            conv_ref[where, :] = ref[rows, quarter + width :]
    count = tokens[0].shape[0]
    for part in range(2):
        rows = slice(2 * part * count, 2 * (part + 1) * count)
        pre = dot(stack_rows(tokens[2 * part : 2 * part + 2]), up_ref[...]) + bias_ref[...]
        act, slope = gelu_both(pre)
        act = act.astype(BF)
        act_ref[rows, :] = act
        slope_ref[rows, :] = slope
        partial = dot(act, down_ref[...])
        even_ref[part] = partial[:count]
        odd_ref[part] = partial[count:].astype(BF)


def grid_masks(count):
    row = lax.broadcasted_iota(jnp.int32, (count, PAD), 0)
    i = (row // GRID) % GRID
    j = row % GRID
    masks = []
    for tap in range(9):
        di, dj = tap // 3 - 1, tap % 3 - 1
        inside = (i + di >= 0) & (i + di < GRID) & (j + dj >= 0) & (j + dj < GRID)
        masks.append(inside.astype(F32))
    return masks


def collect_taps(taps, masks, first_lanes):
    count = taps.shape[0]
    total = None
    for tap in range(9):
        offset = (tap // 3 - 1) * GRID + tap % 3 - 1
        moved = pltpu.roll(taps, (PAD - tap * CH) % PAD, 1) if tap else taps
        moved = pltpu.roll(moved, (-offset) % count, 0) if offset else moved
        moved = moved * masks[tap]
        total = moved if total is None else total + moved
    return total * first_lanes


def spread_taps(values, masks):
    count = values.shape[0]
    total = None
    for tap in range(9):
        offset = (tap // 3 - 1) * GRID + tap % 3 - 1
        moved = pltpu.roll(values, tap * CH, 1) if tap else values
        moved = pltpu.roll(moved, offset % count, 0) if offset else moved
        moved = moved * masks[8 - tap]
        total = moved if total is None else total + moved
    return total


def store_rows(ref, start, values):
    for index in range(values.shape[1] // PAD):
        ref[start + index : start + index + 1, :] = values[:, index * PAD : (index + 1) * PAD]


def load_rows(ref, start, count):
    return jnp.concatenate(
        [ref[start + index : start + index + 1, :] for index in range(count)], axis=1
    )


def tail_kernel(vectors, unused_ref, *refs):
    sum_ref, even_ref, arrived_ref, far_ref, bias_ref, gains_ref, shifts_ref = refs[:7]
    conv_ref, first_bias_ref, mid_ref, mid_bias_ref, moved_ref = refs[7:12]
    learned_ref, low_ref, grad_ref, normed_ref, spread_ref, small_ref = refs[12:]
    count = low_ref.shape[0]
    frames = count // (GRID * GRID)
    patches = GRID * GRID
    value = (
        sum_ref[...]
        + even_ref[0]
        + arrived_ref[0].astype(F32)
        + far_ref[...].astype(F32)
        + bias_ref[...]
    )
    normed, inverse = norm_stats(value)
    gain = gains_ref[2:3, :]
    normed_low = (normed * gain + shifts_ref[2:3, :]).astype(BF)
    normed_ref[...] = normed_low
    masks = grid_masks(count)
    lane = lax.broadcasted_iota(jnp.int32, (count, PAD), 1)
    first_lanes = (lane < CH).astype(F32)
    first = collect_taps(dot(normed_low, conv_ref[...]), masks, first_lanes)
    hidden, slope = gelu_both(first + first_bias_ref[...])
    hidden = hidden * first_lanes
    hiddens, slopes = [hidden], [slope]
    maps = None
    for layer in range(3):
        pre = collect_taps(exact(hiddens[layer], mid_ref[layer]), masks, first_lanes)
        pre = pre + mid_bias_ref[layer : layer + 1, :]
        if layer < 2:
            hidden, slope = gelu_both(pre)
            hiddens.append(hidden * first_lanes)
            slopes.append(slope)
        else:
            maps = jax.nn.sigmoid(pre) * first_lanes
    pooled_parts, map_parts = [], []
    zero_rows = jnp.zeros((PAD - CH, value.shape[1]), F32)
    for frame in range(frames):
        rows = slice(frame * patches, (frame + 1) * patches)
        start = count + frame * CH
        cotangent = jnp.concatenate(
            [moved_ref[start : start + CH, :].astype(F32), zero_rows], axis=0
        )
        learned = exact(maps[rows], value[rows], 0, 0)[:CH] * (1.0 / patches)
        learned_ref[frame * CH : (frame + 1) * CH, :] = learned
        pooled_parts.append(exact(maps[rows], cotangent) * (1.0 / patches))
        map_parts.append(exact(value[rows], cotangent, 1, 1) * (1.0 / patches))
    grad = jnp.concatenate(map_parts, axis=0) * maps * (1.0 - maps)
    small_ref[...] = jnp.zeros_like(small_ref)
    conv_start = 7 * vectors + 4 * vectors
    for layer in range(2, -1, -1):
        taps = spread_taps(grad, masks)
        weight = exact(hiddens[layer], taps, 0, 0)[:CH]
        small_ref[conv_start + layer * CH : conv_start + (layer + 1) * CH, :] = weight
        bias_row = conv_start + 3 * CH + 1 + layer
        small_ref[bias_row : bias_row + 1, :] = column_sum(grad)
        grad = exact(taps, mid_ref[layer], 1, 1) * slopes[layer]
    grad_low = grad.astype(BF).astype(F32)
    small_ref[conv_start + 3 * CH : conv_start + 3 * CH + 1, :] = column_sum(grad_low)
    spread = spread_taps(grad_low, masks).astype(BF)
    spread_ref[...] = spread
    grad_normed = dot(spread, conv_ref[...], 1, 1)
    scaled = grad_normed * gain
    mean_scaled = jnp.mean(scaled, axis=-1, keepdims=True)
    mean_cross = jnp.mean(scaled * normed, axis=-1, keepdims=True)
    grad_value = inverse * (scaled - mean_scaled - normed * mean_cross)
    grad_value = grad_value + jnp.concatenate(pooled_parts, axis=0)
    grad_ref[...] = grad_value
    low = grad_value.astype(BF)
    low_ref[...] = low
    store_rows(small_ref, 2 * vectors, column_sum(grad_normed * normed))
    store_rows(small_ref, 5 * vectors, column_sum(grad_normed))
    store_rows(small_ref, 6 * vectors, column_sum(low.astype(F32)))


def mlp_back_kernel(unused_ref, *refs):
    grads = refs[:4]
    slope_ref, up_ref, down_ref = refs[4:7]
    pre_ref, even_ref, odd_ref, bias_ref = refs[7:]
    count = grads[0].shape[0]
    total = None
    for part in range(2):
        rows = slice(2 * part * count, 2 * (part + 1) * count)
        grad_act = dot(stack_rows(grads[2 * part : 2 * part + 2]), down_ref[...], 1, 1)
        grad_pre = (grad_act * slope_ref[rows, :]).astype(BF)
        pre_ref[rows, :] = grad_pre
        term = column_sum(grad_pre.astype(F32))
        total = term if total is None else total + term
        partial = dot(grad_pre, up_ref[...], 1, 1)
        even_ref[part] = partial[:count]
        odd_ref[part] = partial[count:].astype(BF)
    bias_ref[...] = total


def mlp_grads_kernel(unused_ref, *refs):
    tokens, grads = refs[:4], refs[4:8]
    act_ref, pre_ref, normed_ref, spread_ref, pack_ref = refs[8:]
    quarter = act_ref.shape[1]
    width = tokens[0].shape[1]
    pack_ref[:, :quarter] = dot(stack_rows(tokens), pre_ref[...], 0, 0).astype(BF)
    pack_ref[:, quarter : quarter + width] = dot(
        act_ref[...], stack_rows(grads), 0, 0
    ).astype(BF)
    pack_ref[:, quarter + width :] = dot(normed_ref[...], spread_ref[...], 0, 0).astype(BF)


def norm_two_back_kernel(unused_ref, *refs):
    sum_ref, grad_ref, even_ref, arrived_ref, far_ref, gains_ref = refs[:6]
    total_ref, low_ref, rows_ref = refs[6:]
    grad_normed = even_ref[0] + arrived_ref[0].astype(F32) + far_ref[...].astype(F32)
    result, gain_row, shift_row = back_of_norm(sum_ref[...], gains_ref[1:2, :], grad_normed)
    total = result + grad_ref[...]
    total_ref[...] = total
    low_ref[...] = total.astype(BF)
    rows_ref[0:1, :] = gain_row
    rows_ref[1:2, :] = shift_row


def attend_back_out_kernel(heads, scale, unused_ref, *refs):
    branches = refs[:4]
    out_ref, q_ref, kv_ref, log_ref, qclip_ref, kclip_ref, w_ref = refs[4:11]
    own_ref, other_ref, even_ref, odd_ref, total_ref = refs[11:]
    width = heads * HEAD_DIM
    count = q_ref.shape[0] // 2
    rows = count // 2
    for part in range(2):
        queries = slice(part * count, (part + 1) * count)
        grad_mixed = dot(
            stack_rows(branches[2 * part : 2 * part + 2]), out_ref[...], 1, 1
        ).astype(BF)
        same = kclip_ref[...] == qclip_ref[:, queries]
        query_parts, key_parts, value_parts = [], [], []
        for head in range(heads):
            lanes = slice(head * HEAD_DIM, (head + 1) * HEAD_DIM)
            values = slice(width + head * HEAD_DIM, width + (head + 1) * HEAD_DIM)
            scores = scores_of(kv_ref, q_ref, queries, lanes, same, scale)
            prob = jnp.exp(scores - log_ref[head : head + 1, queries])
            grad_prob = dot(kv_ref[:, values], grad_mixed[:, lanes], 1, 1)
            delta = jnp.sum(prob * grad_prob, axis=0, keepdims=True)
            grad_score = (prob * (grad_prob - delta)).astype(BF)
            query_parts.append(dot(kv_ref[:, lanes], grad_score, 0, 0) * scale)
            key_parts.append(dot(grad_score, q_ref[queries, lanes]) * scale)
            value_parts.append(dot(prob.astype(BF), grad_mixed[:, lanes]))
        own_ref[queries, :width] = jnp.concatenate(query_parts, axis=0).T.astype(BF)
        terms = jnp.concatenate(key_parts + value_parts, axis=1)
        if part == 0:
            total_ref[...] = terms
        else:
            total_ref[...] += terms
    own_ref[:, width:] = total_ref[: 2 * count, :].astype(BF)
    other_ref[...] = total_ref[2 * count :, :].astype(BF)
    own = dot(own_ref[...], w_ref[...], 1, 1)
    other = dot(other_ref[...], w_ref[:, width:], 1, 1)
    for part in range(2):
        even_ref[part] = own[2 * part * rows : (2 * part + 1) * rows]
        odd_ref[part] = own[(2 * part + 1) * rows : (2 * part + 2) * rows].astype(BF)
        even_ref[part + 2] = other[2 * part * rows : (2 * part + 1) * rows]
        odd_ref[part + 2] = other[(2 * part + 1) * rows : (2 * part + 2) * rows].astype(BF)


def qkv_grads_kernel(place_ref, *refs):
    tokens, branches, mixes = refs[:8], refs[8:12], refs[12:16]
    own_ref, other_ref, kept_ref, sent_ref, all_ref = refs[16:]
    quarter = mixes[0].shape[0]
    size = all_ref.shape[0] // 8
    full = dot(stack_rows(tokens[:4]), own_ref[...], 0, 0)
    more = dot(stack_rows(tokens[4:]), other_ref[...], 0, 0)
    all_ref[:, :quarter] = full[:, :quarter]
    all_ref[:, quarter : 3 * quarter] = full[:, quarter:] + more
    rank = place_ref[0]
    low = place_ref[1]
    branch = stack_rows(branches)
    wanted = branch[:, :quarter]
    for index in range(1, 4):
        wanted = jnp.where(
            rank == index, branch[:, index * quarter : (index + 1) * quarter], wanted
        )
    count = branches[0].shape[0]
    for bits in range(4):
        turned = jnp.concatenate(
            [wanted[(item ^ bits) * count : ((item ^ bits) + 1) * count] for item in range(4)],
            axis=0,
        )
        all_ref[rows_at(rank ^ bits, quarter), 3 * quarter :] = dot(mixes[bits][...], turned)
    for hi in range(4):
        rows = slice(hi * size, (hi + 1) * size)
        kept_ref[rows, :] = all_ref[rows_at(2 * hi + low, size), :]
        sent_ref[rows, :] = all_ref[rows_at(2 * hi + 1 - low, size), :].astype(BF)


def half_kernel(high_ref, kept_ref, arrived_ref, own_ref, *refs):
    size = own_ref.shape[0]
    for step in range(4):
        where = rows_at(lax.rem(high_ref[0] + step, 4), size)
        total = kept_ref[where, :] + arrived_ref[where, :].astype(F32)
        if step == 0:
            own_ref[...] = total
        else:
            refs[step - 1][...] = total.astype(BF)


def total_kernel(unused_ref, kept_ref, *refs):
    total = kept_ref[...]
    for ref in refs[:-1]:
        total = total + ref[...].astype(F32)
    refs[-1][...] = total.astype(BF)


def norm_one_back_kernel(vectors, rank_ref, *refs):
    moved_ref, grad_ref, even_ref, arrived_ref, far_ref, side_ref, gains_ref = refs[:7]
    learned_ref, small_ref, two_ref, up_ref, back_ref, sums_ref = refs[7:]
    count = grad_ref.shape[0]
    grad_normed = (
        even_ref[0]
        + arrived_ref[0].astype(F32)
        + far_ref[...].astype(F32)
        + side_ref[...].astype(F32)
    )
    result, gain_row, shift_row = back_of_norm(
        moved_ref[:count, :].astype(F32), gains_ref[0:1, :], grad_normed
    )
    back_ref[:count, :] = (result + grad_ref[...]).astype(BF)
    back_ref[count:, :] = learned_ref[...].astype(BF)
    sums_ref[...] = small_ref[...]
    store_rows(sums_ref, 0, gain_row)
    store_rows(sums_ref, vectors, two_ref[0:1, :])
    store_rows(sums_ref, 3 * vectors, shift_row)
    store_rows(sums_ref, 4 * vectors, two_ref[1:2, :])
    for index in range(4):
        store_rows(
            sums_ref,
            (7 + index) * vectors,
            jnp.where(rank_ref[0] == index, up_ref[...], 0.0),
        )


def unpack_kernel(vectors, unused_ref, sums_ref, *refs):
    gains_ref, shifts_ref, up_ref, down_ref, first_ref, mid_ref, mid_bias_ref = refs
    for index in range(3):
        gains_ref[index : index + 1, :] = load_rows(sums_ref, index * vectors, vectors)
        shifts_ref[index : index + 1, :] = load_rows(sums_ref, (3 + index) * vectors, vectors)
    down_ref[...] = load_rows(sums_ref, 6 * vectors, vectors)
    quarters = [load_rows(sums_ref, (7 + index) * vectors, vectors) for index in range(4)]
    unit = quarters[0].shape[1] // 8
    up_ref[...] = jnp.concatenate(
        [
            quarters[index][:, group * unit : (group + 1) * unit]
            for group in range(8)
            for index in range(4)
        ],
        axis=1,
    )
    start = 11 * vectors
    for layer in range(3):
        mid_ref[layer] = sums_ref[start + layer * CH : start + (layer + 1) * CH, : 9 * CH]
    start = start + 3 * CH
    first_ref[...] = sums_ref[start : start + 1, :CH]
    mid_bias_ref[...] = sums_ref[start + 1 : start + 4, :CH]


def shards_square(
    ranks,
    frame_size,
    inputs,
    clip_id,
    ln_gains,
    ln_biases,
    w_qkv,
    w_out,
    w_up,
    w_down,
    up_bias,
    down_bias,
    conv_first,
    conv_first_bias,
    conv_mid,
    conv_mid_bias,
    cotangent,
):
    lows = 2
    frames_dev = inputs.shape[1]
    patches = inputs.shape[2]
    width = inputs.shape[3]
    rows = frames_dev * patches
    learned_rows = frames_dev * CH
    hidden = up_bias.shape[0]
    quarter = width // ranks
    heads = quarter // HEAD_DIM
    hidden_quarter = hidden // ranks
    unit = hidden_quarter // frame_size
    size = width // frame_size
    vectors = width // PAD
    own_count = ranks * rows
    rank = lax.axis_index("seq")
    place = lax.axis_index("frame")
    high = place // lows
    low = place % lows
    core = rank % 2
    rank_one = rank.reshape(1)
    low_one = low.reshape(1)

    def permute(array, target):
        pairs = []
        for seq in range(ranks):
            for hi in range(ranks):
                for lo in range(lows):
                    to_seq, to_hi, to_lo = target(seq, hi, lo)
                    pairs.append(
                        (
                            seq * frame_size + hi * lows + lo,
                            to_seq * frame_size + to_hi * lows + to_lo,
                        )
                    )
        return lax.ppermute(array, AXES, pairs)

    def flip(array, seq_bits, hi_bits=0, lo_bits=0):
        return permute(
            array, lambda seq, hi, lo: (seq ^ seq_bits, hi ^ hi_bits, lo ^ lo_bits)
        )

    def after(array, *others):
        return lax.optimization_barrier((array,) + others)[0]

    def to_planes(array):
        return permute(array, lambda seq, hi, lo: (RANK_OF[hi], PLANE_OF[seq], lo))

    def from_planes(array):
        return permute(
            array, lambda seq, hi, lo: (PLANE_OF.index(hi), RANK_OF.index(seq), lo)
        )

    def gather_four(block):
        far = flip(block, 2)
        near = flip(block, 1)
        return [block, near, far, flip(far, 1)]

    def gather_eight(block):
        far = flip(block, 2)
        side = flip(block, 0, 0, 1)
        near = flip(block, 1)
        corner = permute(
            jnp.where(core == 0, far, side),
            lambda seq, hi, lo: (seq, hi, lo ^ 1) if seq % 2 == 0 else (seq ^ 2, hi, lo),
        )
        return [
            block,
            near,
            far,
            flip(far, 1),
            side,
            flip(side, 1),
            corner,
            flip(corner, 1),
        ]

    def scatter_four(even, odd):
        arrived = flip(odd, 1)
        far = flip((even[1] + arrived[1].astype(F32)).astype(BF), 2)
        return arrived, far

    def scatter_eight(even, odd):
        arrived = flip(odd, 1)
        corner = permute(
            (even[3] + arrived[3].astype(F32)).astype(BF),
            lambda seq, hi, lo: (seq ^ 2, hi, lo) if seq % 2 == 0 else (seq, hi, lo ^ 1),
        ).astype(F32)
        far = even[1] + arrived[1].astype(F32) + jnp.where(core == 1, corner, 0.0)
        side = even[2] + arrived[2].astype(F32) + jnp.where(core == 0, corner, 0.0)
        return arrived, flip(far.astype(BF), 2), flip(side.astype(BF), 0, 0, 1)

    moved = to_planes(
        jnp.concatenate(
            [
                inputs[0].reshape(rows, width),
                cotangent[0].reshape(learned_rows, width),
                jnp.pad(clip_id.astype(BF), ((0, 15), (0, width - clip_id.shape[1]))),
            ],
            axis=0,
        )
    )
    frame_count = clip_id.shape[1]
    clips = moved[rows + learned_rows, :frame_count].astype(jnp.int32)

    own_pack = jnp.concatenate(
        [
            lax.dynamic_slice_in_dim(w_qkv, part * width + rank * quarter, quarter, 1)
            for part in range(3)
        ]
        + [lax.dynamic_slice_in_dim(w_out, rank * quarter, quarter, 1)],
        axis=1,
    )
    packs = [own_pack] + [flip(own_pack, 0, bits // 2, bits % 2) for bits in range(1, 8)]
    places = [place ^ bits for bits in range(8)]

    columns = jnp.arange(hidden_quarter, dtype=jnp.int32)
    wanted = (columns // unit) * (unit * ranks) + rank * unit + columns % unit
    choose = (jnp.arange(hidden, dtype=jnp.int32)[:, None] == wanted[None, :]).astype(BF)
    own_mlp = jnp.concatenate(
        [
            dot(w_up, choose).astype(BF),
            lax.dynamic_slice_in_dim(w_down, rank * unit, unit, 0),
            conv_first,
            jnp.zeros((size, PAD - 9 * CH), BF),
        ],
        axis=1,
    )
    mlp_own = lax.all_gather(
        own_mlp,
        "frame",
        axis=0,
        tiled=True,
        axis_index_groups=[[hi * lows + lo for hi in range(ranks)] for lo in range(lows)],
    )
    mlp_side = flip(mlp_own, 0, 0, 1)
    up_bias_own = lax.dynamic_index_in_dim(
        up_bias.reshape(frame_size, ranks, unit), rank, 1, False
    ).reshape(1, hidden_quarter)

    mid_pad = jnp.pad(conv_mid, ((0, 0), (0, PAD - CH), (0, PAD - 9 * CH)))
    mid_bias_pad = jnp.pad(conv_mid_bias, ((0, 0), (0, PAD - CH)))
    first_bias_pad = jnp.pad(conv_first_bias, (0, PAD - CH)).reshape(1, PAD)

    frame_ids = jnp.arange(frame_count, dtype=jnp.int32)
    inverse = jnp.array([RANK_OF.index(item) for item in range(ranks)], jnp.int32)

    def clip_tokens(lo):
        blocks = []
        for bits in range(ranks):
            hi = lax.dynamic_index_in_dim(inverse, rank ^ bits, 0, False)
            for frame in range(frames_dev):
                blocks.append((hi * lows + lo) * frames_dev + frame)
        found = jnp.sum(
            jnp.where(jnp.stack(blocks)[:, None] == frame_ids[None, :], clips[None, :], 0),
            axis=1,
        )
        return jnp.broadcast_to(found[:, None], (found.shape[0], patches)).reshape(-1)

    query_clip = clip_tokens(low)
    key_clip = jnp.concatenate([query_clip, clip_tokens(1 - low)])[:, None]
    query_clip = query_clip[None, :]

    (low_one_norm,) = run(
        norm_one_kernel, "norm_one", low_one, [moved, ln_gains, ln_biases], [((rows, width), BF)]
    )
    all_one = gather_eight(after(low_one_norm, own_mlp))
    own_out, near_out, other_out = run(
        functools.partial(place_out_kernel, quarter),
        "place_out",
        jnp.stack(places + [rank]),
        packs,
        [((quarter, quarter), BF)] * 2 + [((2, quarter, quarter), BF)],
        [pltpu.VMEM((width, quarter), BF)],
    )
    other_out = flip(other_out, 2)
    near_out = flip(near_out, 1)
    both_out = flip(other_out[1], 1)
    queries, keyvals, qkv_quarter = run(
        functools.partial(project_kernel, quarter),
        "project",
        jnp.stack(places),
        all_one + packs,
        [
            ((own_count, quarter), BF),
            ((2 * own_count, 2 * quarter), BF),
            ((width, 3 * quarter), BF),
        ],
    )
    scale = HEAD_DIM ** (-0.5)
    attended, logs = run(
        functools.partial(attend_wide_kernel, heads, scale),
        "attend",
        rank_one,
        [queries, keyvals, query_clip, key_clip],
        [((quarter, own_count), BF), ((8, own_count), F32)],
    )
    halves = [((2, rows, width), F32), ((2, rows, width), BF)]
    even, odd, out_quarter = run(
        out_kernel,
        "out",
        rank_one,
        [attended, own_out, near_out, other_out, both_out],
        halves + [((quarter, width), BF)],
    )
    arrived, far = scatter_four(even, odd)
    after_attention, low_two = run(
        norm_two_kernel,
        "norm_two",
        low_one,
        [moved, even, arrived, far, ln_gains, ln_biases],
        [((rows, width), F32), ((rows, width), BF)],
    )
    all_two = gather_four(low_two)
    act, slope, up_full, down_full, conv_full, even, odd = run(
        mlp_kernel,
        "mlp",
        low_one,
        all_two + [mlp_own, mlp_side, up_bias_own],
        [
            ((own_count, hidden_quarter), BF),
            ((own_count, hidden_quarter), F32),
            ((width, hidden_quarter), BF),
            ((hidden_quarter, width), BF),
            ((width, PAD), BF),
        ]
        + halves,
    )
    arrived, far = scatter_four(even, odd)

    small_rows = -(-(11 * vectors + 3 * CH + 4) // 8) * 8
    learned, low_mlp, grad_block, low_three, spread, small = run(
        functools.partial(tail_kernel, vectors),
        "tail",
        low_one,
        [
            after_attention,
            even,
            arrived,
            far,
            down_bias.reshape(1, width),
            ln_gains,
            ln_biases,
            conv_full,
            first_bias_pad,
            mid_pad,
            mid_bias_pad,
            moved,
        ],
        [
            ((learned_rows, width), F32),
            ((rows, width), BF),
            ((rows, width), F32),
            ((rows, width), BF),
            ((rows, PAD), BF),
            ((small_rows, PAD), F32),
        ],
    )
    mixes = gather_four(after(attended, far))

    all_mlp = gather_four(low_mlp)
    grad_pre, even, odd, grad_up_bias = run(
        mlp_back_kernel,
        "mlp_back",
        low_one,
        all_mlp + [slope, up_full, down_full],
        [((own_count, hidden_quarter), BF)] + halves + [((1, hidden_quarter), F32)],
    )
    (mlp_grads,) = run(
        mlp_grads_kernel,
        "mlp_grads",
        low_one,
        all_two + all_mlp + [act, grad_pre, low_three, spread],
        [((width, hidden_quarter + width + PAD), BF)],
    )
    mlp_share = lax.psum_scatter(mlp_grads, "frame", scatter_dimension=0, tiled=True)
    arrived, far = scatter_four(even, odd)
    grad_after, low_branch, rows_two = run(
        norm_two_back_kernel,
        "norm_two_back",
        low_one,
        [after_attention, grad_block, even, arrived, far, ln_gains],
        [((rows, width), F32), ((rows, width), BF), ((2, width), F32)],
    )

    all_branch = gather_four(low_branch)
    grads_own, grads_other, even, odd = run(
        functools.partial(attend_back_out_kernel, heads, scale),
        "attend_back_out",
        low_one,
        all_branch + [out_quarter, queries, keyvals, logs, query_clip, key_clip, qkv_quarter],
        [
            ((own_count, 3 * quarter), BF),
            ((own_count, 2 * quarter), BF),
            ((4, rows, width), F32),
            ((4, rows, width), BF),
        ],
        [pltpu.VMEM((2 * own_count, 2 * quarter), F32)],
    )
    kept, sent = run(
        qkv_grads_kernel,
        "qkv_grads",
        jnp.stack([rank, low]),
        all_one + all_branch + mixes + [grads_own, grads_other],
        [((width // 2, width), F32), ((width // 2, width), BF)],
        [pltpu.VMEM((width, width), F32)],
    )
    arrived, far, side = scatter_eight(even, odd)
    moved_back, sums = run(
        functools.partial(norm_one_back_kernel, vectors),
        "norm_one_back",
        rank_one,
        [moved, grad_after, even, arrived, far, side, ln_gains]
        + [learned, small, rows_two, grad_up_bias],
        [((rows + learned_rows, width), BF), ((small_rows, PAD), F32)],
    )
    moved_back = from_planes(moved_back).astype(F32)

    own_half, *pieces = run(
        half_kernel,
        "half",
        high.reshape(1),
        [kept, flip(sent, 0, 0, 1)],
        [((size, width), F32)] + [((size, width), BF)] * 3,
    )
    pieces = [
        permute(piece, lambda seq, hi, lo, step=step: (seq, (hi + step) % ranks, lo))
        for step, piece in enumerate(pieces, 1)
    ]
    (qkv_share,) = run(
        total_kernel, "total", low_one, [own_half] + pieces, [((size, width), BF)]
    )
    for seq_bits, hi_bits, lo_bits in ((1, 0, 0), (2, 0, 0), (0, 0, 1), (0, 1, 0), (0, 2, 0)):
        sums = sums + flip(sums, seq_bits, hi_bits, lo_bits)
    sum_gains, sum_shifts, sum_up_bias, sum_down_bias, sum_first, sum_mid, sum_mid_bias = run(
        functools.partial(unpack_kernel, vectors),
        "unpack",
        low_one,
        [sums],
        [
            ((3, width), F32),
            ((3, width), F32),
            ((1, hidden), F32),
            ((1, width), F32),
            ((1, CH), F32),
            ((3, CH, 9 * CH), F32),
            ((3, CH), F32),
        ],
    )
    sum_up, sum_down, sum_conv = run(
        functools.partial(finish_mlp_kernel, ranks, hidden_quarter, width, unit),
        "finish_mlp",
        rank_one,
        gather_four(mlp_share),
        [((size, hidden), F32), ((ranks * unit, width), F32), ((size, PAD), F32)],
    )
    sum_qkv, sum_out = run(
        functools.partial(finish_qkv_kernel, ranks, quarter),
        "finish_qkv",
        rank_one,
        gather_four(qkv_share),
        [((size, 3 * width), F32), ((size, width), F32)],
    )
    return (
        moved_back[rows:].reshape(1, frames_dev, CH, width),
        moved_back[:rows].reshape(1, frames_dev, patches, width),
        sum_qkv,
        sum_out,
        sum_up,
        sum_down,
        sum_conv[:, : 9 * CH],
        sum_gains,
        sum_shifts,
        sum_up_bias.reshape(hidden),
        sum_down_bias.reshape(width),
        sum_first.reshape(CH),
        sum_mid,
        sum_mid_bias,
    )


def solution(mesh):
    placed = (
        P("seq", "frame", None, None),
        P("seq", None),
        P(),
        P(),
        P("frame", None),
        P("frame", None),
        P("frame", None),
        P("frame", None),
        P(),
        P(),
        P("frame", None),
        P(),
        P(),
        P(),
        P("seq", "frame", None, None),
    )
    ranks, frame_size = mesh.shape["seq"], mesh.shape["frame"]
    body = shards_square if ranks == 4 and frame_size == 8 else shards_general
    return jax.shard_map(
        functools.partial(body, ranks, frame_size),
        mesh=mesh,
        in_specs=placed,
        out_specs=(
            P("seq", "frame", None, None),
            P("seq", "frame", None, None),
            P("frame", None),
            P("frame", None),
            P("frame", None),
            P("frame", None),
            P("frame", None),
            P(),
            P(),
            P(),
            P(),
            P(),
            P(),
            P(),
        ),
        check_vma=False,
    )
```

```python
import functools

import jax
import jax.numpy as jnp
from jax import lax
from jax.experimental import pallas as pl
from jax.experimental.pallas import tpu as pltpu
from jax.sharding import PartitionSpec as P

HEADS = 12
HEAD_DIM = 64
CH = 8
GRID = 8

EPSILON = 1e-06
FLOOR_SCORE = -1e30
HIGHEST = lax.Precision.HIGHEST
AXES = ("seq", "frame")
PLANE_OF = (0, 2, 1, 3)
RANK_OF = (0, 2, 1, 3)
VMEM_LIMIT = 56 * 1024 * 1024
BF = jnp.bfloat16
F32 = jnp.float32


def norm_stats(values):
    centre = jnp.mean(values, axis=-1, keepdims=True)
    centred = values - centre
    variance = jnp.mean(centred * centred, axis=-1, keepdims=True)
    inverse = lax.rsqrt(variance + EPSILON)
    return centred * inverse, inverse


def norm_back(normed, inverse, gain, grad):
    scaled = grad * gain
    mean_scaled = jnp.mean(scaled, axis=-1, keepdims=True)
    mean_cross = jnp.mean(scaled * normed, axis=-1, keepdims=True)
    grad_values = inverse * (scaled - mean_scaled - normed * mean_cross)
    return grad_values, jnp.sum(grad * normed, axis=0), jnp.sum(grad, axis=0)


def gelu(values):
    return jax.nn.gelu(values, approximate=False)


def conv_grid(taps):
    side = taps.shape[1]
    width = taps.shape[-1] // 9
    padded = jnp.pad(taps, ((0, 0), (1, 1), (1, 1), (0, 0)))
    total = jnp.zeros(taps.shape[:-1] + (width,), taps.dtype)
    for tap in range(9):
        offset_row = tap // 3
        offset_column = tap % 3
        total = (
            total
            + padded[
                :,
                offset_row : offset_row + side,
                offset_column : offset_column + side,
                tap * width : (tap + 1) * width,
            ]
        )
    return total


def token_maps(first, conv_mid, conv_mid_bias):
    hidden = gelu(first)
    for layer in range(3):
        frames = hidden.shape[0]
        side = hidden.shape[1]
        flat = hidden.reshape(-1, hidden.shape[-1])
        taps = jnp.dot(flat, conv_mid[layer], precision=HIGHEST).reshape(frames, side, side, -1)
        hidden = conv_grid(taps) + conv_mid_bias[layer]
        if layer < 2:
            hidden = gelu(hidden)
    return jax.nn.sigmoid(hidden)


def pool_tokens(maps, features):
    return jnp.einsum("fpk,fpd->fkd", maps, features, precision=HIGHEST) / maps.shape[1]


def dot(left, right, left_dim=1, right_dim=0):
    return lax.dot_general(
        left, right, (((left_dim,), (right_dim,)), ((), ())), preferred_element_type=F32
    )


def attend_kernel(heads, scale, q_ref, kv_ref, qclip_ref, kclip_ref, mixed_ref, log_ref):
    width = heads * HEAD_DIM
    same = kclip_ref[...] == qclip_ref[...]
    for head in range(heads):
        lanes = slice(head * HEAD_DIM, (head + 1) * HEAD_DIM)
        value_lanes = slice(width + head * HEAD_DIM, width + (head + 1) * HEAD_DIM)
        scores = dot(kv_ref[:, lanes], q_ref[:, lanes], 1, 1) * scale
        scores = jnp.where(same, scores, FLOOR_SCORE)
        top = jnp.max(scores, axis=0, keepdims=True)
        shifted = jnp.exp(scores - top)
        total = jnp.sum(shifted, axis=0, keepdims=True)
        prob = (shifted * (1.0 / total)).astype(BF)
        mixed = dot(kv_ref[:, value_lanes], prob, 0, 0)
        mixed_ref[head * HEAD_DIM : (head + 1) * HEAD_DIM, :] = mixed.astype(BF)
        log_ref[head : head + 1, :] = top + jnp.log(total)


def attend_back_kernel(
    heads, scale, q_ref, kv_ref, grad_ref, log_ref, qclip_ref, kclip_ref, dq_ref, dkv_ref
):
    width = heads * HEAD_DIM
    same = kclip_ref[...] == qclip_ref[...]

    @pl.when(pl.program_id(0) == 0)
    def _():
        dkv_ref[...] = jnp.zeros_like(dkv_ref)

    key_parts = []
    value_parts = []
    for head in range(heads):
        lanes = slice(head * HEAD_DIM, (head + 1) * HEAD_DIM)
        value_lanes = slice(width + head * HEAD_DIM, width + (head + 1) * HEAD_DIM)
        scores = dot(kv_ref[:, lanes], q_ref[:, lanes], 1, 1) * scale
        scores = jnp.where(same, scores, FLOOR_SCORE)
        prob = jnp.exp(scores - log_ref[head : head + 1, :])
        grad_prob = dot(kv_ref[:, value_lanes], grad_ref[:, lanes], 1, 1)
        delta = jnp.sum(prob * grad_prob, axis=0, keepdims=True)
        grad_score = (prob * (grad_prob - delta)).astype(BF)
        grad_query = dot(kv_ref[:, lanes], grad_score, 0, 0) * scale
        dq_ref[head * HEAD_DIM : (head + 1) * HEAD_DIM, :] = grad_query.astype(BF)
        key_parts.append(dot(grad_score, q_ref[:, lanes]) * scale)
        value_parts.append(dot(prob.astype(BF), grad_ref[:, lanes]))
    dkv_ref[...] += jnp.concatenate(key_parts + value_parts, axis=1)


def query_block(count, keys):
    return min(count, 256) if keys <= 1024 else 128


def attend(queries, keyvals, query_clip, key_clip):
    count, width = queries.shape
    keys = keyvals.shape[0]
    heads = width // HEAD_DIM
    block = query_block(count, keys)
    return pl.pallas_call(
        functools.partial(attend_kernel, heads, HEAD_DIM ** (-0.5)),
        grid=(count // block,),
        in_specs=[
            pl.BlockSpec((block, width), lambda i: (i, 0)),
            pl.BlockSpec((keys, 2 * width), lambda i: (0, 0)),
            pl.BlockSpec((1, block), lambda i: (0, i)),
            pl.BlockSpec((keys, 1), lambda i: (0, 0)),
        ],
        out_specs=[
            pl.BlockSpec((width, block), lambda i: (0, i)),
            pl.BlockSpec((8, block), lambda i: (0, i)),
        ],
        out_shape=[
            jax.ShapeDtypeStruct((width, count), BF),
            jax.ShapeDtypeStruct((8, count), F32),
        ],
        compiler_params=pltpu.CompilerParams(vmem_limit_bytes=VMEM_LIMIT),
        name="attend",
    )(queries, keyvals, query_clip, key_clip)


def attend_back(queries, keyvals, grads, logs, query_clip, key_clip):
    count, width = queries.shape
    keys = keyvals.shape[0]
    heads = width // HEAD_DIM
    block = query_block(count, keys)
    return pl.pallas_call(
        functools.partial(attend_back_kernel, heads, HEAD_DIM ** (-0.5)),
        grid=(count // block,),
        in_specs=[
            pl.BlockSpec((block, width), lambda i: (i, 0)),
            pl.BlockSpec((keys, 2 * width), lambda i: (0, 0)),
            pl.BlockSpec((block, width), lambda i: (i, 0)),
            pl.BlockSpec((8, block), lambda i: (0, i)),
            pl.BlockSpec((1, block), lambda i: (0, i)),
            pl.BlockSpec((keys, 1), lambda i: (0, 0)),
        ],
        out_specs=[
            pl.BlockSpec((width, block), lambda i: (0, i)),
            pl.BlockSpec((keys, 2 * width), lambda i: (0, 0)),
        ],
        out_shape=[
            jax.ShapeDtypeStruct((width, count), BF),
            jax.ShapeDtypeStruct((keys, 2 * width), F32),
        ],
        compiler_params=pltpu.CompilerParams(vmem_limit_bytes=VMEM_LIMIT),
        name="attend_back",
    )(queries, keyvals, grads, logs, query_clip, key_clip)


def place_kernel(size, place_ref, *refs):
    pieces, out_ref = refs[:-1], refs[-1]
    index = 0
    for piece in pieces:
        for start in range(0, piece.shape[0], size):
            place = pl.multiple_of(place_ref[index] * size, size)
            out_ref[pl.ds(place, size), :] = piece[start : start + size, :]
            index += 1


def place_rows(pieces, places, size):
    columns = pieces[0].shape[1]
    return pl.pallas_call(
        functools.partial(place_kernel, size),
        in_specs=[pl.BlockSpec(memory_space=pltpu.SMEM)]
        + [pl.BlockSpec(memory_space=pltpu.VMEM)] * len(pieces),
        out_specs=pl.BlockSpec(memory_space=pltpu.VMEM),
        out_shape=jax.ShapeDtypeStruct((len(places) * size, columns), pieces[0].dtype),
        name="place_rows",
    )(jnp.stack(places), *pieces)


def ordered(refs, rank, lanes):
    blocks = [ref[:, lanes].astype(F32) for ref in refs]
    result = []
    for index in range(len(refs)):
        found = blocks[0]
        for bits in range(1, len(refs)):
            found = jnp.where(rank == index ^ bits, blocks[bits], found)
        result.append(found)
    return result


def finish_mlp_kernel(ranks, hidden_quarter, width, unit, rank_ref, *refs):
    parts = refs[:ranks]
    up_ref, down_ref, conv_ref = refs[ranks:]
    rank = rank_ref[0]
    ups = ordered(parts, rank, slice(0, hidden_quarter))
    pieces = []
    for group in range(hidden_quarter // unit):
        for block in ups:
            pieces.append(block[:, group * unit : (group + 1) * unit])
    up_ref[...] = jnp.concatenate(pieces, axis=1)
    size = parts[0].shape[0]
    downs = ordered(parts, rank, slice(hidden_quarter, hidden_quarter + width))
    for index in range(ranks):
        down_ref[index * size : (index + 1) * size, :] = downs[index]
    convs = ordered(parts, rank, slice(hidden_quarter + width, parts[0].shape[1]))
    total = convs[0]
    for block in convs[1:]:
        total = total + block
    conv_ref[...] = total[:, : conv_ref.shape[1]]


def finish_qkv_kernel(ranks, quarter, rank_ref, *refs):
    parts = refs[:ranks]
    qkv_ref, out_ref = refs[ranks:]
    rank = rank_ref[0]
    blocks = ordered(parts, rank, slice(0, parts[0].shape[1]))
    pieces = []
    for part in range(3):
        for block in blocks:
            pieces.append(block[:, part * quarter : (part + 1) * quarter])
    qkv_ref[...] = jnp.concatenate(pieces, axis=1)
    out_ref[...] = jnp.concatenate([block[:, 3 * quarter :] for block in blocks], axis=1)


def finish(kernel, rank, parts, shapes, name):
    return pl.pallas_call(
        kernel,
        in_specs=[pl.BlockSpec(memory_space=pltpu.SMEM)]
        + [pl.BlockSpec(memory_space=pltpu.VMEM)] * len(parts),
        out_specs=[pl.BlockSpec(memory_space=pltpu.VMEM)] * len(shapes),
        out_shape=[jax.ShapeDtypeStruct(shape, F32) for shape in shapes],
        compiler_params=pltpu.CompilerParams(vmem_limit_bytes=VMEM_LIMIT),
        name=name,
    )(rank.reshape(1), *parts)


def shards_general(
    ranks,
    frame_size,
    inputs,
    clip_id,
    ln_gains,
    ln_biases,
    w_qkv,
    w_out,
    w_up,
    w_down,
    up_bias,
    down_bias,
    conv_first,
    conv_first_bias,
    conv_mid,
    conv_mid_bias,
    cotangent,
):
    lows = frame_size // ranks
    frames_dev = inputs.shape[1]
    patches = inputs.shape[2]
    width = inputs.shape[3]
    rows = frames_dev * patches
    hidden = up_bias.shape[0]
    quarter = width // ranks
    hidden_quarter = hidden // ranks
    row_shard = width // frame_size
    rank = lax.axis_index("seq")
    place = lax.axis_index("frame")
    high = place // lows
    low = place % lows

    def permute(array, target):
        pairs = []
        for seq in range(ranks):
            for hi in range(ranks):
                for lo in range(lows):
                    to_seq, to_hi, to_lo = target(seq, hi, lo)
                    pairs.append(
                        (
                            seq * frame_size + hi * lows + lo,
                            to_seq * frame_size + to_hi * lows + to_lo,
                        )
                    )
        return lax.ppermute(array, AXES, pairs)

    def across(array, bits):
        return permute(array, lambda seq, hi, lo: (seq ^ bits, hi, lo))

    def along_high(array, step):
        return permute(array, lambda seq, hi, lo: (seq, (hi + step) % ranks, lo))

    def along_low(array, step):
        return permute(array, lambda seq, hi, lo: (seq, hi, (lo + step) % lows))

    def to_planes(array):
        return permute(array, lambda seq, hi, lo: (RANK_OF[hi], PLANE_OF[seq], lo))

    def from_planes(array):
        return permute(
            array, lambda seq, hi, lo: (PLANE_OF.index(hi), RANK_OF.index(seq), lo)
        )

    def flip_high(array, bits):
        return permute(array, lambda seq, hi, lo: (seq, hi ^ bits, lo))

    def gather_tokens(block):
        far = across(block, 2)
        near = across(block, 1)
        both = across(far, 1)
        return jnp.concatenate([block, near, far, both], axis=0)

    def scatter_tokens(partial):
        blocks = partial.astype(BF).reshape(ranks, rows, partial.shape[1])
        arrived_far = across(blocks[3], 1)
        arrived_near = across(blocks[1], 1)
        far = partial[2 * rows : 3 * rows] + arrived_far.astype(F32)
        arrived = across(far.astype(BF), 2)
        return partial[:rows] + arrived_near.astype(F32) + arrived.astype(F32)

    half_rows = rows // 2

    def gather_plane(block):
        if lows != 2:
            own = gather_tokens(block)
            return jnp.concatenate(
                [own] + [along_low(own, step) for step in range(1, lows)], axis=0
            )
        far = across(block, 2)
        side = along_low(block, 1)
        near = across(block, 1)
        corner = jnp.concatenate(
            [along_low(far[:half_rows], 1), across(side[half_rows:], 2)], axis=0
        )
        return jnp.concatenate(
            [
                block,
                near,
                far,
                across(far, 1),
                side,
                across(side, 1),
                corner,
                across(corner, 1),
            ],
            axis=0,
        )

    def scatter_plane(partial):
        if lows != 2:
            count = ranks * rows
            own = partial[:count]
            for step in range(1, lows):
                piece = partial[step * count : (step + 1) * count].astype(BF)
                own = own + along_low(piece, -step).astype(F32)
            return scatter_tokens(own)
        blocks = [partial[index * rows : (index + 1) * rows] for index in range(2 * ranks)]
        sums = {}
        for index in (6, 4, 2, 0):
            sums[index] = blocks[index] + across(blocks[index + 1].astype(BF), 1).astype(F32)
        corner = sums[6].astype(BF)
        by_far = across(corner[:half_rows], 2).astype(F32)
        by_side = along_low(corner[half_rows:], 1).astype(F32)
        side = jnp.concatenate([sums[4][:half_rows] + by_far, sums[4][half_rows:]], axis=0)
        far = jnp.concatenate([sums[2][:half_rows], sums[2][half_rows:] + by_side], axis=0)
        return (
            sums[0]
            + across(far.astype(BF), 2).astype(F32)
            + along_low(side.astype(BF), 1).astype(F32)
        )

    places = [(high ^ bits) * lows + low for bits in (0, 2, 1, 3)] + [
        (high ^ bits) * lows + (low + 1) % lows for bits in (0, 2, 1, 3)
    ]

    def after(array, *others):
        return lax.optimization_barrier((array,) + others)[0]

    staged = lows == 2

    def gather_two(block):
        return jnp.concatenate([block, flip_high(block, 2)], axis=0) if staged else block

    def gather_four(two):
        return jnp.concatenate([two, flip_high(two, 1)], axis=0) if staged else two

    def gather_all(four):
        if not staged:
            return lax.all_gather(four, "frame", axis=0, tiled=True)
        return place_rows([four, along_low(four, 1)], places, four.shape[0] // ranks)

    def scatter_half(partials):
        if not staged:
            return jnp.concatenate([partial.astype(BF) for partial in partials], axis=1)
        columns = [partial.shape[1] for partial in partials]
        cuts = [sum(columns[:index]) for index in range(len(columns) + 1)]
        count = partials[0].shape[0] // frame_size
        splits = [
            partial.reshape(ranks, lows, count, partial.shape[1]) for partial in partials
        ]
        sent = jnp.concatenate(
            [lax.dynamic_index_in_dim(split.astype(BF), 1 - low, 1, False) for split in splits],
            axis=2,
        )
        arrived = along_low(sent, 1)
        return jnp.concatenate(
            [
                lax.dynamic_index_in_dim(split, low, 1, False)
                + arrived[:, :, cuts[index] : cuts[index + 1]].astype(F32)
                for index, split in enumerate(splits)
            ],
            axis=2,
        ).reshape(2, 2, count, cuts[-1])

    def scatter_rest(half):
        if not staged:
            return lax.psum_scatter(half, "frame", scatter_dimension=0, tiled=True)
        sent = lax.dynamic_index_in_dim(half, 1 - high % 2, 1, False).astype(BF)
        kept = lax.dynamic_index_in_dim(half, high % 2, 1, False)
        two = kept + flip_high(sent, 1).astype(F32)
        sent = lax.dynamic_index_in_dim(two, 1 - high // 2, 0, False).astype(BF)
        kept = lax.dynamic_index_in_dim(two, high // 2, 0, False)
        return (kept + flip_high(sent, 2).astype(F32)).astype(BF)

    def swap_ranks(blocks):
        split = blocks.reshape((2, 2) + blocks.shape[1:])
        kept = lax.dynamic_index_in_dim(split, rank // 2, 0, False)
        found = across(lax.dynamic_index_in_dim(split, 1 - rank // 2, 0, False), 2)
        own = lax.dynamic_index_in_dim(kept, rank % 2, 0, False)
        far = lax.dynamic_index_in_dim(found, rank % 2, 0, False)
        near = across(lax.dynamic_index_in_dim(kept, 1 - rank % 2, 0, False), 1)
        both = across(lax.dynamic_index_in_dim(found, 1 - rank % 2, 0, False), 1)
        return in_rank_order([own, near, far, both])

    def sum_everywhere(array):
        bits = 1
        while bits < ranks:
            array = array + across(array, bits)
            bits *= 2
        bits = 1
        while bits < frame_size:
            pairs = [
                (seq * frame_size + item, seq * frame_size + (item ^ bits))
                for seq in range(ranks)
                for item in range(frame_size)
            ]
            array = array + lax.ppermute(array, AXES, pairs)
            bits *= 2
        return array

    def in_rank_order(items):
        stacked = jnp.stack(items)
        return [
            lax.dynamic_index_in_dim(stacked, rank ^ index, 0, False) for index in range(ranks)
        ]

    def gather_ranks(block):
        far = across(block, 2)
        near = across(block, 1)
        both = across(far, 1)
        return [block, near, far, both]

    token_rows = inputs[0].reshape(rows, width)
    grad_rows = cotangent[0].reshape(frames_dev * CH, width)
    frame_count = clip_id.shape[1]
    clip_rows = jnp.pad(
        clip_id.astype(BF), ((0, 15), (0, width - frame_count))
    )
    moved = to_planes(jnp.concatenate([token_rows, grad_rows, clip_rows], axis=0))
    tokens = moved[:rows].astype(F32)
    grad_learned = moved[rows : rows + frames_dev * CH].astype(F32)
    clips = moved[rows + frames_dev * CH, :frame_count].astype(jnp.int32)

    own_qkv = jnp.concatenate(
        [
            lax.dynamic_slice_in_dim(w_qkv, part * width + rank * quarter, quarter, 1)
            for part in range(3)
        ],
        axis=1,
    )
    two_qkv = gather_two(own_qkv)
    unit = hidden // (frame_size * ranks)
    columns = jnp.arange(hidden_quarter, dtype=jnp.int32)
    wanted = (columns // unit) * (unit * ranks) + rank * unit + columns % unit
    choose = (jnp.arange(hidden, dtype=jnp.int32)[:, None] == wanted[None, :]).astype(BF)
    own_up = dot(w_up, choose).astype(BF)
    own_down = lax.dynamic_slice_in_dim(w_down, rank * unit, unit, 0)
    own_out = lax.dynamic_slice_in_dim(w_out, rank * quarter, quarter, 1)
    own_out = jnp.concatenate([own_out, conv_first], axis=1)
    two_out = gather_two(after(own_out, two_qkv))
    four_qkv = gather_four(two_qkv)
    two_up = gather_two(after(own_up, two_out))
    four_out = gather_four(after(two_out, four_qkv))
    qkv_quarter = gather_all(four_qkv)
    two_down = gather_two(after(own_down, two_up))
    four_up = gather_four(after(two_up, four_out))
    qkv_quarter = after(qkv_quarter, four_out, two_up)
    packed = gather_all(after(four_out, qkv_quarter))
    out_columns = packed[:, :quarter]
    full_conv = packed[:, quarter:]
    out_quarter = jnp.concatenate(
        swap_ranks(out_columns.reshape(ranks, quarter, quarter)), axis=1
    )
    up_bias_quarter = lax.dynamic_index_in_dim(
        up_bias.reshape(frame_size, ranks, unit), rank, 1, False
    ).reshape(1, hidden_quarter)

    frame_ids = jnp.arange(frame_count, dtype=jnp.int32)

    def clip_tokens(lo):
        blocks = []
        inverse = jnp.array([RANK_OF.index(item) for item in range(ranks)], jnp.int32)
        for bits in range(ranks):
            hi = lax.dynamic_index_in_dim(inverse, rank ^ bits, 0, False)
            for frame in range(frames_dev):
                blocks.append((hi * lows + lo) * frames_dev + frame)
        wanted_frames = jnp.stack(blocks)
        found = jnp.sum(
            jnp.where(wanted_frames[:, None] == frame_ids[None, :], clips[None, :], 0), axis=1
        )
        return jnp.broadcast_to(found[:, None], (found.shape[0], patches)).reshape(-1)

    query_clip = clip_tokens(low)
    key_clip = jnp.concatenate(
        [query_clip] + [clip_tokens((low - step) % lows) for step in range(1, lows)]
    )
    query_clip = query_clip[None, :]
    key_clip = key_clip[:, None]

    normed_one, inverse_one = norm_stats(tokens)
    own_count = ranks * rows
    all_one = gather_plane((normed_one * ln_gains[0] + ln_biases[0]).astype(BF))
    queries = dot(all_one[:own_count], qkv_quarter[:, :quarter]).astype(BF)
    keyvals = dot(all_one, qkv_quarter[:, quarter:]).astype(BF)
    queries = after(queries, packed, four_up, two_down)
    up_quarter = gather_all(after(four_up, packed))
    four_down = gather_four(two_down)
    attended, logs = attend(queries, keyvals, query_clip, key_clip)
    after_attention = tokens + scatter_tokens(dot(attended, out_quarter, 0, 0))
    after_attention = after(after_attention, four_down)
    down_quarter = gather_all(after(four_down, up_quarter))
    normed_two, inverse_two = norm_stats(after_attention)
    all_two = gather_tokens((normed_two * ln_gains[1] + ln_biases[1]).astype(BF))
    pre_act = dot(all_two, up_quarter) + up_bias_quarter
    act_low = gelu(pre_act).astype(BF)
    block_out = after_attention + scatter_tokens(dot(act_low, down_quarter)) + down_bias

    normed_three, inverse_three = norm_stats(block_out)
    normed_three_low = (normed_three * ln_gains[2] + ln_biases[2]).astype(BF)
    tap_rows = dot(normed_three_low, full_conv).reshape(frames_dev, GRID, GRID, 9 * CH)
    first = conv_grid(tap_rows) + conv_first_bias
    features = block_out.reshape(frames_dev, patches, width)

    def tail(first_arg, features_arg, mid_arg, mid_bias_arg):
        maps = token_maps(first_arg, mid_arg, mid_bias_arg).reshape(frames_dev, patches, CH)
        return pool_tokens(maps, features_arg)

    learned, tail_back = jax.vjp(tail, first, features, conv_mid, conv_mid_bias)
    grad_first, grad_pool, grad_mid, grad_mid_bias = tail_back(
        grad_learned.reshape(frames_dev, CH, width)
    )
    grad_first_low = grad_first.astype(BF)
    grad_first_bias = jnp.sum(grad_first_low.astype(F32), axis=(0, 1, 2))
    spread_unused, spread_back = jax.vjp(conv_grid, tap_rows)
    spread = spread_back(grad_first_low.astype(F32))[0].reshape(rows, 9 * CH).astype(BF)
    grad_conv = dot(normed_three_low, spread, 0, 0)
    grad_normed_three = dot(spread, full_conv, 1, 1)
    grad_block, grad_gain_three, grad_shift_three = norm_back(
        normed_three, inverse_three, ln_gains[2], grad_normed_three
    )
    grad_block = grad_block + grad_pool.reshape(rows, width)
    grad_mlp = grad_block.astype(BF)
    grad_down_bias = jnp.sum(grad_mlp.astype(F32), axis=0)

    all_mlp = gather_tokens(grad_mlp)
    grad_act = dot(all_mlp, down_quarter, 1, 1)
    gelu_unused, gelu_back = jax.vjp(gelu, pre_act)
    grad_pre = gelu_back(grad_act)[0].astype(BF)
    grad_up_bias = jnp.sum(grad_pre.astype(F32), axis=0)
    grad_normed_two = scatter_tokens(dot(grad_pre, up_quarter, 1, 1))
    grad_down = dot(act_low, all_mlp, 0, 0)
    grad_up = dot(all_two, grad_pre, 0, 0)
    mlp_half = scatter_half([grad_up, grad_down, grad_conv])
    grad_after, grad_gain_two, grad_shift_two = norm_back(
        normed_two, inverse_two, ln_gains[1], grad_normed_two
    )
    grad_after = grad_after + grad_block

    all_branch = gather_tokens(grad_after.astype(BF))
    grad_attended = dot(all_branch, out_quarter, 1, 1).astype(BF)
    grad_out = dot(attended, all_branch)
    grad_attended = after(grad_attended, mlp_half)
    mlp_share = scatter_rest(mlp_half)
    grad_queries, grad_keyvals = attend_back(
        queries, keyvals, grad_attended, logs, query_clip, key_clip
    )
    grad_queries = grad_queries.T
    grad_keyvals = grad_keyvals.astype(BF)
    grad_normed_own = dot(grad_keyvals, qkv_quarter[:, quarter:], 1, 1)
    grad_normed_own = jnp.concatenate(
        [
            grad_normed_own[:own_count] + dot(grad_queries, qkv_quarter[:, :quarter], 1, 1),
            grad_normed_own[own_count:],
        ],
        axis=0,
    )
    grad_normed_one = scatter_plane(grad_normed_own)
    grad_q = dot(all_one[:own_count], grad_queries, 0, 0)
    grad_kv = dot(all_one, grad_keyvals, 0, 0)
    grad_out_columns = jnp.concatenate(
        swap_ranks(grad_out.astype(BF).reshape(quarter, ranks, quarter).transpose(1, 0, 2)),
        axis=0,
    )
    qkv_share = scatter_rest(
        after(scatter_half([grad_q, grad_kv, grad_out_columns]), mlp_share)
    )
    grad_tokens, grad_gain_one, grad_shift_one = norm_back(
        normed_one, inverse_one, ln_gains[0], grad_normed_one
    )
    moved_back = from_planes(
        jnp.concatenate(
            [
                (grad_after + grad_tokens).astype(BF),
                learned.astype(BF).reshape(frames_dev * CH, width),
            ],
            axis=0,
        )
    ).astype(F32)
    grad_input = moved_back[:rows]
    learned = moved_back[rows:]

    sum_up, sum_down, sum_conv = finish(
        functools.partial(finish_mlp_kernel, ranks, hidden_quarter, width, unit),
        rank,
        gather_ranks(mlp_share),
        [(row_shard, hidden), (ranks * unit, width), (row_shard, 9 * CH)],
        "finish_mlp",
    )
    sum_qkv, sum_out = finish(
        functools.partial(finish_qkv_kernel, ranks, quarter),
        rank,
        gather_ranks(qkv_share),
        [(row_shard, 3 * width), (row_shard, width)],
        "finish_qkv",
    )

    conv_terms = jnp.concatenate(
        [grad_first_bias.reshape(-1), grad_mid.reshape(-1), grad_mid_bias.reshape(-1)]
    )
    conv_rows = -(-conv_terms.shape[0] // width)
    conv_terms = jnp.pad(conv_terms, (0, conv_rows * width - conv_terms.shape[0]))
    up_terms = jnp.where(
        jnp.arange(ranks, dtype=jnp.int32)[:, None] == rank,
        grad_up_bias.reshape(1, hidden_quarter),
        0.0,
    )
    early = sum_everywhere(
        jnp.concatenate(
            [
                jnp.stack(
                    [
                        grad_gain_one,
                        grad_gain_two,
                        grad_gain_three,
                        grad_shift_one,
                        grad_shift_two,
                        grad_shift_three,
                        grad_down_bias,
                    ]
                ),
                conv_terms.reshape(conv_rows, width),
                up_terms.reshape(-1, width),
            ],
            axis=0,
        )
    )
    sum_gains = early[0:3]
    sum_shifts = early[3:6]
    conv_sums = early[7 : 7 + conv_rows].reshape(-1)
    sum_up_bias = (
        early[7 + conv_rows :]
        .reshape(ranks, frame_size, unit)
        .transpose(1, 0, 2)
        .reshape(hidden)
    )
    mid_count = grad_mid.size
    sum_mid = conv_sums[CH : CH + mid_count].reshape(grad_mid.shape)
    sum_mid_bias = conv_sums[CH + mid_count : CH + mid_count + grad_mid_bias.size]
    return (
        learned.reshape(1, frames_dev, CH, width),
        grad_input.reshape(1, frames_dev, patches, width),
        sum_qkv,
        sum_out,
        sum_up,
        sum_down,
        sum_conv,
        sum_gains,
        sum_shifts,
        sum_up_bias,
        early[6],
        conv_sums[:CH],
        sum_mid,
        sum_mid_bias.reshape(grad_mid_bias.shape),
    )


PAD = 128


def run(kernel, name, scalars, arrays, outs, scratch=(), limit=16):
    vmem = pl.BlockSpec(memory_space=pltpu.VMEM)
    return pl.pallas_call(
        kernel,
        in_specs=[pl.BlockSpec(memory_space=pltpu.SMEM)] + [vmem] * len(arrays),
        out_specs=[vmem] * len(outs),
        out_shape=[jax.ShapeDtypeStruct(shape, kind) for shape, kind in outs],
        scratch_shapes=list(scratch),
        compiler_params=pltpu.CompilerParams(vmem_limit_bytes=limit * 1024 * 1024),
        name=name,
    )(scalars, *arrays)


def rows_at(start, size):
    return pl.ds(pl.multiple_of(start * size, size), size)


def stack_rows(refs):
    return jnp.concatenate([ref[...] for ref in refs], axis=0)


def exact(left, right, left_dim=1, right_dim=0):
    return lax.dot_general(
        left,
        right,
        (((left_dim,), (right_dim,)), ((), ())),
        precision=HIGHEST,
        preferred_element_type=F32,
    )


def column_sum(values):
    return jnp.sum(values, axis=0, keepdims=True)


def back_of_norm(values, gain, grad):
    normed, inverse = norm_stats(values)
    scaled = grad * gain
    mean_scaled = jnp.mean(scaled, axis=-1, keepdims=True)
    mean_cross = jnp.mean(scaled * normed, axis=-1, keepdims=True)
    result = inverse * (scaled - mean_scaled - normed * mean_cross)
    return result, column_sum(grad * normed), column_sum(grad)


def pack_kernel(unused_ref, tokens_ref, grads_ref, clip_ref, pack_ref):
    count, width = tokens_ref.shape
    more = grads_ref.shape[0]
    pack_ref[:count, :] = tokens_ref[...]
    pack_ref[count : count + more, :] = grads_ref[...]
    clips = clip_ref[...].astype(F32)
    clips = jnp.concatenate([clips, jnp.zeros((1, PAD - clips.shape[1]), F32)], axis=1)
    pack_ref[count + more :, :] = jnp.zeros((pack_ref.shape[0] - count - more, width), BF)
    pack_ref[count + more :, :PAD] = jnp.broadcast_to(
        clips, (pack_ref.shape[0] - count - more, PAD)
    ).astype(BF)


def select_kernel(ids_ref, qkv_ref, out_ref, own_ref):
    width = out_ref.shape[1]
    quarter = width // 4
    for rank in range(4):

        @pl.when(ids_ref[0] == rank)
        def _(rank=rank):
            pieces = [
                qkv_ref[:, part * width + rank * quarter : part * width + (rank + 1) * quarter]
                for part in range(3)
            ]
            pieces.append(out_ref[:, rank * quarter : (rank + 1) * quarter])
            own_ref[...] = jnp.concatenate(pieces, axis=1)


def prepare_kernel(ids_ref, up_ref, down_ref, conv_ref, own_ref, more_ref):
    size = own_ref.shape[0]
    unit = down_ref.shape[0] // 4
    quarter = 8 * unit
    for rank in range(4):

        @pl.when(ids_ref[0] == rank)
        def _(rank=rank):
            own_ref[:, :quarter] = jnp.concatenate(
                [
                    up_ref[:, (4 * group + rank) * unit : (4 * group + rank + 1) * unit]
                    for group in range(8)
                ],
                axis=1,
            )
            more_ref[...] = down_ref[rank * unit : (rank + 1) * unit, :]

    taps = conv_ref.shape[1]
    own_ref[:, quarter:] = jnp.concatenate(
        [conv_ref[...], jnp.zeros((size, PAD - taps), BF)], axis=1
    )


def norm_one_kernel(ids_ref, moved_ref, gains_ref, shifts_ref, low_ref, qclip_ref, kclip_ref):
    count = low_ref.shape[0]
    frames = count // (GRID * GRID)
    patches = GRID * GRID
    normed, unused = norm_stats(moved_ref[:count, :].astype(F32))
    low_ref[...] = (normed * gains_ref[0:1, :] + shifts_ref[0:1, :]).astype(BF)
    start = count + frames * CH
    clips = moved_ref[start : start + 16, :PAD].astype(F32)[0:1]
    lane = lax.broadcasted_iota(jnp.int32, (1, PAD), 1)
    rank, low = ids_ref[0], ids_ref[2]
    for side in range(2):
        for bits in range(4):
            for frame in range(frames):
                hi = sum(jnp.where(rank ^ bits == RANK_OF[item], item, 0) for item in range(4))
                wanted = (2 * hi + (low ^ side)) * frames + frame
                clip = jnp.sum(jnp.where(lane == wanted, clips, 0.0), axis=1, keepdims=True)
                first = ((4 * side + bits) * frames + frame) * patches
                kclip_ref[first : first + patches, :] = jnp.broadcast_to(clip, (patches, 1))
                if side == 0:
                    qclip_ref[:, first : first + patches] = jnp.broadcast_to(clip, (1, patches))


def pass_sum_kernel(index, unused_ref, even_ref, arrived_ref, out_ref):
    out_ref[...] = (even_ref[index] + arrived_ref[...].astype(F32)).astype(BF)


def add_kernel(unused_ref, left_ref, right_ref, out_ref):
    out_ref[...] = left_ref[...] + right_ref[...]


def pick_kernel(ids_ref, far_ref, side_ref, out_ref):
    @pl.when(lax.rem(ids_ref[0], 2) == 0)
    def _():
        out_ref[...] = far_ref[...]

    @pl.when(lax.rem(ids_ref[0], 2) == 1)
    def _():
        out_ref[...] = side_ref[...]


def pass_on_kernel(ids_ref, even_ref, second_ref, third_ref, corner_ref, far_ref, side_ref):
    core = lax.rem(ids_ref[0], 2)
    corner = corner_ref[...].astype(F32)
    far = even_ref[1] + second_ref[...].astype(F32)
    side = even_ref[2] + third_ref[...].astype(F32)
    far_ref[...] = (far + jnp.where(core == 1, corner, 0.0)).astype(BF)
    side_ref[...] = (side + jnp.where(core == 0, corner, 0.0)).astype(BF)


def place_of(ids_ref, bits):
    return (2 * ids_ref[1] + ids_ref[2]) ^ bits


def project_kernel(quarter, ids_ref, *refs):
    tokens, blocks = refs[:8], refs[8:16]
    q_ref, kv_ref, w_ref = refs[16:19]
    out_refs, all_ref = refs[19:23], refs[23]
    size = blocks[0].shape[0]
    for bits in range(8):
        where = rows_at(place_of(ids_ref, bits), size)
        w_ref[where, :] = blocks[bits][:, : 3 * quarter]
        all_ref[where, :] = blocks[bits][:, 3 * quarter :]
    rank = ids_ref[0]
    for bits in range(4):
        out_refs[bits][...] = all_ref[rows_at(rank ^ bits, quarter), :]
    own = dot(stack_rows(tokens[:4]), w_ref[...]).astype(BF)
    q_ref[...] = own[:, :quarter]
    half = own.shape[0]
    kv_ref[:half, :] = own[:, quarter:]
    kv_ref[half:, :] = dot(stack_rows(tokens[4:]), w_ref[:, quarter:]).astype(BF)


def scores_of(kv_ref, q_ref, queries, lanes, same, scale):
    raw = dot(kv_ref[:, lanes], q_ref[queries, lanes], 1, 1) * scale
    return jnp.where(same, raw, FLOOR_SCORE)


def attend_wide_kernel(heads, scale, unused_ref, *refs):
    q_ref, kv_ref, qclip_ref, kclip_ref, mixed_ref, log_ref = refs
    width = heads * HEAD_DIM
    count = q_ref.shape[0] // 2
    for part in range(2):
        queries = slice(part * count, (part + 1) * count)
        same = kclip_ref[...] == qclip_ref[:, queries]
        for head in range(heads):
            lanes = slice(head * HEAD_DIM, (head + 1) * HEAD_DIM)
            values = slice(width + head * HEAD_DIM, width + (head + 1) * HEAD_DIM)
            scores = scores_of(kv_ref, q_ref, queries, lanes, same, scale)
            top = jnp.max(scores, axis=0, keepdims=True)
            shifted = jnp.exp(scores - top)
            total = jnp.sum(shifted, axis=0, keepdims=True)
            prob = (shifted * (1.0 / total)).astype(BF)
            mixed_ref[lanes, queries] = dot(kv_ref[:, values], prob, 0, 0).astype(BF)
            log_ref[head : head + 1, queries] = top + jnp.log(total)


def split_blocks(values, even_ref, odd_refs):
    rows = even_ref.shape[1]
    for part in range(even_ref.shape[0]):
        even_ref[part] = values[2 * part * rows : (2 * part + 1) * rows]
        odd_refs[part][...] = values[(2 * part + 1) * rows : (2 * part + 2) * rows].astype(BF)


def out_kernel(rank_ref, *refs):
    mixed_ref = refs[0]
    even_ref, odd_refs, w_ref = refs[5], refs[6:8], refs[8]
    blocks = [ref[...] for ref in refs[1:5]]
    rank = rank_ref[0]
    width = blocks[0].shape[0]
    for index in range(4):
        found = blocks[0]
        for bits in range(1, 4):
            found = jnp.where(rank == index ^ bits, blocks[bits], found)
        w_ref[:, index * width : (index + 1) * width] = found
    split_blocks(dot(mixed_ref[...], w_ref[...], 0, 0), even_ref, odd_refs)


def norm_two_kernel(unused_ref, *refs):
    moved_ref, even_ref, arrived_ref, far_ref, gains_ref, shifts_ref = refs[:6]
    sum_ref, low_ref = refs[6:]
    count = low_ref.shape[0]
    values = (
        moved_ref[:count, :].astype(F32)
        + even_ref[0]
        + arrived_ref[...].astype(F32)
        + far_ref[...].astype(F32)
    )
    sum_ref[...] = values
    normed, unused = norm_stats(values)
    low_ref[...] = (normed * gains_ref[1:2, :] + shifts_ref[1:2, :]).astype(BF)


def gelu_both(values):
    size = jnp.abs(values) * 0.7071067811865476
    ratio = 1.0 / (1.0 + 0.3275911 * size)
    bell = jnp.exp(-size * size)
    series = ratio * (
        0.254829592
        + ratio
        * (-0.284496736 + ratio * (1.421413741 + ratio * (-1.453152027 + ratio * 1.061405429)))
    )
    tail = 0.5 * series * bell
    below = jnp.where(values >= 0.0, 1.0 - tail, tail)
    return values * below, below + values * bell * 0.3989422804014327


def join_kernel(unused_ref, *refs):
    for index, ref in enumerate(refs[4:]):
        size = ref.shape[0] // 2
        ref[:size, :] = refs[2 * index][...]
        ref[size:, :] = refs[2 * index + 1][...]


def mlp_kernel(ids_ref, *refs):
    tokens = refs[:4]
    a_refs, b_refs, bias_ref = refs[4:6], refs[6:8], refs[8]
    act_ref, slope_ref, up_ref, down_ref, conv_ref, even_ref = refs[9:15]
    odd_refs = refs[15:]
    rank = ids_ref[0]
    size = a_refs[0].shape[0] // 4
    quarter = up_ref.shape[1]
    for ref, order in zip(a_refs, ((0, 4, 2, 6), (1, 5, 3, 7))):
        for index, bits in enumerate(order):
            where = rows_at(place_of(ids_ref, bits), size)
            rows = slice(index * size, (index + 1) * size)
            up_ref[where, :] = ref[rows, :quarter]
            conv_ref[where, :] = ref[rows, quarter:]
    for ref, order in zip(b_refs, ((0, 1, 4, 5), (2, 3, 6, 7))):
        for index, bits in enumerate(order):
            where = rows_at(place_of(ids_ref, bits), size)
            down_ref[where, :] = ref[index * size : (index + 1) * size, :]
    count = tokens[0].shape[0]
    unit = quarter // 8
    bias = None
    for index in range(4):
        found = jnp.concatenate(
            [
                bias_ref[:, (4 * group + index) * unit : (4 * group + index + 1) * unit]
                for group in range(8)
            ],
            axis=1,
        )
        bias = found if bias is None else jnp.where(rank == index, found, bias)
    for part in range(2):
        rows = slice(2 * part * count, 2 * (part + 1) * count)
        pre = dot(stack_rows(tokens[2 * part : 2 * part + 2]), up_ref[...]) + bias
        act, slope = gelu_both(pre)
        act = act.astype(BF)
        act_ref[rows, :] = act
        slope_ref[rows, :] = slope
        partial = dot(act, down_ref[...])
        even_ref[part] = partial[:count]
        odd_refs[part][...] = partial[count:].astype(BF)


def grid_masks(count):
    row = lax.broadcasted_iota(jnp.int32, (count, PAD), 0)
    i = (row // GRID) % GRID
    j = row % GRID
    masks = []
    for tap in range(9):
        di, dj = tap // 3 - 1, tap % 3 - 1
        inside = (i + di >= 0) & (i + di < GRID) & (j + dj >= 0) & (j + dj < GRID)
        masks.append(inside.astype(F32))
    return masks


def collect_taps(taps, masks, first_lanes):
    count = taps.shape[0]
    total = None
    for tap in range(9):
        offset = (tap // 3 - 1) * GRID + tap % 3 - 1
        moved = pltpu.roll(taps, (PAD - tap * CH) % PAD, 1) if tap else taps
        moved = pltpu.roll(moved, (-offset) % count, 0) if offset else moved
        moved = moved * masks[tap]
        total = moved if total is None else total + moved
    return total * first_lanes


def spread_taps(values, masks):
    count = values.shape[0]
    total = None
    for tap in range(9):
        offset = (tap // 3 - 1) * GRID + tap % 3 - 1
        moved = pltpu.roll(values, tap * CH, 1) if tap else values
        moved = pltpu.roll(moved, offset % count, 0) if offset else moved
        moved = moved * masks[8 - tap]
        total = moved if total is None else total + moved
    return total


def store_rows(ref, start, values):
    for index in range(values.shape[1] // PAD):
        ref[start + index : start + index + 1, :] = values[:, index * PAD : (index + 1) * PAD]


def load_rows(ref, start, count):
    return jnp.concatenate(
        [ref[start + index : start + index + 1, :] for index in range(count)], axis=1
    )


def tail_kernel(vectors, unused_ref, *refs):
    sum_ref, even_ref, arrived_ref, far_ref, bias_ref, gains_ref, shifts_ref = refs[:7]
    conv_ref, first_bias_ref, mid_ref, mid_bias_ref, moved_ref = refs[7:12]
    learned_ref, low_ref, grad_ref, normed_ref, spread_ref, small_ref = refs[12:]
    count = low_ref.shape[0]
    frames = count // (GRID * GRID)
    patches = GRID * GRID
    value = (
        sum_ref[...]
        + even_ref[0]
        + arrived_ref[...].astype(F32)
        + far_ref[...].astype(F32)
        + bias_ref[...]
    )
    normed, inverse = norm_stats(value)
    gain = gains_ref[2:3, :]
    normed_low = (normed * gain + shifts_ref[2:3, :]).astype(BF)
    normed_ref[...] = normed_low
    masks = grid_masks(count)
    lane = lax.broadcasted_iota(jnp.int32, (count, PAD), 1)
    first_lanes = (lane < CH).astype(F32)
    first = collect_taps(dot(normed_low, conv_ref[...]), masks, first_lanes)
    hidden, slope = gelu_both(first + first_bias_ref[...])
    hidden = hidden * first_lanes
    hiddens, slopes = [hidden], [slope]
    maps = None
    for layer in range(3):
        pre = collect_taps(exact(hiddens[layer], mid_ref[layer]), masks, first_lanes)
        pre = pre + mid_bias_ref[layer : layer + 1, :]
        if layer < 2:
            hidden, slope = gelu_both(pre)
            hiddens.append(hidden * first_lanes)
            slopes.append(slope)
        else:
            maps = jax.nn.sigmoid(pre) * first_lanes
    pooled_parts, map_parts = [], []
    zero_rows = jnp.zeros((PAD - CH, value.shape[1]), F32)
    for frame in range(frames):
        rows = slice(frame * patches, (frame + 1) * patches)
        start = count + frame * CH
        cotangent = jnp.concatenate(
            [moved_ref[start : start + CH, :].astype(F32), zero_rows], axis=0
        )
        learned = exact(maps[rows], value[rows], 0, 0)[:CH] * (1.0 / patches)
        learned_ref[frame * CH : (frame + 1) * CH, :] = learned
        pooled_parts.append(exact(maps[rows], cotangent) * (1.0 / patches))
        map_parts.append(exact(value[rows], cotangent, 1, 1) * (1.0 / patches))
    grad = jnp.concatenate(map_parts, axis=0) * maps * (1.0 - maps)
    small_ref[...] = jnp.zeros_like(small_ref)
    conv_start = 7 * vectors + 4 * vectors
    for layer in range(2, -1, -1):
        taps = spread_taps(grad, masks)
        weight = exact(hiddens[layer], taps, 0, 0)[:CH]
        small_ref[conv_start + layer * CH : conv_start + (layer + 1) * CH, :] = weight
        bias_row = conv_start + 3 * CH + 1 + layer
        small_ref[bias_row : bias_row + 1, :] = column_sum(grad)
        grad = exact(taps, mid_ref[layer], 1, 1) * slopes[layer]
    grad_low = grad.astype(BF).astype(F32)
    small_ref[conv_start + 3 * CH : conv_start + 3 * CH + 1, :] = column_sum(grad_low)
    spread = spread_taps(grad_low, masks).astype(BF)
    spread_ref[...] = spread
    grad_normed = dot(spread, conv_ref[...], 1, 1)
    scaled = grad_normed * gain
    mean_scaled = jnp.mean(scaled, axis=-1, keepdims=True)
    mean_cross = jnp.mean(scaled * normed, axis=-1, keepdims=True)
    grad_value = inverse * (scaled - mean_scaled - normed * mean_cross)
    grad_value = grad_value + jnp.concatenate(pooled_parts, axis=0)
    grad_ref[...] = grad_value
    low = grad_value.astype(BF)
    low_ref[...] = low
    store_rows(small_ref, 2 * vectors, column_sum(grad_normed * normed))
    store_rows(small_ref, 5 * vectors, column_sum(grad_normed))
    store_rows(small_ref, 6 * vectors, column_sum(low.astype(F32)))


def mlp_back_kernel(unused_ref, *refs):
    grads = refs[:4]
    slope_ref, up_ref, down_ref = refs[4:7]
    pre_ref, even_ref, bias_ref = refs[7], refs[8], refs[11]
    odd_refs = refs[9:11]
    count = grads[0].shape[0]
    total = None
    for part in range(2):
        rows = slice(2 * part * count, 2 * (part + 1) * count)
        grad_act = dot(stack_rows(grads[2 * part : 2 * part + 2]), down_ref[...], 1, 1)
        grad_pre = (grad_act * slope_ref[rows, :]).astype(BF)
        pre_ref[rows, :] = grad_pre
        term = column_sum(grad_pre.astype(F32))
        total = term if total is None else total + term
        partial = dot(grad_pre, up_ref[...], 1, 1)
        even_ref[part] = partial[:count]
        odd_refs[part][...] = partial[count:].astype(BF)
    bias_ref[...] = total


def divide_rows(ids_ref, all_ref, refs):
    kept_ref, sent_ref, more_kept_ref, more_sent_ref = refs
    high, low = ids_ref[1], ids_ref[2]
    size = all_ref.shape[0] // 8
    columns = kept_ref.shape[1]
    for index in range(4):
        rows = slice(index * size, (index + 1) * size)
        kept_ref[rows, :] = all_ref[rows_at(2 * index + low, size), :columns]
        sent_ref[rows, :] = all_ref[rows_at(2 * index + 1 - low, size), :columns].astype(BF)
        hi = high ^ (index // 2 * 2)
        lo = low ^ (index % 2)
        more_kept_ref[rows, :] = all_ref[rows_at(2 * hi + lo, size), columns:]
        more_sent_ref[rows, :] = all_ref[rows_at(2 * (hi ^ 1) + lo, size), columns:].astype(BF)


def mlp_grads_kernel(ids_ref, *refs):
    tokens, grads = refs[:4], refs[4:8]
    act_ref, pre_ref, normed_ref, spread_ref = refs[8:12]
    all_ref = refs[16]
    quarter = act_ref.shape[1]
    width = tokens[0].shape[1]
    all_ref[:, :quarter] = dot(stack_rows(tokens), pre_ref[...], 0, 0)
    all_ref[:, quarter : quarter + width] = dot(act_ref[...], stack_rows(grads), 0, 0)
    all_ref[:, quarter + width :] = dot(normed_ref[...], spread_ref[...], 0, 0)
    divide_rows(ids_ref, all_ref, refs[12:16])


def norm_two_back_kernel(unused_ref, *refs):
    sum_ref, grad_ref, even_ref, arrived_ref, far_ref, gains_ref = refs[:6]
    total_ref, low_ref, rows_ref = refs[6:]
    grad_normed = even_ref[0] + arrived_ref[...].astype(F32) + far_ref[...].astype(F32)
    result, gain_row, shift_row = back_of_norm(sum_ref[...], gains_ref[1:2, :], grad_normed)
    total = result + grad_ref[...]
    total_ref[...] = total
    low_ref[...] = total.astype(BF)
    rows_ref[0:1, :] = gain_row
    rows_ref[1:2, :] = shift_row


def attend_back_out_kernel(heads, scale, unused_ref, *refs):
    branches = refs[:4]
    out_ref, q_ref, kv_ref, log_ref, qclip_ref, kclip_ref, w_ref = refs[4:11]
    own_ref, other_ref, even_ref = refs[11:14]
    odd_refs, total_ref = refs[14:18], refs[18]
    width = heads * HEAD_DIM
    count = q_ref.shape[0] // 2
    rows = count // 2
    for part in range(2):
        queries = slice(part * count, (part + 1) * count)
        grad_mixed = dot(
            stack_rows(branches[2 * part : 2 * part + 2]), out_ref[...], 1, 1
        ).astype(BF)
        same = kclip_ref[...] == qclip_ref[:, queries]
        query_parts, key_parts, value_parts = [], [], []
        for head in range(heads):
            lanes = slice(head * HEAD_DIM, (head + 1) * HEAD_DIM)
            values = slice(width + head * HEAD_DIM, width + (head + 1) * HEAD_DIM)
            scores = scores_of(kv_ref, q_ref, queries, lanes, same, scale)
            prob = jnp.exp(scores - log_ref[head : head + 1, queries])
            grad_prob = dot(kv_ref[:, values], grad_mixed[:, lanes], 1, 1)
            delta = jnp.sum(prob * grad_prob, axis=0, keepdims=True)
            grad_score = (prob * (grad_prob - delta)).astype(BF)
            query_parts.append(dot(kv_ref[:, lanes], grad_score, 0, 0) * scale)
            key_parts.append(dot(grad_score, q_ref[queries, lanes]) * scale)
            value_parts.append(dot(prob.astype(BF), grad_mixed[:, lanes]))
        own_ref[queries, :width] = jnp.concatenate(query_parts, axis=0).T.astype(BF)
        terms = jnp.concatenate(key_parts + value_parts, axis=1)
        if part == 0:
            total_ref[...] = terms
        else:
            total_ref[...] += terms
    own_ref[:, width:] = total_ref[: 2 * count, :].astype(BF)
    other_ref[...] = total_ref[2 * count :, :].astype(BF)
    own = dot(own_ref[...], w_ref[...], 1, 1)
    other = dot(other_ref[...], w_ref[:, width:], 1, 1)
    split_blocks(jnp.concatenate([own, other], axis=0), even_ref, odd_refs)


def qkv_grads_kernel(ids_ref, *refs):
    tokens, branches, mixes = refs[:8], refs[8:12], refs[12:16]
    own_ref, other_ref = refs[16:18]
    all_ref = refs[22]
    quarter = mixes[0].shape[0]
    full = dot(stack_rows(tokens[:4]), own_ref[...], 0, 0)
    more = dot(stack_rows(tokens[4:]), other_ref[...], 0, 0)
    all_ref[:, :quarter] = full[:, :quarter]
    all_ref[:, quarter : 3 * quarter] = full[:, quarter:] + more
    rank = ids_ref[0]
    branch = stack_rows(branches)
    wanted = branch[:, :quarter]
    for index in range(1, 4):
        wanted = jnp.where(
            rank == index, branch[:, index * quarter : (index + 1) * quarter], wanted
        )
    count = branches[0].shape[0]
    for bits in range(4):
        turned = jnp.concatenate(
            [wanted[(item ^ bits) * count : ((item ^ bits) + 1) * count] for item in range(4)],
            axis=0,
        )
        all_ref[rows_at(rank ^ bits, quarter), 3 * quarter :] = dot(mixes[bits][...], turned)
    divide_rows(ids_ref, all_ref, refs[18:22])


def half_kernel(ids_ref, *refs):
    kept_ref, arrived_ref, more_kept_ref, more_arrived_ref = refs[:4]
    own_ref, sent_ref, more_own_ref, more_sent_ref = refs[4:]
    size = own_ref.shape[0] // 2
    high = ids_ref[1]
    for step in range(2):
        rows = slice(step * size, (step + 1) * size)
        where = rows_at(high ^ (2 * step), size)
        own_ref[rows, :] = kept_ref[where, :] + arrived_ref[where, :].astype(F32)
        where = rows_at(high ^ (2 * step + 1), size)
        sent_ref[rows, :] = (kept_ref[where, :] + arrived_ref[where, :].astype(F32)).astype(BF)
    more = more_kept_ref[...] + more_arrived_ref[...].astype(F32)
    more_own_ref[...] = more[: 2 * size]
    more_sent_ref[...] = more[2 * size :].astype(BF)


def fourth_kernel(unused_ref, *refs):
    for kept_ref, arrived_ref, own_ref, sent_ref in (refs[0:2] + refs[4:6], refs[2:4] + refs[6:8]):
        size = own_ref.shape[0]
        own_ref[...] = kept_ref[:size, :] + arrived_ref[:size, :].astype(F32)
        sent_ref[...] = (kept_ref[size:, :] + arrived_ref[size:, :].astype(F32)).astype(BF)


def total_kernel(unused_ref, kept_ref, arrived_ref, more_kept_ref, more_arrived_ref, out_ref):
    columns = kept_ref.shape[1]
    out_ref[:, :columns] = (kept_ref[...] + arrived_ref[...].astype(F32)).astype(BF)
    out_ref[:, columns:] = (more_kept_ref[...] + more_arrived_ref[...].astype(F32)).astype(BF)


def norm_one_back_kernel(vectors, rank_ref, *refs):
    moved_ref, grad_ref, even_ref, arrived_ref, far_ref, side_ref, gains_ref = refs[:7]
    learned_ref, small_ref, two_ref, up_ref, back_ref, sums_ref = refs[7:]
    count = grad_ref.shape[0]
    grad_normed = (
        even_ref[0]
        + arrived_ref[...].astype(F32)
        + far_ref[...].astype(F32)
        + side_ref[...].astype(F32)
    )
    result, gain_row, shift_row = back_of_norm(
        moved_ref[:count, :].astype(F32), gains_ref[0:1, :], grad_normed
    )
    back_ref[:count, :] = (result + grad_ref[...]).astype(BF)
    back_ref[count:, :] = learned_ref[...].astype(BF)
    sums_ref[...] = small_ref[...]
    store_rows(sums_ref, 0, gain_row)
    store_rows(sums_ref, vectors, two_ref[0:1, :])
    store_rows(sums_ref, 3 * vectors, shift_row)
    store_rows(sums_ref, 4 * vectors, two_ref[1:2, :])
    for index in range(4):
        store_rows(
            sums_ref,
            (7 + index) * vectors,
            jnp.where(rank_ref[0] == index, up_ref[...], 0.0),
        )


def back_kernel(unused_ref, moved_ref, grad_ref, learned_ref):
    count = grad_ref.shape[0]
    grad_ref[...] = moved_ref[:count, :].astype(F32)
    learned_ref[...] = moved_ref[count:, :].astype(F32)


def unpack_kernel(vectors, unused_ref, part_ref, arrived_ref, *refs):
    sums_ref = refs[-1]
    refs = refs[:-1]
    sums_ref[...] = part_ref[...] + arrived_ref[...]
    gains_ref, shifts_ref, up_ref, down_ref, first_ref, mid_ref, mid_bias_ref = refs
    for index in range(3):
        gains_ref[index : index + 1, :] = load_rows(sums_ref, index * vectors, vectors)
        shifts_ref[index : index + 1, :] = load_rows(sums_ref, (3 + index) * vectors, vectors)
    down_ref[...] = load_rows(sums_ref, 6 * vectors, vectors)
    quarters = [load_rows(sums_ref, (7 + index) * vectors, vectors) for index in range(4)]
    unit = quarters[0].shape[1] // 8
    up_ref[...] = jnp.concatenate(
        [
            quarters[index][:, group * unit : (group + 1) * unit]
            for group in range(8)
            for index in range(4)
        ],
        axis=1,
    )
    start = 11 * vectors
    for layer in range(3):
        mid_ref[layer] = sums_ref[start + layer * CH : start + (layer + 1) * CH, : 9 * CH]
    start = start + 3 * CH
    first_ref[...] = sums_ref[start : start + 1, :CH]
    mid_bias_ref[...] = sums_ref[start + 1 : start + 4, :CH]


def shards_square(
    ranks,
    frame_size,
    inputs,
    clip_id,
    ln_gains,
    ln_biases,
    w_qkv,
    w_out,
    w_up,
    w_down,
    up_bias,
    down_bias,
    conv_first,
    conv_first_bias,
    conv_mid,
    conv_mid_bias,
    cotangent,
):
    lows = 2
    frames_dev = inputs.shape[1]
    patches = inputs.shape[2]
    width = inputs.shape[3]
    rows = frames_dev * patches
    learned_rows = frames_dev * CH
    hidden = up_bias.shape[0]
    quarter = width // ranks
    heads = quarter // HEAD_DIM
    hidden_quarter = hidden // ranks
    unit = hidden_quarter // frame_size
    size = width // frame_size
    vectors = width // PAD
    own_count = ranks * rows
    place = lax.axis_index("frame")
    ids = jnp.stack([lax.axis_index("seq"), place // lows, place % lows])

    def permute(array, target):
        pairs = []
        for seq in range(ranks):
            for hi in range(ranks):
                for lo in range(lows):
                    to_seq, to_hi, to_lo = target(seq, hi, lo)
                    pairs.append(
                        (
                            seq * frame_size + hi * lows + lo,
                            to_seq * frame_size + to_hi * lows + to_lo,
                        )
                    )
        return lax.ppermute(array, AXES, pairs)

    def flip(array, seq_bits, hi_bits=0, lo_bits=0):
        return permute(
            array, lambda seq, hi, lo: (seq ^ seq_bits, hi ^ hi_bits, lo ^ lo_bits)
        )

    def after(array, *others):
        return lax.optimization_barrier((array,) + others)[0]

    last = []

    def ordered_run(kernel, name, scalars, arrays, outs, scratch=()):
        if last:
            arrays = [after(arrays[0], last[0])] + list(arrays[1:])
        results = run(kernel, name, scalars, arrays, outs, scratch)
        last[:] = [results[-1]]
        return results

    def to_planes(array):
        return permute(array, lambda seq, hi, lo: (RANK_OF[hi], PLANE_OF[seq], lo))

    def from_planes(array):
        return permute(
            array, lambda seq, hi, lo: (PLANE_OF.index(hi), RANK_OF.index(seq), lo)
        )

    def gather_four(block):
        far = flip(block, 2)
        near = flip(block, 1)
        return [block, near, far, flip(far, 1)]

    def pass_sum(even, arrived, index, name):
        (result,) = ordered_run(
            functools.partial(pass_sum_kernel, index),
            name,
            ids,
            [even, arrived],
            [((rows, width), BF)],
        )
        return result

    def scatter_four(even, odds, name):
        far = flip(pass_sum(even, flip(odds[1], 1), 1, name), 2)
        return flip(odds[0], 1), far

    def row_parts(blocks, first, second):
        return [
            ((blocks * size, columns), kind) for columns in (first, second) for kind in (F32, BF)
        ]

    def scatter_half(parts, name):
        kept, sent, more_kept, more_sent = parts
        return ordered_run(
            half_kernel,
            name,
            ids,
            [kept, flip(sent, 0, 0, 1), more_kept, flip(more_sent, 0, 1)],
            row_parts(2, kept.shape[1], more_kept.shape[1]),
        )

    def scatter_fourth(parts, name):
        kept, sent, more_kept, more_sent = parts
        return ordered_run(
            fourth_kernel,
            name,
            ids,
            [kept, flip(sent, 0, 1), more_kept, flip(more_sent, 0, 2)],
            row_parts(1, kept.shape[1], more_kept.shape[1]),
        )

    def scatter_last(parts, name):
        kept, sent, more_kept, more_sent = parts
        (share,) = ordered_run(
            total_kernel,
            name,
            ids,
            [kept, flip(sent, 0, 2), more_kept, flip(more_sent, 0, 0, 1)],
            [((size, kept.shape[1] + more_kept.shape[1]), BF)],
        )
        return share

    def add(left, right, name):
        return ordered_run(add_kernel, name, ids, [left, right], [(left.shape, F32)])[0]

    (pack,) = ordered_run(
        pack_kernel,
        "pack",
        ids,
        [inputs.reshape(rows, width), cotangent.reshape(learned_rows, width), clip_id],
        [((rows + learned_rows + 16, width), BF)],
    )
    moved = to_planes(pack)

    (own_pack,) = ordered_run(
        select_kernel, "select", ids, [w_qkv, w_out], [((size, width), BF)]
    )
    pack_two = flip(own_pack, 0, 2)
    pack_one = flip(own_pack, 0, 1)
    pack_side = flip(own_pack, 0, 0, 1)
    pack_three = flip(pack_two, 0, 1)
    packs = [own_pack, pack_side]
    for item in (pack_one, pack_two, pack_three):
        packs += [item, flip(item, 0, 0, 1)]

    low_norm, query_clip, key_clip = ordered_run(
        norm_one_kernel,
        "norm_one",
        ids,
        [moved, ln_gains, ln_biases],
        [((rows, width), BF), ((1, own_count), F32), ((2 * own_count, 1), F32)],
    )
    low_norm = after(low_norm, pack_side, pack_one, pack_two)

    mid_pad = jnp.pad(conv_mid, ((0, 0), (0, PAD - CH), (0, PAD - 9 * CH)))
    mid_bias_pad = jnp.pad(conv_mid_bias, ((0, 0), (0, PAD - CH)))
    first_bias_pad = jnp.pad(conv_first_bias, (0, PAD - CH)).reshape(1, PAD)
    up_bias_row = up_bias.reshape(1, hidden)
    down_bias_row = down_bias.reshape(1, width)

    own_a, own_b = ordered_run(
        prepare_kernel,
        "prepare",
        ids,
        [
            after(w_up, mid_pad, mid_bias_pad, first_bias_pad, up_bias_row, down_bias_row),
            w_down,
            conv_first,
        ],
        [((size, hidden_quarter + PAD), BF), ((size, width), BF)],
    )

    def join(pairs, name):
        flat = [item for pair in pairs for item in pair]
        outs = [((2 * pair[0].shape[0], pair[0].shape[1]), BF) for pair in pairs]
        return ordered_run(join_kernel, name, ids, flat, outs)

    far = flip(low_norm, 2)
    side = flip(low_norm, 0, 0, 1)
    near = flip(low_norm, 1)
    (picked,) = ordered_run(
        pick_kernel,
        "pick",
        ids,
        [after(far, *[packs[item] for item in (3, 5, 6)]), side],
        [((rows, width), BF)],
    )
    corner = permute(
        picked,
        lambda seq, hi, lo: (seq, hi, lo ^ 1) if seq % 2 == 0 else (seq ^ 2, hi, lo),
    )
    far_near = flip(far, 1)
    side_near = flip(side, 1)
    corner = after(corner, near, far_near, side_near, packs[7])
    all_one = [near, far, far_near, side, side_near, corner, flip(corner, 1)]
    all_one = [low_norm] + all_one
    two_a, two_b = join(
        [(own_a, flip(own_a, 0, 2)), (own_b, flip(own_b, 0, 0, 1))], "join_two"
    )

    queries, keyvals, qkv_quarter, own_out, near_out, far_out, both_out = ordered_run(
        functools.partial(project_kernel, quarter),
        "project",
        ids,
        all_one + packs,
        [
            ((own_count, quarter), BF),
            ((2 * own_count, 2 * quarter), BF),
            ((width, 3 * quarter), BF),
        ]
        + [((quarter, quarter), BF)] * 4,
        [pltpu.VMEM((width, quarter), BF)],
    )
    out_blocks = [own_out, flip(near_out, 1), flip(far_out, 2), flip(both_out, 3)]
    scale = HEAD_DIM ** (-0.5)
    attended, logs = ordered_run(
        functools.partial(attend_wide_kernel, heads, scale),
        "attend",
        ids,
        [queries, keyvals, query_clip, key_clip],
        [((quarter, own_count), BF), ((8, own_count), F32)],
    )
    halves = [((2, rows, width), F32)] + [((rows, width), BF)] * 2
    even, *odds, out_quarter = ordered_run(
        out_kernel,
        "out",
        ids,
        [attended] + out_blocks,
        halves + [((quarter, width), BF)],
    )
    arrived, far = scatter_four(even, odds, "out_pass")
    four_a, four_b = join(
        [(two_a, flip(two_a, 0, 1)), (two_b, flip(two_b, 0, 2))], "join_four"
    )
    after_attention, low_two = ordered_run(
        norm_two_kernel,
        "norm_two",
        ids,
        [moved, even, arrived, far, ln_gains, ln_biases],
        [((rows, width), F32), ((rows, width), BF)],
    )
    all_two = gather_four(low_two)
    act, slope, up_full, down_full, conv_full, even, *odds = ordered_run(
        mlp_kernel,
        "mlp",
        ids,
        all_two
        + [four_a, flip(four_a, 0, 0, 1), four_b, flip(four_b, 0, 1), up_bias_row],
        [
            ((own_count, hidden_quarter), BF),
            ((own_count, hidden_quarter), F32),
            ((width, hidden_quarter), BF),
            ((hidden_quarter, width), BF),
            ((width, PAD), BF),
        ]
        + halves,
    )
    arrived, far = scatter_four(even, odds, "mlp_pass")

    small_rows = -(-(11 * vectors + 3 * CH + 4) // 8) * 8
    learned, low_mlp, grad_block, low_three, spread, small = ordered_run(
        functools.partial(tail_kernel, vectors),
        "tail",
        ids,
        [
            after_attention,
            even,
            arrived,
            far,
            down_bias_row,
            ln_gains,
            ln_biases,
            conv_full,
            first_bias_pad,
            mid_pad,
            mid_bias_pad,
            moved,
        ],
        [
            ((learned_rows, width), F32),
            ((rows, width), BF),
            ((rows, width), F32),
            ((rows, width), BF),
            ((rows, PAD), BF),
            ((small_rows, PAD), F32),
        ],
    )
    mixes = gather_four(after(attended, far))

    all_mlp = gather_four(low_mlp)
    grad_pre, even, *odds, grad_up_bias = ordered_run(
        mlp_back_kernel,
        "mlp_back",
        ids,
        all_mlp + [after(slope, *mixes), up_full, down_full],
        [((own_count, hidden_quarter), BF)] + halves + [((1, hidden_quarter), F32)],
    )
    arrived, far = scatter_four(even, odds, "mlp_back_pass")
    columns = hidden_quarter + width + PAD
    mlp_parts = ordered_run(
        mlp_grads_kernel,
        "mlp_grads",
        ids,
        all_two + all_mlp + [act, grad_pre, low_three, spread],
        row_parts(4, hidden_quarter, width + PAD),
        [pltpu.VMEM((width, columns), F32)],
    )
    grad_after, low_branch, rows_two = ordered_run(
        norm_two_back_kernel,
        "norm_two_back",
        ids,
        [after_attention, grad_block, even, arrived, far, ln_gains],
        [((rows, width), F32), ((rows, width), BF), ((2, width), F32)],
    )

    all_branch = gather_four(low_branch)
    grads_own, grads_other, even, *odds = ordered_run(
        functools.partial(attend_back_out_kernel, heads, scale),
        "attend_back_out",
        ids,
        all_branch + [out_quarter, queries, keyvals, logs, query_clip, key_clip, qkv_quarter],
        [
            ((own_count, 3 * quarter), BF),
            ((own_count, 2 * quarter), BF),
            ((4, rows, width), F32),
        ]
        + [((rows, width), BF)] * 4,
        [pltpu.VMEM((2 * own_count, 2 * quarter), F32)],
    )
    arrived = [flip(item, 1) for item in odds]
    corner = permute(
        pass_sum(even, arrived[3], 3, "corner_pass"),
        lambda seq, hi, lo: (seq ^ 2, hi, lo) if seq % 2 == 0 else (seq, hi, lo ^ 1),
    )
    mlp_parts = scatter_half(mlp_parts, "mlp_half")
    qkv_parts = ordered_run(
        qkv_grads_kernel,
        "qkv_grads",
        ids,
        all_one + all_branch + mixes + [grads_own, grads_other],
        row_parts(4, width // 2, width // 2),
        [pltpu.VMEM((width, width), F32)],
    )
    far, side = ordered_run(
        pass_on_kernel,
        "pass_on",
        ids,
        [even, arrived[1], arrived[2], corner],
        [((rows, width), BF), ((rows, width), BF)],
    )
    far, side = flip(far, 2), flip(side, 0, 0, 1)
    mlp_parts = scatter_fourth(mlp_parts, "mlp_fourth")
    qkv_parts = list(lax.optimization_barrier(tuple(qkv_parts) + (mlp_parts[0],))[:4])
    moved_back, sums = ordered_run(
        functools.partial(norm_one_back_kernel, vectors),
        "norm_one_back",
        ids,
        [moved, grad_after, even, arrived[0], far, side, ln_gains]
        + [learned, small, rows_two, grad_up_bias],
        [((rows + learned_rows, width), BF), ((small_rows, PAD), F32)],
    )

    mlp_share = scatter_last(mlp_parts, "mlp_total")
    qkv_parts = scatter_half(qkv_parts, "qkv_half")
    sums = add(sums, flip(sums, 1), "sum_core")
    grad_input, learned = ordered_run(
        back_kernel,
        "back",
        ids,
        [from_planes(moved_back)],
        [((rows, width), F32), ((learned_rows, width), F32)],
    )
    sums = add(sums, flip(sums, 2), "sum_x")
    qkv_parts = scatter_fourth(qkv_parts, "qkv_fourth")
    sums = add(sums, flip(sums, 0, 0, 1), "sum_y")
    sum_up, sum_down, sum_conv = ordered_run(
        functools.partial(finish_mlp_kernel, ranks, hidden_quarter, width, unit),
        "finish_mlp",
        ids,
        gather_four(mlp_share),
        [((size, hidden), F32), ((ranks * unit, width), F32), ((size, 9 * CH), F32)],
    )
    qkv_share = scatter_last(qkv_parts, "qkv_total")
    sums = add(sums, flip(sums, 0, 1), "sum_z")
    sum_gains, sum_shifts, sum_up_bias, sum_down_bias, sum_first, sum_mid, sum_mid_bias = (
        ordered_run(
            functools.partial(unpack_kernel, vectors),
            "unpack",
            ids,
            [sums, flip(sums, 0, 2)],
            [
                ((3, width), F32),
                ((3, width), F32),
                ((1, hidden), F32),
                ((1, width), F32),
                ((1, CH), F32),
                ((3, CH, 9 * CH), F32),
                ((3, CH), F32),
            ],
            [pltpu.VMEM((small_rows, PAD), F32)],
        )
    )
    sum_qkv, sum_out = ordered_run(
        functools.partial(finish_qkv_kernel, ranks, quarter),
        "finish_qkv",
        ids,
        gather_four(qkv_share),
        [((size, 3 * width), F32), ((size, width), F32)],
    )
    return (
        learned.reshape(1, frames_dev, CH, width),
        grad_input.reshape(1, frames_dev, patches, width),
        sum_qkv,
        sum_out,
        sum_up,
        sum_down,
        sum_conv,
        sum_gains,
        sum_shifts,
        sum_up_bias.reshape(hidden),
        sum_down_bias.reshape(width),
        sum_first.reshape(CH),
        sum_mid,
        sum_mid_bias,
    )


def solution(mesh):
    placed = (
        P("seq", "frame", None, None),
        P("seq", None),
        P(),
        P(),
        P("frame", None),
        P("frame", None),
        P("frame", None),
        P("frame", None),
        P(),
        P(),
        P("frame", None),
        P(),
        P(),
        P(),
        P("seq", "frame", None, None),
    )
    ranks, frame_size = mesh.shape["seq"], mesh.shape["frame"]
    body = shards_square if ranks == 4 and frame_size == 8 else shards_general
    return jax.shard_map(
        functools.partial(body, ranks, frame_size),
        mesh=mesh,
        in_specs=placed,
        out_specs=(
            P("seq", "frame", None, None),
            P("seq", "frame", None, None),
            P("frame", None),
            P("frame", None),
            P("frame", None),
            P("frame", None),
            P("frame", None),
            P(),
            P(),
            P(),
            P(),
            P(),
            P(),
            P(),
        ),
        check_vma=False,
    )
```

```python
import functools

import jax
import jax.numpy as jnp
from jax import lax
from jax.experimental import pallas as pl
from jax.experimental.pallas import tpu as pltpu
from jax.sharding import PartitionSpec as P

HEADS = 12
HEAD_DIM = 64
CH = 8
GRID = 8

EPSILON = 1e-06
FLOOR_SCORE = -1e30
HIGHEST = lax.Precision.HIGHEST
AXES = ("seq", "frame")
PLANE_OF = (0, 2, 1, 3)
RANK_OF = (0, 2, 1, 3)
VMEM_LIMIT = 56 * 1024 * 1024
BF = jnp.bfloat16
F32 = jnp.float32


def norm_stats(values):
    centre = jnp.mean(values, axis=-1, keepdims=True)
    centred = values - centre
    variance = jnp.mean(centred * centred, axis=-1, keepdims=True)
    inverse = lax.rsqrt(variance + EPSILON)
    return centred * inverse, inverse


def norm_back(normed, inverse, gain, grad):
    scaled = grad * gain
    mean_scaled = jnp.mean(scaled, axis=-1, keepdims=True)
    mean_cross = jnp.mean(scaled * normed, axis=-1, keepdims=True)
    grad_values = inverse * (scaled - mean_scaled - normed * mean_cross)
    return grad_values, jnp.sum(grad * normed, axis=0), jnp.sum(grad, axis=0)


def gelu(values):
    return jax.nn.gelu(values, approximate=False)


def conv_grid(taps):
    side = taps.shape[1]
    width = taps.shape[-1] // 9
    padded = jnp.pad(taps, ((0, 0), (1, 1), (1, 1), (0, 0)))
    total = jnp.zeros(taps.shape[:-1] + (width,), taps.dtype)
    for tap in range(9):
        offset_row = tap // 3
        offset_column = tap % 3
        total = (
            total
            + padded[
                :,
                offset_row : offset_row + side,
                offset_column : offset_column + side,
                tap * width : (tap + 1) * width,
            ]
        )
    return total


def token_maps(first, conv_mid, conv_mid_bias):
    hidden = gelu(first)
    for layer in range(3):
        frames = hidden.shape[0]
        side = hidden.shape[1]
        flat = hidden.reshape(-1, hidden.shape[-1])
        taps = jnp.dot(flat, conv_mid[layer], precision=HIGHEST).reshape(frames, side, side, -1)
        hidden = conv_grid(taps) + conv_mid_bias[layer]
        if layer < 2:
            hidden = gelu(hidden)
    return jax.nn.sigmoid(hidden)


def pool_tokens(maps, features):
    return jnp.einsum("fpk,fpd->fkd", maps, features, precision=HIGHEST) / maps.shape[1]


def dot(left, right, left_dim=1, right_dim=0):
    return lax.dot_general(
        left, right, (((left_dim,), (right_dim,)), ((), ())), preferred_element_type=F32
    )


def attend_kernel(heads, scale, q_ref, kv_ref, qclip_ref, kclip_ref, mixed_ref, log_ref):
    width = heads * HEAD_DIM
    same = kclip_ref[...] == qclip_ref[...]
    for head in range(heads):
        lanes = slice(head * HEAD_DIM, (head + 1) * HEAD_DIM)
        value_lanes = slice(width + head * HEAD_DIM, width + (head + 1) * HEAD_DIM)
        scores = dot(kv_ref[:, lanes], q_ref[:, lanes], 1, 1) * scale
        scores = jnp.where(same, scores, FLOOR_SCORE)
        top = jnp.max(scores, axis=0, keepdims=True)
        shifted = jnp.exp(scores - top)
        total = jnp.sum(shifted, axis=0, keepdims=True)
        prob = (shifted * (1.0 / total)).astype(BF)
        mixed = dot(kv_ref[:, value_lanes], prob, 0, 0)
        mixed_ref[head * HEAD_DIM : (head + 1) * HEAD_DIM, :] = mixed.astype(BF)
        log_ref[head : head + 1, :] = top + jnp.log(total)


def attend_back_kernel(
    heads, scale, q_ref, kv_ref, grad_ref, log_ref, qclip_ref, kclip_ref, dq_ref, dkv_ref
):
    width = heads * HEAD_DIM
    same = kclip_ref[...] == qclip_ref[...]

    @pl.when(pl.program_id(0) == 0)
    def _():
        dkv_ref[...] = jnp.zeros_like(dkv_ref)

    key_parts = []
    value_parts = []
    for head in range(heads):
        lanes = slice(head * HEAD_DIM, (head + 1) * HEAD_DIM)
        value_lanes = slice(width + head * HEAD_DIM, width + (head + 1) * HEAD_DIM)
        scores = dot(kv_ref[:, lanes], q_ref[:, lanes], 1, 1) * scale
        scores = jnp.where(same, scores, FLOOR_SCORE)
        prob = jnp.exp(scores - log_ref[head : head + 1, :])
        grad_prob = dot(kv_ref[:, value_lanes], grad_ref[:, lanes], 1, 1)
        delta = jnp.sum(prob * grad_prob, axis=0, keepdims=True)
        grad_score = (prob * (grad_prob - delta)).astype(BF)
        grad_query = dot(kv_ref[:, lanes], grad_score, 0, 0) * scale
        dq_ref[head * HEAD_DIM : (head + 1) * HEAD_DIM, :] = grad_query.astype(BF)
        key_parts.append(dot(grad_score, q_ref[:, lanes]) * scale)
        value_parts.append(dot(prob.astype(BF), grad_ref[:, lanes]))
    dkv_ref[...] += jnp.concatenate(key_parts + value_parts, axis=1)


def query_block(count, keys):
    return min(count, 256) if keys <= 1024 else 128


def attend(queries, keyvals, query_clip, key_clip):
    count, width = queries.shape
    keys = keyvals.shape[0]
    heads = width // HEAD_DIM
    block = query_block(count, keys)
    return pl.pallas_call(
        functools.partial(attend_kernel, heads, HEAD_DIM ** (-0.5)),
        grid=(count // block,),
        in_specs=[
            pl.BlockSpec((block, width), lambda i: (i, 0)),
            pl.BlockSpec((keys, 2 * width), lambda i: (0, 0)),
            pl.BlockSpec((1, block), lambda i: (0, i)),
            pl.BlockSpec((keys, 1), lambda i: (0, 0)),
        ],
        out_specs=[
            pl.BlockSpec((width, block), lambda i: (0, i)),
            pl.BlockSpec((8, block), lambda i: (0, i)),
        ],
        out_shape=[
            jax.ShapeDtypeStruct((width, count), BF),
            jax.ShapeDtypeStruct((8, count), F32),
        ],
        compiler_params=pltpu.CompilerParams(vmem_limit_bytes=VMEM_LIMIT),
        name="attend",
    )(queries, keyvals, query_clip, key_clip)


def attend_back(queries, keyvals, grads, logs, query_clip, key_clip):
    count, width = queries.shape
    keys = keyvals.shape[0]
    heads = width // HEAD_DIM
    block = query_block(count, keys)
    return pl.pallas_call(
        functools.partial(attend_back_kernel, heads, HEAD_DIM ** (-0.5)),
        grid=(count // block,),
        in_specs=[
            pl.BlockSpec((block, width), lambda i: (i, 0)),
            pl.BlockSpec((keys, 2 * width), lambda i: (0, 0)),
            pl.BlockSpec((block, width), lambda i: (i, 0)),
            pl.BlockSpec((8, block), lambda i: (0, i)),
            pl.BlockSpec((1, block), lambda i: (0, i)),
            pl.BlockSpec((keys, 1), lambda i: (0, 0)),
        ],
        out_specs=[
            pl.BlockSpec((width, block), lambda i: (0, i)),
            pl.BlockSpec((keys, 2 * width), lambda i: (0, 0)),
        ],
        out_shape=[
            jax.ShapeDtypeStruct((width, count), BF),
            jax.ShapeDtypeStruct((keys, 2 * width), F32),
        ],
        compiler_params=pltpu.CompilerParams(vmem_limit_bytes=VMEM_LIMIT),
        name="attend_back",
    )(queries, keyvals, grads, logs, query_clip, key_clip)


def place_kernel(size, place_ref, *refs):
    pieces, out_ref = refs[:-1], refs[-1]
    index = 0
    for piece in pieces:
        for start in range(0, piece.shape[0], size):
            place = pl.multiple_of(place_ref[index] * size, size)
            out_ref[pl.ds(place, size), :] = piece[start : start + size, :]
            index += 1


def place_rows(pieces, places, size):
    columns = pieces[0].shape[1]
    return pl.pallas_call(
        functools.partial(place_kernel, size),
        in_specs=[pl.BlockSpec(memory_space=pltpu.SMEM)]
        + [pl.BlockSpec(memory_space=pltpu.VMEM)] * len(pieces),
        out_specs=pl.BlockSpec(memory_space=pltpu.VMEM),
        out_shape=jax.ShapeDtypeStruct((len(places) * size, columns), pieces[0].dtype),
        name="place_rows",
    )(jnp.stack(places), *pieces)


def ordered(refs, rank, lanes):
    blocks = [ref[:, lanes].astype(F32) for ref in refs]
    result = []
    for index in range(len(refs)):
        found = blocks[0]
        for bits in range(1, len(refs)):
            found = jnp.where(rank == index ^ bits, blocks[bits], found)
        result.append(found)
    return result


def finish_mlp_kernel(ranks, hidden_quarter, width, unit, rank_ref, *refs):
    parts = refs[:ranks]
    up_ref, down_ref, conv_ref = refs[ranks:]
    rank = rank_ref[0]
    ups = ordered(parts, rank, slice(0, hidden_quarter))
    pieces = []
    for group in range(hidden_quarter // unit):
        for block in ups:
            pieces.append(block[:, group * unit : (group + 1) * unit])
    up_ref[...] = jnp.concatenate(pieces, axis=1)
    size = parts[0].shape[0]
    downs = ordered(parts, rank, slice(hidden_quarter, hidden_quarter + width))
    for index in range(ranks):
        down_ref[index * size : (index + 1) * size, :] = downs[index]
    convs = ordered(parts, rank, slice(hidden_quarter + width, parts[0].shape[1]))
    total = convs[0]
    for block in convs[1:]:
        total = total + block
    conv_ref[...] = total[:, : conv_ref.shape[1]]


def finish_qkv_kernel(ranks, quarter, rank_ref, *refs):
    parts = refs[:ranks]
    qkv_ref, out_ref = refs[ranks:]
    rank = rank_ref[0]
    blocks = ordered(parts, rank, slice(0, parts[0].shape[1]))
    pieces = []
    for part in range(3):
        for block in blocks:
            pieces.append(block[:, part * quarter : (part + 1) * quarter])
    qkv_ref[...] = jnp.concatenate(pieces, axis=1)
    out_ref[...] = jnp.concatenate([block[:, 3 * quarter :] for block in blocks], axis=1)


def finish(kernel, rank, parts, shapes, name):
    return pl.pallas_call(
        kernel,
        in_specs=[pl.BlockSpec(memory_space=pltpu.SMEM)]
        + [pl.BlockSpec(memory_space=pltpu.VMEM)] * len(parts),
        out_specs=[pl.BlockSpec(memory_space=pltpu.VMEM)] * len(shapes),
        out_shape=[jax.ShapeDtypeStruct(shape, F32) for shape in shapes],
        compiler_params=pltpu.CompilerParams(vmem_limit_bytes=VMEM_LIMIT),
        name=name,
    )(rank.reshape(1), *parts)


def shards_general(
    ranks,
    frame_size,
    inputs,
    clip_id,
    ln_gains,
    ln_biases,
    w_qkv,
    w_out,
    w_up,
    w_down,
    up_bias,
    down_bias,
    conv_first,
    conv_first_bias,
    conv_mid,
    conv_mid_bias,
    cotangent,
):
    lows = frame_size // ranks
    frames_dev = inputs.shape[1]
    patches = inputs.shape[2]
    width = inputs.shape[3]
    rows = frames_dev * patches
    hidden = up_bias.shape[0]
    quarter = width // ranks
    hidden_quarter = hidden // ranks
    row_shard = width // frame_size
    rank = lax.axis_index("seq")
    place = lax.axis_index("frame")
    high = place // lows
    low = place % lows

    def permute(array, target):
        pairs = []
        for seq in range(ranks):
            for hi in range(ranks):
                for lo in range(lows):
                    to_seq, to_hi, to_lo = target(seq, hi, lo)
                    pairs.append(
                        (
                            seq * frame_size + hi * lows + lo,
                            to_seq * frame_size + to_hi * lows + to_lo,
                        )
                    )
        return lax.ppermute(array, AXES, pairs)

    def across(array, bits):
        return permute(array, lambda seq, hi, lo: (seq ^ bits, hi, lo))

    def along_high(array, step):
        return permute(array, lambda seq, hi, lo: (seq, (hi + step) % ranks, lo))

    def along_low(array, step):
        return permute(array, lambda seq, hi, lo: (seq, hi, (lo + step) % lows))

    def to_planes(array):
        return permute(array, lambda seq, hi, lo: (RANK_OF[hi], PLANE_OF[seq], lo))

    def from_planes(array):
        return permute(
            array, lambda seq, hi, lo: (PLANE_OF.index(hi), RANK_OF.index(seq), lo)
        )

    def flip_high(array, bits):
        return permute(array, lambda seq, hi, lo: (seq, hi ^ bits, lo))

    def gather_tokens(block):
        far = across(block, 2)
        near = across(block, 1)
        both = across(far, 1)
        return jnp.concatenate([block, near, far, both], axis=0)

    def scatter_tokens(partial):
        blocks = partial.astype(BF).reshape(ranks, rows, partial.shape[1])
        arrived_far = across(blocks[3], 1)
        arrived_near = across(blocks[1], 1)
        far = partial[2 * rows : 3 * rows] + arrived_far.astype(F32)
        arrived = across(far.astype(BF), 2)
        return partial[:rows] + arrived_near.astype(F32) + arrived.astype(F32)

    half_rows = rows // 2

    def gather_plane(block):
        if lows != 2:
            own = gather_tokens(block)
            return jnp.concatenate(
                [own] + [along_low(own, step) for step in range(1, lows)], axis=0
            )
        far = across(block, 2)
        side = along_low(block, 1)
        near = across(block, 1)
        corner = jnp.concatenate(
            [along_low(far[:half_rows], 1), across(side[half_rows:], 2)], axis=0
        )
        return jnp.concatenate(
            [
                block,
                near,
                far,
                across(far, 1),
                side,
                across(side, 1),
                corner,
                across(corner, 1),
            ],
            axis=0,
        )

    def scatter_plane(partial):
        if lows != 2:
            count = ranks * rows
            own = partial[:count]
            for step in range(1, lows):
                piece = partial[step * count : (step + 1) * count].astype(BF)
                own = own + along_low(piece, -step).astype(F32)
            return scatter_tokens(own)
        blocks = [partial[index * rows : (index + 1) * rows] for index in range(2 * ranks)]
        sums = {}
        for index in (6, 4, 2, 0):
            sums[index] = blocks[index] + across(blocks[index + 1].astype(BF), 1).astype(F32)
        corner = sums[6].astype(BF)
        by_far = across(corner[:half_rows], 2).astype(F32)
        by_side = along_low(corner[half_rows:], 1).astype(F32)
        side = jnp.concatenate([sums[4][:half_rows] + by_far, sums[4][half_rows:]], axis=0)
        far = jnp.concatenate([sums[2][:half_rows], sums[2][half_rows:] + by_side], axis=0)
        return (
            sums[0]
            + across(far.astype(BF), 2).astype(F32)
            + along_low(side.astype(BF), 1).astype(F32)
        )

    places = [(high ^ bits) * lows + low for bits in (0, 2, 1, 3)] + [
        (high ^ bits) * lows + (low + 1) % lows for bits in (0, 2, 1, 3)
    ]

    def after(array, *others):
        return lax.optimization_barrier((array,) + others)[0]

    staged = lows == 2

    def gather_two(block):
        return jnp.concatenate([block, flip_high(block, 2)], axis=0) if staged else block

    def gather_four(two):
        return jnp.concatenate([two, flip_high(two, 1)], axis=0) if staged else two

    def gather_all(four):
        if not staged:
            return lax.all_gather(four, "frame", axis=0, tiled=True)
        return place_rows([four, along_low(four, 1)], places, four.shape[0] // ranks)

    def scatter_half(partials):
        if not staged:
            return jnp.concatenate([partial.astype(BF) for partial in partials], axis=1)
        columns = [partial.shape[1] for partial in partials]
        cuts = [sum(columns[:index]) for index in range(len(columns) + 1)]
        count = partials[0].shape[0] // frame_size
        splits = [
            partial.reshape(ranks, lows, count, partial.shape[1]) for partial in partials
        ]
        sent = jnp.concatenate(
            [lax.dynamic_index_in_dim(split.astype(BF), 1 - low, 1, False) for split in splits],
            axis=2,
        )
        arrived = along_low(sent, 1)
        return jnp.concatenate(
            [
                lax.dynamic_index_in_dim(split, low, 1, False)
                + arrived[:, :, cuts[index] : cuts[index + 1]].astype(F32)
                for index, split in enumerate(splits)
            ],
            axis=2,
        ).reshape(2, 2, count, cuts[-1])

    def scatter_rest(half):
        if not staged:
            return lax.psum_scatter(half, "frame", scatter_dimension=0, tiled=True)
        sent = lax.dynamic_index_in_dim(half, 1 - high % 2, 1, False).astype(BF)
        kept = lax.dynamic_index_in_dim(half, high % 2, 1, False)
        two = kept + flip_high(sent, 1).astype(F32)
        sent = lax.dynamic_index_in_dim(two, 1 - high // 2, 0, False).astype(BF)
        kept = lax.dynamic_index_in_dim(two, high // 2, 0, False)
        return (kept + flip_high(sent, 2).astype(F32)).astype(BF)

    def swap_ranks(blocks):
        split = blocks.reshape((2, 2) + blocks.shape[1:])
        kept = lax.dynamic_index_in_dim(split, rank // 2, 0, False)
        found = across(lax.dynamic_index_in_dim(split, 1 - rank // 2, 0, False), 2)
        own = lax.dynamic_index_in_dim(kept, rank % 2, 0, False)
        far = lax.dynamic_index_in_dim(found, rank % 2, 0, False)
        near = across(lax.dynamic_index_in_dim(kept, 1 - rank % 2, 0, False), 1)
        both = across(lax.dynamic_index_in_dim(found, 1 - rank % 2, 0, False), 1)
        return in_rank_order([own, near, far, both])

    def sum_everywhere(array):
        bits = 1
        while bits < ranks:
            array = array + across(array, bits)
            bits *= 2
        bits = 1
        while bits < frame_size:
            pairs = [
                (seq * frame_size + item, seq * frame_size + (item ^ bits))
                for seq in range(ranks)
                for item in range(frame_size)
            ]
            array = array + lax.ppermute(array, AXES, pairs)
            bits *= 2
        return array

    def in_rank_order(items):
        stacked = jnp.stack(items)
        return [
            lax.dynamic_index_in_dim(stacked, rank ^ index, 0, False) for index in range(ranks)
        ]

    def gather_ranks(block):
        far = across(block, 2)
        near = across(block, 1)
        both = across(far, 1)
        return [block, near, far, both]

    token_rows = inputs[0].reshape(rows, width)
    grad_rows = cotangent[0].reshape(frames_dev * CH, width)
    frame_count = clip_id.shape[1]
    clip_rows = jnp.pad(
        clip_id.astype(BF), ((0, 15), (0, width - frame_count))
    )
    moved = to_planes(jnp.concatenate([token_rows, grad_rows, clip_rows], axis=0))
    tokens = moved[:rows].astype(F32)
    grad_learned = moved[rows : rows + frames_dev * CH].astype(F32)
    clips = moved[rows + frames_dev * CH, :frame_count].astype(jnp.int32)

    own_qkv = jnp.concatenate(
        [
            lax.dynamic_slice_in_dim(w_qkv, part * width + rank * quarter, quarter, 1)
            for part in range(3)
        ],
        axis=1,
    )
    two_qkv = gather_two(own_qkv)
    unit = hidden // (frame_size * ranks)
    columns = jnp.arange(hidden_quarter, dtype=jnp.int32)
    wanted = (columns // unit) * (unit * ranks) + rank * unit + columns % unit
    choose = (jnp.arange(hidden, dtype=jnp.int32)[:, None] == wanted[None, :]).astype(BF)
    own_up = dot(w_up, choose).astype(BF)
    own_down = lax.dynamic_slice_in_dim(w_down, rank * unit, unit, 0)
    own_out = lax.dynamic_slice_in_dim(w_out, rank * quarter, quarter, 1)
    own_out = jnp.concatenate([own_out, conv_first], axis=1)
    two_out = gather_two(after(own_out, two_qkv))
    four_qkv = gather_four(two_qkv)
    two_up = gather_two(after(own_up, two_out))
    four_out = gather_four(after(two_out, four_qkv))
    qkv_quarter = gather_all(four_qkv)
    two_down = gather_two(after(own_down, two_up))
    four_up = gather_four(after(two_up, four_out))
    qkv_quarter = after(qkv_quarter, four_out, two_up)
    packed = gather_all(after(four_out, qkv_quarter))
    out_columns = packed[:, :quarter]
    full_conv = packed[:, quarter:]
    out_quarter = jnp.concatenate(
        swap_ranks(out_columns.reshape(ranks, quarter, quarter)), axis=1
    )
    up_bias_quarter = lax.dynamic_index_in_dim(
        up_bias.reshape(frame_size, ranks, unit), rank, 1, False
    ).reshape(1, hidden_quarter)

    frame_ids = jnp.arange(frame_count, dtype=jnp.int32)

    def clip_tokens(lo):
        blocks = []
        inverse = jnp.array([RANK_OF.index(item) for item in range(ranks)], jnp.int32)
        for bits in range(ranks):
            hi = lax.dynamic_index_in_dim(inverse, rank ^ bits, 0, False)
            for frame in range(frames_dev):
                blocks.append((hi * lows + lo) * frames_dev + frame)
        wanted_frames = jnp.stack(blocks)
        found = jnp.sum(
            jnp.where(wanted_frames[:, None] == frame_ids[None, :], clips[None, :], 0), axis=1
        )
        return jnp.broadcast_to(found[:, None], (found.shape[0], patches)).reshape(-1)

    query_clip = clip_tokens(low)
    key_clip = jnp.concatenate(
        [query_clip] + [clip_tokens((low - step) % lows) for step in range(1, lows)]
    )
    query_clip = query_clip[None, :]
    key_clip = key_clip[:, None]

    normed_one, inverse_one = norm_stats(tokens)
    own_count = ranks * rows
    all_one = gather_plane((normed_one * ln_gains[0] + ln_biases[0]).astype(BF))
    queries = dot(all_one[:own_count], qkv_quarter[:, :quarter]).astype(BF)
    keyvals = dot(all_one, qkv_quarter[:, quarter:]).astype(BF)
    queries = after(queries, packed, four_up, two_down)
    up_quarter = gather_all(after(four_up, packed))
    four_down = gather_four(two_down)
    attended, logs = attend(queries, keyvals, query_clip, key_clip)
    after_attention = tokens + scatter_tokens(dot(attended, out_quarter, 0, 0))
    after_attention = after(after_attention, four_down)
    down_quarter = gather_all(after(four_down, up_quarter))
    normed_two, inverse_two = norm_stats(after_attention)
    all_two = gather_tokens((normed_two * ln_gains[1] + ln_biases[1]).astype(BF))
    pre_act = dot(all_two, up_quarter) + up_bias_quarter
    act_low = gelu(pre_act).astype(BF)
    block_out = after_attention + scatter_tokens(dot(act_low, down_quarter)) + down_bias

    normed_three, inverse_three = norm_stats(block_out)
    normed_three_low = (normed_three * ln_gains[2] + ln_biases[2]).astype(BF)
    tap_rows = dot(normed_three_low, full_conv).reshape(frames_dev, GRID, GRID, 9 * CH)
    first = conv_grid(tap_rows) + conv_first_bias
    features = block_out.reshape(frames_dev, patches, width)

    def tail(first_arg, features_arg, mid_arg, mid_bias_arg):
        maps = token_maps(first_arg, mid_arg, mid_bias_arg).reshape(frames_dev, patches, CH)
        return pool_tokens(maps, features_arg)

    learned, tail_back = jax.vjp(tail, first, features, conv_mid, conv_mid_bias)
    grad_first, grad_pool, grad_mid, grad_mid_bias = tail_back(
        grad_learned.reshape(frames_dev, CH, width)
    )
    grad_first_low = grad_first.astype(BF)
    grad_first_bias = jnp.sum(grad_first_low.astype(F32), axis=(0, 1, 2))
    spread_unused, spread_back = jax.vjp(conv_grid, tap_rows)
    spread = spread_back(grad_first_low.astype(F32))[0].reshape(rows, 9 * CH).astype(BF)
    grad_conv = dot(normed_three_low, spread, 0, 0)
    grad_normed_three = dot(spread, full_conv, 1, 1)
    grad_block, grad_gain_three, grad_shift_three = norm_back(
        normed_three, inverse_three, ln_gains[2], grad_normed_three
    )
    grad_block = grad_block + grad_pool.reshape(rows, width)
    grad_mlp = grad_block.astype(BF)
    grad_down_bias = jnp.sum(grad_mlp.astype(F32), axis=0)

    all_mlp = gather_tokens(grad_mlp)
    grad_act = dot(all_mlp, down_quarter, 1, 1)
    gelu_unused, gelu_back = jax.vjp(gelu, pre_act)
    grad_pre = gelu_back(grad_act)[0].astype(BF)
    grad_up_bias = jnp.sum(grad_pre.astype(F32), axis=0)
    grad_normed_two = scatter_tokens(dot(grad_pre, up_quarter, 1, 1))
    grad_down = dot(act_low, all_mlp, 0, 0)
    grad_up = dot(all_two, grad_pre, 0, 0)
    mlp_half = scatter_half([grad_up, grad_down, grad_conv])
    grad_after, grad_gain_two, grad_shift_two = norm_back(
        normed_two, inverse_two, ln_gains[1], grad_normed_two
    )
    grad_after = grad_after + grad_block

    all_branch = gather_tokens(grad_after.astype(BF))
    grad_attended = dot(all_branch, out_quarter, 1, 1).astype(BF)
    grad_out = dot(attended, all_branch)
    grad_attended = after(grad_attended, mlp_half)
    mlp_share = scatter_rest(mlp_half)
    grad_queries, grad_keyvals = attend_back(
        queries, keyvals, grad_attended, logs, query_clip, key_clip
    )
    grad_queries = grad_queries.T
    grad_keyvals = grad_keyvals.astype(BF)
    grad_normed_own = dot(grad_keyvals, qkv_quarter[:, quarter:], 1, 1)
    grad_normed_own = jnp.concatenate(
        [
            grad_normed_own[:own_count] + dot(grad_queries, qkv_quarter[:, :quarter], 1, 1),
            grad_normed_own[own_count:],
        ],
        axis=0,
    )
    grad_normed_one = scatter_plane(grad_normed_own)
    grad_q = dot(all_one[:own_count], grad_queries, 0, 0)
    grad_kv = dot(all_one, grad_keyvals, 0, 0)
    grad_out_columns = jnp.concatenate(
        swap_ranks(grad_out.astype(BF).reshape(quarter, ranks, quarter).transpose(1, 0, 2)),
        axis=0,
    )
    qkv_share = scatter_rest(
        after(scatter_half([grad_q, grad_kv, grad_out_columns]), mlp_share)
    )
    grad_tokens, grad_gain_one, grad_shift_one = norm_back(
        normed_one, inverse_one, ln_gains[0], grad_normed_one
    )
    moved_back = from_planes(
        jnp.concatenate(
            [
                (grad_after + grad_tokens).astype(BF),
                learned.astype(BF).reshape(frames_dev * CH, width),
            ],
            axis=0,
        )
    ).astype(F32)
    grad_input = moved_back[:rows]
    learned = moved_back[rows:]

    sum_up, sum_down, sum_conv = finish(
        functools.partial(finish_mlp_kernel, ranks, hidden_quarter, width, unit),
        rank,
        gather_ranks(mlp_share),
        [(row_shard, hidden), (ranks * unit, width), (row_shard, 9 * CH)],
        "finish_mlp",
    )
    sum_qkv, sum_out = finish(
        functools.partial(finish_qkv_kernel, ranks, quarter),
        rank,
        gather_ranks(qkv_share),
        [(row_shard, 3 * width), (row_shard, width)],
        "finish_qkv",
    )

    conv_terms = jnp.concatenate(
        [grad_first_bias.reshape(-1), grad_mid.reshape(-1), grad_mid_bias.reshape(-1)]
    )
    conv_rows = -(-conv_terms.shape[0] // width)
    conv_terms = jnp.pad(conv_terms, (0, conv_rows * width - conv_terms.shape[0]))
    up_terms = jnp.where(
        jnp.arange(ranks, dtype=jnp.int32)[:, None] == rank,
        grad_up_bias.reshape(1, hidden_quarter),
        0.0,
    )
    early = sum_everywhere(
        jnp.concatenate(
            [
                jnp.stack(
                    [
                        grad_gain_one,
                        grad_gain_two,
                        grad_gain_three,
                        grad_shift_one,
                        grad_shift_two,
                        grad_shift_three,
                        grad_down_bias,
                    ]
                ),
                conv_terms.reshape(conv_rows, width),
                up_terms.reshape(-1, width),
            ],
            axis=0,
        )
    )
    sum_gains = early[0:3]
    sum_shifts = early[3:6]
    conv_sums = early[7 : 7 + conv_rows].reshape(-1)
    sum_up_bias = (
        early[7 + conv_rows :]
        .reshape(ranks, frame_size, unit)
        .transpose(1, 0, 2)
        .reshape(hidden)
    )
    mid_count = grad_mid.size
    sum_mid = conv_sums[CH : CH + mid_count].reshape(grad_mid.shape)
    sum_mid_bias = conv_sums[CH + mid_count : CH + mid_count + grad_mid_bias.size]
    return (
        learned.reshape(1, frames_dev, CH, width),
        grad_input.reshape(1, frames_dev, patches, width),
        sum_qkv,
        sum_out,
        sum_up,
        sum_down,
        sum_conv,
        sum_gains,
        sum_shifts,
        sum_up_bias,
        early[6],
        conv_sums[:CH],
        sum_mid,
        sum_mid_bias.reshape(grad_mid_bias.shape),
    )


PAD = 128


def run(kernel, name, scalars, arrays, outs, scratch=(), limit=16):
    vmem = pl.BlockSpec(memory_space=pltpu.VMEM)
    return pl.pallas_call(
        kernel,
        in_specs=[pl.BlockSpec(memory_space=pltpu.SMEM)] + [vmem] * len(arrays),
        out_specs=[vmem] * len(outs),
        out_shape=[jax.ShapeDtypeStruct(shape, kind) for shape, kind in outs],
        scratch_shapes=list(scratch),
        compiler_params=pltpu.CompilerParams(vmem_limit_bytes=limit * 1024 * 1024),
        name=name,
    )(scalars, *arrays)


def rows_at(start, size):
    return pl.ds(pl.multiple_of(start * size, size), size)


def stack_rows(refs):
    return jnp.concatenate([ref[...] for ref in refs], axis=0)


def exact(left, right, left_dim=1, right_dim=0):
    return lax.dot_general(
        left,
        right,
        (((left_dim,), (right_dim,)), ((), ())),
        precision=HIGHEST,
        preferred_element_type=F32,
    )


def column_sum(values):
    return jnp.sum(values, axis=0, keepdims=True)


def back_of_norm(values, gain, grad):
    normed, inverse = norm_stats(values)
    scaled = grad * gain
    mean_scaled = jnp.mean(scaled, axis=-1, keepdims=True)
    mean_cross = jnp.mean(scaled * normed, axis=-1, keepdims=True)
    result = inverse * (scaled - mean_scaled - normed * mean_cross)
    return result, column_sum(grad * normed), column_sum(grad)


def pack_kernel(unused_ref, tokens_ref, grads_ref, clip_ref, pack_ref):
    count, width = tokens_ref.shape
    more = grads_ref.shape[0]
    pack_ref[:count, :] = tokens_ref[...]
    pack_ref[count : count + more, :] = grads_ref[...]
    clips = clip_ref[...].astype(F32)
    clips = jnp.concatenate([clips, jnp.zeros((1, PAD - clips.shape[1]), F32)], axis=1)
    pack_ref[count + more :, :] = jnp.zeros((pack_ref.shape[0] - count - more, width), BF)
    pack_ref[count + more :, :PAD] = jnp.broadcast_to(
        clips, (pack_ref.shape[0] - count - more, PAD)
    ).astype(BF)


def select_kernel(ids_ref, qkv_ref, out_ref, own_ref):
    width = out_ref.shape[1]
    quarter = width // 4
    for rank in range(4):

        @pl.when(ids_ref[0] == rank)
        def _(rank=rank):
            pieces = [
                qkv_ref[:, part * width + rank * quarter : part * width + (rank + 1) * quarter]
                for part in range(3)
            ]
            pieces.append(out_ref[:, rank * quarter : (rank + 1) * quarter])
            own_ref[...] = jnp.concatenate(pieces, axis=1)


def prepare_kernel(ids_ref, up_ref, down_ref, conv_ref, own_ref, more_ref):
    size = own_ref.shape[0]
    unit = down_ref.shape[0] // 4
    quarter = 8 * unit
    for rank in range(4):

        @pl.when(ids_ref[0] == rank)
        def _(rank=rank):
            own_ref[:, :quarter] = jnp.concatenate(
                [
                    up_ref[:, (4 * group + rank) * unit : (4 * group + rank + 1) * unit]
                    for group in range(8)
                ],
                axis=1,
            )
            more_ref[...] = down_ref[rank * unit : (rank + 1) * unit, :]

    taps = conv_ref.shape[1]
    own_ref[:, quarter:] = jnp.concatenate(
        [conv_ref[...], jnp.zeros((size, PAD - taps), BF)], axis=1
    )


def norm_one_kernel(ids_ref, moved_ref, gains_ref, shifts_ref, low_ref, qclip_ref, kclip_ref):
    count = low_ref.shape[0]
    frames = count // (GRID * GRID)
    patches = GRID * GRID
    normed, unused = norm_stats(moved_ref[:count, :].astype(F32))
    low_ref[...] = (normed * gains_ref[0:1, :] + shifts_ref[0:1, :]).astype(BF)
    start = count + frames * CH
    clips = moved_ref[start : start + 16, :PAD].astype(F32)[0:1]
    lane = lax.broadcasted_iota(jnp.int32, (1, PAD), 1)
    rank, low = ids_ref[0], ids_ref[2]
    for side in range(2):
        for bits in range(4):
            for frame in range(frames):
                hi = sum(jnp.where(rank ^ bits == RANK_OF[item], item, 0) for item in range(4))
                wanted = (2 * hi + (low ^ side)) * frames + frame
                clip = jnp.sum(jnp.where(lane == wanted, clips, 0.0), axis=1, keepdims=True)
                first = ((4 * side + bits) * frames + frame) * patches
                kclip_ref[first : first + patches, :] = jnp.broadcast_to(clip, (patches, 1))
                if side == 0:
                    qclip_ref[:, first : first + patches] = jnp.broadcast_to(clip, (1, patches))


def pass_sum_kernel(unused_ref, even_ref, arrived_ref, out_ref):
    out_ref[...] = (even_ref[...] + arrived_ref[...].astype(F32)).astype(BF)


def add_kernel(unused_ref, left_ref, right_ref, out_ref):
    out_ref[...] = left_ref[...] + right_ref[...]


def pick_kernel(ids_ref, far_ref, side_ref, out_ref):
    @pl.when(lax.rem(ids_ref[0], 2) == 0)
    def _():
        out_ref[...] = far_ref[...]

    @pl.when(lax.rem(ids_ref[0], 2) == 1)
    def _():
        out_ref[...] = side_ref[...]


def pass_on_kernel(ids_ref, *refs):
    far_even_ref, side_even_ref, second_ref, third_ref, corner_ref, far_ref, side_ref = refs
    core = lax.rem(ids_ref[0], 2)
    corner = corner_ref[...].astype(F32)
    far = far_even_ref[...] + second_ref[...].astype(F32)
    side = side_even_ref[...] + third_ref[...].astype(F32)
    far_ref[...] = (far + jnp.where(core == 1, corner, 0.0)).astype(BF)
    side_ref[...] = (side + jnp.where(core == 0, corner, 0.0)).astype(BF)


def place_of(ids_ref, bits):
    return (2 * ids_ref[1] + ids_ref[2]) ^ bits


def project_kernel(quarter, ids_ref, *refs):
    tokens, blocks = refs[:8], refs[8:16]
    q_ref, kv_ref, w_ref = refs[16:19]
    out_refs, all_ref = refs[19:23], refs[23]
    size = blocks[0].shape[0]
    for bits in range(8):
        where = rows_at(place_of(ids_ref, bits), size)
        w_ref[where, :] = blocks[bits][:, : 3 * quarter]
        all_ref[where, :] = blocks[bits][:, 3 * quarter :]
    rank = ids_ref[0]
    for bits in range(4):
        out_refs[bits][...] = all_ref[rows_at(rank ^ bits, quarter), :]
    own = dot(stack_rows(tokens[:4]), w_ref[...]).astype(BF)
    q_ref[...] = own[:, :quarter]
    half = own.shape[0]
    kv_ref[:half, :] = own[:, quarter:]
    kv_ref[half:, :] = dot(stack_rows(tokens[4:]), w_ref[:, quarter:]).astype(BF)


def scores_of(kv_ref, q_ref, queries, lanes, same, scale):
    raw = dot(kv_ref[:, lanes], q_ref[queries, lanes], 1, 1) * scale
    return jnp.where(same, raw, FLOOR_SCORE)


def attend_wide_kernel(heads, scale, unused_ref, *refs):
    q_ref, kv_ref, qclip_ref, kclip_ref, mixed_ref, log_ref = refs
    width = heads * HEAD_DIM
    count = q_ref.shape[0] // 2

    def one(part, carry):
        queries = pl.ds(pl.multiple_of(part * count, count), count)
        same = kclip_ref[...] == qclip_ref[:, queries]
        for head in range(heads):
            lanes = slice(head * HEAD_DIM, (head + 1) * HEAD_DIM)
            values = slice(width + head * HEAD_DIM, width + (head + 1) * HEAD_DIM)
            scores = scores_of(kv_ref, q_ref, queries, lanes, same, scale)
            top = jnp.max(scores, axis=0, keepdims=True)
            shifted = jnp.exp(scores - top)
            total = jnp.sum(shifted, axis=0, keepdims=True)
            prob = (shifted * (1.0 / total)).astype(BF)
            mixed_ref[lanes, queries] = dot(kv_ref[:, values], prob, 0, 0).astype(BF)
            log_ref[head : head + 1, queries] = top + jnp.log(total)
        return carry

    lax.fori_loop(0, 2, one, 0)


def split_blocks(values, even_refs, odd_refs):
    rows = even_refs[0].shape[0]
    for part in range(len(odd_refs)):
        even_refs[part][...] = values[2 * part * rows : (2 * part + 1) * rows]
        odd_refs[part][...] = values[(2 * part + 1) * rows : (2 * part + 2) * rows].astype(BF)


def out_kernel(rank_ref, *refs):
    mixed_ref = refs[0]
    even_refs, odd_refs, w_ref = refs[5:7], refs[7:9], refs[9]
    blocks = [ref[...] for ref in refs[1:5]]
    rank = rank_ref[0]
    width = blocks[0].shape[0]
    for index in range(4):
        found = blocks[0]
        for bits in range(1, 4):
            found = jnp.where(rank == index ^ bits, blocks[bits], found)
        w_ref[:, index * width : (index + 1) * width] = found
    split_blocks(dot(mixed_ref[...], w_ref[...], 0, 0), even_refs, odd_refs)


def norm_two_kernel(unused_ref, *refs):
    moved_ref, even_ref, arrived_ref, far_ref, gains_ref, shifts_ref = refs[:6]
    sum_ref, low_ref = refs[6:]
    count = low_ref.shape[0]
    values = (
        moved_ref[:count, :].astype(F32)
        + even_ref[...]
        + arrived_ref[...].astype(F32)
        + far_ref[...].astype(F32)
    )
    sum_ref[...] = values
    normed, unused = norm_stats(values)
    low_ref[...] = (normed * gains_ref[1:2, :] + shifts_ref[1:2, :]).astype(BF)


def gelu_both(values):
    size = jnp.abs(values) * 0.7071067811865476
    ratio = 1.0 / (1.0 + 0.3275911 * size)
    bell = jnp.exp(-size * size)
    series = ratio * (
        0.254829592
        + ratio
        * (-0.284496736 + ratio * (1.421413741 + ratio * (-1.453152027 + ratio * 1.061405429)))
    )
    tail = 0.5 * series * bell
    below = jnp.where(values >= 0.0, 1.0 - tail, tail)
    return values * below, below + values * bell * 0.3989422804014327


def join_kernel(unused_ref, *refs):
    for index, ref in enumerate(refs[4:]):
        size = ref.shape[0] // 2
        ref[:size, :] = refs[2 * index][...]
        ref[size:, :] = refs[2 * index + 1][...]


def mlp_part(tokens, up_ref, down_ref, bias, act_ref, slope_ref, even_ref, odd_ref):
    pre = dot(stack_rows(tokens), up_ref[...]) + bias
    act, slope = gelu_both(pre)
    act = act.astype(BF)
    act_ref[...] = act
    slope_ref[...] = slope
    partial = dot(act, down_ref[...])
    count = even_ref.shape[0]
    even_ref[...] = partial[:count]
    odd_ref[...] = partial[count:].astype(BF)


def mlp_kernel(ids_ref, *refs):
    tokens = refs[:2]
    a_refs, b_refs, bias_ref = refs[2:4], refs[4:6], refs[6]
    up_ref, down_ref, conv_ref, own_bias_ref = refs[7:11]
    rank = ids_ref[0]
    size = a_refs[0].shape[0] // 4
    quarter = up_ref.shape[1]
    for ref, order in zip(a_refs, ((0, 4, 2, 6), (1, 5, 3, 7))):
        for index, bits in enumerate(order):
            where = rows_at(place_of(ids_ref, bits), size)
            rows = slice(index * size, (index + 1) * size)
            up_ref[where, :] = ref[rows, :quarter]
            conv_ref[where, :] = ref[rows, quarter:]
    for ref, order in zip(b_refs, ((0, 1, 4, 5), (2, 3, 6, 7))):
        for index, bits in enumerate(order):
            where = rows_at(place_of(ids_ref, bits), size)
            down_ref[where, :] = ref[index * size : (index + 1) * size, :]
    unit = quarter // 8
    bias = None
    for index in range(4):
        found = jnp.concatenate(
            [
                bias_ref[:, (4 * group + index) * unit : (4 * group + index + 1) * unit]
                for group in range(8)
            ],
            axis=1,
        )
        bias = found if bias is None else jnp.where(rank == index, found, bias)
    own_bias_ref[...] = bias
    mlp_part(tokens, up_ref, down_ref, bias, *refs[11:])


def mlp_more_kernel(unused_ref, *refs):
    up_ref, down_ref, bias_ref = refs[2:5]
    mlp_part(refs[:2], up_ref, down_ref, bias_ref[...], *refs[5:])


def grid_masks(count):
    row = lax.broadcasted_iota(jnp.int32, (count, PAD), 0)
    i = (row // GRID) % GRID
    j = row % GRID
    masks = []
    for tap in range(9):
        di, dj = tap // 3 - 1, tap % 3 - 1
        inside = (i + di >= 0) & (i + di < GRID) & (j + dj >= 0) & (j + dj < GRID)
        masks.append(inside.astype(F32))
    return masks


def collect_taps(taps, masks, first_lanes):
    count = taps.shape[0]
    total = None
    for tap in range(9):
        offset = (tap // 3 - 1) * GRID + tap % 3 - 1
        moved = pltpu.roll(taps, (PAD - tap * CH) % PAD, 1) if tap else taps
        moved = pltpu.roll(moved, (-offset) % count, 0) if offset else moved
        moved = moved * masks[tap]
        total = moved if total is None else total + moved
    return total * first_lanes


def spread_taps(values, masks):
    count = values.shape[0]
    total = None
    for tap in range(9):
        offset = (tap // 3 - 1) * GRID + tap % 3 - 1
        moved = pltpu.roll(values, tap * CH, 1) if tap else values
        moved = pltpu.roll(moved, offset % count, 0) if offset else moved
        moved = moved * masks[8 - tap]
        total = moved if total is None else total + moved
    return total


def store_rows(ref, start, values):
    for index in range(values.shape[1] // PAD):
        ref[start + index : start + index + 1, :] = values[:, index * PAD : (index + 1) * PAD]


def load_rows(ref, start, count):
    return jnp.concatenate(
        [ref[start + index : start + index + 1, :] for index in range(count)], axis=1
    )


def tail_kernel(vectors, unused_ref, *refs):
    sum_ref, even_ref, arrived_ref, far_ref, bias_ref, gains_ref, shifts_ref = refs[:7]
    conv_ref, first_bias_ref, mid_ref, mid_bias_ref, moved_ref = refs[7:12]
    learned_ref, low_ref, grad_ref, normed_ref, spread_ref, small_ref = refs[12:]
    count = low_ref.shape[0]
    frames = count // (GRID * GRID)
    patches = GRID * GRID
    value = (
        sum_ref[...]
        + even_ref[...]
        + arrived_ref[...].astype(F32)
        + far_ref[...].astype(F32)
        + bias_ref[...]
    )
    normed, inverse = norm_stats(value)
    gain = gains_ref[2:3, :]
    normed_low = (normed * gain + shifts_ref[2:3, :]).astype(BF)
    normed_ref[...] = normed_low
    masks = grid_masks(count)
    lane = lax.broadcasted_iota(jnp.int32, (count, PAD), 1)
    first_lanes = (lane < CH).astype(F32)
    first = collect_taps(dot(normed_low, conv_ref[...]), masks, first_lanes)
    hidden, slope = gelu_both(first + first_bias_ref[...])
    hidden = hidden * first_lanes
    hiddens, slopes = [hidden], [slope]
    maps = None
    for layer in range(3):
        pre = collect_taps(exact(hiddens[layer], mid_ref[layer]), masks, first_lanes)
        pre = pre + mid_bias_ref[layer : layer + 1, :]
        if layer < 2:
            hidden, slope = gelu_both(pre)
            hiddens.append(hidden * first_lanes)
            slopes.append(slope)
        else:
            maps = jax.nn.sigmoid(pre) * first_lanes
    frame_of_row = lax.broadcasted_iota(jnp.int32, (count, PAD), 0) // patches
    wide = None
    for frame in range(frames):
        moved = pltpu.roll(maps, frame * CH, 1) if frame else maps
        moved = moved * (frame_of_row == frame).astype(F32)
        wide = moved if wide is None else wide + moved
    cotangent = jnp.concatenate(
        [
            moved_ref[count : count + frames * CH, :].astype(F32),
            jnp.zeros((PAD - frames * CH, value.shape[1]), F32),
        ],
        axis=0,
    )
    learned_ref[...] = exact(wide, value, 0, 0)[: frames * CH] * (1.0 / patches)
    pooled = exact(wide, cotangent) * (1.0 / patches)
    products = exact(value, cotangent, 1, 1) * (1.0 / patches)
    grad = None
    for frame in range(frames):
        moved = pltpu.roll(products, PAD - frame * CH, 1) if frame else products
        moved = moved * (frame_of_row == frame).astype(F32)
        grad = moved if grad is None else grad + moved
    grad = grad * maps * (1.0 - maps)
    small_ref[...] = jnp.zeros_like(small_ref)
    conv_start = 7 * vectors + 4 * vectors
    for layer in range(2, -1, -1):
        taps = spread_taps(grad, masks)
        weight = exact(hiddens[layer], taps, 0, 0)[:CH]
        small_ref[conv_start + layer * CH : conv_start + (layer + 1) * CH, :] = weight
        bias_row = conv_start + 3 * CH + 1 + layer
        small_ref[bias_row : bias_row + 1, :] = column_sum(grad)
        grad = exact(taps, mid_ref[layer], 1, 1) * slopes[layer]
    grad_low = grad.astype(BF).astype(F32)
    small_ref[conv_start + 3 * CH : conv_start + 3 * CH + 1, :] = column_sum(grad_low)
    spread = spread_taps(grad_low, masks).astype(BF)
    spread_ref[...] = spread
    grad_normed = dot(spread, conv_ref[...], 1, 1)
    scaled = grad_normed * gain
    mean_scaled = jnp.mean(scaled, axis=-1, keepdims=True)
    mean_cross = jnp.mean(scaled * normed, axis=-1, keepdims=True)
    grad_value = inverse * (scaled - mean_scaled - normed * mean_cross)
    grad_value = grad_value + pooled
    grad_ref[...] = grad_value
    low = grad_value.astype(BF)
    low_ref[...] = low
    store_rows(small_ref, 2 * vectors, column_sum(grad_normed * normed))
    store_rows(small_ref, 5 * vectors, column_sum(grad_normed))
    store_rows(small_ref, 6 * vectors, column_sum(low.astype(F32)))


def mlp_back_kernel(unused_ref, *refs):
    grads = refs[:2]
    slope_ref, up_ref, down_ref = refs[2:5]
    pre_ref, even_ref, odd_ref, bias_ref = refs[5:]
    grad_act = dot(stack_rows(grads), down_ref[...], 1, 1)
    grad_pre = (grad_act * slope_ref[...]).astype(BF)
    pre_ref[...] = grad_pre
    bias_ref[...] = column_sum(grad_pre.astype(F32))
    partial = dot(grad_pre, up_ref[...], 1, 1)
    count = even_ref.shape[0]
    even_ref[...] = partial[:count]
    odd_ref[...] = partial[count:].astype(BF)


def divide_rows(ids_ref, all_ref, refs):
    kept_ref, sent_ref, more_kept_ref, more_sent_ref = refs
    high, low = ids_ref[1], ids_ref[2]
    size = all_ref.shape[0] // 8
    columns = kept_ref.shape[1]
    for index in range(4):
        rows = slice(index * size, (index + 1) * size)
        kept_ref[rows, :] = all_ref[rows_at(2 * index + low, size), :columns]
        sent_ref[rows, :] = all_ref[rows_at(2 * index + 1 - low, size), :columns].astype(BF)
        hi = high ^ (index // 2 * 2)
        lo = low ^ (index % 2)
        more_kept_ref[rows, :] = all_ref[rows_at(2 * hi + lo, size), columns:]
        more_sent_ref[rows, :] = all_ref[rows_at(2 * (hi ^ 1) + lo, size), columns:].astype(BF)


def mlp_grads_kernel(ids_ref, *refs):
    tokens, grads = refs[:4], refs[4:8]
    act, pre = stack_rows(refs[8:10]), stack_rows(refs[10:12])
    normed_ref, spread_ref = refs[12:14]
    all_ref = refs[18]
    quarter = act.shape[1]
    width = tokens[0].shape[1]
    all_ref[:, :quarter] = dot(stack_rows(tokens), pre, 0, 0)
    all_ref[:, quarter : quarter + width] = dot(act, stack_rows(grads), 0, 0)
    all_ref[:, quarter + width :] = dot(normed_ref[...], spread_ref[...], 0, 0)
    divide_rows(ids_ref, all_ref, refs[14:18])


def norm_two_back_kernel(unused_ref, *refs):
    sum_ref, grad_ref, even_ref, arrived_ref, far_ref, gains_ref = refs[:6]
    total_ref, low_ref, rows_ref = refs[6:]
    grad_normed = even_ref[...] + arrived_ref[...].astype(F32) + far_ref[...].astype(F32)
    result, gain_row, shift_row = back_of_norm(sum_ref[...], gains_ref[1:2, :], grad_normed)
    total = result + grad_ref[...]
    total_ref[...] = total
    low_ref[...] = total.astype(BF)
    rows_ref[0:1, :] = gain_row
    rows_ref[1:2, :] = shift_row


def attend_back_part(heads, scale, first, branches, refs, prior_ref, own_ref, total_ref):
    out_ref, q_ref, kv_ref, log_ref, qclip_ref, kclip_ref = refs
    width = heads * HEAD_DIM
    count = own_ref.shape[0]
    queries = slice(first, first + count)
    grad_mixed = dot(stack_rows(branches), out_ref[...], 1, 1).astype(BF)
    same = kclip_ref[...] == qclip_ref[:, queries]
    query_parts, key_parts, value_parts = [], [], []
    for head in range(heads):
        lanes = slice(head * HEAD_DIM, (head + 1) * HEAD_DIM)
        values = slice(width + head * HEAD_DIM, width + (head + 1) * HEAD_DIM)
        scores = scores_of(kv_ref, q_ref, queries, lanes, same, scale)
        prob = jnp.exp(scores - log_ref[head : head + 1, queries])
        grad_prob = dot(kv_ref[:, values], grad_mixed[:, lanes], 1, 1)
        delta = jnp.sum(prob * grad_prob, axis=0, keepdims=True)
        grad_score = (prob * (grad_prob - delta)).astype(BF)
        query_parts.append(dot(kv_ref[:, lanes], grad_score, 0, 0) * scale)
        key_parts.append(dot(grad_score, q_ref[queries, lanes]) * scale)
        value_parts.append(dot(prob.astype(BF), grad_mixed[:, lanes]))
    own_ref[...] = jnp.concatenate(query_parts, axis=0).T.astype(BF)
    terms = jnp.concatenate(key_parts + value_parts, axis=1)
    total_ref[...] = terms if prior_ref is None else prior_ref[...] + terms


def attend_back_first_kernel(heads, scale, unused_ref, *refs):
    attend_back_part(heads, scale, 0, refs[:2], refs[2:8], None, refs[8], refs[9])


def attend_back_next_kernel(heads, scale, first, unused_ref, *refs):
    attend_back_part(heads, scale, first, refs[:1], refs[1:7], refs[7], refs[8], refs[9])


def attend_back_last_kernel(heads, scale, first, unused_ref, *refs):
    prior_ref, first_ref, next_ref, w_ref = refs[7:11]
    own_ref, other_ref = refs[11:13]
    even_refs, odd_refs = refs[13:17], refs[17:21]
    part_ref, total_ref = refs[21:]
    attend_back_part(heads, scale, first, refs[:1], refs[1:7], prior_ref, part_ref, total_ref)
    width = heads * HEAD_DIM
    count = own_ref.shape[0]
    middle = first_ref.shape[0]
    own_ref[:middle, :width] = first_ref[...]
    own_ref[middle:first, :width] = next_ref[...]
    own_ref[first:, :width] = part_ref[...]
    own_ref[:, width:] = total_ref[:count, :].astype(BF)
    other_ref[...] = total_ref[count:, :].astype(BF)
    own = dot(own_ref[...], w_ref[...], 1, 1)
    other = dot(other_ref[...], w_ref[:, width:], 1, 1)
    split_blocks(jnp.concatenate([own, other], axis=0), even_refs, odd_refs)


def qkv_grads_kernel(ids_ref, *refs):
    tokens, branches, mixes = refs[:8], refs[8:12], refs[12:16]
    own_ref, other_ref = refs[16:18]
    all_ref = refs[22]
    quarter = mixes[0].shape[0]
    full = dot(stack_rows(tokens[:4]), own_ref[...], 0, 0)
    more = dot(stack_rows(tokens[4:]), other_ref[...], 0, 0)
    all_ref[:, :quarter] = full[:, :quarter]
    all_ref[:, quarter : 3 * quarter] = full[:, quarter:] + more
    rank = ids_ref[0]
    branch = stack_rows(branches)
    wanted = branch[:, :quarter]
    for index in range(1, 4):
        wanted = jnp.where(
            rank == index, branch[:, index * quarter : (index + 1) * quarter], wanted
        )
    count = branches[0].shape[0]
    for bits in range(4):
        turned = jnp.concatenate(
            [wanted[(item ^ bits) * count : ((item ^ bits) + 1) * count] for item in range(4)],
            axis=0,
        )
        all_ref[rows_at(rank ^ bits, quarter), 3 * quarter :] = dot(mixes[bits][...], turned)
    divide_rows(ids_ref, all_ref, refs[18:22])


def half_kernel(ids_ref, *refs):
    kept_ref, arrived_ref, more_kept_ref, more_arrived_ref = refs[:4]
    own_ref, sent_ref, more_own_ref, more_sent_ref = refs[4:]
    size = own_ref.shape[0] // 2
    high = ids_ref[1]
    for step in range(2):
        rows = slice(step * size, (step + 1) * size)
        where = rows_at(high ^ (2 * step), size)
        own_ref[rows, :] = kept_ref[where, :] + arrived_ref[where, :].astype(F32)
        where = rows_at(high ^ (2 * step + 1), size)
        sent_ref[rows, :] = (kept_ref[where, :] + arrived_ref[where, :].astype(F32)).astype(BF)
    more = more_kept_ref[...] + more_arrived_ref[...].astype(F32)
    more_own_ref[...] = more[: 2 * size]
    more_sent_ref[...] = more[2 * size :].astype(BF)


def fourth_kernel(unused_ref, *refs):
    for kept_ref, arrived_ref, own_ref, sent_ref in (refs[0:2] + refs[4:6], refs[2:4] + refs[6:8]):
        size = own_ref.shape[0]
        own_ref[...] = kept_ref[:size, :] + arrived_ref[:size, :].astype(F32)
        sent_ref[...] = (kept_ref[size:, :] + arrived_ref[size:, :].astype(F32)).astype(BF)


def total_kernel(unused_ref, kept_ref, arrived_ref, more_kept_ref, more_arrived_ref, out_ref):
    columns = kept_ref.shape[1]
    out_ref[:, :columns] = (kept_ref[...] + arrived_ref[...].astype(F32)).astype(BF)
    out_ref[:, columns:] = (more_kept_ref[...] + more_arrived_ref[...].astype(F32)).astype(BF)


def norm_one_back_kernel(vectors, rank_ref, *refs):
    moved_ref, grad_ref, even_ref, arrived_ref, far_ref, side_ref, gains_ref = refs[:7]
    learned_ref, small_ref, two_ref, up_ref, more_up_ref, back_ref, sums_ref = refs[7:]
    count = grad_ref.shape[0]
    grad_normed = (
        even_ref[...]
        + arrived_ref[...].astype(F32)
        + far_ref[...].astype(F32)
        + side_ref[...].astype(F32)
    )
    result, gain_row, shift_row = back_of_norm(
        moved_ref[:count, :].astype(F32), gains_ref[0:1, :], grad_normed
    )
    back_ref[:count, :] = (result + grad_ref[...]).astype(BF)
    back_ref[count:, :] = learned_ref[...].astype(BF)
    sums_ref[...] = small_ref[...]
    store_rows(sums_ref, 0, gain_row)
    store_rows(sums_ref, vectors, two_ref[0:1, :])
    store_rows(sums_ref, 3 * vectors, shift_row)
    store_rows(sums_ref, 4 * vectors, two_ref[1:2, :])
    for index in range(4):
        store_rows(
            sums_ref,
            (7 + index) * vectors,
            jnp.where(rank_ref[0] == index, up_ref[...] + more_up_ref[...], 0.0),
        )


def back_kernel(unused_ref, moved_ref, grad_ref, learned_ref):
    count = grad_ref.shape[0]
    grad_ref[...] = moved_ref[:count, :].astype(F32)
    learned_ref[...] = moved_ref[count:, :].astype(F32)


def unpack_kernel(vectors, unused_ref, part_ref, arrived_ref, *refs):
    sums_ref = refs[-1]
    refs = refs[:-1]
    sums_ref[...] = part_ref[...] + arrived_ref[...]
    gains_ref, shifts_ref, up_ref, down_ref, first_ref, mid_ref, mid_bias_ref = refs
    for index in range(3):
        gains_ref[index : index + 1, :] = load_rows(sums_ref, index * vectors, vectors)
        shifts_ref[index : index + 1, :] = load_rows(sums_ref, (3 + index) * vectors, vectors)
    down_ref[...] = load_rows(sums_ref, 6 * vectors, vectors)
    quarters = [load_rows(sums_ref, (7 + index) * vectors, vectors) for index in range(4)]
    unit = quarters[0].shape[1] // 8
    up_ref[...] = jnp.concatenate(
        [
            quarters[index][:, group * unit : (group + 1) * unit]
            for group in range(8)
            for index in range(4)
        ],
        axis=1,
    )
    start = 11 * vectors
    for layer in range(3):
        mid_ref[layer] = sums_ref[start + layer * CH : start + (layer + 1) * CH, : 9 * CH]
    start = start + 3 * CH
    first_ref[...] = sums_ref[start : start + 1, :CH]
    mid_bias_ref[...] = sums_ref[start + 1 : start + 4, :CH]


def shards_square(
    ranks,
    frame_size,
    inputs,
    clip_id,
    ln_gains,
    ln_biases,
    w_qkv,
    w_out,
    w_up,
    w_down,
    up_bias,
    down_bias,
    conv_first,
    conv_first_bias,
    conv_mid,
    conv_mid_bias,
    cotangent,
):
    lows = 2
    frames_dev = inputs.shape[1]
    patches = inputs.shape[2]
    width = inputs.shape[3]
    rows = frames_dev * patches
    learned_rows = frames_dev * CH
    hidden = up_bias.shape[0]
    quarter = width // ranks
    heads = quarter // HEAD_DIM
    hidden_quarter = hidden // ranks
    unit = hidden_quarter // frame_size
    size = width // frame_size
    vectors = width // PAD
    own_count = ranks * rows
    place = lax.axis_index("frame")
    ids = jnp.stack([lax.axis_index("seq"), place // lows, place % lows])

    def permute(array, target):
        pairs = []
        for seq in range(ranks):
            for hi in range(ranks):
                for lo in range(lows):
                    to_seq, to_hi, to_lo = target(seq, hi, lo)
                    pairs.append(
                        (
                            seq * frame_size + hi * lows + lo,
                            to_seq * frame_size + to_hi * lows + to_lo,
                        )
                    )
        return lax.ppermute(array, AXES, pairs)

    def flip(array, seq_bits, hi_bits=0, lo_bits=0):
        return permute(
            array, lambda seq, hi, lo: (seq ^ seq_bits, hi ^ hi_bits, lo ^ lo_bits)
        )

    def after(array, *others):
        return lax.optimization_barrier((array,) + others)[0]

    last = []

    def ordered_run(kernel, name, scalars, arrays, outs, scratch=()):
        if last:
            arrays = [after(arrays[0], last[0])] + list(arrays[1:])
        results = run(kernel, name, scalars, arrays, outs, scratch)
        last[:] = [results[-1]]
        return results

    def to_planes(array):
        return permute(array, lambda seq, hi, lo: (RANK_OF[hi], PLANE_OF[seq], lo))

    def from_planes(array):
        return permute(
            array, lambda seq, hi, lo: (PLANE_OF.index(hi), RANK_OF.index(seq), lo)
        )

    def gather_four(block):
        far = flip(block, 2)
        near = flip(block, 1)
        return [block, near, far, flip(far, 1)]

    def pass_sum(even, arrived, name):
        (result,) = ordered_run(
            pass_sum_kernel,
            name,
            ids,
            [even, arrived],
            [((rows, width), BF)],
        )
        return result

    def scatter_four(evens, odds, name):
        far = flip(pass_sum(evens[1], flip(odds[1], 1), name), 2)
        return flip(odds[0], 1), far

    def row_parts(blocks, first, second):
        return [
            ((blocks * size, columns), kind) for columns in (first, second) for kind in (F32, BF)
        ]

    def scatter_half(parts, name):
        kept, sent, more_kept, more_sent = parts
        return ordered_run(
            half_kernel,
            name,
            ids,
            [kept, flip(sent, 0, 0, 1), more_kept, flip(more_sent, 0, 1)],
            row_parts(2, kept.shape[1], more_kept.shape[1]),
        )

    def scatter_fourth(parts, name):
        kept, sent, more_kept, more_sent = parts
        return ordered_run(
            fourth_kernel,
            name,
            ids,
            [kept, flip(sent, 0, 1), more_kept, flip(more_sent, 0, 2)],
            row_parts(1, kept.shape[1], more_kept.shape[1]),
        )

    def scatter_last(parts, name):
        kept, sent, more_kept, more_sent = parts
        (share,) = ordered_run(
            total_kernel,
            name,
            ids,
            [kept, flip(sent, 0, 2), more_kept, flip(more_sent, 0, 0, 1)],
            [((size, kept.shape[1] + more_kept.shape[1]), BF)],
        )
        return share

    def add(left, right, name):
        return ordered_run(add_kernel, name, ids, [left, right], [(left.shape, F32)])[0]

    (pack,) = ordered_run(
        pack_kernel,
        "pack",
        ids,
        [inputs.reshape(rows, width), cotangent.reshape(learned_rows, width), clip_id],
        [((rows + learned_rows + 16, width), BF)],
    )
    moved = to_planes(pack)

    (own_pack,) = ordered_run(
        select_kernel, "select", ids, [w_qkv, w_out], [((size, width), BF)]
    )
    pack_two = flip(own_pack, 0, 2)
    pack_one = flip(own_pack, 0, 1)
    pack_side = flip(own_pack, 0, 0, 1)
    pack_three = flip(pack_two, 0, 1)
    packs = [own_pack, pack_side]
    for item in (pack_one, pack_two, pack_three):
        packs += [item, flip(item, 0, 0, 1)]

    mid_pad = jnp.pad(conv_mid, ((0, 0), (0, PAD - CH), (0, PAD - 9 * CH)))
    mid_bias_pad = jnp.pad(conv_mid_bias, ((0, 0), (0, PAD - CH)))
    first_bias_pad = jnp.pad(conv_first_bias, (0, PAD - CH)).reshape(1, PAD)
    up_bias_row = up_bias.reshape(1, hidden)
    down_bias_row = down_bias.reshape(1, width)

    own_a, own_b = ordered_run(
        prepare_kernel,
        "prepare",
        ids,
        [
            after(w_up, mid_pad, mid_bias_pad, first_bias_pad, up_bias_row, down_bias_row),
            w_down,
            conv_first,
        ],
        [((size, hidden_quarter + PAD), BF), ((size, width), BF)],
    )

    low_norm, query_clip, key_clip = ordered_run(
        norm_one_kernel,
        "norm_one",
        ids,
        [moved, ln_gains, ln_biases],
        [((rows, width), BF), ((1, own_count), F32), ((2 * own_count, 1), F32)],
    )
    low_norm = after(low_norm, pack_side, pack_one, pack_two)

    def join(pairs, name):
        flat = [item for pair in pairs for item in pair]
        outs = [((2 * pair[0].shape[0], pair[0].shape[1]), BF) for pair in pairs]
        return ordered_run(join_kernel, name, ids, flat, outs)

    far = flip(low_norm, 2)
    side = flip(low_norm, 0, 0, 1)
    near = flip(low_norm, 1)
    far_a, side_b = flip(own_a, 0, 2), flip(own_b, 0, 0, 1)
    (picked,) = ordered_run(
        pick_kernel,
        "pick",
        ids,
        [after(far, far_a, side_b, *packs[1:]), side],
        [((rows, width), BF)],
    )
    two_a, two_b = join(
        [(own_a, far_a), (own_b, side_b)], "join_two"
    )
    corner = permute(
        picked,
        lambda seq, hi, lo: (seq, hi, lo ^ 1) if seq % 2 == 0 else (seq ^ 2, hi, lo),
    )
    far_near = flip(far, 1)
    side_near = flip(side, 1)
    corner = after(corner, near, far_near, side_near)
    all_one = [near, far, far_near, side, side_near, corner, flip(corner, 1)]
    all_one = [low_norm] + all_one
    queries, keyvals, qkv_quarter, own_out, near_out, far_out, both_out = ordered_run(
        functools.partial(project_kernel, quarter),
        "project",
        ids,
        all_one + packs,
        [
            ((own_count, quarter), BF),
            ((2 * own_count, 2 * quarter), BF),
            ((width, 3 * quarter), BF),
        ]
        + [((quarter, quarter), BF)] * 4,
        [pltpu.VMEM((width, quarter), BF)],
    )
    out_blocks = [own_out, flip(near_out, 1), flip(far_out, 2), flip(both_out, 3)]
    scale = HEAD_DIM ** (-0.5)
    attended, logs = ordered_run(
        functools.partial(attend_wide_kernel, heads, scale),
        "attend",
        ids,
        [queries, keyvals, query_clip, key_clip],
        [((quarter, own_count), BF), ((8, own_count), F32)],
    )
    blocks_of = [((rows, width), F32)] * 2 + [((rows, width), BF)] * 2
    *parts, out_quarter = ordered_run(
        out_kernel,
        "out",
        ids,
        [attended] + out_blocks,
        blocks_of + [((quarter, width), BF)],
    )
    evens, odds = parts[:2], parts[2:]
    arrived, far = scatter_four(evens, odds, "out_pass")
    four_a, four_b = join(
        [(two_a, flip(two_a, 0, 1)), (two_b, flip(two_b, 0, 2))], "join_four"
    )
    after_attention, low_two = ordered_run(
        norm_two_kernel,
        "norm_two",
        ids,
        [moved, evens[0], arrived, far, ln_gains, ln_biases],
        [((rows, width), F32), ((rows, width), BF)],
    )
    near_two, far_two = flip(low_two, 1), flip(low_two, 2)
    pair = [
        ((2 * rows, hidden_quarter), BF),
        ((2 * rows, hidden_quarter), F32),
        ((rows, width), F32),
        ((rows, width), BF),
    ]
    up_full, down_full, conv_full, own_bias, act, slope, even, odd = ordered_run(
        mlp_kernel,
        "mlp",
        ids,
        [low_two, near_two]
        + [four_a, flip(four_a, 0, 0, 1), four_b, flip(four_b, 0, 1), up_bias_row],
        [
            ((width, hidden_quarter), BF),
            ((hidden_quarter, width), BF),
            ((width, PAD), BF),
            ((1, hidden_quarter), F32),
        ]
        + pair,
    )
    far_two = after(far_two, even)
    all_two = [low_two, near_two, far_two, flip(far_two, 1)]
    acts, slopes, evens, odds = [act], [slope], [even], [odd]
    for item, rest in zip(
        (acts, slopes, evens, odds),
        ordered_run(
            mlp_more_kernel, "mlp_more", ids, all_two[2:] + [up_full, down_full, own_bias], pair
        ),
    ):
        item.append(rest)
    arrived, far = scatter_four(evens, odds, "mlp_pass")

    small_rows = -(-(11 * vectors + 3 * CH + 4) // 8) * 8
    learned, low_mlp, grad_block, low_three, spread, small = ordered_run(
        functools.partial(tail_kernel, vectors),
        "tail",
        ids,
        [
            after_attention,
            evens[0],
            arrived,
            far,
            down_bias_row,
            ln_gains,
            ln_biases,
            conv_full,
            first_bias_pad,
            mid_pad,
            mid_bias_pad,
            moved,
        ],
        [
            ((learned_rows, width), F32),
            ((rows, width), BF),
            ((rows, width), F32),
            ((rows, width), BF),
            ((rows, PAD), BF),
            ((small_rows, PAD), F32),
        ],
    )

    near_mlp, far_mlp = flip(low_mlp, 1), flip(low_mlp, 2)
    pair = [
        ((2 * rows, hidden_quarter), BF),
        ((rows, width), F32),
        ((rows, width), BF),
        ((1, hidden_quarter), F32),
    ]
    pre, even, odd, bias = ordered_run(
        mlp_back_kernel,
        "mlp_back",
        ids,
        [low_mlp, near_mlp, slopes[0], up_full, down_full],
        pair,
    )
    far_mlp = after(far_mlp, even)
    all_mlp = [low_mlp, near_mlp, far_mlp, flip(far_mlp, 1)]
    pres, evens, odds, biases = [pre], [even], [odd], [bias]
    for item, rest in zip(
        (pres, evens, odds, biases),
        ordered_run(
            mlp_back_kernel,
            "mlp_back_more",
            ids,
            all_mlp[2:] + [slopes[1], up_full, down_full],
            pair,
        ),
    ):
        item.append(rest)
    arrived, far = scatter_four(evens, odds, "mlp_back_pass")
    columns = hidden_quarter + width + PAD
    mlp_parts = ordered_run(
        mlp_grads_kernel,
        "mlp_grads",
        ids,
        all_two + all_mlp + acts + pres + [low_three, spread],
        row_parts(4, hidden_quarter, width + PAD),
        [pltpu.VMEM((width, columns), F32)],
    )
    grad_after, low_branch, rows_two = ordered_run(
        norm_two_back_kernel,
        "norm_two_back",
        ids,
        [after_attention, grad_block, evens[0], arrived, far, ln_gains],
        [((rows, width), F32), ((rows, width), BF), ((2, width), F32)],
    )

    near_branch, far_branch = flip(low_branch, 1), flip(low_branch, 2)
    mixes = gather_four(after(attended, far_branch))
    common = [out_quarter, queries, keyvals, logs, query_clip, key_clip]
    total = ((2 * own_count, 2 * quarter), F32)
    grads_first, sums_first = ordered_run(
        functools.partial(attend_back_first_kernel, heads, scale),
        "attend_back",
        ids,
        [low_branch, near_branch] + common,
        [((2 * rows, quarter), BF), total],
    )
    far_branch = after(far_branch, sums_first)
    all_branch = [low_branch, near_branch, far_branch, flip(far_branch, 1)]
    grads_next, sums_next = ordered_run(
        functools.partial(attend_back_next_kernel, heads, scale, 2 * rows),
        "attend_back_next",
        ids,
        [far_branch] + common + [sums_first],
        [((rows, quarter), BF), total],
    )
    grads_own, grads_other, *parts = ordered_run(
        functools.partial(attend_back_last_kernel, heads, scale, 3 * rows),
        "attend_back_last",
        ids,
        all_branch[3:] + common + [sums_next, grads_first, grads_next, qkv_quarter],
        [((own_count, 3 * quarter), BF), ((own_count, 2 * quarter), BF)]
        + [((rows, width), F32)] * 4
        + [((rows, width), BF)] * 4,
        [
            pltpu.VMEM((rows, quarter), BF),
            pltpu.VMEM((2 * own_count, 2 * quarter), F32),
        ],
    )
    evens = parts[:4]
    arrived = [flip(item, 1) for item in parts[4:]]
    corner = permute(
        pass_sum(evens[3], arrived[3], "corner_pass"),
        lambda seq, hi, lo: (seq ^ 2, hi, lo) if seq % 2 == 0 else (seq, hi, lo ^ 1),
    )
    mlp_parts = scatter_half(mlp_parts, "mlp_half")
    qkv_parts = ordered_run(
        qkv_grads_kernel,
        "qkv_grads",
        ids,
        all_one + all_branch + mixes + [grads_own, grads_other],
        row_parts(4, width // 2, width // 2),
        [pltpu.VMEM((width, width), F32)],
    )
    far, side = ordered_run(
        pass_on_kernel,
        "pass_on",
        ids,
        [evens[1], evens[2], arrived[1], arrived[2], corner],
        [((rows, width), BF), ((rows, width), BF)],
    )
    far, side = flip(far, 2), flip(side, 0, 0, 1)
    mlp_parts = scatter_fourth(mlp_parts, "mlp_fourth")
    moved_back, sums = ordered_run(
        functools.partial(norm_one_back_kernel, vectors),
        "norm_one_back",
        ids,
        [moved, grad_after, evens[0], arrived[0], far, side, ln_gains]
        + [learned, small, rows_two]
        + biases,
        [((rows + learned_rows, width), BF), ((small_rows, PAD), F32)],
    )
    qkv_parts = list(lax.optimization_barrier(tuple(qkv_parts) + (sums,))[:4])

    sums = add(sums, flip(sums, 1), "sum_core")
    mlp_share = scatter_last(mlp_parts, "mlp_total")
    sums = add(sums, flip(sums, 2), "sum_x")
    qkv_parts = scatter_half(qkv_parts, "qkv_half")
    grad_input, learned = ordered_run(
        back_kernel,
        "back",
        ids,
        [from_planes(moved_back)],
        [((rows, width), F32), ((learned_rows, width), F32)],
    )
    sums = add(sums, flip(sums, 0, 0, 1), "sum_y")
    mlp_share = after(mlp_share, qkv_parts[0])
    mlp_far, mlp_near = flip(mlp_share, 2), flip(mlp_share, 1)
    qkv_parts = scatter_fourth(qkv_parts, "qkv_fourth")
    sums = add(sums, flip(sums, 0, 1), "sum_z")
    sum_gains, sum_shifts, sum_up_bias, sum_down_bias, sum_first, sum_mid, sum_mid_bias = (
        ordered_run(
            functools.partial(unpack_kernel, vectors),
            "unpack",
            ids,
            [sums, flip(sums, 0, 2)],
            [
                ((3, width), F32),
                ((3, width), F32),
                ((1, hidden), F32),
                ((1, width), F32),
                ((1, CH), F32),
                ((3, CH, 9 * CH), F32),
                ((3, CH), F32),
            ],
            [pltpu.VMEM((small_rows, PAD), F32)],
        )
    )
    qkv_share = scatter_last(qkv_parts, "qkv_total")
    mlp_far = after(mlp_far, qkv_share)
    qkv_far, qkv_near = flip(qkv_share, 2), flip(qkv_share, 1)
    sum_up, sum_down, sum_conv = ordered_run(
        functools.partial(finish_mlp_kernel, ranks, hidden_quarter, width, unit),
        "finish_mlp",
        ids,
        [mlp_share, mlp_near, mlp_far, flip(mlp_far, 1)],
        [((size, hidden), F32), ((ranks * unit, width), F32), ((size, 9 * CH), F32)],
    )
    sum_qkv, sum_out = ordered_run(
        functools.partial(finish_qkv_kernel, ranks, quarter),
        "finish_qkv",
        ids,
        [qkv_share, qkv_near, qkv_far, flip(after(qkv_far, sum_down), 1)],
        [((size, 3 * width), F32), ((size, width), F32)],
    )
    return (
        learned.reshape(1, frames_dev, CH, width),
        grad_input.reshape(1, frames_dev, patches, width),
        sum_qkv,
        sum_out,
        sum_up,
        sum_down,
        sum_conv,
        sum_gains,
        sum_shifts,
        sum_up_bias.reshape(hidden),
        sum_down_bias.reshape(width),
        sum_first.reshape(CH),
        sum_mid,
        sum_mid_bias,
    )


def solution(mesh):
    placed = (
        P("seq", "frame", None, None),
        P("seq", None),
        P(),
        P(),
        P("frame", None),
        P("frame", None),
        P("frame", None),
        P("frame", None),
        P(),
        P(),
        P("frame", None),
        P(),
        P(),
        P(),
        P("seq", "frame", None, None),
    )
    ranks, frame_size = mesh.shape["seq"], mesh.shape["frame"]
    body = shards_square if ranks == 4 and frame_size == 8 else shards_general
    return jax.shard_map(
        functools.partial(body, ranks, frame_size),
        mesh=mesh,
        in_specs=placed,
        out_specs=(
            P("seq", "frame", None, None),
            P("seq", "frame", None, None),
            P("frame", None),
            P("frame", None),
            P("frame", None),
            P("frame", None),
            P("frame", None),
            P(),
            P(),
            P(),
            P(),
            P(),
            P(),
            P(),
        ),
        check_vma=False,
    )
```

```python
import functools

import jax
import jax.numpy as jnp
from jax import lax
from jax.experimental import pallas as pl
from jax.experimental.pallas import tpu as pltpu
from jax.sharding import PartitionSpec as P

HEADS = 12
HEAD_DIM = 64
CH = 8
GRID = 8

EPSILON = 1e-06
FLOOR_SCORE = -1e30
HIGHEST = lax.Precision.HIGHEST
AXES = ("seq", "frame")
PLANE_OF = (0, 2, 1, 3)
RANK_OF = (0, 2, 1, 3)
VMEM_LIMIT = 56 * 1024 * 1024
BF = jnp.bfloat16
F32 = jnp.float32


def norm_stats(values):
    centre = jnp.mean(values, axis=-1, keepdims=True)
    centred = values - centre
    variance = jnp.mean(centred * centred, axis=-1, keepdims=True)
    inverse = lax.rsqrt(variance + EPSILON)
    return centred * inverse, inverse


def norm_back(normed, inverse, gain, grad):
    scaled = grad * gain
    mean_scaled = jnp.mean(scaled, axis=-1, keepdims=True)
    mean_cross = jnp.mean(scaled * normed, axis=-1, keepdims=True)
    grad_values = inverse * (scaled - mean_scaled - normed * mean_cross)
    return grad_values, jnp.sum(grad * normed, axis=0), jnp.sum(grad, axis=0)


def gelu(values):
    return jax.nn.gelu(values, approximate=False)


def conv_grid(taps):
    side = taps.shape[1]
    width = taps.shape[-1] // 9
    padded = jnp.pad(taps, ((0, 0), (1, 1), (1, 1), (0, 0)))
    total = jnp.zeros(taps.shape[:-1] + (width,), taps.dtype)
    for tap in range(9):
        offset_row = tap // 3
        offset_column = tap % 3
        total = (
            total
            + padded[
                :,
                offset_row : offset_row + side,
                offset_column : offset_column + side,
                tap * width : (tap + 1) * width,
            ]
        )
    return total


def token_maps(first, conv_mid, conv_mid_bias):
    hidden = gelu(first)
    for layer in range(3):
        frames = hidden.shape[0]
        side = hidden.shape[1]
        flat = hidden.reshape(-1, hidden.shape[-1])
        taps = jnp.dot(flat, conv_mid[layer], precision=HIGHEST).reshape(frames, side, side, -1)
        hidden = conv_grid(taps) + conv_mid_bias[layer]
        if layer < 2:
            hidden = gelu(hidden)
    return jax.nn.sigmoid(hidden)


def pool_tokens(maps, features):
    return jnp.einsum("fpk,fpd->fkd", maps, features, precision=HIGHEST) / maps.shape[1]


def dot(left, right, left_dim=1, right_dim=0):
    return lax.dot_general(
        left, right, (((left_dim,), (right_dim,)), ((), ())), preferred_element_type=F32
    )


def attend_kernel(heads, scale, q_ref, kv_ref, qclip_ref, kclip_ref, mixed_ref, log_ref):
    width = heads * HEAD_DIM
    same = kclip_ref[...] == qclip_ref[...]
    for head in range(heads):
        lanes = slice(head * HEAD_DIM, (head + 1) * HEAD_DIM)
        value_lanes = slice(width + head * HEAD_DIM, width + (head + 1) * HEAD_DIM)
        scores = dot(kv_ref[:, lanes], q_ref[:, lanes], 1, 1) * scale
        scores = jnp.where(same, scores, FLOOR_SCORE)
        top = jnp.max(scores, axis=0, keepdims=True)
        shifted = jnp.exp(scores - top)
        total = jnp.sum(shifted, axis=0, keepdims=True)
        prob = (shifted * (1.0 / total)).astype(BF)
        mixed = dot(kv_ref[:, value_lanes], prob, 0, 0)
        mixed_ref[head * HEAD_DIM : (head + 1) * HEAD_DIM, :] = mixed.astype(BF)
        log_ref[head : head + 1, :] = top + jnp.log(total)


def attend_back_kernel(
    heads, scale, q_ref, kv_ref, grad_ref, log_ref, qclip_ref, kclip_ref, dq_ref, dkv_ref
):
    width = heads * HEAD_DIM
    same = kclip_ref[...] == qclip_ref[...]

    @pl.when(pl.program_id(0) == 0)
    def _():
        dkv_ref[...] = jnp.zeros_like(dkv_ref)

    key_parts = []
    value_parts = []
    for head in range(heads):
        lanes = slice(head * HEAD_DIM, (head + 1) * HEAD_DIM)
        value_lanes = slice(width + head * HEAD_DIM, width + (head + 1) * HEAD_DIM)
        scores = dot(kv_ref[:, lanes], q_ref[:, lanes], 1, 1) * scale
        scores = jnp.where(same, scores, FLOOR_SCORE)
        prob = jnp.exp(scores - log_ref[head : head + 1, :])
        grad_prob = dot(kv_ref[:, value_lanes], grad_ref[:, lanes], 1, 1)
        delta = jnp.sum(prob * grad_prob, axis=0, keepdims=True)
        grad_score = (prob * (grad_prob - delta)).astype(BF)
        grad_query = dot(kv_ref[:, lanes], grad_score, 0, 0) * scale
        dq_ref[head * HEAD_DIM : (head + 1) * HEAD_DIM, :] = grad_query.astype(BF)
        key_parts.append(dot(grad_score, q_ref[:, lanes]) * scale)
        value_parts.append(dot(prob.astype(BF), grad_ref[:, lanes]))
    dkv_ref[...] += jnp.concatenate(key_parts + value_parts, axis=1)


def query_block(count, keys):
    return min(count, 256) if keys <= 1024 else 128


def attend(queries, keyvals, query_clip, key_clip):
    count, width = queries.shape
    keys = keyvals.shape[0]
    heads = width // HEAD_DIM
    block = query_block(count, keys)
    return pl.pallas_call(
        functools.partial(attend_kernel, heads, HEAD_DIM ** (-0.5)),
        grid=(count // block,),
        in_specs=[
            pl.BlockSpec((block, width), lambda i: (i, 0)),
            pl.BlockSpec((keys, 2 * width), lambda i: (0, 0)),
            pl.BlockSpec((1, block), lambda i: (0, i)),
            pl.BlockSpec((keys, 1), lambda i: (0, 0)),
        ],
        out_specs=[
            pl.BlockSpec((width, block), lambda i: (0, i)),
            pl.BlockSpec((8, block), lambda i: (0, i)),
        ],
        out_shape=[
            jax.ShapeDtypeStruct((width, count), BF),
            jax.ShapeDtypeStruct((8, count), F32),
        ],
        compiler_params=pltpu.CompilerParams(vmem_limit_bytes=VMEM_LIMIT),
        name="attend",
    )(queries, keyvals, query_clip, key_clip)


def attend_back(queries, keyvals, grads, logs, query_clip, key_clip):
    count, width = queries.shape
    keys = keyvals.shape[0]
    heads = width // HEAD_DIM
    block = query_block(count, keys)
    return pl.pallas_call(
        functools.partial(attend_back_kernel, heads, HEAD_DIM ** (-0.5)),
        grid=(count // block,),
        in_specs=[
            pl.BlockSpec((block, width), lambda i: (i, 0)),
            pl.BlockSpec((keys, 2 * width), lambda i: (0, 0)),
            pl.BlockSpec((block, width), lambda i: (i, 0)),
            pl.BlockSpec((8, block), lambda i: (0, i)),
            pl.BlockSpec((1, block), lambda i: (0, i)),
            pl.BlockSpec((keys, 1), lambda i: (0, 0)),
        ],
        out_specs=[
            pl.BlockSpec((width, block), lambda i: (0, i)),
            pl.BlockSpec((keys, 2 * width), lambda i: (0, 0)),
        ],
        out_shape=[
            jax.ShapeDtypeStruct((width, count), BF),
            jax.ShapeDtypeStruct((keys, 2 * width), F32),
        ],
        compiler_params=pltpu.CompilerParams(vmem_limit_bytes=VMEM_LIMIT),
        name="attend_back",
    )(queries, keyvals, grads, logs, query_clip, key_clip)


def place_kernel(size, place_ref, *refs):
    pieces, out_ref = refs[:-1], refs[-1]
    index = 0
    for piece in pieces:
        for start in range(0, piece.shape[0], size):
            place = pl.multiple_of(place_ref[index] * size, size)
            out_ref[pl.ds(place, size), :] = piece[start : start + size, :]
            index += 1


def place_rows(pieces, places, size):
    columns = pieces[0].shape[1]
    return pl.pallas_call(
        functools.partial(place_kernel, size),
        in_specs=[pl.BlockSpec(memory_space=pltpu.SMEM)]
        + [pl.BlockSpec(memory_space=pltpu.VMEM)] * len(pieces),
        out_specs=pl.BlockSpec(memory_space=pltpu.VMEM),
        out_shape=jax.ShapeDtypeStruct((len(places) * size, columns), pieces[0].dtype),
        name="place_rows",
    )(jnp.stack(places), *pieces)


def ordered(refs, rank, lanes):
    blocks = [ref[:, lanes].astype(F32) for ref in refs]
    result = []
    for index in range(len(refs)):
        found = blocks[0]
        for bits in range(1, len(refs)):
            found = jnp.where(rank == index ^ bits, blocks[bits], found)
        result.append(found)
    return result


def finish_mlp_kernel(ranks, hidden_quarter, width, unit, rank_ref, *refs):
    parts = refs[:ranks]
    up_ref, down_ref, conv_ref = refs[ranks:]
    rank = rank_ref[0]
    ups = ordered(parts, rank, slice(0, hidden_quarter))
    pieces = []
    for group in range(hidden_quarter // unit):
        for block in ups:
            pieces.append(block[:, group * unit : (group + 1) * unit])
    up_ref[...] = jnp.concatenate(pieces, axis=1)
    size = parts[0].shape[0]
    downs = ordered(parts, rank, slice(hidden_quarter, hidden_quarter + width))
    for index in range(ranks):
        down_ref[index * size : (index + 1) * size, :] = downs[index]
    convs = ordered(parts, rank, slice(hidden_quarter + width, parts[0].shape[1]))
    total = convs[0]
    for block in convs[1:]:
        total = total + block
    conv_ref[...] = total[:, : conv_ref.shape[1]]


def finish_qkv_kernel(ranks, quarter, rank_ref, *refs):
    parts = refs[:ranks]
    qkv_ref, out_ref = refs[ranks:]
    rank = rank_ref[0]
    blocks = ordered(parts, rank, slice(0, 4 * quarter))
    pieces = []
    for part in range(3):
        for block in blocks:
            pieces.append(block[:, part * quarter : (part + 1) * quarter])
    qkv_ref[...] = jnp.concatenate(pieces, axis=1)
    out_ref[...] = jnp.concatenate([block[:, 3 * quarter :] for block in blocks], axis=1)


def finish(kernel, rank, parts, shapes, name):
    return pl.pallas_call(
        kernel,
        in_specs=[pl.BlockSpec(memory_space=pltpu.SMEM)]
        + [pl.BlockSpec(memory_space=pltpu.VMEM)] * len(parts),
        out_specs=[pl.BlockSpec(memory_space=pltpu.VMEM)] * len(shapes),
        out_shape=[jax.ShapeDtypeStruct(shape, F32) for shape in shapes],
        compiler_params=pltpu.CompilerParams(vmem_limit_bytes=VMEM_LIMIT),
        name=name,
    )(rank.reshape(1), *parts)


def shards_general(
    ranks,
    frame_size,
    inputs,
    clip_id,
    ln_gains,
    ln_biases,
    w_qkv,
    w_out,
    w_up,
    w_down,
    up_bias,
    down_bias,
    conv_first,
    conv_first_bias,
    conv_mid,
    conv_mid_bias,
    cotangent,
):
    lows = frame_size // ranks
    frames_dev = inputs.shape[1]
    patches = inputs.shape[2]
    width = inputs.shape[3]
    rows = frames_dev * patches
    hidden = up_bias.shape[0]
    quarter = width // ranks
    hidden_quarter = hidden // ranks
    row_shard = width // frame_size
    rank = lax.axis_index("seq")
    place = lax.axis_index("frame")
    high = place // lows
    low = place % lows

    def permute(array, target):
        pairs = []
        for seq in range(ranks):
            for hi in range(ranks):
                for lo in range(lows):
                    to_seq, to_hi, to_lo = target(seq, hi, lo)
                    pairs.append(
                        (
                            seq * frame_size + hi * lows + lo,
                            to_seq * frame_size + to_hi * lows + to_lo,
                        )
                    )
        return lax.ppermute(array, AXES, pairs)

    def across(array, bits):
        return permute(array, lambda seq, hi, lo: (seq ^ bits, hi, lo))

    def along_high(array, step):
        return permute(array, lambda seq, hi, lo: (seq, (hi + step) % ranks, lo))

    def along_low(array, step):
        return permute(array, lambda seq, hi, lo: (seq, hi, (lo + step) % lows))

    def to_planes(array):
        return permute(array, lambda seq, hi, lo: (RANK_OF[hi], PLANE_OF[seq], lo))

    def from_planes(array):
        return permute(
            array, lambda seq, hi, lo: (PLANE_OF.index(hi), RANK_OF.index(seq), lo)
        )

    def flip_high(array, bits):
        return permute(array, lambda seq, hi, lo: (seq, hi ^ bits, lo))

    def gather_tokens(block):
        far = across(block, 2)
        near = across(block, 1)
        both = across(far, 1)
        return jnp.concatenate([block, near, far, both], axis=0)

    def scatter_tokens(partial):
        blocks = partial.astype(BF).reshape(ranks, rows, partial.shape[1])
        arrived_far = across(blocks[3], 1)
        arrived_near = across(blocks[1], 1)
        far = partial[2 * rows : 3 * rows] + arrived_far.astype(F32)
        arrived = across(far.astype(BF), 2)
        return partial[:rows] + arrived_near.astype(F32) + arrived.astype(F32)

    half_rows = rows // 2

    def gather_plane(block):
        if lows != 2:
            own = gather_tokens(block)
            return jnp.concatenate(
                [own] + [along_low(own, step) for step in range(1, lows)], axis=0
            )
        far = across(block, 2)
        side = along_low(block, 1)
        near = across(block, 1)
        corner = jnp.concatenate(
            [along_low(far[:half_rows], 1), across(side[half_rows:], 2)], axis=0
        )
        return jnp.concatenate(
            [
                block,
                near,
                far,
                across(far, 1),
                side,
                across(side, 1),
                corner,
                across(corner, 1),
            ],
            axis=0,
        )

    def scatter_plane(partial):
        if lows != 2:
            count = ranks * rows
            own = partial[:count]
            for step in range(1, lows):
                piece = partial[step * count : (step + 1) * count].astype(BF)
                own = own + along_low(piece, -step).astype(F32)
            return scatter_tokens(own)
        blocks = [partial[index * rows : (index + 1) * rows] for index in range(2 * ranks)]
        sums = {}
        for index in (6, 4, 2, 0):
            sums[index] = blocks[index] + across(blocks[index + 1].astype(BF), 1).astype(F32)
        corner = sums[6].astype(BF)
        by_far = across(corner[:half_rows], 2).astype(F32)
        by_side = along_low(corner[half_rows:], 1).astype(F32)
        side = jnp.concatenate([sums[4][:half_rows] + by_far, sums[4][half_rows:]], axis=0)
        far = jnp.concatenate([sums[2][:half_rows], sums[2][half_rows:] + by_side], axis=0)
        return (
            sums[0]
            + across(far.astype(BF), 2).astype(F32)
            + along_low(side.astype(BF), 1).astype(F32)
        )

    places = [(high ^ bits) * lows + low for bits in (0, 2, 1, 3)] + [
        (high ^ bits) * lows + (low + 1) % lows for bits in (0, 2, 1, 3)
    ]

    def after(array, *others):
        return lax.optimization_barrier((array,) + others)[0]

    staged = lows == 2

    def gather_two(block):
        return jnp.concatenate([block, flip_high(block, 2)], axis=0) if staged else block

    def gather_four(two):
        return jnp.concatenate([two, flip_high(two, 1)], axis=0) if staged else two

    def gather_all(four):
        if not staged:
            return lax.all_gather(four, "frame", axis=0, tiled=True)
        return place_rows([four, along_low(four, 1)], places, four.shape[0] // ranks)

    def scatter_half(partials):
        if not staged:
            return jnp.concatenate([partial.astype(BF) for partial in partials], axis=1)
        columns = [partial.shape[1] for partial in partials]
        cuts = [sum(columns[:index]) for index in range(len(columns) + 1)]
        count = partials[0].shape[0] // frame_size
        splits = [
            partial.reshape(ranks, lows, count, partial.shape[1]) for partial in partials
        ]
        sent = jnp.concatenate(
            [lax.dynamic_index_in_dim(split.astype(BF), 1 - low, 1, False) for split in splits],
            axis=2,
        )
        arrived = along_low(sent, 1)
        return jnp.concatenate(
            [
                lax.dynamic_index_in_dim(split, low, 1, False)
                + arrived[:, :, cuts[index] : cuts[index + 1]].astype(F32)
                for index, split in enumerate(splits)
            ],
            axis=2,
        ).reshape(2, 2, count, cuts[-1])

    def scatter_rest(half):
        if not staged:
            return lax.psum_scatter(half, "frame", scatter_dimension=0, tiled=True)
        sent = lax.dynamic_index_in_dim(half, 1 - high % 2, 1, False).astype(BF)
        kept = lax.dynamic_index_in_dim(half, high % 2, 1, False)
        two = kept + flip_high(sent, 1).astype(F32)
        sent = lax.dynamic_index_in_dim(two, 1 - high // 2, 0, False).astype(BF)
        kept = lax.dynamic_index_in_dim(two, high // 2, 0, False)
        return (kept + flip_high(sent, 2).astype(F32)).astype(BF)

    def swap_ranks(blocks):
        split = blocks.reshape((2, 2) + blocks.shape[1:])
        kept = lax.dynamic_index_in_dim(split, rank // 2, 0, False)
        found = across(lax.dynamic_index_in_dim(split, 1 - rank // 2, 0, False), 2)
        own = lax.dynamic_index_in_dim(kept, rank % 2, 0, False)
        far = lax.dynamic_index_in_dim(found, rank % 2, 0, False)
        near = across(lax.dynamic_index_in_dim(kept, 1 - rank % 2, 0, False), 1)
        both = across(lax.dynamic_index_in_dim(found, 1 - rank % 2, 0, False), 1)
        return in_rank_order([own, near, far, both])

    def sum_everywhere(array):
        bits = 1
        while bits < ranks:
            array = array + across(array, bits)
            bits *= 2
        bits = 1
        while bits < frame_size:
            pairs = [
                (seq * frame_size + item, seq * frame_size + (item ^ bits))
                for seq in range(ranks)
                for item in range(frame_size)
            ]
            array = array + lax.ppermute(array, AXES, pairs)
            bits *= 2
        return array

    def in_rank_order(items):
        stacked = jnp.stack(items)
        return [
            lax.dynamic_index_in_dim(stacked, rank ^ index, 0, False) for index in range(ranks)
        ]

    def gather_ranks(block):
        far = across(block, 2)
        near = across(block, 1)
        both = across(far, 1)
        return [block, near, far, both]

    token_rows = inputs[0].reshape(rows, width)
    grad_rows = cotangent[0].reshape(frames_dev * CH, width)
    frame_count = clip_id.shape[1]
    clip_rows = jnp.pad(
        clip_id.astype(BF), ((0, 15), (0, width - frame_count))
    )
    moved = to_planes(jnp.concatenate([token_rows, grad_rows, clip_rows], axis=0))
    tokens = moved[:rows].astype(F32)
    grad_learned = moved[rows : rows + frames_dev * CH].astype(F32)
    clips = moved[rows + frames_dev * CH, :frame_count].astype(jnp.int32)

    own_qkv = jnp.concatenate(
        [
            lax.dynamic_slice_in_dim(w_qkv, part * width + rank * quarter, quarter, 1)
            for part in range(3)
        ],
        axis=1,
    )
    two_qkv = gather_two(own_qkv)
    unit = hidden // (frame_size * ranks)
    columns = jnp.arange(hidden_quarter, dtype=jnp.int32)
    wanted = (columns // unit) * (unit * ranks) + rank * unit + columns % unit
    choose = (jnp.arange(hidden, dtype=jnp.int32)[:, None] == wanted[None, :]).astype(BF)
    own_up = dot(w_up, choose).astype(BF)
    own_down = lax.dynamic_slice_in_dim(w_down, rank * unit, unit, 0)
    own_out = lax.dynamic_slice_in_dim(w_out, rank * quarter, quarter, 1)
    own_out = jnp.concatenate([own_out, conv_first], axis=1)
    two_out = gather_two(after(own_out, two_qkv))
    four_qkv = gather_four(two_qkv)
    two_up = gather_two(after(own_up, two_out))
    four_out = gather_four(after(two_out, four_qkv))
    qkv_quarter = gather_all(four_qkv)
    two_down = gather_two(after(own_down, two_up))
    four_up = gather_four(after(two_up, four_out))
    qkv_quarter = after(qkv_quarter, four_out, two_up)
    packed = gather_all(after(four_out, qkv_quarter))
    out_columns = packed[:, :quarter]
    full_conv = packed[:, quarter:]
    out_quarter = jnp.concatenate(
        swap_ranks(out_columns.reshape(ranks, quarter, quarter)), axis=1
    )
    up_bias_quarter = lax.dynamic_index_in_dim(
        up_bias.reshape(frame_size, ranks, unit), rank, 1, False
    ).reshape(1, hidden_quarter)

    frame_ids = jnp.arange(frame_count, dtype=jnp.int32)

    def clip_tokens(lo):
        blocks = []
        inverse = jnp.array([RANK_OF.index(item) for item in range(ranks)], jnp.int32)
        for bits in range(ranks):
            hi = lax.dynamic_index_in_dim(inverse, rank ^ bits, 0, False)
            for frame in range(frames_dev):
                blocks.append((hi * lows + lo) * frames_dev + frame)
        wanted_frames = jnp.stack(blocks)
        found = jnp.sum(
            jnp.where(wanted_frames[:, None] == frame_ids[None, :], clips[None, :], 0), axis=1
        )
        return jnp.broadcast_to(found[:, None], (found.shape[0], patches)).reshape(-1)

    query_clip = clip_tokens(low)
    key_clip = jnp.concatenate(
        [query_clip] + [clip_tokens((low - step) % lows) for step in range(1, lows)]
    )
    query_clip = query_clip[None, :]
    key_clip = key_clip[:, None]

    normed_one, inverse_one = norm_stats(tokens)
    own_count = ranks * rows
    all_one = gather_plane((normed_one * ln_gains[0] + ln_biases[0]).astype(BF))
    queries = dot(all_one[:own_count], qkv_quarter[:, :quarter]).astype(BF)
    keyvals = dot(all_one, qkv_quarter[:, quarter:]).astype(BF)
    queries = after(queries, packed, four_up, two_down)
    up_quarter = gather_all(after(four_up, packed))
    four_down = gather_four(two_down)
    attended, logs = attend(queries, keyvals, query_clip, key_clip)
    after_attention = tokens + scatter_tokens(dot(attended, out_quarter, 0, 0))
    after_attention = after(after_attention, four_down)
    down_quarter = gather_all(after(four_down, up_quarter))
    normed_two, inverse_two = norm_stats(after_attention)
    all_two = gather_tokens((normed_two * ln_gains[1] + ln_biases[1]).astype(BF))
    pre_act = dot(all_two, up_quarter) + up_bias_quarter
    act_low = gelu(pre_act).astype(BF)
    block_out = after_attention + scatter_tokens(dot(act_low, down_quarter)) + down_bias

    normed_three, inverse_three = norm_stats(block_out)
    normed_three_low = (normed_three * ln_gains[2] + ln_biases[2]).astype(BF)
    tap_rows = dot(normed_three_low, full_conv).reshape(frames_dev, GRID, GRID, 9 * CH)
    first = conv_grid(tap_rows) + conv_first_bias
    features = block_out.reshape(frames_dev, patches, width)

    def tail(first_arg, features_arg, mid_arg, mid_bias_arg):
        maps = token_maps(first_arg, mid_arg, mid_bias_arg).reshape(frames_dev, patches, CH)
        return pool_tokens(maps, features_arg)

    learned, tail_back = jax.vjp(tail, first, features, conv_mid, conv_mid_bias)
    grad_first, grad_pool, grad_mid, grad_mid_bias = tail_back(
        grad_learned.reshape(frames_dev, CH, width)
    )
    grad_first_low = grad_first.astype(BF)
    grad_first_bias = jnp.sum(grad_first_low.astype(F32), axis=(0, 1, 2))
    spread_unused, spread_back = jax.vjp(conv_grid, tap_rows)
    spread = spread_back(grad_first_low.astype(F32))[0].reshape(rows, 9 * CH).astype(BF)
    grad_conv = dot(normed_three_low, spread, 0, 0)
    grad_normed_three = dot(spread, full_conv, 1, 1)
    grad_block, grad_gain_three, grad_shift_three = norm_back(
        normed_three, inverse_three, ln_gains[2], grad_normed_three
    )
    grad_block = grad_block + grad_pool.reshape(rows, width)
    grad_mlp = grad_block.astype(BF)
    grad_down_bias = jnp.sum(grad_mlp.astype(F32), axis=0)

    all_mlp = gather_tokens(grad_mlp)
    grad_act = dot(all_mlp, down_quarter, 1, 1)
    gelu_unused, gelu_back = jax.vjp(gelu, pre_act)
    grad_pre = gelu_back(grad_act)[0].astype(BF)
    grad_up_bias = jnp.sum(grad_pre.astype(F32), axis=0)
    grad_normed_two = scatter_tokens(dot(grad_pre, up_quarter, 1, 1))
    grad_down = dot(act_low, all_mlp, 0, 0)
    grad_up = dot(all_two, grad_pre, 0, 0)
    mlp_half = scatter_half([grad_up, grad_down, grad_conv])
    grad_after, grad_gain_two, grad_shift_two = norm_back(
        normed_two, inverse_two, ln_gains[1], grad_normed_two
    )
    grad_after = grad_after + grad_block

    all_branch = gather_tokens(grad_after.astype(BF))
    grad_attended = dot(all_branch, out_quarter, 1, 1).astype(BF)
    grad_out = dot(attended, all_branch)
    grad_attended = after(grad_attended, mlp_half)
    mlp_share = scatter_rest(mlp_half)
    grad_queries, grad_keyvals = attend_back(
        queries, keyvals, grad_attended, logs, query_clip, key_clip
    )
    grad_queries = grad_queries.T
    grad_keyvals = grad_keyvals.astype(BF)
    grad_normed_own = dot(grad_keyvals, qkv_quarter[:, quarter:], 1, 1)
    grad_normed_own = jnp.concatenate(
        [
            grad_normed_own[:own_count] + dot(grad_queries, qkv_quarter[:, :quarter], 1, 1),
            grad_normed_own[own_count:],
        ],
        axis=0,
    )
    grad_normed_one = scatter_plane(grad_normed_own)
    grad_q = dot(all_one[:own_count], grad_queries, 0, 0)
    grad_kv = dot(all_one, grad_keyvals, 0, 0)
    grad_out_columns = jnp.concatenate(
        swap_ranks(grad_out.astype(BF).reshape(quarter, ranks, quarter).transpose(1, 0, 2)),
        axis=0,
    )
    qkv_share = scatter_rest(
        after(scatter_half([grad_q, grad_kv, grad_out_columns]), mlp_share)
    )
    grad_tokens, grad_gain_one, grad_shift_one = norm_back(
        normed_one, inverse_one, ln_gains[0], grad_normed_one
    )
    moved_back = from_planes(
        jnp.concatenate(
            [
                (grad_after + grad_tokens).astype(BF),
                learned.astype(BF).reshape(frames_dev * CH, width),
            ],
            axis=0,
        )
    ).astype(F32)
    grad_input = moved_back[:rows]
    learned = moved_back[rows:]

    sum_up, sum_down, sum_conv = finish(
        functools.partial(finish_mlp_kernel, ranks, hidden_quarter, width, unit),
        rank,
        gather_ranks(mlp_share),
        [(row_shard, hidden), (ranks * unit, width), (row_shard, 9 * CH)],
        "finish_mlp",
    )
    sum_qkv, sum_out = finish(
        functools.partial(finish_qkv_kernel, ranks, quarter),
        rank,
        gather_ranks(qkv_share),
        [(row_shard, 3 * width), (row_shard, width)],
        "finish_qkv",
    )

    conv_terms = jnp.concatenate(
        [grad_first_bias.reshape(-1), grad_mid.reshape(-1), grad_mid_bias.reshape(-1)]
    )
    conv_rows = -(-conv_terms.shape[0] // width)
    conv_terms = jnp.pad(conv_terms, (0, conv_rows * width - conv_terms.shape[0]))
    up_terms = jnp.where(
        jnp.arange(ranks, dtype=jnp.int32)[:, None] == rank,
        grad_up_bias.reshape(1, hidden_quarter),
        0.0,
    )
    early = sum_everywhere(
        jnp.concatenate(
            [
                jnp.stack(
                    [
                        grad_gain_one,
                        grad_gain_two,
                        grad_gain_three,
                        grad_shift_one,
                        grad_shift_two,
                        grad_shift_three,
                        grad_down_bias,
                    ]
                ),
                conv_terms.reshape(conv_rows, width),
                up_terms.reshape(-1, width),
            ],
            axis=0,
        )
    )
    sum_gains = early[0:3]
    sum_shifts = early[3:6]
    conv_sums = early[7 : 7 + conv_rows].reshape(-1)
    sum_up_bias = (
        early[7 + conv_rows :]
        .reshape(ranks, frame_size, unit)
        .transpose(1, 0, 2)
        .reshape(hidden)
    )
    mid_count = grad_mid.size
    sum_mid = conv_sums[CH : CH + mid_count].reshape(grad_mid.shape)
    sum_mid_bias = conv_sums[CH + mid_count : CH + mid_count + grad_mid_bias.size]
    return (
        learned.reshape(1, frames_dev, CH, width),
        grad_input.reshape(1, frames_dev, patches, width),
        sum_qkv,
        sum_out,
        sum_up,
        sum_down,
        sum_conv,
        sum_gains,
        sum_shifts,
        sum_up_bias,
        early[6],
        conv_sums[:CH],
        sum_mid,
        sum_mid_bias.reshape(grad_mid_bias.shape),
    )


PAD = 128


def run(kernel, name, scalars, arrays, outs, scratch=(), limit=16):
    vmem = pl.BlockSpec(memory_space=pltpu.VMEM)
    return pl.pallas_call(
        kernel,
        in_specs=[pl.BlockSpec(memory_space=pltpu.SMEM)] + [vmem] * len(arrays),
        out_specs=[vmem] * len(outs),
        out_shape=[jax.ShapeDtypeStruct(shape, kind) for shape, kind in outs],
        scratch_shapes=list(scratch),
        compiler_params=pltpu.CompilerParams(vmem_limit_bytes=limit * 1024 * 1024),
        name=name,
    )(scalars, *arrays)


def rows_at(start, size):
    return pl.ds(pl.multiple_of(start * size, size), size)


def stack_rows(refs):
    return jnp.concatenate([ref[...] for ref in refs], axis=0)


def exact(left, right, left_dim=1, right_dim=0):
    return lax.dot_general(
        left,
        right,
        (((left_dim,), (right_dim,)), ((), ())),
        precision=HIGHEST,
        preferred_element_type=F32,
    )


def column_sum(values):
    return jnp.sum(values, axis=0, keepdims=True)


def back_of_norm(values, gain, grad):
    normed, inverse = norm_stats(values)
    scaled = grad * gain
    mean_scaled = jnp.mean(scaled, axis=-1, keepdims=True)
    mean_cross = jnp.mean(scaled * normed, axis=-1, keepdims=True)
    result = inverse * (scaled - mean_scaled - normed * mean_cross)
    return result, column_sum(grad * normed), column_sum(grad)


def pack_kernel(unused_ref, tokens_ref, grads_ref, clip_ref, pack_ref):
    count, width = tokens_ref.shape
    more = grads_ref.shape[0]
    pack_ref[:count, :] = tokens_ref[...]
    pack_ref[count : count + more, :] = grads_ref[...]
    clips = clip_ref[...].astype(F32)
    clips = jnp.concatenate([clips, jnp.zeros((1, PAD - clips.shape[1]), F32)], axis=1)
    pack_ref[count + more :, :] = jnp.zeros((pack_ref.shape[0] - count - more, width), BF)
    pack_ref[count + more :, :PAD] = jnp.broadcast_to(
        clips, (pack_ref.shape[0] - count - more, PAD)
    ).astype(BF)


def select_kernel(ids_ref, qkv_ref, out_ref, own_ref):
    width = out_ref.shape[1]
    quarter = width // 4
    for rank in range(4):

        @pl.when(ids_ref[0] == rank)
        def _(rank=rank):
            pieces = [
                qkv_ref[:, part * width + rank * quarter : part * width + (rank + 1) * quarter]
                for part in range(3)
            ]
            pieces.append(out_ref[:, rank * quarter : (rank + 1) * quarter])
            own_ref[...] = jnp.concatenate(pieces, axis=1)


def prepare_kernel(ids_ref, up_ref, down_ref, conv_ref, own_ref, more_ref):
    size = own_ref.shape[0]
    unit = down_ref.shape[0] // 4
    quarter = 8 * unit
    for rank in range(4):

        @pl.when(ids_ref[0] == rank)
        def _(rank=rank):
            own_ref[:, :quarter] = jnp.concatenate(
                [
                    up_ref[:, (4 * group + rank) * unit : (4 * group + rank + 1) * unit]
                    for group in range(8)
                ],
                axis=1,
            )
            more_ref[...] = down_ref[rank * unit : (rank + 1) * unit, :]

    taps = conv_ref.shape[1]
    own_ref[:, quarter:] = jnp.concatenate(
        [conv_ref[...], jnp.zeros((size, PAD - taps), BF)], axis=1
    )


def norm_one_kernel(ids_ref, moved_ref, gains_ref, shifts_ref, low_ref, qclip_ref, kclip_ref):
    count = low_ref.shape[0]
    frames = count // (GRID * GRID)
    patches = GRID * GRID
    normed, unused = norm_stats(moved_ref[:count, :].astype(F32))
    low_ref[...] = (normed * gains_ref[0:1, :] + shifts_ref[0:1, :]).astype(BF)
    start = count + frames * CH
    clips = moved_ref[start : start + 16, :PAD].astype(F32)[0:1]
    lane = lax.broadcasted_iota(jnp.int32, (1, PAD), 1)
    rank, low = ids_ref[0], ids_ref[2]
    for side in range(2):
        for bits in range(4):
            for frame in range(frames):
                hi = sum(jnp.where(rank ^ bits == RANK_OF[item], item, 0) for item in range(4))
                wanted = (2 * hi + (low ^ side)) * frames + frame
                clip = jnp.sum(jnp.where(lane == wanted, clips, 0.0), axis=1, keepdims=True)
                first = ((4 * side + bits) * frames + frame) * patches
                kclip_ref[first : first + patches, :] = jnp.broadcast_to(clip, (patches, 1))
                if side == 0:
                    qclip_ref[:, first : first + patches] = jnp.broadcast_to(clip, (1, patches))


def pass_sum_kernel(unused_ref, even_ref, arrived_ref, out_ref):
    out_ref[...] = (even_ref[...] + arrived_ref[...].astype(F32)).astype(BF)


def add_kernel(unused_ref, left_ref, right_ref, out_ref):
    out_ref[...] = left_ref[...] + right_ref[...]


def pick_kernel(ids_ref, far_ref, side_ref, out_ref):
    @pl.when(lax.rem(ids_ref[0], 2) == 0)
    def _():
        out_ref[...] = far_ref[...]

    @pl.when(lax.rem(ids_ref[0], 2) == 1)
    def _():
        out_ref[...] = side_ref[...]


def pass_on_kernel(ids_ref, *refs):
    far_even_ref, side_even_ref, second_ref, third_ref, corner_ref, far_ref, side_ref = refs
    core = lax.rem(ids_ref[0], 2)
    corner = corner_ref[...].astype(F32)
    far = far_even_ref[...] + second_ref[...].astype(F32)
    side = side_even_ref[...] + third_ref[...].astype(F32)
    far_ref[...] = (far + jnp.where(core == 1, corner, 0.0)).astype(BF)
    side_ref[...] = (side + jnp.where(core == 0, corner, 0.0)).astype(BF)


def place_of(ids_ref, bits):
    return (2 * ids_ref[1] + ids_ref[2]) ^ bits


def project_kernel(quarter, ids_ref, *refs):
    tokens, blocks = refs[:8], refs[8:16]
    q_ref, kv_ref, w_ref = refs[16:19]
    out_refs, all_ref = refs[19:23], refs[23]
    size = blocks[0].shape[0]
    for bits in range(8):
        where = rows_at(place_of(ids_ref, bits), size)
        w_ref[where, :] = blocks[bits][:, : 3 * quarter]
        all_ref[where, :] = blocks[bits][:, 3 * quarter :]
    rank = ids_ref[0]
    for bits in range(4):
        out_refs[bits][...] = all_ref[rows_at(rank ^ bits, quarter), :]
    own = dot(stack_rows(tokens[:4]), w_ref[...]).astype(BF)
    q_ref[...] = own[:, :quarter]
    half = own.shape[0]
    kv_ref[:half, :] = own[:, quarter:]
    kv_ref[half:, :] = dot(stack_rows(tokens[4:]), w_ref[:, quarter:]).astype(BF)


def scores_of(kv_ref, q_ref, queries, lanes, same, scale):
    raw = dot(kv_ref[:, lanes], q_ref[queries, lanes], 1, 1) * scale
    return jnp.where(same, raw, FLOOR_SCORE)


def attend_wide_kernel(heads, scale, unused_ref, *refs):
    q_ref, kv_ref, qclip_ref, kclip_ref, mixed_ref, log_ref = refs
    width = heads * HEAD_DIM
    count = q_ref.shape[0] // 2

    def one(part, carry):
        queries = pl.ds(pl.multiple_of(part * count, count), count)
        same = kclip_ref[...] == qclip_ref[:, queries]
        for head in range(heads):
            lanes = slice(head * HEAD_DIM, (head + 1) * HEAD_DIM)
            values = slice(width + head * HEAD_DIM, width + (head + 1) * HEAD_DIM)
            scores = scores_of(kv_ref, q_ref, queries, lanes, same, scale)
            top = jnp.max(scores, axis=0, keepdims=True)
            shifted = jnp.exp(scores - top)
            total = jnp.sum(shifted, axis=0, keepdims=True)
            prob = (shifted * (1.0 / total)).astype(BF)
            mixed_ref[lanes, queries] = dot(kv_ref[:, values], prob, 0, 0).astype(BF)
            log_ref[head : head + 1, queries] = top + jnp.log(total)
        return carry

    lax.fori_loop(0, 2, one, 0)


def split_blocks(values, even_refs, odd_refs):
    rows = even_refs[0].shape[0]
    for part in range(len(odd_refs)):
        even_refs[part][...] = values[2 * part * rows : (2 * part + 1) * rows]
        odd_refs[part][...] = values[(2 * part + 1) * rows : (2 * part + 2) * rows].astype(BF)


def out_kernel(rank_ref, *refs):
    mixed_ref = refs[0]
    even_refs, odd_refs, w_ref = refs[5:7], refs[7:9], refs[9]
    blocks = [ref[...] for ref in refs[1:5]]
    rank = rank_ref[0]
    width = blocks[0].shape[0]
    for index in range(4):
        found = blocks[0]
        for bits in range(1, 4):
            found = jnp.where(rank == index ^ bits, blocks[bits], found)
        w_ref[:, index * width : (index + 1) * width] = found
    split_blocks(dot(mixed_ref[...], w_ref[...], 0, 0), even_refs, odd_refs)


def norm_two_kernel(unused_ref, *refs):
    moved_ref, even_ref, arrived_ref, far_ref, gains_ref, shifts_ref = refs[:6]
    sum_ref, low_ref = refs[6:]
    count = low_ref.shape[0]
    values = (
        moved_ref[:count, :].astype(F32)
        + even_ref[...]
        + arrived_ref[...].astype(F32)
        + far_ref[...].astype(F32)
    )
    sum_ref[...] = values
    normed, unused = norm_stats(values)
    low_ref[...] = (normed * gains_ref[1:2, :] + shifts_ref[1:2, :]).astype(BF)


def gelu_both(values):
    size = jnp.abs(values) * 0.7071067811865476
    ratio = 1.0 / (1.0 + 0.3275911 * size)
    bell = jnp.exp(-size * size)
    series = ratio * (
        0.254829592
        + ratio
        * (-0.284496736 + ratio * (1.421413741 + ratio * (-1.453152027 + ratio * 1.061405429)))
    )
    tail = 0.5 * series * bell
    below = jnp.where(values >= 0.0, 1.0 - tail, tail)
    return values * below, below + values * bell * 0.3989422804014327


def join_kernel(unused_ref, *refs):
    for index, ref in enumerate(refs[4:]):
        size = ref.shape[0] // 2
        ref[:size, :] = refs[2 * index][...]
        ref[size:, :] = refs[2 * index + 1][...]


def mlp_part(tokens, up_ref, down_ref, bias, act_ref, slope_ref, even_ref, odd_ref):
    pre = dot(stack_rows(tokens), up_ref[...]) + bias
    act, slope = gelu_both(pre)
    act = act.astype(BF)
    act_ref[...] = act
    slope_ref[...] = slope
    partial = dot(act, down_ref[...])
    count = even_ref.shape[0]
    even_ref[...] = partial[:count]
    odd_ref[...] = partial[count:].astype(BF)


def mlp_kernel(ids_ref, *refs):
    tokens = refs[:2]
    a_refs, b_refs, bias_ref = refs[2:4], refs[4:6], refs[6]
    up_ref, down_ref, conv_ref, own_bias_ref = refs[7:11]
    rank = ids_ref[0]
    size = a_refs[0].shape[0] // 4
    quarter = up_ref.shape[1]
    for ref, order in zip(a_refs, ((0, 4, 2, 6), (1, 5, 3, 7))):
        for index, bits in enumerate(order):
            where = rows_at(place_of(ids_ref, bits), size)
            rows = slice(index * size, (index + 1) * size)
            up_ref[where, :] = ref[rows, :quarter]
            conv_ref[where, :] = ref[rows, quarter:]
    for ref, order in zip(b_refs, ((0, 1, 4, 5), (2, 3, 6, 7))):
        for index, bits in enumerate(order):
            where = rows_at(place_of(ids_ref, bits), size)
            down_ref[where, :] = ref[index * size : (index + 1) * size, :]
    unit = quarter // 8
    bias = None
    for index in range(4):
        found = jnp.concatenate(
            [
                bias_ref[:, (4 * group + index) * unit : (4 * group + index + 1) * unit]
                for group in range(8)
            ],
            axis=1,
        )
        bias = found if bias is None else jnp.where(rank == index, found, bias)
    own_bias_ref[...] = bias
    mlp_part(tokens, up_ref, down_ref, bias, *refs[11:])


def mlp_more_kernel(unused_ref, *refs):
    up_ref, down_ref, bias_ref = refs[2:5]
    mlp_part(refs[:2], up_ref, down_ref, bias_ref[...], *refs[5:])


def grid_masks(count):
    row = lax.broadcasted_iota(jnp.int32, (count, PAD), 0)
    i = (row // GRID) % GRID
    j = row % GRID
    masks = []
    for tap in range(9):
        di, dj = tap // 3 - 1, tap % 3 - 1
        inside = (i + di >= 0) & (i + di < GRID) & (j + dj >= 0) & (j + dj < GRID)
        masks.append(inside.astype(F32))
    return masks


def collect_taps(taps, masks, first_lanes):
    count = taps.shape[0]
    total = None
    for tap in range(9):
        offset = (tap // 3 - 1) * GRID + tap % 3 - 1
        moved = pltpu.roll(taps, (PAD - tap * CH) % PAD, 1) if tap else taps
        moved = pltpu.roll(moved, (-offset) % count, 0) if offset else moved
        moved = moved * masks[tap]
        total = moved if total is None else total + moved
    return total * first_lanes


def spread_taps(values, masks):
    count = values.shape[0]
    total = None
    for tap in range(9):
        offset = (tap // 3 - 1) * GRID + tap % 3 - 1
        moved = pltpu.roll(values, tap * CH, 1) if tap else values
        moved = pltpu.roll(moved, offset % count, 0) if offset else moved
        moved = moved * masks[8 - tap]
        total = moved if total is None else total + moved
    return total


def store_rows(ref, start, values):
    for index in range(values.shape[1] // PAD):
        ref[start + index : start + index + 1, :] = values[:, index * PAD : (index + 1) * PAD]


def load_rows(ref, start, count):
    return jnp.concatenate(
        [ref[start + index : start + index + 1, :] for index in range(count)], axis=1
    )


def tail_kernel(vectors, unused_ref, *refs):
    sum_ref, even_ref, arrived_ref, far_ref, bias_ref, gains_ref, shifts_ref = refs[:7]
    conv_ref, first_bias_ref, mid_ref, mid_bias_ref, moved_ref = refs[7:12]
    learned_ref, low_ref, grad_ref, normed_ref, spread_ref, small_ref = refs[12:]
    count = low_ref.shape[0]
    frames = count // (GRID * GRID)
    patches = GRID * GRID
    value = (
        sum_ref[...]
        + even_ref[...]
        + arrived_ref[...].astype(F32)
        + far_ref[...].astype(F32)
        + bias_ref[...]
    )
    normed, inverse = norm_stats(value)
    gain = gains_ref[2:3, :]
    normed_low = (normed * gain + shifts_ref[2:3, :]).astype(BF)
    normed_ref[...] = normed_low
    masks = grid_masks(count)
    lane = lax.broadcasted_iota(jnp.int32, (count, PAD), 1)
    first_lanes = (lane < CH).astype(F32)
    first = collect_taps(dot(normed_low, conv_ref[...]), masks, first_lanes)
    hidden, slope = gelu_both(first + first_bias_ref[...])
    hidden = hidden * first_lanes
    hiddens, slopes = [hidden], [slope]
    maps = None
    for layer in range(3):
        pre = collect_taps(exact(hiddens[layer], mid_ref[layer]), masks, first_lanes)
        pre = pre + mid_bias_ref[layer : layer + 1, :]
        if layer < 2:
            hidden, slope = gelu_both(pre)
            hiddens.append(hidden * first_lanes)
            slopes.append(slope)
        else:
            maps = jax.nn.sigmoid(pre) * first_lanes
    frame_of_row = lax.broadcasted_iota(jnp.int32, (count, PAD), 0) // patches
    wide = None
    for frame in range(frames):
        moved = pltpu.roll(maps, frame * CH, 1) if frame else maps
        moved = moved * (frame_of_row == frame).astype(F32)
        wide = moved if wide is None else wide + moved
    cotangent = jnp.concatenate(
        [
            moved_ref[count : count + frames * CH, :].astype(F32),
            jnp.zeros((PAD - frames * CH, value.shape[1]), F32),
        ],
        axis=0,
    )
    learned_ref[...] = exact(wide, value, 0, 0)[: frames * CH] * (1.0 / patches)
    pooled = exact(wide, cotangent) * (1.0 / patches)
    products = exact(value, cotangent, 1, 1) * (1.0 / patches)
    grad = None
    for frame in range(frames):
        moved = pltpu.roll(products, PAD - frame * CH, 1) if frame else products
        moved = moved * (frame_of_row == frame).astype(F32)
        grad = moved if grad is None else grad + moved
    grad = grad * maps * (1.0 - maps)
    small_ref[...] = jnp.zeros_like(small_ref)
    conv_start = 7 * vectors + 4 * vectors
    for layer in range(2, -1, -1):
        taps = spread_taps(grad, masks)
        weight = exact(hiddens[layer], taps, 0, 0)[:CH]
        small_ref[conv_start + layer * CH : conv_start + (layer + 1) * CH, :] = weight
        bias_row = conv_start + 3 * CH + 1 + layer
        small_ref[bias_row : bias_row + 1, :] = column_sum(grad)
        grad = exact(taps, mid_ref[layer], 1, 1) * slopes[layer]
    grad_low = grad.astype(BF).astype(F32)
    small_ref[conv_start + 3 * CH : conv_start + 3 * CH + 1, :] = column_sum(grad_low)
    spread = spread_taps(grad_low, masks).astype(BF)
    spread_ref[...] = spread
    grad_normed = dot(spread, conv_ref[...], 1, 1)
    scaled = grad_normed * gain
    mean_scaled = jnp.mean(scaled, axis=-1, keepdims=True)
    mean_cross = jnp.mean(scaled * normed, axis=-1, keepdims=True)
    grad_value = inverse * (scaled - mean_scaled - normed * mean_cross)
    grad_value = grad_value + pooled
    grad_ref[...] = grad_value
    low = grad_value.astype(BF)
    low_ref[...] = low
    store_rows(small_ref, 2 * vectors, column_sum(grad_normed * normed))
    store_rows(small_ref, 5 * vectors, column_sum(grad_normed))
    store_rows(small_ref, 6 * vectors, column_sum(low.astype(F32)))


def mlp_back_kernel(unused_ref, *refs):
    grads = refs[:2]
    slope_ref, up_ref, down_ref = refs[2:5]
    pre_ref, even_ref, odd_ref, bias_ref = refs[5:]
    grad_act = dot(stack_rows(grads), down_ref[...], 1, 1)
    grad_pre = (grad_act * slope_ref[...]).astype(BF)
    pre_ref[...] = grad_pre
    bias_ref[...] = column_sum(grad_pre.astype(F32))
    partial = dot(grad_pre, up_ref[...], 1, 1)
    count = even_ref.shape[0]
    even_ref[...] = partial[:count]
    odd_ref[...] = partial[count:].astype(BF)


def divide_rows(ids_ref, all_ref, refs):
    kept_ref, sent_ref, more_kept_ref, more_sent_ref = refs
    high, low = ids_ref[1], ids_ref[2]
    size = all_ref.shape[0] // 8
    columns = kept_ref.shape[1]
    for index in range(4):
        rows = slice(index * size, (index + 1) * size)
        kept_ref[rows, :] = all_ref[rows_at(2 * index + low, size), :columns]
        sent_ref[rows, :] = all_ref[rows_at(2 * index + 1 - low, size), :columns].astype(BF)
        hi = high ^ (2 * (index % 2))
        lo = low ^ (index // 2)
        more_kept_ref[rows, :] = all_ref[rows_at(2 * hi + lo, size), columns:]
        more_sent_ref[rows, :] = all_ref[rows_at(2 * (hi ^ 1) + lo, size), columns:].astype(BF)


def fold(values, count):
    size = values.shape[0] // count
    return jnp.concatenate(
        [values[index * size : (index + 1) * size] for index in range(count)], axis=1
    )


def unfold(values, count):
    lanes = values.shape[1] // count
    return jnp.concatenate(
        [values[:, index * lanes : (index + 1) * lanes] for index in range(count)], axis=0
    )


def rounded(values):
    return values.astype(BF).astype(F32)


def mlp_grads_kernel(ids_ref, *refs):
    tokens, grads = refs[:4], refs[4:8]
    act, pre = stack_rows(refs[8:10]), stack_rows(refs[10:12])
    normed_ref, spread_ref = refs[12:14]
    all_ref = refs[18]
    quarter = act.shape[1]
    width = tokens[0].shape[1]
    all_ref[:, :quarter] = dot(stack_rows(tokens), pre, 0, 0)
    all_ref[:, quarter : quarter + width] = dot(act, stack_rows(grads), 0, 0)
    all_ref[:, quarter + width :] = dot(normed_ref[...], spread_ref[...], 0, 0)
    divide_rows(ids_ref, all_ref, refs[14:18])


def norm_two_back_kernel(unused_ref, *refs):
    sum_ref, grad_ref, even_ref, arrived_ref, far_ref, gains_ref = refs[:6]
    total_ref, low_ref, rows_ref = refs[6:]
    grad_normed = even_ref[...] + arrived_ref[...].astype(F32) + far_ref[...].astype(F32)
    result, gain_row, shift_row = back_of_norm(sum_ref[...], gains_ref[1:2, :], grad_normed)
    total = result + grad_ref[...]
    total_ref[...] = total
    low_ref[...] = total.astype(BF)
    rows_ref[0:1, :] = gain_row
    rows_ref[1:2, :] = shift_row


def attend_back_part(heads, scale, first, branches, refs, prior_ref, own_ref, total_ref):
    out_ref, q_ref, kv_ref, log_ref, qclip_ref, kclip_ref = refs
    width = heads * HEAD_DIM
    count = own_ref.shape[0]
    queries = slice(first, first + count)
    grad_mixed = dot(stack_rows(branches), out_ref[...], 1, 1).astype(BF)
    same = kclip_ref[...] == qclip_ref[:, queries]
    query_parts, key_parts, value_parts = [], [], []
    for head in range(heads):
        lanes = slice(head * HEAD_DIM, (head + 1) * HEAD_DIM)
        values = slice(width + head * HEAD_DIM, width + (head + 1) * HEAD_DIM)
        scores = scores_of(kv_ref, q_ref, queries, lanes, same, scale)
        prob = jnp.exp(scores - log_ref[head : head + 1, queries])
        grad_prob = dot(kv_ref[:, values], grad_mixed[:, lanes], 1, 1)
        delta = jnp.sum(prob * grad_prob, axis=0, keepdims=True)
        grad_score = (prob * (grad_prob - delta)).astype(BF)
        query_parts.append(dot(kv_ref[:, lanes], grad_score, 0, 0) * scale)
        key_parts.append(dot(grad_score, q_ref[queries, lanes]) * scale)
        value_parts.append(dot(prob.astype(BF), grad_mixed[:, lanes]))
    own_ref[...] = jnp.concatenate(query_parts, axis=0).T.astype(BF)
    terms = jnp.concatenate(key_parts + value_parts, axis=1)
    total_ref[...] = terms if prior_ref is None else prior_ref[...] + terms


def attend_back_first_kernel(heads, scale, unused_ref, *refs):
    attend_back_part(heads, scale, 0, refs[:2], refs[2:8], None, refs[8], refs[9])


def attend_back_next_kernel(heads, scale, first, unused_ref, *refs):
    attend_back_part(heads, scale, first, refs[:1], refs[1:7], refs[7], refs[8], refs[9])


def attend_back_last_kernel(heads, scale, first, unused_ref, *refs):
    prior_ref, first_ref, next_ref, w_ref = refs[7:11]
    own_ref, other_ref = refs[11:13]
    even_refs, odd_refs = refs[13:17], refs[17:21]
    part_ref, total_ref = refs[21:]
    attend_back_part(heads, scale, first, refs[:1], refs[1:7], prior_ref, part_ref, total_ref)
    width = heads * HEAD_DIM
    count = own_ref.shape[0]
    middle = first_ref.shape[0]
    own_ref[:middle, :width] = first_ref[...]
    own_ref[middle:first, :width] = next_ref[...]
    own_ref[first:, :width] = part_ref[...]
    own_ref[:, width:] = total_ref[:count, :].astype(BF)
    other_ref[...] = total_ref[count:, :].astype(BF)
    own = dot(own_ref[...], w_ref[...], 1, 1)
    other = dot(other_ref[...], w_ref[:, width:], 1, 1)
    split_blocks(jnp.concatenate([own, other], axis=0), even_refs, odd_refs)


def qkv_grads_kernel(ids_ref, *refs):
    tokens, branches, mixes = refs[:8], refs[8:12], refs[12:16]
    own_ref, other_ref = refs[16:18]
    all_ref = refs[22]
    quarter = mixes[0].shape[0]
    full = dot(stack_rows(tokens[:4]), own_ref[...], 0, 0)
    more = dot(stack_rows(tokens[4:]), other_ref[...], 0, 0)
    all_ref[:, :quarter] = full[:, :quarter]
    all_ref[:, quarter : 3 * quarter] = full[:, quarter:] + more
    rank = ids_ref[0]
    branch = stack_rows(branches)
    wanted = branch[:, :quarter]
    for index in range(1, 4):
        wanted = jnp.where(
            rank == index, branch[:, index * quarter : (index + 1) * quarter], wanted
        )
    count = branches[0].shape[0]
    for bits in range(4):
        turned = jnp.concatenate(
            [wanted[(item ^ bits) * count : ((item ^ bits) + 1) * count] for item in range(4)],
            axis=0,
        )
        all_ref[rows_at(rank ^ bits, quarter), 3 * quarter :] = dot(mixes[bits][...], turned)
    divide_rows(ids_ref, all_ref, refs[18:22])


def half_rows(ids_ref, refs, outs):
    kept_ref, arrived_ref, more_kept_ref, more_arrived_ref = refs
    own_ref, sent_ref, more_own_ref, more_sent_ref = outs
    size = own_ref.shape[0] // 2
    high = ids_ref[1]
    for step in range(2):
        rows = slice(step * size, (step + 1) * size)
        where = rows_at(high ^ (2 * step), size)
        own_ref[rows, :] = kept_ref[where, :] + arrived_ref[where, :].astype(F32)
        where = rows_at(high ^ (2 * step + 1), size)
        sent_ref[rows, :] = (kept_ref[where, :] + arrived_ref[where, :].astype(F32)).astype(BF)
    more = more_kept_ref[...] + more_arrived_ref[...].astype(F32)
    more_own_ref[...] = more[: 2 * size]
    more_sent_ref[: 2 * size, :] = more[2 * size :].astype(BF)


def half_kernel(ids_ref, *refs):
    half_rows(ids_ref, refs[:4], refs[4:])


def half_sums_kernel(ids_ref, *refs):
    half_rows(ids_ref, refs[:4], (refs[6], refs[7], refs[8], refs[9]))
    sums = refs[4][...].astype(F32) + refs[5][...].astype(F32)
    refs[9][refs[8].shape[0] :, :] = fold(sums, 3).astype(BF)
    refs[10][...] = rounded(sums)


def fourth_rows(refs, own_ref, sent_ref):
    size = own_ref.shape[0]
    start = 0
    for kept_ref, arrived_ref in (refs[:2], refs[2:4]):
        columns = slice(start, start + kept_ref.shape[1])
        own_ref[:, columns] = kept_ref[:size, :] + arrived_ref[:size, :].astype(F32)
        sent_ref[:size, columns] = (
            kept_ref[size:, :] + arrived_ref[size : 2 * size, :].astype(F32)
        ).astype(BF)
        start += kept_ref.shape[1]


def fourth_kernel(unused_ref, *refs):
    fourth_rows(refs[:4], *refs[4:])


def fourth_sums_kernel(unused_ref, *refs):
    arrived_ref, sums_ref = refs[3], refs[4]
    own_ref, sent_ref, out_ref = refs[5:]
    fourth_rows(refs[:4], own_ref, sent_ref)
    sums = sums_ref[...] + unfold(arrived_ref[refs[2].shape[0] :, :].astype(F32), 3)
    sent_ref[own_ref.shape[0] :, :] = fold(sums, 6).astype(BF)
    out_ref[...] = rounded(sums)


def total_kernel(unused_ref, kept_ref, arrived_ref, out_ref):
    out_ref[...] = (kept_ref[...] + arrived_ref[...].astype(F32)).astype(BF)


def total_sums_kernel(unused_ref, kept_ref, arrived_ref, sums_ref, out_ref):
    size, columns = kept_ref.shape
    out_ref[:, :columns] = (kept_ref[...] + arrived_ref[:size, :].astype(F32)).astype(BF)
    out_ref[:, columns:] = (
        sums_ref[...] + unfold(arrived_ref[size:, :].astype(F32), 6)
    ).astype(BF)


def norm_one_back_kernel(vectors, rank_ref, *refs):
    moved_ref, grad_ref, even_ref, arrived_ref, far_ref, side_ref, gains_ref = refs[:7]
    learned_ref, small_ref, two_ref, up_ref, more_up_ref = refs[7:12]
    back_ref, rounded_ref, sums_ref = refs[12:]
    count = grad_ref.shape[0]
    grad_normed = (
        even_ref[...]
        + arrived_ref[...].astype(F32)
        + far_ref[...].astype(F32)
        + side_ref[...].astype(F32)
    )
    result, gain_row, shift_row = back_of_norm(
        moved_ref[:count, :].astype(F32), gains_ref[0:1, :], grad_normed
    )
    back_ref[:count, :] = (result + grad_ref[...]).astype(BF)
    back_ref[count:, :] = learned_ref[...].astype(BF)
    sums_ref[...] = small_ref[...]
    store_rows(sums_ref, 0, gain_row)
    store_rows(sums_ref, vectors, two_ref[0:1, :])
    store_rows(sums_ref, 3 * vectors, shift_row)
    store_rows(sums_ref, 4 * vectors, two_ref[1:2, :])
    for index in range(4):
        store_rows(
            sums_ref,
            (7 + index) * vectors,
            jnp.where(rank_ref[0] == index, up_ref[...] + more_up_ref[...], 0.0),
        )
    rounded_ref[...] = sums_ref[...].astype(BF)


def back_kernel(unused_ref, moved_ref, grad_ref, learned_ref):
    count = grad_ref.shape[0]
    grad_ref[...] = moved_ref[:count, :].astype(F32)
    learned_ref[...] = moved_ref[count:, :].astype(F32)


def finish_sums_kernel(vectors, quarter, rank_ref, *refs):
    parts, sums_ref = refs[:4], refs[-1]
    finish_qkv_kernel(4, quarter, rank_ref, *parts, *refs[4:6])
    total = None
    for block in ordered(parts, rank_ref[0], slice(4 * quarter, parts[0].shape[1])):
        total = block if total is None else total + block
    sums_ref[...] = total
    refs = refs[6:-1]
    gains_ref, shifts_ref, up_ref, down_ref, first_ref, mid_ref, mid_bias_ref = refs
    for index in range(3):
        gains_ref[index : index + 1, :] = load_rows(sums_ref, index * vectors, vectors)
        shifts_ref[index : index + 1, :] = load_rows(sums_ref, (3 + index) * vectors, vectors)
    down_ref[...] = load_rows(sums_ref, 6 * vectors, vectors)
    quarters = [load_rows(sums_ref, (7 + index) * vectors, vectors) for index in range(4)]
    unit = quarters[0].shape[1] // 8
    up_ref[...] = jnp.concatenate(
        [
            quarters[index][:, group * unit : (group + 1) * unit]
            for group in range(8)
            for index in range(4)
        ],
        axis=1,
    )
    start = 11 * vectors
    for layer in range(3):
        mid_ref[layer] = sums_ref[start + layer * CH : start + (layer + 1) * CH, : 9 * CH]
    start = start + 3 * CH
    first_ref[...] = sums_ref[start : start + 1, :CH]
    mid_bias_ref[...] = sums_ref[start + 1 : start + 4, :CH]


def shards_square(
    ranks,
    frame_size,
    inputs,
    clip_id,
    ln_gains,
    ln_biases,
    w_qkv,
    w_out,
    w_up,
    w_down,
    up_bias,
    down_bias,
    conv_first,
    conv_first_bias,
    conv_mid,
    conv_mid_bias,
    cotangent,
):
    lows = 2
    frames_dev = inputs.shape[1]
    patches = inputs.shape[2]
    width = inputs.shape[3]
    rows = frames_dev * patches
    learned_rows = frames_dev * CH
    hidden = up_bias.shape[0]
    quarter = width // ranks
    heads = quarter // HEAD_DIM
    hidden_quarter = hidden // ranks
    unit = hidden_quarter // frame_size
    size = width // frame_size
    vectors = width // PAD
    own_count = ranks * rows
    place = lax.axis_index("frame")
    ids = jnp.stack([lax.axis_index("seq"), place // lows, place % lows])

    def permute(array, target):
        pairs = []
        for seq in range(ranks):
            for hi in range(ranks):
                for lo in range(lows):
                    to_seq, to_hi, to_lo = target(seq, hi, lo)
                    pairs.append(
                        (
                            seq * frame_size + hi * lows + lo,
                            to_seq * frame_size + to_hi * lows + to_lo,
                        )
                    )
        return lax.ppermute(array, AXES, pairs)

    def flip(array, seq_bits, hi_bits=0, lo_bits=0):
        return permute(
            array, lambda seq, hi, lo: (seq ^ seq_bits, hi ^ hi_bits, lo ^ lo_bits)
        )

    def after(array, *others):
        return lax.optimization_barrier((array,) + others)[0]

    last = []

    def ordered_run(kernel, name, scalars, arrays, outs, scratch=()):
        if last:
            arrays = [after(arrays[0], last[0])] + list(arrays[1:])
        results = list(run(kernel, name, scalars, arrays, outs, scratch))
        last[:] = [results[-1]]
        return results

    def to_planes(array):
        return permute(array, lambda seq, hi, lo: (RANK_OF[hi], PLANE_OF[seq], lo))

    def from_planes(array):
        return permute(
            array, lambda seq, hi, lo: (PLANE_OF.index(hi), RANK_OF.index(seq), lo)
        )

    def gather_four(block):
        far = flip(block, 2)
        near = flip(block, 1)
        return [block, near, far, flip(far, 1)]

    def pass_sum(even, arrived, name):
        (result,) = ordered_run(
            pass_sum_kernel,
            name,
            ids,
            [even, arrived],
            [((rows, width), BF)],
        )
        return result

    def scatter_four(evens, odds, name):
        far = flip(pass_sum(evens[1], flip(odds[1], 1), name), 2)
        return flip(odds[0], 1), far

    def row_parts(blocks, first, second):
        return [
            ((blocks * size, columns), kind) for columns in (first, second) for kind in (F32, BF)
        ]

    def scatter_half(parts, sums, name):
        kept, sent, more_kept, more_sent = parts
        shapes = row_parts(2, kept.shape[1], more_kept.shape[1])
        arrays = [kept, flip(sent, 0, 0, 1), more_kept, flip(more_sent, 0, 1)]
        if sums is None:
            return ordered_run(half_kernel, name, ids, arrays, shapes), None
        shapes[3] = ((2 * size + small_rows // 3, more_kept.shape[1]), BF)
        arrays += [sums, flip(sums, 0, 1)]
        *parts, sums = ordered_run(
            half_sums_kernel, name, ids, arrays, shapes + [(sums.shape, F32)]
        )
        return parts, sums

    def scatter_fourth(parts, sums, name):
        kept, sent, more_kept, more_sent = parts
        columns = kept.shape[1] + more_kept.shape[1]
        arrays = [kept, flip(sent, 0, 1), more_kept, flip(more_sent, 0, 0, 1)]
        if sums is None:
            shapes = [((size, columns), F32), ((size, columns), BF)]
            return ordered_run(fourth_kernel, name, ids, arrays, shapes), None
        shapes = [((size, columns), F32), ((size + small_rows // 6, columns), BF)]
        *parts, sums = ordered_run(
            fourth_sums_kernel, name, ids, arrays + [sums], shapes + [(sums.shape, F32)]
        )
        return parts, sums

    def scatter_last(parts, sums, name):
        kept, sent = parts
        arrays = [kept, flip(sent, 0, 2)]
        if sums is None:
            return ordered_run(total_kernel, name, ids, arrays, [(kept.shape, BF)])[0]
        shape = (size, kept.shape[1] + PAD)
        return ordered_run(total_sums_kernel, name, ids, arrays + [sums], [(shape, BF)])[0]

    (pack,) = ordered_run(
        pack_kernel,
        "pack",
        ids,
        [inputs.reshape(rows, width), cotangent.reshape(learned_rows, width), clip_id],
        [((rows + learned_rows + 16, width), BF)],
    )
    moved = to_planes(pack)

    (own_pack,) = ordered_run(
        select_kernel, "select", ids, [w_qkv, w_out], [((size, width), BF)]
    )
    pack_two = flip(own_pack, 0, 2)
    pack_one = flip(own_pack, 0, 1)
    pack_side = flip(own_pack, 0, 0, 1)
    pack_three = flip(pack_two, 0, 1)
    packs = [own_pack, pack_side]
    for item in (pack_one, pack_two, pack_three):
        packs += [item, flip(item, 0, 0, 1)]

    mid_pad = jnp.pad(conv_mid, ((0, 0), (0, PAD - CH), (0, PAD - 9 * CH)))
    mid_bias_pad = jnp.pad(conv_mid_bias, ((0, 0), (0, PAD - CH)))
    first_bias_pad = jnp.pad(conv_first_bias, (0, PAD - CH)).reshape(1, PAD)
    up_bias_row = up_bias.reshape(1, hidden)
    down_bias_row = down_bias.reshape(1, width)

    own_a, own_b = ordered_run(
        prepare_kernel,
        "prepare",
        ids,
        [
            after(w_up, mid_pad, mid_bias_pad, first_bias_pad, up_bias_row, down_bias_row),
            w_down,
            conv_first,
        ],
        [((size, hidden_quarter + PAD), BF), ((size, width), BF)],
    )

    low_norm, query_clip, key_clip = ordered_run(
        norm_one_kernel,
        "norm_one",
        ids,
        [moved, ln_gains, ln_biases],
        [((rows, width), BF), ((1, own_count), F32), ((2 * own_count, 1), F32)],
    )
    low_norm = after(low_norm, pack_side, pack_one, pack_two)

    def join(pairs, name):
        flat = [item for pair in pairs for item in pair]
        outs = [((2 * pair[0].shape[0], pair[0].shape[1]), BF) for pair in pairs]
        return ordered_run(join_kernel, name, ids, flat, outs)

    far = flip(low_norm, 2)
    side = flip(low_norm, 0, 0, 1)
    near = flip(low_norm, 1)
    far_a, side_b = flip(own_a, 0, 2), flip(own_b, 0, 0, 1)
    (picked,) = ordered_run(
        pick_kernel,
        "pick",
        ids,
        [after(far, far_a, side_b, *packs[1:]), side],
        [((rows, width), BF)],
    )
    two_a, two_b = join(
        [(own_a, far_a), (own_b, side_b)], "join_two"
    )
    corner = permute(
        picked,
        lambda seq, hi, lo: (seq, hi, lo ^ 1) if seq % 2 == 0 else (seq ^ 2, hi, lo),
    )
    far_near = flip(far, 1)
    side_near = flip(side, 1)
    corner = after(corner, near, far_near, side_near)
    all_one = [near, far, far_near, side, side_near, corner, flip(corner, 1)]
    all_one = [low_norm] + all_one
    queries, keyvals, qkv_quarter, own_out, near_out, far_out, both_out = ordered_run(
        functools.partial(project_kernel, quarter),
        "project",
        ids,
        all_one + packs,
        [
            ((own_count, quarter), BF),
            ((2 * own_count, 2 * quarter), BF),
            ((width, 3 * quarter), BF),
        ]
        + [((quarter, quarter), BF)] * 4,
        [pltpu.VMEM((width, quarter), BF)],
    )
    out_blocks = [own_out, flip(near_out, 1), flip(far_out, 2), flip(both_out, 3)]
    scale = HEAD_DIM ** (-0.5)
    attended, logs = ordered_run(
        functools.partial(attend_wide_kernel, heads, scale),
        "attend",
        ids,
        [queries, keyvals, query_clip, key_clip],
        [((quarter, own_count), BF), ((8, own_count), F32)],
    )
    blocks_of = [((rows, width), F32)] * 2 + [((rows, width), BF)] * 2
    *parts, out_quarter = ordered_run(
        out_kernel,
        "out",
        ids,
        [attended] + out_blocks,
        blocks_of + [((quarter, width), BF)],
    )
    evens, odds = parts[:2], parts[2:]
    arrived, far = scatter_four(evens, odds, "out_pass")
    four_a, four_b = join(
        [(two_a, flip(two_a, 0, 1)), (two_b, flip(two_b, 0, 2))], "join_four"
    )
    after_attention, low_two = ordered_run(
        norm_two_kernel,
        "norm_two",
        ids,
        [moved, evens[0], arrived, far, ln_gains, ln_biases],
        [((rows, width), F32), ((rows, width), BF)],
    )
    near_two, far_two = flip(low_two, 1), flip(low_two, 2)
    pair = [
        ((2 * rows, hidden_quarter), BF),
        ((2 * rows, hidden_quarter), F32),
        ((rows, width), F32),
        ((rows, width), BF),
    ]
    up_full, down_full, conv_full, own_bias, act, slope, even, odd = ordered_run(
        mlp_kernel,
        "mlp",
        ids,
        [low_two, near_two]
        + [four_a, flip(four_a, 0, 0, 1), four_b, flip(four_b, 0, 1), up_bias_row],
        [
            ((width, hidden_quarter), BF),
            ((hidden_quarter, width), BF),
            ((width, PAD), BF),
            ((1, hidden_quarter), F32),
        ]
        + pair,
    )
    far_two = after(far_two, even)
    all_two = [low_two, near_two, far_two, flip(far_two, 1)]
    acts, slopes, evens, odds = [act], [slope], [even], [odd]
    for item, rest in zip(
        (acts, slopes, evens, odds),
        ordered_run(
            mlp_more_kernel, "mlp_more", ids, all_two[2:] + [up_full, down_full, own_bias], pair
        ),
    ):
        item.append(rest)
    arrived, far = scatter_four(evens, odds, "mlp_pass")

    small_rows = -(-(11 * vectors + 3 * CH + 4) // 8) * 8
    learned, low_mlp, grad_block, low_three, spread, small = ordered_run(
        functools.partial(tail_kernel, vectors),
        "tail",
        ids,
        [
            after_attention,
            evens[0],
            arrived,
            far,
            down_bias_row,
            ln_gains,
            ln_biases,
            conv_full,
            first_bias_pad,
            mid_pad,
            mid_bias_pad,
            moved,
        ],
        [
            ((learned_rows, width), F32),
            ((rows, width), BF),
            ((rows, width), F32),
            ((rows, width), BF),
            ((rows, PAD), BF),
            ((small_rows, PAD), F32),
        ],
    )

    near_mlp, far_mlp = flip(low_mlp, 1), flip(low_mlp, 2)
    pair = [
        ((2 * rows, hidden_quarter), BF),
        ((rows, width), F32),
        ((rows, width), BF),
        ((1, hidden_quarter), F32),
    ]
    pre, even, odd, bias = ordered_run(
        mlp_back_kernel,
        "mlp_back",
        ids,
        [low_mlp, near_mlp, slopes[0], up_full, down_full],
        pair,
    )
    far_mlp = after(far_mlp, even)
    all_mlp = [low_mlp, near_mlp, far_mlp, flip(far_mlp, 1)]
    pres, evens, odds, biases = [pre], [even], [odd], [bias]
    for item, rest in zip(
        (pres, evens, odds, biases),
        ordered_run(
            mlp_back_kernel,
            "mlp_back_more",
            ids,
            all_mlp[2:] + [slopes[1], up_full, down_full],
            pair,
        ),
    ):
        item.append(rest)
    arrived, far = scatter_four(evens, odds, "mlp_back_pass")
    columns = hidden_quarter + width + PAD
    mlp_parts = ordered_run(
        mlp_grads_kernel,
        "mlp_grads",
        ids,
        all_two + all_mlp + acts + pres + [low_three, spread],
        row_parts(4, hidden_quarter, width + PAD),
        [pltpu.VMEM((width, columns), F32)],
    )
    grad_after, low_branch, rows_two = ordered_run(
        norm_two_back_kernel,
        "norm_two_back",
        ids,
        [after_attention, grad_block, evens[0], arrived, far, ln_gains],
        [((rows, width), F32), ((rows, width), BF), ((2, width), F32)],
    )

    near_branch, far_branch = flip(low_branch, 1), flip(low_branch, 2)
    mixes = gather_four(after(attended, far_branch))
    common = [out_quarter, queries, keyvals, logs, query_clip, key_clip]
    total = ((2 * own_count, 2 * quarter), F32)
    grads_first, sums_first = ordered_run(
        functools.partial(attend_back_first_kernel, heads, scale),
        "attend_back",
        ids,
        [low_branch, near_branch] + common,
        [((2 * rows, quarter), BF), total],
    )
    far_branch = after(far_branch, sums_first)
    all_branch = [low_branch, near_branch, far_branch, flip(far_branch, 1)]
    grads_next, sums_next = ordered_run(
        functools.partial(attend_back_next_kernel, heads, scale, 2 * rows),
        "attend_back_next",
        ids,
        [far_branch] + common + [sums_first],
        [((rows, quarter), BF), total],
    )
    grads_own, grads_other, *parts = ordered_run(
        functools.partial(attend_back_last_kernel, heads, scale, 3 * rows),
        "attend_back_last",
        ids,
        all_branch[3:] + common + [sums_next, grads_first, grads_next, qkv_quarter],
        [((own_count, 3 * quarter), BF), ((own_count, 2 * quarter), BF)]
        + [((rows, width), F32)] * 4
        + [((rows, width), BF)] * 4,
        [
            pltpu.VMEM((rows, quarter), BF),
            pltpu.VMEM((2 * own_count, 2 * quarter), F32),
        ],
    )
    evens = parts[:4]
    arrived = [flip(item, 1) for item in parts[4:]]
    corner = permute(
        pass_sum(evens[3], arrived[3], "corner_pass"),
        lambda seq, hi, lo: (seq ^ 2, hi, lo) if seq % 2 == 0 else (seq, hi, lo ^ 1),
    )
    mlp_parts, unused = scatter_half(mlp_parts, None, "mlp_half")
    qkv_parts = ordered_run(
        qkv_grads_kernel,
        "qkv_grads",
        ids,
        all_one + all_branch + mixes + [grads_own, grads_other],
        row_parts(4, width // 2, width // 2),
        [pltpu.VMEM((width, width), F32)],
    )
    far, side = ordered_run(
        pass_on_kernel,
        "pass_on",
        ids,
        [evens[1], evens[2], arrived[1], arrived[2], corner],
        [((rows, width), BF), ((rows, width), BF)],
    )
    qkv_parts[1], qkv_parts[3] = after(qkv_parts[1], far), after(qkv_parts[3], far)
    far, side = flip(far, 2), flip(side, 0, 0, 1)
    mlp_parts, unused = scatter_fourth(mlp_parts, None, "mlp_fourth")
    moved_back, sums = ordered_run(
        functools.partial(norm_one_back_kernel, vectors),
        "norm_one_back",
        ids,
        [moved, grad_after, evens[0], arrived[0], far, side, ln_gains]
        + [learned, small, rows_two]
        + biases,
        [((rows + learned_rows, width), BF), ((small_rows, PAD), BF)],
        [pltpu.VMEM((small_rows, PAD), F32)],
    )

    qkv_parts, sums = scatter_half(qkv_parts, sums, "qkv_half")
    mlp_share = scatter_last(mlp_parts, None, "mlp_total")
    qkv_parts, sums = scatter_fourth(qkv_parts, sums, "qkv_fourth")
    mlp_share = after(mlp_share, sums)
    mlp_far, mlp_near = flip(mlp_share, 2), flip(mlp_share, 1)
    qkv_share = scatter_last(qkv_parts, sums, "qkv_total")
    mlp_far = after(mlp_far, qkv_share)
    qkv_far, qkv_near = flip(qkv_share, 2), flip(qkv_share, 1)
    sum_up, sum_down, sum_conv = ordered_run(
        functools.partial(finish_mlp_kernel, ranks, hidden_quarter, width, unit),
        "finish_mlp",
        ids,
        [mlp_share, mlp_near, mlp_far, flip(mlp_far, 1)],
        [((size, hidden), F32), ((ranks * unit, width), F32), ((size, 9 * CH), F32)],
    )
    grad_input, learned = ordered_run(
        back_kernel,
        "back",
        ids,
        [from_planes(moved_back)],
        [((rows, width), F32), ((learned_rows, width), F32)],
    )
    (
        sum_qkv,
        sum_out,
        sum_gains,
        sum_shifts,
        sum_up_bias,
        sum_down_bias,
        sum_first,
        sum_mid,
        sum_mid_bias,
    ) = ordered_run(
        functools.partial(finish_sums_kernel, vectors, quarter),
        "finish_qkv",
        ids,
        [qkv_share, qkv_near, qkv_far, flip(after(qkv_far, sum_down), 1)],
        [
            ((size, 3 * width), F32),
            ((size, width), F32),
            ((3, width), F32),
            ((3, width), F32),
            ((1, hidden), F32),
            ((1, width), F32),
            ((1, CH), F32),
            ((3, CH, 9 * CH), F32),
            ((3, CH), F32),
        ],
        [pltpu.VMEM((small_rows, PAD), F32)],
    )
    return (
        learned.reshape(1, frames_dev, CH, width),
        grad_input.reshape(1, frames_dev, patches, width),
        sum_qkv,
        sum_out,
        sum_up,
        sum_down,
        sum_conv,
        sum_gains,
        sum_shifts,
        sum_up_bias.reshape(hidden),
        sum_down_bias.reshape(width),
        sum_first.reshape(CH),
        sum_mid,
        sum_mid_bias,
    )


def solution(mesh):
    placed = (
        P("seq", "frame", None, None),
        P("seq", None),
        P(),
        P(),
        P("frame", None),
        P("frame", None),
        P("frame", None),
        P("frame", None),
        P(),
        P(),
        P("frame", None),
        P(),
        P(),
        P(),
        P("seq", "frame", None, None),
    )
    ranks, frame_size = mesh.shape["seq"], mesh.shape["frame"]
    body = shards_square if ranks == 4 and frame_size == 8 else shards_general
    return jax.shard_map(
        functools.partial(body, ranks, frame_size),
        mesh=mesh,
        in_specs=placed,
        out_specs=(
            P("seq", "frame", None, None),
            P("seq", "frame", None, None),
            P("frame", None),
            P("frame", None),
            P("frame", None),
            P("frame", None),
            P("frame", None),
            P(),
            P(),
            P(),
            P(),
            P(),
            P(),
            P(),
        ),
        check_vma=False,
    )
```

```python
import functools

import jax
import jax.numpy as jnp
from jax import lax
from jax.experimental import pallas as pl
from jax.experimental.pallas import tpu as pltpu
from jax.sharding import PartitionSpec as P

HEADS = 12
HEAD_DIM = 64
CH = 8
GRID = 8

EPSILON = 1e-06
FLOOR_SCORE = -1e30
HIGHEST = lax.Precision.HIGHEST
AXES = ("seq", "frame")
PLANE_OF = (0, 2, 1, 3)
RANK_OF = (0, 2, 1, 3)
VMEM_LIMIT = 56 * 1024 * 1024
BF = jnp.bfloat16
F32 = jnp.float32


def norm_stats(values):
    centre = jnp.mean(values, axis=-1, keepdims=True)
    centred = values - centre
    variance = jnp.mean(centred * centred, axis=-1, keepdims=True)
    inverse = lax.rsqrt(variance + EPSILON)
    return centred * inverse, inverse


def norm_back(normed, inverse, gain, grad):
    scaled = grad * gain
    mean_scaled = jnp.mean(scaled, axis=-1, keepdims=True)
    mean_cross = jnp.mean(scaled * normed, axis=-1, keepdims=True)
    grad_values = inverse * (scaled - mean_scaled - normed * mean_cross)
    return grad_values, jnp.sum(grad * normed, axis=0), jnp.sum(grad, axis=0)


def gelu(values):
    return jax.nn.gelu(values, approximate=False)


def conv_grid(taps):
    side = taps.shape[1]
    width = taps.shape[-1] // 9
    padded = jnp.pad(taps, ((0, 0), (1, 1), (1, 1), (0, 0)))
    total = jnp.zeros(taps.shape[:-1] + (width,), taps.dtype)
    for tap in range(9):
        offset_row = tap // 3
        offset_column = tap % 3
        total = (
            total
            + padded[
                :,
                offset_row : offset_row + side,
                offset_column : offset_column + side,
                tap * width : (tap + 1) * width,
            ]
        )
    return total


def token_maps(first, conv_mid, conv_mid_bias):
    hidden = gelu(first)
    for layer in range(3):
        frames = hidden.shape[0]
        side = hidden.shape[1]
        flat = hidden.reshape(-1, hidden.shape[-1])
        taps = jnp.dot(flat, conv_mid[layer], precision=HIGHEST).reshape(frames, side, side, -1)
        hidden = conv_grid(taps) + conv_mid_bias[layer]
        if layer < 2:
            hidden = gelu(hidden)
    return jax.nn.sigmoid(hidden)


def pool_tokens(maps, features):
    return jnp.einsum("fpk,fpd->fkd", maps, features, precision=HIGHEST) / maps.shape[1]


def dot(left, right, left_dim=1, right_dim=0):
    return lax.dot_general(
        left, right, (((left_dim,), (right_dim,)), ((), ())), preferred_element_type=F32
    )


def attend_kernel(heads, scale, q_ref, kv_ref, qclip_ref, kclip_ref, mixed_ref, log_ref):
    width = heads * HEAD_DIM
    same = kclip_ref[...] == qclip_ref[...]
    for head in range(heads):
        lanes = slice(head * HEAD_DIM, (head + 1) * HEAD_DIM)
        value_lanes = slice(width + head * HEAD_DIM, width + (head + 1) * HEAD_DIM)
        scores = dot(kv_ref[:, lanes], q_ref[:, lanes], 1, 1) * scale
        scores = jnp.where(same, scores, FLOOR_SCORE)
        top = jnp.max(scores, axis=0, keepdims=True)
        shifted = jnp.exp(scores - top)
        total = jnp.sum(shifted, axis=0, keepdims=True)
        prob = (shifted * (1.0 / total)).astype(BF)
        mixed = dot(kv_ref[:, value_lanes], prob, 0, 0)
        mixed_ref[head * HEAD_DIM : (head + 1) * HEAD_DIM, :] = mixed.astype(BF)
        log_ref[head : head + 1, :] = top + jnp.log(total)


def attend_back_kernel(
    heads, scale, q_ref, kv_ref, grad_ref, log_ref, qclip_ref, kclip_ref, dq_ref, dkv_ref
):
    width = heads * HEAD_DIM
    same = kclip_ref[...] == qclip_ref[...]

    @pl.when(pl.program_id(0) == 0)
    def _():
        dkv_ref[...] = jnp.zeros_like(dkv_ref)

    key_parts = []
    value_parts = []
    for head in range(heads):
        lanes = slice(head * HEAD_DIM, (head + 1) * HEAD_DIM)
        value_lanes = slice(width + head * HEAD_DIM, width + (head + 1) * HEAD_DIM)
        scores = dot(kv_ref[:, lanes], q_ref[:, lanes], 1, 1) * scale
        scores = jnp.where(same, scores, FLOOR_SCORE)
        prob = jnp.exp(scores - log_ref[head : head + 1, :])
        grad_prob = dot(kv_ref[:, value_lanes], grad_ref[:, lanes], 1, 1)
        delta = jnp.sum(prob * grad_prob, axis=0, keepdims=True)
        grad_score = (prob * (grad_prob - delta)).astype(BF)
        grad_query = dot(kv_ref[:, lanes], grad_score, 0, 0) * scale
        dq_ref[head * HEAD_DIM : (head + 1) * HEAD_DIM, :] = grad_query.astype(BF)
        key_parts.append(dot(grad_score, q_ref[:, lanes]) * scale)
        value_parts.append(dot(prob.astype(BF), grad_ref[:, lanes]))
    dkv_ref[...] += jnp.concatenate(key_parts + value_parts, axis=1)


def query_block(count, keys):
    return min(count, 256) if keys <= 1024 else 128


def attend(queries, keyvals, query_clip, key_clip):
    count, width = queries.shape
    keys = keyvals.shape[0]
    heads = width // HEAD_DIM
    block = query_block(count, keys)
    return pl.pallas_call(
        functools.partial(attend_kernel, heads, HEAD_DIM ** (-0.5)),
        grid=(count // block,),
        in_specs=[
            pl.BlockSpec((block, width), lambda i: (i, 0)),
            pl.BlockSpec((keys, 2 * width), lambda i: (0, 0)),
            pl.BlockSpec((1, block), lambda i: (0, i)),
            pl.BlockSpec((keys, 1), lambda i: (0, 0)),
        ],
        out_specs=[
            pl.BlockSpec((width, block), lambda i: (0, i)),
            pl.BlockSpec((8, block), lambda i: (0, i)),
        ],
        out_shape=[
            jax.ShapeDtypeStruct((width, count), BF),
            jax.ShapeDtypeStruct((8, count), F32),
        ],
        compiler_params=pltpu.CompilerParams(vmem_limit_bytes=VMEM_LIMIT),
        name="attend",
    )(queries, keyvals, query_clip, key_clip)


def attend_back(queries, keyvals, grads, logs, query_clip, key_clip):
    count, width = queries.shape
    keys = keyvals.shape[0]
    heads = width // HEAD_DIM
    block = query_block(count, keys)
    return pl.pallas_call(
        functools.partial(attend_back_kernel, heads, HEAD_DIM ** (-0.5)),
        grid=(count // block,),
        in_specs=[
            pl.BlockSpec((block, width), lambda i: (i, 0)),
            pl.BlockSpec((keys, 2 * width), lambda i: (0, 0)),
            pl.BlockSpec((block, width), lambda i: (i, 0)),
            pl.BlockSpec((8, block), lambda i: (0, i)),
            pl.BlockSpec((1, block), lambda i: (0, i)),
            pl.BlockSpec((keys, 1), lambda i: (0, 0)),
        ],
        out_specs=[
            pl.BlockSpec((width, block), lambda i: (0, i)),
            pl.BlockSpec((keys, 2 * width), lambda i: (0, 0)),
        ],
        out_shape=[
            jax.ShapeDtypeStruct((width, count), BF),
            jax.ShapeDtypeStruct((keys, 2 * width), F32),
        ],
        compiler_params=pltpu.CompilerParams(vmem_limit_bytes=VMEM_LIMIT),
        name="attend_back",
    )(queries, keyvals, grads, logs, query_clip, key_clip)


def place_kernel(size, place_ref, *refs):
    pieces, out_ref = refs[:-1], refs[-1]
    index = 0
    for piece in pieces:
        for start in range(0, piece.shape[0], size):
            place = pl.multiple_of(place_ref[index] * size, size)
            out_ref[pl.ds(place, size), :] = piece[start : start + size, :]
            index += 1


def place_rows(pieces, places, size):
    columns = pieces[0].shape[1]
    return pl.pallas_call(
        functools.partial(place_kernel, size),
        in_specs=[pl.BlockSpec(memory_space=pltpu.SMEM)]
        + [pl.BlockSpec(memory_space=pltpu.VMEM)] * len(pieces),
        out_specs=pl.BlockSpec(memory_space=pltpu.VMEM),
        out_shape=jax.ShapeDtypeStruct((len(places) * size, columns), pieces[0].dtype),
        name="place_rows",
    )(jnp.stack(places), *pieces)


def ordered(refs, rank, lanes):
    blocks = [ref[:, lanes].astype(F32) for ref in refs]
    result = []
    for index in range(len(refs)):
        found = blocks[0]
        for bits in range(1, len(refs)):
            found = jnp.where(rank == index ^ bits, blocks[bits], found)
        result.append(found)
    return result


def finish_mlp_kernel(ranks, hidden_quarter, width, unit, rank_ref, *refs):
    parts = refs[:ranks]
    up_ref, down_ref, conv_ref = refs[ranks:]
    rank = rank_ref[0]
    ups = ordered(parts, rank, slice(0, hidden_quarter))
    pieces = []
    for group in range(hidden_quarter // unit):
        for block in ups:
            pieces.append(block[:, group * unit : (group + 1) * unit])
    up_ref[...] = jnp.concatenate(pieces, axis=1)
    size = parts[0].shape[0]
    downs = ordered(parts, rank, slice(hidden_quarter, hidden_quarter + width))
    for index in range(ranks):
        down_ref[index * size : (index + 1) * size, :] = downs[index]
    convs = ordered(parts, rank, slice(hidden_quarter + width, parts[0].shape[1]))
    total = convs[0]
    for block in convs[1:]:
        total = total + block
    conv_ref[...] = total[:, : conv_ref.shape[1]]


def finish_qkv_kernel(ranks, quarter, rank_ref, *refs):
    parts = refs[:ranks]
    qkv_ref, out_ref = refs[ranks:]
    rank = rank_ref[0]
    blocks = ordered(parts, rank, slice(0, 4 * quarter))
    pieces = []
    for part in range(3):
        for block in blocks:
            pieces.append(block[:, part * quarter : (part + 1) * quarter])
    qkv_ref[...] = jnp.concatenate(pieces, axis=1)
    out_ref[...] = jnp.concatenate([block[:, 3 * quarter :] for block in blocks], axis=1)


def finish(kernel, rank, parts, shapes, name):
    return pl.pallas_call(
        kernel,
        in_specs=[pl.BlockSpec(memory_space=pltpu.SMEM)]
        + [pl.BlockSpec(memory_space=pltpu.VMEM)] * len(parts),
        out_specs=[pl.BlockSpec(memory_space=pltpu.VMEM)] * len(shapes),
        out_shape=[jax.ShapeDtypeStruct(shape, F32) for shape in shapes],
        compiler_params=pltpu.CompilerParams(vmem_limit_bytes=VMEM_LIMIT),
        name=name,
    )(rank.reshape(1), *parts)


def shards_general(
    ranks,
    frame_size,
    inputs,
    clip_id,
    ln_gains,
    ln_biases,
    w_qkv,
    w_out,
    w_up,
    w_down,
    up_bias,
    down_bias,
    conv_first,
    conv_first_bias,
    conv_mid,
    conv_mid_bias,
    cotangent,
):
    lows = frame_size // ranks
    frames_dev = inputs.shape[1]
    patches = inputs.shape[2]
    width = inputs.shape[3]
    rows = frames_dev * patches
    hidden = up_bias.shape[0]
    quarter = width // ranks
    hidden_quarter = hidden // ranks
    row_shard = width // frame_size
    rank = lax.axis_index("seq")
    place = lax.axis_index("frame")
    high = place // lows
    low = place % lows

    def permute(array, target):
        pairs = []
        for seq in range(ranks):
            for hi in range(ranks):
                for lo in range(lows):
                    to_seq, to_hi, to_lo = target(seq, hi, lo)
                    pairs.append(
                        (
                            seq * frame_size + hi * lows + lo,
                            to_seq * frame_size + to_hi * lows + to_lo,
                        )
                    )
        return lax.ppermute(array, AXES, pairs)

    def across(array, bits):
        return permute(array, lambda seq, hi, lo: (seq ^ bits, hi, lo))

    def along_high(array, step):
        return permute(array, lambda seq, hi, lo: (seq, (hi + step) % ranks, lo))

    def along_low(array, step):
        return permute(array, lambda seq, hi, lo: (seq, hi, (lo + step) % lows))

    def to_planes(array):
        return permute(array, lambda seq, hi, lo: (RANK_OF[hi], PLANE_OF[seq], lo))

    def from_planes(array):
        return permute(
            array, lambda seq, hi, lo: (PLANE_OF.index(hi), RANK_OF.index(seq), lo)
        )

    def flip_high(array, bits):
        return permute(array, lambda seq, hi, lo: (seq, hi ^ bits, lo))

    def gather_tokens(block):
        far = across(block, 2)
        near = across(block, 1)
        both = across(far, 1)
        return jnp.concatenate([block, near, far, both], axis=0)

    def scatter_tokens(partial):
        blocks = partial.astype(BF).reshape(ranks, rows, partial.shape[1])
        arrived_far = across(blocks[3], 1)
        arrived_near = across(blocks[1], 1)
        far = partial[2 * rows : 3 * rows] + arrived_far.astype(F32)
        arrived = across(far.astype(BF), 2)
        return partial[:rows] + arrived_near.astype(F32) + arrived.astype(F32)

    half_rows = rows // 2

    def gather_plane(block):
        if lows != 2:
            own = gather_tokens(block)
            return jnp.concatenate(
                [own] + [along_low(own, step) for step in range(1, lows)], axis=0
            )
        far = across(block, 2)
        side = along_low(block, 1)
        near = across(block, 1)
        corner = jnp.concatenate(
            [along_low(far[:half_rows], 1), across(side[half_rows:], 2)], axis=0
        )
        return jnp.concatenate(
            [
                block,
                near,
                far,
                across(far, 1),
                side,
                across(side, 1),
                corner,
                across(corner, 1),
            ],
            axis=0,
        )

    def scatter_plane(partial):
        if lows != 2:
            count = ranks * rows
            own = partial[:count]
            for step in range(1, lows):
                piece = partial[step * count : (step + 1) * count].astype(BF)
                own = own + along_low(piece, -step).astype(F32)
            return scatter_tokens(own)
        blocks = [partial[index * rows : (index + 1) * rows] for index in range(2 * ranks)]
        sums = {}
        for index in (6, 4, 2, 0):
            sums[index] = blocks[index] + across(blocks[index + 1].astype(BF), 1).astype(F32)
        corner = sums[6].astype(BF)
        by_far = across(corner[:half_rows], 2).astype(F32)
        by_side = along_low(corner[half_rows:], 1).astype(F32)
        side = jnp.concatenate([sums[4][:half_rows] + by_far, sums[4][half_rows:]], axis=0)
        far = jnp.concatenate([sums[2][:half_rows], sums[2][half_rows:] + by_side], axis=0)
        return (
            sums[0]
            + across(far.astype(BF), 2).astype(F32)
            + along_low(side.astype(BF), 1).astype(F32)
        )

    places = [(high ^ bits) * lows + low for bits in (0, 2, 1, 3)] + [
        (high ^ bits) * lows + (low + 1) % lows for bits in (0, 2, 1, 3)
    ]

    def after(array, *others):
        return lax.optimization_barrier((array,) + others)[0]

    staged = lows == 2

    def gather_two(block):
        return jnp.concatenate([block, flip_high(block, 2)], axis=0) if staged else block

    def gather_four(two):
        return jnp.concatenate([two, flip_high(two, 1)], axis=0) if staged else two

    def gather_all(four):
        if not staged:
            return lax.all_gather(four, "frame", axis=0, tiled=True)
        return place_rows([four, along_low(four, 1)], places, four.shape[0] // ranks)

    def scatter_half(partials):
        if not staged:
            return jnp.concatenate([partial.astype(BF) for partial in partials], axis=1)
        columns = [partial.shape[1] for partial in partials]
        cuts = [sum(columns[:index]) for index in range(len(columns) + 1)]
        count = partials[0].shape[0] // frame_size
        splits = [
            partial.reshape(ranks, lows, count, partial.shape[1]) for partial in partials
        ]
        sent = jnp.concatenate(
            [lax.dynamic_index_in_dim(split.astype(BF), 1 - low, 1, False) for split in splits],
            axis=2,
        )
        arrived = along_low(sent, 1)
        return jnp.concatenate(
            [
                lax.dynamic_index_in_dim(split, low, 1, False)
                + arrived[:, :, cuts[index] : cuts[index + 1]].astype(F32)
                for index, split in enumerate(splits)
            ],
            axis=2,
        ).reshape(2, 2, count, cuts[-1])

    def scatter_rest(half):
        if not staged:
            return lax.psum_scatter(half, "frame", scatter_dimension=0, tiled=True)
        sent = lax.dynamic_index_in_dim(half, 1 - high % 2, 1, False).astype(BF)
        kept = lax.dynamic_index_in_dim(half, high % 2, 1, False)
        two = kept + flip_high(sent, 1).astype(F32)
        sent = lax.dynamic_index_in_dim(two, 1 - high // 2, 0, False).astype(BF)
        kept = lax.dynamic_index_in_dim(two, high // 2, 0, False)
        return (kept + flip_high(sent, 2).astype(F32)).astype(BF)

    def swap_ranks(blocks):
        split = blocks.reshape((2, 2) + blocks.shape[1:])
        kept = lax.dynamic_index_in_dim(split, rank // 2, 0, False)
        found = across(lax.dynamic_index_in_dim(split, 1 - rank // 2, 0, False), 2)
        own = lax.dynamic_index_in_dim(kept, rank % 2, 0, False)
        far = lax.dynamic_index_in_dim(found, rank % 2, 0, False)
        near = across(lax.dynamic_index_in_dim(kept, 1 - rank % 2, 0, False), 1)
        both = across(lax.dynamic_index_in_dim(found, 1 - rank % 2, 0, False), 1)
        return in_rank_order([own, near, far, both])

    def sum_everywhere(array):
        bits = 1
        while bits < ranks:
            array = array + across(array, bits)
            bits *= 2
        bits = 1
        while bits < frame_size:
            pairs = [
                (seq * frame_size + item, seq * frame_size + (item ^ bits))
                for seq in range(ranks)
                for item in range(frame_size)
            ]
            array = array + lax.ppermute(array, AXES, pairs)
            bits *= 2
        return array

    def in_rank_order(items):
        stacked = jnp.stack(items)
        return [
            lax.dynamic_index_in_dim(stacked, rank ^ index, 0, False) for index in range(ranks)
        ]

    def gather_ranks(block):
        far = across(block, 2)
        near = across(block, 1)
        both = across(far, 1)
        return [block, near, far, both]

    token_rows = inputs[0].reshape(rows, width)
    grad_rows = cotangent[0].reshape(frames_dev * CH, width)
    frame_count = clip_id.shape[1]
    clip_rows = jnp.pad(
        clip_id.astype(BF), ((0, 15), (0, width - frame_count))
    )
    moved = to_planes(jnp.concatenate([token_rows, grad_rows, clip_rows], axis=0))
    tokens = moved[:rows].astype(F32)
    grad_learned = moved[rows : rows + frames_dev * CH].astype(F32)
    clips = moved[rows + frames_dev * CH, :frame_count].astype(jnp.int32)

    own_qkv = jnp.concatenate(
        [
            lax.dynamic_slice_in_dim(w_qkv, part * width + rank * quarter, quarter, 1)
            for part in range(3)
        ],
        axis=1,
    )
    two_qkv = gather_two(own_qkv)
    unit = hidden // (frame_size * ranks)
    columns = jnp.arange(hidden_quarter, dtype=jnp.int32)
    wanted = (columns // unit) * (unit * ranks) + rank * unit + columns % unit
    choose = (jnp.arange(hidden, dtype=jnp.int32)[:, None] == wanted[None, :]).astype(BF)
    own_up = dot(w_up, choose).astype(BF)
    own_down = lax.dynamic_slice_in_dim(w_down, rank * unit, unit, 0)
    own_out = lax.dynamic_slice_in_dim(w_out, rank * quarter, quarter, 1)
    own_out = jnp.concatenate([own_out, conv_first], axis=1)
    two_out = gather_two(after(own_out, two_qkv))
    four_qkv = gather_four(two_qkv)
    two_up = gather_two(after(own_up, two_out))
    four_out = gather_four(after(two_out, four_qkv))
    qkv_quarter = gather_all(four_qkv)
    two_down = gather_two(after(own_down, two_up))
    four_up = gather_four(after(two_up, four_out))
    qkv_quarter = after(qkv_quarter, four_out, two_up)
    packed = gather_all(after(four_out, qkv_quarter))
    out_columns = packed[:, :quarter]
    full_conv = packed[:, quarter:]
    out_quarter = jnp.concatenate(
        swap_ranks(out_columns.reshape(ranks, quarter, quarter)), axis=1
    )
    up_bias_quarter = lax.dynamic_index_in_dim(
        up_bias.reshape(frame_size, ranks, unit), rank, 1, False
    ).reshape(1, hidden_quarter)

    frame_ids = jnp.arange(frame_count, dtype=jnp.int32)

    def clip_tokens(lo):
        blocks = []
        inverse = jnp.array([RANK_OF.index(item) for item in range(ranks)], jnp.int32)
        for bits in range(ranks):
            hi = lax.dynamic_index_in_dim(inverse, rank ^ bits, 0, False)
            for frame in range(frames_dev):
                blocks.append((hi * lows + lo) * frames_dev + frame)
        wanted_frames = jnp.stack(blocks)
        found = jnp.sum(
            jnp.where(wanted_frames[:, None] == frame_ids[None, :], clips[None, :], 0), axis=1
        )
        return jnp.broadcast_to(found[:, None], (found.shape[0], patches)).reshape(-1)

    query_clip = clip_tokens(low)
    key_clip = jnp.concatenate(
        [query_clip] + [clip_tokens((low - step) % lows) for step in range(1, lows)]
    )
    query_clip = query_clip[None, :]
    key_clip = key_clip[:, None]

    normed_one, inverse_one = norm_stats(tokens)
    own_count = ranks * rows
    all_one = gather_plane((normed_one * ln_gains[0] + ln_biases[0]).astype(BF))
    queries = dot(all_one[:own_count], qkv_quarter[:, :quarter]).astype(BF)
    keyvals = dot(all_one, qkv_quarter[:, quarter:]).astype(BF)
    queries = after(queries, packed, four_up, two_down)
    up_quarter = gather_all(after(four_up, packed))
    four_down = gather_four(two_down)
    attended, logs = attend(queries, keyvals, query_clip, key_clip)
    after_attention = tokens + scatter_tokens(dot(attended, out_quarter, 0, 0))
    after_attention = after(after_attention, four_down)
    down_quarter = gather_all(after(four_down, up_quarter))
    normed_two, inverse_two = norm_stats(after_attention)
    all_two = gather_tokens((normed_two * ln_gains[1] + ln_biases[1]).astype(BF))
    pre_act = dot(all_two, up_quarter) + up_bias_quarter
    act_low = gelu(pre_act).astype(BF)
    block_out = after_attention + scatter_tokens(dot(act_low, down_quarter)) + down_bias

    normed_three, inverse_three = norm_stats(block_out)
    normed_three_low = (normed_three * ln_gains[2] + ln_biases[2]).astype(BF)
    tap_rows = dot(normed_three_low, full_conv).reshape(frames_dev, GRID, GRID, 9 * CH)
    first = conv_grid(tap_rows) + conv_first_bias
    features = block_out.reshape(frames_dev, patches, width)

    def tail(first_arg, features_arg, mid_arg, mid_bias_arg):
        maps = token_maps(first_arg, mid_arg, mid_bias_arg).reshape(frames_dev, patches, CH)
        return pool_tokens(maps, features_arg)

    learned, tail_back = jax.vjp(tail, first, features, conv_mid, conv_mid_bias)
    grad_first, grad_pool, grad_mid, grad_mid_bias = tail_back(
        grad_learned.reshape(frames_dev, CH, width)
    )
    grad_first_low = grad_first.astype(BF)
    grad_first_bias = jnp.sum(grad_first_low.astype(F32), axis=(0, 1, 2))
    spread_unused, spread_back = jax.vjp(conv_grid, tap_rows)
    spread = spread_back(grad_first_low.astype(F32))[0].reshape(rows, 9 * CH).astype(BF)
    grad_conv = dot(normed_three_low, spread, 0, 0)
    grad_normed_three = dot(spread, full_conv, 1, 1)
    grad_block, grad_gain_three, grad_shift_three = norm_back(
        normed_three, inverse_three, ln_gains[2], grad_normed_three
    )
    grad_block = grad_block + grad_pool.reshape(rows, width)
    grad_mlp = grad_block.astype(BF)
    grad_down_bias = jnp.sum(grad_mlp.astype(F32), axis=0)

    all_mlp = gather_tokens(grad_mlp)
    grad_act = dot(all_mlp, down_quarter, 1, 1)
    gelu_unused, gelu_back = jax.vjp(gelu, pre_act)
    grad_pre = gelu_back(grad_act)[0].astype(BF)
    grad_up_bias = jnp.sum(grad_pre.astype(F32), axis=0)
    grad_normed_two = scatter_tokens(dot(grad_pre, up_quarter, 1, 1))
    grad_down = dot(act_low, all_mlp, 0, 0)
    grad_up = dot(all_two, grad_pre, 0, 0)
    mlp_half = scatter_half([grad_up, grad_down, grad_conv])
    grad_after, grad_gain_two, grad_shift_two = norm_back(
        normed_two, inverse_two, ln_gains[1], grad_normed_two
    )
    grad_after = grad_after + grad_block

    all_branch = gather_tokens(grad_after.astype(BF))
    grad_attended = dot(all_branch, out_quarter, 1, 1).astype(BF)
    grad_out = dot(attended, all_branch)
    grad_attended = after(grad_attended, mlp_half)
    mlp_share = scatter_rest(mlp_half)
    grad_queries, grad_keyvals = attend_back(
        queries, keyvals, grad_attended, logs, query_clip, key_clip
    )
    grad_queries = grad_queries.T
    grad_keyvals = grad_keyvals.astype(BF)
    grad_normed_own = dot(grad_keyvals, qkv_quarter[:, quarter:], 1, 1)
    grad_normed_own = jnp.concatenate(
        [
            grad_normed_own[:own_count] + dot(grad_queries, qkv_quarter[:, :quarter], 1, 1),
            grad_normed_own[own_count:],
        ],
        axis=0,
    )
    grad_normed_one = scatter_plane(grad_normed_own)
    grad_q = dot(all_one[:own_count], grad_queries, 0, 0)
    grad_kv = dot(all_one, grad_keyvals, 0, 0)
    grad_out_columns = jnp.concatenate(
        swap_ranks(grad_out.astype(BF).reshape(quarter, ranks, quarter).transpose(1, 0, 2)),
        axis=0,
    )
    qkv_share = scatter_rest(
        after(scatter_half([grad_q, grad_kv, grad_out_columns]), mlp_share)
    )
    grad_tokens, grad_gain_one, grad_shift_one = norm_back(
        normed_one, inverse_one, ln_gains[0], grad_normed_one
    )
    moved_back = from_planes(
        jnp.concatenate(
            [
                (grad_after + grad_tokens).astype(BF),
                learned.astype(BF).reshape(frames_dev * CH, width),
            ],
            axis=0,
        )
    ).astype(F32)
    grad_input = moved_back[:rows]
    learned = moved_back[rows:]

    sum_up, sum_down, sum_conv = finish(
        functools.partial(finish_mlp_kernel, ranks, hidden_quarter, width, unit),
        rank,
        gather_ranks(mlp_share),
        [(row_shard, hidden), (ranks * unit, width), (row_shard, 9 * CH)],
        "finish_mlp",
    )
    sum_qkv, sum_out = finish(
        functools.partial(finish_qkv_kernel, ranks, quarter),
        rank,
        gather_ranks(qkv_share),
        [(row_shard, 3 * width), (row_shard, width)],
        "finish_qkv",
    )

    conv_terms = jnp.concatenate(
        [grad_first_bias.reshape(-1), grad_mid.reshape(-1), grad_mid_bias.reshape(-1)]
    )
    conv_rows = -(-conv_terms.shape[0] // width)
    conv_terms = jnp.pad(conv_terms, (0, conv_rows * width - conv_terms.shape[0]))
    up_terms = jnp.where(
        jnp.arange(ranks, dtype=jnp.int32)[:, None] == rank,
        grad_up_bias.reshape(1, hidden_quarter),
        0.0,
    )
    early = sum_everywhere(
        jnp.concatenate(
            [
                jnp.stack(
                    [
                        grad_gain_one,
                        grad_gain_two,
                        grad_gain_three,
                        grad_shift_one,
                        grad_shift_two,
                        grad_shift_three,
                        grad_down_bias,
                    ]
                ),
                conv_terms.reshape(conv_rows, width),
                up_terms.reshape(-1, width),
            ],
            axis=0,
        )
    )
    sum_gains = early[0:3]
    sum_shifts = early[3:6]
    conv_sums = early[7 : 7 + conv_rows].reshape(-1)
    sum_up_bias = (
        early[7 + conv_rows :]
        .reshape(ranks, frame_size, unit)
        .transpose(1, 0, 2)
        .reshape(hidden)
    )
    mid_count = grad_mid.size
    sum_mid = conv_sums[CH : CH + mid_count].reshape(grad_mid.shape)
    sum_mid_bias = conv_sums[CH + mid_count : CH + mid_count + grad_mid_bias.size]
    return (
        learned.reshape(1, frames_dev, CH, width),
        grad_input.reshape(1, frames_dev, patches, width),
        sum_qkv,
        sum_out,
        sum_up,
        sum_down,
        sum_conv,
        sum_gains,
        sum_shifts,
        sum_up_bias,
        early[6],
        conv_sums[:CH],
        sum_mid,
        sum_mid_bias.reshape(grad_mid_bias.shape),
    )


PAD = 128


def run(kernel, name, scalars, arrays, outs, scratch=(), limit=16):
    vmem = pl.BlockSpec(memory_space=pltpu.VMEM)
    return pl.pallas_call(
        kernel,
        in_specs=[pl.BlockSpec(memory_space=pltpu.SMEM)] + [vmem] * len(arrays),
        out_specs=[vmem] * len(outs),
        out_shape=[jax.ShapeDtypeStruct(shape, kind) for shape, kind in outs],
        scratch_shapes=list(scratch),
        compiler_params=pltpu.CompilerParams(vmem_limit_bytes=limit * 1024 * 1024),
        name=name,
    )(scalars, *arrays)


def rows_at(start, size):
    return pl.ds(pl.multiple_of(start * size, size), size)


def stack_rows(refs):
    return jnp.concatenate([ref[...] for ref in refs], axis=0)


def exact(left, right, left_dim=1, right_dim=0):
    return lax.dot_general(
        left,
        right,
        (((left_dim,), (right_dim,)), ((), ())),
        precision=HIGHEST,
        preferred_element_type=F32,
    )


def column_sum(values):
    return jnp.sum(values, axis=0, keepdims=True)


def back_of_norm(values, gain, grad):
    normed, inverse = norm_stats(values)
    scaled = grad * gain
    mean_scaled = jnp.mean(scaled, axis=-1, keepdims=True)
    mean_cross = jnp.mean(scaled * normed, axis=-1, keepdims=True)
    result = inverse * (scaled - mean_scaled - normed * mean_cross)
    return result, column_sum(grad * normed), column_sum(grad)


def pack_kernel(unused_ref, grads_ref, clip_ref, pack_ref):
    more, width = grads_ref.shape
    rest = pack_ref.shape[0] - more
    pack_ref[:more, :] = grads_ref[...]
    clips = clip_ref[...].astype(F32)
    clips = jnp.concatenate([clips, jnp.zeros((1, PAD - clips.shape[1]), F32)], axis=1)
    pack_ref[more:, :] = jnp.zeros((rest, width), BF)
    pack_ref[more:, :PAD] = jnp.broadcast_to(clips, (rest, PAD)).astype(BF)


def select_kernel(ids_ref, qkv_ref, out_ref, own_ref):
    width = out_ref.shape[1]
    quarter = width // 4
    for rank in range(4):

        @pl.when(ids_ref[0] == rank)
        def _(rank=rank):
            pieces = [
                qkv_ref[:, part * width + rank * quarter : part * width + (rank + 1) * quarter]
                for part in range(3)
            ]
            pieces.append(out_ref[:, rank * quarter : (rank + 1) * quarter])
            own_ref[...] = jnp.concatenate(pieces, axis=1)


def prepare_kernel(ids_ref, up_ref, down_ref, conv_ref, own_ref, more_ref):
    size = own_ref.shape[0]
    unit = down_ref.shape[0] // 4
    quarter = 8 * unit
    for rank in range(4):

        @pl.when(ids_ref[0] == rank)
        def _(rank=rank):
            own_ref[:, :quarter] = jnp.concatenate(
                [
                    up_ref[:, (4 * group + rank) * unit : (4 * group + rank + 1) * unit]
                    for group in range(8)
                ],
                axis=1,
            )
            more_ref[...] = down_ref[rank * unit : (rank + 1) * unit, :]

    taps = conv_ref.shape[1]
    own_ref[:, quarter:] = jnp.concatenate(
        [conv_ref[...], jnp.zeros((size, PAD - taps), BF)], axis=1
    )


def norm_one_kernel(ids_ref, *refs):
    moved_ref, extra_ref, gains_ref, shifts_ref, low_ref, qclip_ref, kclip_ref = refs
    count = low_ref.shape[0]
    frames = count // (GRID * GRID)
    patches = GRID * GRID
    normed, unused = norm_stats(moved_ref[:count, :].astype(F32))
    low_ref[...] = (normed * gains_ref[0:1, :] + shifts_ref[0:1, :]).astype(BF)
    start = frames * CH
    clips = extra_ref[start : start + 16, :PAD].astype(F32)[0:1]
    lane = lax.broadcasted_iota(jnp.int32, (1, PAD), 1)
    rank, low = ids_ref[0], ids_ref[2]
    for side in range(2):
        for bits in range(4):
            for frame in range(frames):
                hi = sum(jnp.where(rank ^ bits == RANK_OF[item], item, 0) for item in range(4))
                wanted = (2 * hi + (low ^ side)) * frames + frame
                clip = jnp.sum(jnp.where(lane == wanted, clips, 0.0), axis=1, keepdims=True)
                first = ((4 * side + bits) * frames + frame) * patches
                kclip_ref[first : first + patches, :] = jnp.broadcast_to(clip, (patches, 1))
                if side == 0:
                    qclip_ref[:, first : first + patches] = jnp.broadcast_to(clip, (1, patches))


def pass_sum_kernel(unused_ref, even_ref, arrived_ref, out_ref):
    out_ref[...] = (even_ref[...] + arrived_ref[...].astype(F32)).astype(BF)


def add_kernel(unused_ref, left_ref, right_ref, out_ref):
    out_ref[...] = left_ref[...] + right_ref[...]


def pick_kernel(ids_ref, far_ref, side_ref, out_ref):
    @pl.when(lax.rem(ids_ref[0], 2) == 0)
    def _():
        out_ref[...] = far_ref[...]

    @pl.when(lax.rem(ids_ref[0], 2) == 1)
    def _():
        out_ref[...] = side_ref[...]


def pass_on_kernel(ids_ref, *refs):
    far_even_ref, side_even_ref, second_ref, third_ref, corner_ref, far_ref, side_ref = refs
    core = lax.rem(ids_ref[0], 2)
    corner = corner_ref[...].astype(F32)
    far = far_even_ref[...] + second_ref[...].astype(F32)
    side = side_even_ref[...] + third_ref[...].astype(F32)
    far_ref[...] = (far + jnp.where(core == 1, corner, 0.0)).astype(BF)
    side_ref[...] = (side + jnp.where(core == 0, corner, 0.0)).astype(BF)


def place_of(ids_ref, bits):
    return (2 * ids_ref[1] + ids_ref[2]) ^ bits


def project_kernel(quarter, ids_ref, *refs):
    tokens, blocks = refs[:8], refs[8:16]
    q_ref, kv_ref, w_ref = refs[16:19]
    out_refs, all_ref = refs[19:23], refs[23]
    size = blocks[0].shape[0]
    for bits in range(8):
        where = rows_at(place_of(ids_ref, bits), size)
        w_ref[where, :] = blocks[bits][:, : 3 * quarter]
        all_ref[where, :] = blocks[bits][:, 3 * quarter :]
    rank = ids_ref[0]
    for bits in range(4):
        out_refs[bits][...] = all_ref[rows_at(rank ^ bits, quarter), :]
    own = dot(stack_rows(tokens[:4]), w_ref[...]).astype(BF)
    q_ref[...] = own[:, :quarter]
    half = own.shape[0]
    kv_ref[:half, :] = own[:, quarter:]
    kv_ref[half:, :] = dot(stack_rows(tokens[4:]), w_ref[:, quarter:]).astype(BF)


def scores_of(kv_ref, q_ref, queries, lanes, same, scale):
    raw = dot(kv_ref[:, lanes], q_ref[queries, lanes], 1, 1) * scale
    return jnp.where(same, raw, FLOOR_SCORE)


def attend_wide_kernel(heads, scale, unused_ref, *refs):
    q_ref, kv_ref, qclip_ref, kclip_ref, mixed_ref, log_ref = refs
    width = heads * HEAD_DIM
    count = q_ref.shape[0] // 2

    def one(part, carry):
        queries = pl.ds(pl.multiple_of(part * count, count), count)
        same = kclip_ref[...] == qclip_ref[:, queries]
        for head in range(heads):
            lanes = slice(head * HEAD_DIM, (head + 1) * HEAD_DIM)
            values = slice(width + head * HEAD_DIM, width + (head + 1) * HEAD_DIM)
            scores = scores_of(kv_ref, q_ref, queries, lanes, same, scale)
            top = jnp.max(scores, axis=0, keepdims=True)
            shifted = jnp.exp(scores - top)
            total = jnp.sum(shifted, axis=0, keepdims=True)
            prob = (shifted * (1.0 / total)).astype(BF)
            mixed_ref[lanes, queries] = dot(kv_ref[:, values], prob, 0, 0).astype(BF)
            log_ref[head : head + 1, queries] = top + jnp.log(total)
        return carry

    lax.fori_loop(0, 2, one, 0)


def split_blocks(values, even_refs, odd_refs):
    rows = even_refs[0].shape[0]
    for part in range(len(odd_refs)):
        even_refs[part][...] = values[2 * part * rows : (2 * part + 1) * rows]
        odd_refs[part][...] = values[(2 * part + 1) * rows : (2 * part + 2) * rows].astype(BF)


def out_kernel(rank_ref, *refs):
    mixed_ref = refs[0]
    even_refs, odd_refs, w_ref = refs[5:7], refs[7:9], refs[9]
    blocks = [ref[...] for ref in refs[1:5]]
    rank = rank_ref[0]
    width = blocks[0].shape[0]
    for index in range(4):
        found = blocks[0]
        for bits in range(1, 4):
            found = jnp.where(rank == index ^ bits, blocks[bits], found)
        w_ref[:, index * width : (index + 1) * width] = found
    split_blocks(dot(mixed_ref[...], w_ref[...], 0, 0), even_refs, odd_refs)


def norm_two_kernel(unused_ref, *refs):
    moved_ref, even_ref, arrived_ref, far_ref, gains_ref, shifts_ref = refs[:6]
    sum_ref, low_ref = refs[6:]
    count = low_ref.shape[0]
    values = (
        moved_ref[:count, :].astype(F32)
        + even_ref[...]
        + arrived_ref[...].astype(F32)
        + far_ref[...].astype(F32)
    )
    sum_ref[...] = values
    normed, unused = norm_stats(values)
    low_ref[...] = (normed * gains_ref[1:2, :] + shifts_ref[1:2, :]).astype(BF)


def gelu_both(values):
    size = jnp.abs(values) * 0.7071067811865476
    ratio = 1.0 / (1.0 + 0.3275911 * size)
    bell = jnp.exp(-size * size)
    series = ratio * (
        0.254829592
        + ratio
        * (-0.284496736 + ratio * (1.421413741 + ratio * (-1.453152027 + ratio * 1.061405429)))
    )
    tail = 0.5 * series * bell
    below = jnp.where(values >= 0.0, 1.0 - tail, tail)
    return values * below, below + values * bell * 0.3989422804014327


def join_kernel(unused_ref, *refs):
    for index, ref in enumerate(refs[4:]):
        size = ref.shape[0] // 2
        ref[:size, :] = refs[2 * index][...]
        ref[size:, :] = refs[2 * index + 1][...]


def mlp_part(tokens, up_ref, down_ref, bias, act_ref, slope_ref, even_ref, odd_ref):
    pre = dot(stack_rows(tokens), up_ref[...]) + bias
    act, slope = gelu_both(pre)
    act = act.astype(BF)
    act_ref[...] = act
    slope_ref[...] = slope
    partial = dot(act, down_ref[...])
    count = even_ref.shape[0]
    even_ref[...] = partial[:count]
    odd_ref[...] = partial[count:].astype(BF)


def mlp_kernel(ids_ref, *refs):
    tokens = refs[:2]
    a_refs, b_refs, bias_ref = refs[2:4], refs[4:6], refs[6]
    up_ref, down_ref, conv_ref, own_bias_ref = refs[7:11]
    rank = ids_ref[0]
    size = a_refs[0].shape[0] // 4
    quarter = up_ref.shape[1]
    for ref, order in zip(a_refs, ((0, 4, 2, 6), (1, 5, 3, 7))):
        for index, bits in enumerate(order):
            where = rows_at(place_of(ids_ref, bits), size)
            rows = slice(index * size, (index + 1) * size)
            up_ref[where, :] = ref[rows, :quarter]
            conv_ref[where, :] = ref[rows, quarter:]
    for ref, order in zip(b_refs, ((0, 1, 4, 5), (2, 3, 6, 7))):
        for index, bits in enumerate(order):
            where = rows_at(place_of(ids_ref, bits), size)
            down_ref[where, :] = ref[index * size : (index + 1) * size, :]
    unit = quarter // 8
    bias = None
    for index in range(4):
        found = jnp.concatenate(
            [
                bias_ref[:, (4 * group + index) * unit : (4 * group + index + 1) * unit]
                for group in range(8)
            ],
            axis=1,
        )
        bias = found if bias is None else jnp.where(rank == index, found, bias)
    own_bias_ref[...] = bias
    mlp_part(tokens, up_ref, down_ref, bias, *refs[11:])


def mlp_more_kernel(unused_ref, *refs):
    up_ref, down_ref, bias_ref = refs[2:5]
    mlp_part(refs[:2], up_ref, down_ref, bias_ref[...], *refs[5:])


def grid_masks(count):
    row = lax.broadcasted_iota(jnp.int32, (count, PAD), 0)
    i = (row // GRID) % GRID
    j = row % GRID
    masks = []
    for tap in range(9):
        di, dj = tap // 3 - 1, tap % 3 - 1
        inside = (i + di >= 0) & (i + di < GRID) & (j + dj >= 0) & (j + dj < GRID)
        masks.append(inside.astype(F32))
    return masks


def collect_taps(taps, masks, first_lanes):
    count = taps.shape[0]
    total = None
    for tap in range(9):
        offset = (tap // 3 - 1) * GRID + tap % 3 - 1
        moved = pltpu.roll(taps, (PAD - tap * CH) % PAD, 1) if tap else taps
        moved = pltpu.roll(moved, (-offset) % count, 0) if offset else moved
        moved = moved * masks[tap]
        total = moved if total is None else total + moved
    return total * first_lanes


def spread_taps(values, masks):
    count = values.shape[0]
    total = None
    for tap in range(9):
        offset = (tap // 3 - 1) * GRID + tap % 3 - 1
        moved = pltpu.roll(values, tap * CH, 1) if tap else values
        moved = pltpu.roll(moved, offset % count, 0) if offset else moved
        moved = moved * masks[8 - tap]
        total = moved if total is None else total + moved
    return total


def store_rows(ref, start, values):
    for index in range(values.shape[1] // PAD):
        ref[start + index : start + index + 1, :] = values[:, index * PAD : (index + 1) * PAD]


def load_rows(ref, start, count):
    return jnp.concatenate(
        [ref[start + index : start + index + 1, :] for index in range(count)], axis=1
    )


def tail_kernel(vectors, unused_ref, *refs):
    sum_ref, even_ref, arrived_ref, far_ref, bias_ref, gains_ref, shifts_ref = refs[:7]
    conv_ref, first_bias_ref, mid_ref, mid_bias_ref, moved_ref = refs[7:12]
    learned_ref, low_ref, grad_ref, normed_ref, spread_ref, small_ref = refs[12:]
    count = low_ref.shape[0]
    frames = count // (GRID * GRID)
    patches = GRID * GRID
    value = (
        sum_ref[...]
        + even_ref[...]
        + arrived_ref[...].astype(F32)
        + far_ref[...].astype(F32)
        + bias_ref[...]
    )
    normed, inverse = norm_stats(value)
    gain = gains_ref[2:3, :]
    normed_low = (normed * gain + shifts_ref[2:3, :]).astype(BF)
    normed_ref[...] = normed_low
    masks = grid_masks(count)
    lane = lax.broadcasted_iota(jnp.int32, (count, PAD), 1)
    first_lanes = (lane < CH).astype(F32)
    first = collect_taps(dot(normed_low, conv_ref[...]), masks, first_lanes)
    hidden, slope = gelu_both(first + first_bias_ref[...])
    hidden = hidden * first_lanes
    hiddens, slopes = [hidden], [slope]
    maps = None
    for layer in range(3):
        pre = collect_taps(exact(hiddens[layer], mid_ref[layer]), masks, first_lanes)
        pre = pre + mid_bias_ref[layer : layer + 1, :]
        if layer < 2:
            hidden, slope = gelu_both(pre)
            hiddens.append(hidden * first_lanes)
            slopes.append(slope)
        else:
            maps = jax.nn.sigmoid(pre) * first_lanes
    frame_of_row = lax.broadcasted_iota(jnp.int32, (count, PAD), 0) // patches
    wide = None
    for frame in range(frames):
        moved = pltpu.roll(maps, frame * CH, 1) if frame else maps
        moved = moved * (frame_of_row == frame).astype(F32)
        wide = moved if wide is None else wide + moved
    cotangent = jnp.concatenate(
        [
            moved_ref[: frames * CH, :].astype(F32),
            jnp.zeros((PAD - frames * CH, value.shape[1]), F32),
        ],
        axis=0,
    )
    learned_ref[...] = exact(wide, value, 0, 0)[: frames * CH] * (1.0 / patches)
    pooled = exact(wide, cotangent) * (1.0 / patches)
    products = exact(value, cotangent, 1, 1) * (1.0 / patches)
    grad = None
    for frame in range(frames):
        moved = pltpu.roll(products, PAD - frame * CH, 1) if frame else products
        moved = moved * (frame_of_row == frame).astype(F32)
        grad = moved if grad is None else grad + moved
    grad = grad * maps * (1.0 - maps)
    small_ref[...] = jnp.zeros_like(small_ref)
    conv_start = 7 * vectors + 4 * vectors
    for layer in range(2, -1, -1):
        taps = spread_taps(grad, masks)
        weight = exact(hiddens[layer], taps, 0, 0)[:CH]
        small_ref[conv_start + layer * CH : conv_start + (layer + 1) * CH, :] = weight
        bias_row = conv_start + 3 * CH + 1 + layer
        small_ref[bias_row : bias_row + 1, :] = column_sum(grad)
        grad = exact(taps, mid_ref[layer], 1, 1) * slopes[layer]
    grad_low = grad.astype(BF).astype(F32)
    small_ref[conv_start + 3 * CH : conv_start + 3 * CH + 1, :] = column_sum(grad_low)
    spread = spread_taps(grad_low, masks).astype(BF)
    spread_ref[...] = spread
    grad_normed = dot(spread, conv_ref[...], 1, 1)
    scaled = grad_normed * gain
    mean_scaled = jnp.mean(scaled, axis=-1, keepdims=True)
    mean_cross = jnp.mean(scaled * normed, axis=-1, keepdims=True)
    grad_value = inverse * (scaled - mean_scaled - normed * mean_cross)
    grad_value = grad_value + pooled
    grad_ref[...] = grad_value
    low = grad_value.astype(BF)
    low_ref[...] = low
    store_rows(small_ref, 2 * vectors, column_sum(grad_normed * normed))
    store_rows(small_ref, 5 * vectors, column_sum(grad_normed))
    store_rows(small_ref, 6 * vectors, column_sum(low.astype(F32)))


def mlp_back_kernel(unused_ref, *refs):
    grads = refs[:2]
    slope_ref, up_ref, down_ref = refs[2:5]
    pre_ref, even_ref, odd_ref, bias_ref = refs[5:]
    grad_act = dot(stack_rows(grads), down_ref[...], 1, 1)
    grad_pre = (grad_act * slope_ref[...]).astype(BF)
    pre_ref[...] = grad_pre
    bias_ref[...] = column_sum(grad_pre.astype(F32))
    partial = dot(grad_pre, up_ref[...], 1, 1)
    count = even_ref.shape[0]
    even_ref[...] = partial[:count]
    odd_ref[...] = partial[count:].astype(BF)


def divide_rows(ids_ref, all_ref, refs):
    kept_ref, sent_ref, more_kept_ref, more_sent_ref = refs
    high, low = ids_ref[1], ids_ref[2]
    size = all_ref.shape[0] // 8
    columns = kept_ref.shape[1]
    for index in range(4):
        rows = slice(index * size, (index + 1) * size)
        kept_ref[rows, :] = all_ref[rows_at(2 * index + low, size), :columns]
        sent_ref[rows, :] = all_ref[rows_at(2 * index + 1 - low, size), :columns].astype(BF)
        hi = high ^ (2 * (index % 2))
        lo = low ^ (index // 2)
        more_kept_ref[rows, :] = all_ref[rows_at(2 * hi + lo, size), columns:]
        more_sent_ref[rows, :] = all_ref[rows_at(2 * (hi ^ 1) + lo, size), columns:].astype(BF)


def fold(values, count):
    size = values.shape[0] // count
    return jnp.concatenate(
        [values[index * size : (index + 1) * size] for index in range(count)], axis=1
    )


def unfold(values, count):
    lanes = values.shape[1] // count
    return jnp.concatenate(
        [values[:, index * lanes : (index + 1) * lanes] for index in range(count)], axis=0
    )


def rounded(values):
    return values.astype(BF).astype(F32)


def mlp_grads_kernel(ids_ref, *refs):
    tokens, grads = refs[:4], refs[4:8]
    act, pre = stack_rows(refs[8:10]), stack_rows(refs[10:12])
    normed_ref, spread_ref = refs[12:14]
    all_ref = refs[18]
    quarter = act.shape[1]
    width = tokens[0].shape[1]
    all_ref[:, :quarter] = dot(stack_rows(tokens), pre, 0, 0)
    all_ref[:, quarter : quarter + width] = dot(act, stack_rows(grads), 0, 0)
    all_ref[:, quarter + width :] = dot(normed_ref[...], spread_ref[...], 0, 0)
    divide_rows(ids_ref, all_ref, refs[14:18])


def norm_two_back_kernel(unused_ref, *refs):
    sum_ref, grad_ref, even_ref, arrived_ref, far_ref, gains_ref = refs[:6]
    total_ref, low_ref, rows_ref = refs[6:]
    grad_normed = even_ref[...] + arrived_ref[...].astype(F32) + far_ref[...].astype(F32)
    result, gain_row, shift_row = back_of_norm(sum_ref[...], gains_ref[1:2, :], grad_normed)
    total = result + grad_ref[...]
    total_ref[...] = total
    low_ref[...] = total.astype(BF)
    rows_ref[0:1, :] = gain_row
    rows_ref[1:2, :] = shift_row


def attend_back_part(heads, scale, first, branches, refs, prior_ref, own_ref, total_ref):
    out_ref, q_ref, kv_ref, log_ref, qclip_ref, kclip_ref = refs
    width = heads * HEAD_DIM
    count = own_ref.shape[0]
    queries = slice(first, first + count)
    grad_mixed = dot(stack_rows(branches), out_ref[...], 1, 1).astype(BF)
    same = kclip_ref[...] == qclip_ref[:, queries]
    query_parts, key_parts, value_parts = [], [], []
    for head in range(heads):
        lanes = slice(head * HEAD_DIM, (head + 1) * HEAD_DIM)
        values = slice(width + head * HEAD_DIM, width + (head + 1) * HEAD_DIM)
        scores = scores_of(kv_ref, q_ref, queries, lanes, same, scale)
        prob = jnp.exp(scores - log_ref[head : head + 1, queries])
        grad_prob = dot(kv_ref[:, values], grad_mixed[:, lanes], 1, 1)
        delta = jnp.sum(prob * grad_prob, axis=0, keepdims=True)
        grad_score = (prob * (grad_prob - delta)).astype(BF)
        query_parts.append(dot(kv_ref[:, lanes], grad_score, 0, 0) * scale)
        key_parts.append(dot(grad_score, q_ref[queries, lanes]) * scale)
        value_parts.append(dot(prob.astype(BF), grad_mixed[:, lanes]))
    own_ref[...] = jnp.concatenate(query_parts, axis=0).T.astype(BF)
    terms = jnp.concatenate(key_parts + value_parts, axis=1)
    total_ref[...] = terms if prior_ref is None else prior_ref[...] + terms


def attend_back_first_kernel(heads, scale, unused_ref, *refs):
    attend_back_part(heads, scale, 0, refs[:2], refs[2:8], None, refs[8], refs[9])


def attend_back_next_kernel(heads, scale, first, unused_ref, *refs):
    attend_back_part(heads, scale, first, refs[:1], refs[1:7], refs[7], refs[8], refs[9])


def attend_back_last_kernel(heads, scale, first, unused_ref, *refs):
    prior_ref, first_ref, next_ref, w_ref = refs[7:11]
    own_ref, other_ref = refs[11:13]
    even_refs, odd_refs = refs[13:17], refs[17:21]
    part_ref, total_ref = refs[21:]
    attend_back_part(heads, scale, first, refs[:1], refs[1:7], prior_ref, part_ref, total_ref)
    width = heads * HEAD_DIM
    count = own_ref.shape[0]
    middle = first_ref.shape[0]
    own_ref[:middle, :width] = first_ref[...]
    own_ref[middle:first, :width] = next_ref[...]
    own_ref[first:, :width] = part_ref[...]
    own_ref[:, width:] = total_ref[:count, :].astype(BF)
    other_ref[...] = total_ref[count:, :].astype(BF)
    own = dot(own_ref[...], w_ref[...], 1, 1)
    other = dot(other_ref[...], w_ref[:, width:], 1, 1)
    split_blocks(jnp.concatenate([own, other], axis=0), even_refs, odd_refs)


def qkv_grads_kernel(ids_ref, *refs):
    tokens, branches, mixes = refs[:8], refs[8:12], refs[12:16]
    own_ref, other_ref = refs[16:18]
    all_ref = refs[22]
    quarter = mixes[0].shape[0]
    full = dot(stack_rows(tokens[:4]), own_ref[...], 0, 0)
    more = dot(stack_rows(tokens[4:]), other_ref[...], 0, 0)
    all_ref[:, :quarter] = full[:, :quarter]
    all_ref[:, quarter : 3 * quarter] = full[:, quarter:] + more
    rank = ids_ref[0]
    branch = stack_rows(branches)
    wanted = branch[:, :quarter]
    for index in range(1, 4):
        wanted = jnp.where(
            rank == index, branch[:, index * quarter : (index + 1) * quarter], wanted
        )
    count = branches[0].shape[0]
    for bits in range(4):
        turned = jnp.concatenate(
            [wanted[(item ^ bits) * count : ((item ^ bits) + 1) * count] for item in range(4)],
            axis=0,
        )
        all_ref[rows_at(rank ^ bits, quarter), 3 * quarter :] = dot(mixes[bits][...], turned)
    divide_rows(ids_ref, all_ref, refs[18:22])


def half_rows(ids_ref, refs, outs):
    kept_ref, arrived_ref, more_kept_ref, more_arrived_ref = refs
    own_ref, sent_ref, more_own_ref, more_sent_ref = outs
    size = own_ref.shape[0] // 2
    high = ids_ref[1]
    for step in range(2):
        rows = slice(step * size, (step + 1) * size)
        where = rows_at(high ^ (2 * step), size)
        own_ref[rows, :] = kept_ref[where, :] + arrived_ref[where, :].astype(F32)
        where = rows_at(high ^ (2 * step + 1), size)
        sent_ref[rows, :] = (kept_ref[where, :] + arrived_ref[where, :].astype(F32)).astype(BF)
    more = more_kept_ref[...] + more_arrived_ref[...].astype(F32)
    more_own_ref[...] = more[: 2 * size]
    more_sent_ref[: 2 * size, :] = more[2 * size :].astype(BF)


def half_kernel(ids_ref, *refs):
    half_rows(ids_ref, refs[:4], refs[4:])


def half_sums_kernel(ids_ref, *refs):
    half_rows(ids_ref, refs[:4], (refs[6], refs[7], refs[8], refs[9]))
    sums = refs[4][...].astype(F32) + refs[5][...].astype(F32)
    refs[9][refs[8].shape[0] :, :] = fold(sums, 3).astype(BF)
    refs[10][...] = rounded(sums)


def fourth_rows(refs, own_ref, sent_ref):
    size = own_ref.shape[0]
    start = 0
    for kept_ref, arrived_ref in (refs[:2], refs[2:4]):
        columns = slice(start, start + kept_ref.shape[1])
        own_ref[:, columns] = kept_ref[:size, :] + arrived_ref[:size, :].astype(F32)
        sent_ref[:size, columns] = (
            kept_ref[size:, :] + arrived_ref[size : 2 * size, :].astype(F32)
        ).astype(BF)
        start += kept_ref.shape[1]


def fourth_kernel(unused_ref, *refs):
    fourth_rows(refs[:4], *refs[4:])


def fourth_sums_kernel(unused_ref, *refs):
    arrived_ref, sums_ref = refs[3], refs[4]
    own_ref, sent_ref, out_ref = refs[5:]
    fourth_rows(refs[:4], own_ref, sent_ref)
    sums = sums_ref[...] + unfold(arrived_ref[refs[2].shape[0] :, :].astype(F32), 3)
    sent_ref[own_ref.shape[0] :, :] = fold(sums, 6).astype(BF)
    out_ref[...] = rounded(sums)


def total_kernel(unused_ref, kept_ref, arrived_ref, out_ref):
    out_ref[...] = (kept_ref[...] + arrived_ref[...].astype(F32)).astype(BF)


def total_sums_kernel(unused_ref, kept_ref, arrived_ref, sums_ref, out_ref):
    size, columns = kept_ref.shape
    out_ref[:, :columns] = (kept_ref[...] + arrived_ref[:size, :].astype(F32)).astype(BF)
    out_ref[:, columns:] = (
        sums_ref[...] + unfold(arrived_ref[size:, :].astype(F32), 6)
    ).astype(BF)


def norm_one_back_kernel(vectors, rank_ref, *refs):
    moved_ref, grad_ref, even_ref, arrived_ref, far_ref, side_ref, gains_ref = refs[:7]
    learned_ref, small_ref, two_ref, up_ref, more_up_ref = refs[7:12]
    back_ref, rounded_ref, sums_ref = refs[12:]
    count = grad_ref.shape[0]
    grad_normed = (
        even_ref[...]
        + arrived_ref[...].astype(F32)
        + far_ref[...].astype(F32)
        + side_ref[...].astype(F32)
    )
    result, gain_row, shift_row = back_of_norm(
        moved_ref[:count, :].astype(F32), gains_ref[0:1, :], grad_normed
    )
    back_ref[:count, :] = (result + grad_ref[...]).astype(BF)
    back_ref[count:, :] = learned_ref[...].astype(BF)
    sums_ref[...] = small_ref[...]
    store_rows(sums_ref, 0, gain_row)
    store_rows(sums_ref, vectors, two_ref[0:1, :])
    store_rows(sums_ref, 3 * vectors, shift_row)
    store_rows(sums_ref, 4 * vectors, two_ref[1:2, :])
    for index in range(4):
        store_rows(
            sums_ref,
            (7 + index) * vectors,
            jnp.where(rank_ref[0] == index, up_ref[...] + more_up_ref[...], 0.0),
        )
    rounded_ref[...] = sums_ref[...].astype(BF)


def back_kernel(unused_ref, moved_ref, grad_ref, learned_ref):
    count = grad_ref.shape[0]
    grad_ref[...] = moved_ref[:count, :].astype(F32)
    learned_ref[...] = moved_ref[count:, :].astype(F32)


def finish_sums_kernel(vectors, quarter, rank_ref, *refs):
    parts, sums_ref = refs[:4], refs[-1]
    finish_qkv_kernel(4, quarter, rank_ref, *parts, *refs[4:6])
    total = None
    for block in ordered(parts, rank_ref[0], slice(4 * quarter, parts[0].shape[1])):
        total = block if total is None else total + block
    sums_ref[...] = total
    refs = refs[6:-1]
    gains_ref, shifts_ref, up_ref, down_ref, first_ref, mid_ref, mid_bias_ref = refs
    for index in range(3):
        gains_ref[index : index + 1, :] = load_rows(sums_ref, index * vectors, vectors)
        shifts_ref[index : index + 1, :] = load_rows(sums_ref, (3 + index) * vectors, vectors)
    down_ref[...] = load_rows(sums_ref, 6 * vectors, vectors)
    quarters = [load_rows(sums_ref, (7 + index) * vectors, vectors) for index in range(4)]
    unit = quarters[0].shape[1] // 8
    up_ref[...] = jnp.concatenate(
        [
            quarters[index][:, group * unit : (group + 1) * unit]
            for group in range(8)
            for index in range(4)
        ],
        axis=1,
    )
    start = 11 * vectors
    for layer in range(3):
        mid_ref[layer] = sums_ref[start + layer * CH : start + (layer + 1) * CH, : 9 * CH]
    start = start + 3 * CH
    first_ref[...] = sums_ref[start : start + 1, :CH]
    mid_bias_ref[...] = sums_ref[start + 1 : start + 4, :CH]


def shards_square(
    ranks,
    frame_size,
    inputs,
    clip_id,
    ln_gains,
    ln_biases,
    w_qkv,
    w_out,
    w_up,
    w_down,
    up_bias,
    down_bias,
    conv_first,
    conv_first_bias,
    conv_mid,
    conv_mid_bias,
    cotangent,
):
    lows = 2
    frames_dev = inputs.shape[1]
    patches = inputs.shape[2]
    width = inputs.shape[3]
    rows = frames_dev * patches
    learned_rows = frames_dev * CH
    hidden = up_bias.shape[0]
    quarter = width // ranks
    heads = quarter // HEAD_DIM
    hidden_quarter = hidden // ranks
    unit = hidden_quarter // frame_size
    size = width // frame_size
    vectors = width // PAD
    own_count = ranks * rows
    place = lax.axis_index("frame")
    ids = jnp.stack([lax.axis_index("seq"), place // lows, place % lows])

    def permute(array, target):
        pairs = []
        for seq in range(ranks):
            for hi in range(ranks):
                for lo in range(lows):
                    to_seq, to_hi, to_lo = target(seq, hi, lo)
                    pairs.append(
                        (
                            seq * frame_size + hi * lows + lo,
                            to_seq * frame_size + to_hi * lows + to_lo,
                        )
                    )
        return lax.ppermute(array, AXES, pairs)

    def flip(array, seq_bits, hi_bits=0, lo_bits=0):
        return permute(
            array, lambda seq, hi, lo: (seq ^ seq_bits, hi ^ hi_bits, lo ^ lo_bits)
        )

    def after(array, *others):
        return lax.optimization_barrier((array,) + others)[0]

    last = []

    def ordered_run(kernel, name, scalars, arrays, outs, scratch=()):
        if last:
            arrays = [after(arrays[0], last[0])] + list(arrays[1:])
        results = list(run(kernel, name, scalars, arrays, outs, scratch))
        last[:] = [results[-1]]
        return results

    def to_planes(array):
        return permute(array, lambda seq, hi, lo: (RANK_OF[hi], PLANE_OF[seq], lo))

    def from_planes(array):
        return permute(
            array, lambda seq, hi, lo: (PLANE_OF.index(hi), RANK_OF.index(seq), lo)
        )

    def gather_four(block):
        far = flip(block, 2)
        near = flip(block, 1)
        return [block, near, far, flip(far, 1)]

    def pass_sum(even, arrived, name):
        (result,) = ordered_run(
            pass_sum_kernel,
            name,
            ids,
            [even, arrived],
            [((rows, width), BF)],
        )
        return result

    def scatter_four(evens, odds, name):
        far = flip(pass_sum(evens[1], flip(odds[1], 1), name), 2)
        return flip(odds[0], 1), far

    def row_parts(blocks, first, second):
        return [
            ((blocks * size, columns), kind) for columns in (first, second) for kind in (F32, BF)
        ]

    def scatter_half(parts, sums, name):
        kept, sent, more_kept, more_sent = parts
        shapes = row_parts(2, kept.shape[1], more_kept.shape[1])
        arrays = [kept, flip(sent, 0, 0, 1), more_kept, flip(more_sent, 0, 1)]
        if sums is None:
            return ordered_run(half_kernel, name, ids, arrays, shapes), None
        shapes[3] = ((2 * size + small_rows // 3, more_kept.shape[1]), BF)
        arrays += [sums, flip(sums, 0, 1)]
        *parts, sums = ordered_run(
            half_sums_kernel, name, ids, arrays, shapes + [(sums.shape, F32)]
        )
        return parts, sums

    def scatter_fourth(parts, sums, name):
        kept, sent, more_kept, more_sent = parts
        columns = kept.shape[1] + more_kept.shape[1]
        arrays = [kept, flip(sent, 0, 1), more_kept, flip(more_sent, 0, 0, 1)]
        if sums is None:
            shapes = [((size, columns), F32), ((size, columns), BF)]
            return ordered_run(fourth_kernel, name, ids, arrays, shapes), None
        shapes = [((size, columns), F32), ((size + small_rows // 6, columns), BF)]
        *parts, sums = ordered_run(
            fourth_sums_kernel, name, ids, arrays + [sums], shapes + [(sums.shape, F32)]
        )
        return parts, sums

    def scatter_last(parts, sums, name):
        kept, sent = parts
        arrays = [kept, flip(sent, 0, 2)]
        if sums is None:
            return ordered_run(total_kernel, name, ids, arrays, [(kept.shape, BF)])[0]
        shape = (size, kept.shape[1] + PAD)
        return ordered_run(total_sums_kernel, name, ids, arrays + [sums], [(shape, BF)])[0]

    (own_pack,) = ordered_run(
        select_kernel, "select", ids, [w_qkv, w_out], [((size, width), BF)]
    )

    moved = to_planes(inputs.reshape(rows, width))
    (pack,) = ordered_run(
        pack_kernel,
        "pack",
        ids,
        [cotangent.reshape(learned_rows, width), clip_id],
        [((learned_rows + 16, width), BF)],
    )
    extra = to_planes(pack)
    pack_two = flip(own_pack, 0, 2)
    pack_one = flip(own_pack, 0, 1)
    pack_side = flip(own_pack, 0, 0, 1)
    pack_three = flip(pack_two, 0, 1)
    packs = [own_pack, pack_side]
    for item in (pack_one, pack_two, pack_three):
        packs += [item, flip(item, 0, 0, 1)]

    mid_pad = jnp.pad(conv_mid, ((0, 0), (0, PAD - CH), (0, PAD - 9 * CH)))
    mid_bias_pad = jnp.pad(conv_mid_bias, ((0, 0), (0, PAD - CH)))
    first_bias_pad = jnp.pad(conv_first_bias, (0, PAD - CH)).reshape(1, PAD)
    up_bias_row = up_bias.reshape(1, hidden)
    down_bias_row = down_bias.reshape(1, width)

    own_a, own_b = ordered_run(
        prepare_kernel,
        "prepare",
        ids,
        [
            after(w_up, mid_pad, mid_bias_pad, first_bias_pad, up_bias_row, down_bias_row),
            w_down,
            conv_first,
        ],
        [((size, hidden_quarter + PAD), BF), ((size, width), BF)],
    )

    low_norm, query_clip, key_clip = ordered_run(
        norm_one_kernel,
        "norm_one",
        ids,
        [moved, extra, ln_gains, ln_biases],
        [((rows, width), BF), ((1, own_count), F32), ((2 * own_count, 1), F32)],
    )
    low_norm = after(low_norm, pack_side, pack_one, pack_two)

    def join(pairs, name):
        flat = [item for pair in pairs for item in pair]
        outs = [((2 * pair[0].shape[0], pair[0].shape[1]), BF) for pair in pairs]
        return ordered_run(join_kernel, name, ids, flat, outs)

    far = flip(low_norm, 2)
    side = flip(low_norm, 0, 0, 1)
    near = flip(low_norm, 1)
    far_a, side_b = flip(own_a, 0, 2), flip(own_b, 0, 0, 1)
    (picked,) = ordered_run(
        pick_kernel,
        "pick",
        ids,
        [after(far, far_a, side_b, *packs[1:]), side],
        [((rows, width), BF)],
    )
    two_a, two_b = join(
        [(own_a, far_a), (own_b, side_b)], "join_two"
    )
    corner = permute(
        picked,
        lambda seq, hi, lo: (seq, hi, lo ^ 1) if seq % 2 == 0 else (seq ^ 2, hi, lo),
    )
    far_near = flip(far, 1)
    side_near = flip(side, 1)
    corner = after(corner, near, far_near, side_near)
    all_one = [near, far, far_near, side, side_near, corner, flip(corner, 1)]
    all_one = [low_norm] + all_one
    queries, keyvals, qkv_quarter, own_out, near_out, far_out, both_out = ordered_run(
        functools.partial(project_kernel, quarter),
        "project",
        ids,
        all_one + packs,
        [
            ((own_count, quarter), BF),
            ((2 * own_count, 2 * quarter), BF),
            ((width, 3 * quarter), BF),
        ]
        + [((quarter, quarter), BF)] * 4,
        [pltpu.VMEM((width, quarter), BF)],
    )
    out_blocks = [own_out, flip(near_out, 1), flip(far_out, 2), flip(both_out, 3)]
    scale = HEAD_DIM ** (-0.5)
    attended, logs = ordered_run(
        functools.partial(attend_wide_kernel, heads, scale),
        "attend",
        ids,
        [queries, keyvals, query_clip, key_clip],
        [((quarter, own_count), BF), ((8, own_count), F32)],
    )
    blocks_of = [((rows, width), F32)] * 2 + [((rows, width), BF)] * 2
    *parts, out_quarter = ordered_run(
        out_kernel,
        "out",
        ids,
        [attended] + out_blocks,
        blocks_of + [((quarter, width), BF)],
    )
    evens, odds = parts[:2], parts[2:]
    arrived, far = scatter_four(evens, odds, "out_pass")
    four_a, four_b = join(
        [(two_a, flip(two_a, 0, 1)), (two_b, flip(two_b, 0, 2))], "join_four"
    )
    after_attention, low_two = ordered_run(
        norm_two_kernel,
        "norm_two",
        ids,
        [moved, evens[0], arrived, far, ln_gains, ln_biases],
        [((rows, width), F32), ((rows, width), BF)],
    )
    near_two, far_two = flip(low_two, 1), flip(low_two, 2)
    pair = [
        ((2 * rows, hidden_quarter), BF),
        ((2 * rows, hidden_quarter), F32),
        ((rows, width), F32),
        ((rows, width), BF),
    ]
    up_full, down_full, conv_full, own_bias, act, slope, even, odd = ordered_run(
        mlp_kernel,
        "mlp",
        ids,
        [low_two, near_two]
        + [four_a, flip(four_a, 0, 0, 1), four_b, flip(four_b, 0, 1), up_bias_row],
        [
            ((width, hidden_quarter), BF),
            ((hidden_quarter, width), BF),
            ((width, PAD), BF),
            ((1, hidden_quarter), F32),
        ]
        + pair,
    )
    far_two = after(far_two, even)
    all_two = [low_two, near_two, far_two, flip(far_two, 1)]
    acts, slopes, evens, odds = [act], [slope], [even], [odd]
    for item, rest in zip(
        (acts, slopes, evens, odds),
        ordered_run(
            mlp_more_kernel, "mlp_more", ids, all_two[2:] + [up_full, down_full, own_bias], pair
        ),
    ):
        item.append(rest)
    arrived, far = scatter_four(evens, odds, "mlp_pass")

    small_rows = -(-(11 * vectors + 3 * CH + 4) // 8) * 8
    learned, low_mlp, grad_block, low_three, spread, small = ordered_run(
        functools.partial(tail_kernel, vectors),
        "tail",
        ids,
        [
            after_attention,
            evens[0],
            arrived,
            far,
            down_bias_row,
            ln_gains,
            ln_biases,
            conv_full,
            first_bias_pad,
            mid_pad,
            mid_bias_pad,
            extra,
        ],
        [
            ((learned_rows, width), F32),
            ((rows, width), BF),
            ((rows, width), F32),
            ((rows, width), BF),
            ((rows, PAD), BF),
            ((small_rows, PAD), F32),
        ],
    )

    near_mlp, far_mlp = flip(low_mlp, 1), flip(low_mlp, 2)
    pair = [
        ((2 * rows, hidden_quarter), BF),
        ((rows, width), F32),
        ((rows, width), BF),
        ((1, hidden_quarter), F32),
    ]
    pre, even, odd, bias = ordered_run(
        mlp_back_kernel,
        "mlp_back",
        ids,
        [low_mlp, near_mlp, slopes[0], up_full, down_full],
        pair,
    )
    far_mlp = after(far_mlp, even)
    all_mlp = [low_mlp, near_mlp, far_mlp, flip(far_mlp, 1)]
    pres, evens, odds, biases = [pre], [even], [odd], [bias]
    for item, rest in zip(
        (pres, evens, odds, biases),
        ordered_run(
            mlp_back_kernel,
            "mlp_back_more",
            ids,
            all_mlp[2:] + [slopes[1], up_full, down_full],
            pair,
        ),
    ):
        item.append(rest)
    arrived, far = scatter_four(evens, odds, "mlp_back_pass")
    columns = hidden_quarter + width + PAD
    mlp_parts = ordered_run(
        mlp_grads_kernel,
        "mlp_grads",
        ids,
        all_two + all_mlp + acts + pres + [low_three, spread],
        row_parts(4, hidden_quarter, width + PAD),
        [pltpu.VMEM((width, columns), F32)],
    )
    grad_after, low_branch, rows_two = ordered_run(
        norm_two_back_kernel,
        "norm_two_back",
        ids,
        [after_attention, grad_block, evens[0], arrived, far, ln_gains],
        [((rows, width), F32), ((rows, width), BF), ((2, width), F32)],
    )

    near_branch, far_branch = flip(low_branch, 1), flip(low_branch, 2)
    mixes = gather_four(after(attended, far_branch))
    common = [out_quarter, queries, keyvals, logs, query_clip, key_clip]
    total = ((2 * own_count, 2 * quarter), F32)
    grads_first, sums_first = ordered_run(
        functools.partial(attend_back_first_kernel, heads, scale),
        "attend_back",
        ids,
        [low_branch, near_branch] + common,
        [((2 * rows, quarter), BF), total],
    )
    far_branch = after(far_branch, sums_first)
    all_branch = [low_branch, near_branch, far_branch, flip(far_branch, 1)]
    grads_next, sums_next = ordered_run(
        functools.partial(attend_back_next_kernel, heads, scale, 2 * rows),
        "attend_back_next",
        ids,
        [far_branch] + common + [sums_first],
        [((rows, quarter), BF), total],
    )
    grads_own, grads_other, *parts = ordered_run(
        functools.partial(attend_back_last_kernel, heads, scale, 3 * rows),
        "attend_back_last",
        ids,
        all_branch[3:] + common + [sums_next, grads_first, grads_next, qkv_quarter],
        [((own_count, 3 * quarter), BF), ((own_count, 2 * quarter), BF)]
        + [((rows, width), F32)] * 4
        + [((rows, width), BF)] * 4,
        [
            pltpu.VMEM((rows, quarter), BF),
            pltpu.VMEM((2 * own_count, 2 * quarter), F32),
        ],
    )
    evens = parts[:4]
    arrived = [flip(item, 1) for item in parts[4:]]
    corner = permute(
        pass_sum(evens[3], arrived[3], "corner_pass"),
        lambda seq, hi, lo: (seq ^ 2, hi, lo) if seq % 2 == 0 else (seq, hi, lo ^ 1),
    )
    mlp_parts, unused = scatter_half(mlp_parts, None, "mlp_half")
    qkv_parts = ordered_run(
        qkv_grads_kernel,
        "qkv_grads",
        ids,
        all_one + all_branch + mixes + [grads_own, grads_other],
        row_parts(4, width // 2, width // 2),
        [pltpu.VMEM((width, width), F32)],
    )
    far, side = ordered_run(
        pass_on_kernel,
        "pass_on",
        ids,
        [evens[1], evens[2], arrived[1], arrived[2], corner],
        [((rows, width), BF), ((rows, width), BF)],
    )
    qkv_parts[1], qkv_parts[3] = after(qkv_parts[1], far), after(qkv_parts[3], far)
    far, side = flip(far, 2), flip(side, 0, 0, 1)
    mlp_parts, unused = scatter_fourth(mlp_parts, None, "mlp_fourth")
    moved_back, sums = ordered_run(
        functools.partial(norm_one_back_kernel, vectors),
        "norm_one_back",
        ids,
        [moved, grad_after, evens[0], arrived[0], far, side, ln_gains]
        + [learned, small, rows_two]
        + biases,
        [((rows + learned_rows, width), BF), ((small_rows, PAD), BF)],
        [pltpu.VMEM((small_rows, PAD), F32)],
    )

    qkv_parts, sums = scatter_half(qkv_parts, sums, "qkv_half")
    mlp_share = scatter_last(mlp_parts, None, "mlp_total")
    qkv_parts, sums = scatter_fourth(qkv_parts, sums, "qkv_fourth")
    mlp_share = after(mlp_share, sums)
    mlp_far, mlp_near = flip(mlp_share, 2), flip(mlp_share, 1)
    qkv_share = scatter_last(qkv_parts, sums, "qkv_total")
    mlp_far = after(mlp_far, qkv_share)
    qkv_far, qkv_near = flip(qkv_share, 2), flip(qkv_share, 1)
    sum_up, sum_down, sum_conv = ordered_run(
        functools.partial(finish_mlp_kernel, ranks, hidden_quarter, width, unit),
        "finish_mlp",
        ids,
        [mlp_share, mlp_near, mlp_far, flip(mlp_far, 1)],
        [((size, hidden), F32), ((ranks * unit, width), F32), ((size, 9 * CH), F32)],
    )
    grad_input, learned = ordered_run(
        back_kernel,
        "back",
        ids,
        [from_planes(moved_back)],
        [((rows, width), F32), ((learned_rows, width), F32)],
    )
    (
        sum_qkv,
        sum_out,
        sum_gains,
        sum_shifts,
        sum_up_bias,
        sum_down_bias,
        sum_first,
        sum_mid,
        sum_mid_bias,
    ) = ordered_run(
        functools.partial(finish_sums_kernel, vectors, quarter),
        "finish_qkv",
        ids,
        [qkv_share, qkv_near, qkv_far, flip(after(qkv_far, sum_down), 1)],
        [
            ((size, 3 * width), F32),
            ((size, width), F32),
            ((3, width), F32),
            ((3, width), F32),
            ((1, hidden), F32),
            ((1, width), F32),
            ((1, CH), F32),
            ((3, CH, 9 * CH), F32),
            ((3, CH), F32),
        ],
        [pltpu.VMEM((small_rows, PAD), F32)],
    )
    return (
        learned.reshape(1, frames_dev, CH, width),
        grad_input.reshape(1, frames_dev, patches, width),
        sum_qkv,
        sum_out,
        sum_up,
        sum_down,
        sum_conv,
        sum_gains,
        sum_shifts,
        sum_up_bias.reshape(hidden),
        sum_down_bias.reshape(width),
        sum_first.reshape(CH),
        sum_mid,
        sum_mid_bias,
    )


def solution(mesh):
    placed = (
        P("seq", "frame", None, None),
        P("seq", None),
        P(),
        P(),
        P("frame", None),
        P("frame", None),
        P("frame", None),
        P("frame", None),
        P(),
        P(),
        P("frame", None),
        P(),
        P(),
        P(),
        P("seq", "frame", None, None),
    )
    ranks, frame_size = mesh.shape["seq"], mesh.shape["frame"]
    body = shards_square if ranks == 4 and frame_size == 8 else shards_general
    return jax.shard_map(
        functools.partial(body, ranks, frame_size),
        mesh=mesh,
        in_specs=placed,
        out_specs=(
            P("seq", "frame", None, None),
            P("seq", "frame", None, None),
            P("frame", None),
            P("frame", None),
            P("frame", None),
            P("frame", None),
            P("frame", None),
            P(),
            P(),
            P(),
            P(),
            P(),
            P(),
            P(),
        ),
        check_vma=False,
    )
```

```python
import functools

import jax
import jax.numpy as jnp
from jax import lax
from jax.experimental import pallas as pl
from jax.experimental.pallas import tpu as pltpu
from jax.sharding import PartitionSpec as P

HEADS = 12
HEAD_DIM = 64
CH = 8
GRID = 8

EPSILON = 1e-06
FLOOR_SCORE = -1e30
HIGHEST = lax.Precision.HIGHEST
AXES = ("seq", "frame")
PLANE_OF = (0, 2, 1, 3)
RANK_OF = (0, 2, 1, 3)
VMEM_LIMIT = 56 * 1024 * 1024
BF = jnp.bfloat16
F32 = jnp.float32


def norm_stats(values):
    centre = jnp.mean(values, axis=-1, keepdims=True)
    centred = values - centre
    variance = jnp.mean(centred * centred, axis=-1, keepdims=True)
    inverse = lax.rsqrt(variance + EPSILON)
    return centred * inverse, inverse


def norm_back(normed, inverse, gain, grad):
    scaled = grad * gain
    mean_scaled = jnp.mean(scaled, axis=-1, keepdims=True)
    mean_cross = jnp.mean(scaled * normed, axis=-1, keepdims=True)
    grad_values = inverse * (scaled - mean_scaled - normed * mean_cross)
    return grad_values, jnp.sum(grad * normed, axis=0), jnp.sum(grad, axis=0)


def gelu(values):
    return jax.nn.gelu(values, approximate=False)


def conv_grid(taps):
    side = taps.shape[1]
    width = taps.shape[-1] // 9
    padded = jnp.pad(taps, ((0, 0), (1, 1), (1, 1), (0, 0)))
    total = jnp.zeros(taps.shape[:-1] + (width,), taps.dtype)
    for tap in range(9):
        offset_row = tap // 3
        offset_column = tap % 3
        total = (
            total
            + padded[
                :,
                offset_row : offset_row + side,
                offset_column : offset_column + side,
                tap * width : (tap + 1) * width,
            ]
        )
    return total


def token_maps(first, conv_mid, conv_mid_bias):
    hidden = gelu(first)
    for layer in range(3):
        frames = hidden.shape[0]
        side = hidden.shape[1]
        flat = hidden.reshape(-1, hidden.shape[-1])
        taps = jnp.dot(flat, conv_mid[layer], precision=HIGHEST).reshape(frames, side, side, -1)
        hidden = conv_grid(taps) + conv_mid_bias[layer]
        if layer < 2:
            hidden = gelu(hidden)
    return jax.nn.sigmoid(hidden)


def pool_tokens(maps, features):
    return jnp.einsum("fpk,fpd->fkd", maps, features, precision=HIGHEST) / maps.shape[1]


def dot(left, right, left_dim=1, right_dim=0):
    return lax.dot_general(
        left, right, (((left_dim,), (right_dim,)), ((), ())), preferred_element_type=F32
    )


def attend_kernel(heads, scale, q_ref, kv_ref, qclip_ref, kclip_ref, mixed_ref, log_ref):
    width = heads * HEAD_DIM
    same = kclip_ref[...] == qclip_ref[...]
    for head in range(heads):
        lanes = slice(head * HEAD_DIM, (head + 1) * HEAD_DIM)
        value_lanes = slice(width + head * HEAD_DIM, width + (head + 1) * HEAD_DIM)
        scores = dot(kv_ref[:, lanes], q_ref[:, lanes], 1, 1) * scale
        scores = jnp.where(same, scores, FLOOR_SCORE)
        top = jnp.max(scores, axis=0, keepdims=True)
        shifted = jnp.exp(scores - top)
        total = jnp.sum(shifted, axis=0, keepdims=True)
        prob = (shifted * (1.0 / total)).astype(BF)
        mixed = dot(kv_ref[:, value_lanes], prob, 0, 0)
        mixed_ref[head * HEAD_DIM : (head + 1) * HEAD_DIM, :] = mixed.astype(BF)
        log_ref[head : head + 1, :] = top + jnp.log(total)


def attend_back_kernel(
    heads, scale, q_ref, kv_ref, grad_ref, log_ref, qclip_ref, kclip_ref, dq_ref, dkv_ref
):
    width = heads * HEAD_DIM
    same = kclip_ref[...] == qclip_ref[...]

    @pl.when(pl.program_id(0) == 0)
    def _():
        dkv_ref[...] = jnp.zeros_like(dkv_ref)

    key_parts = []
    value_parts = []
    for head in range(heads):
        lanes = slice(head * HEAD_DIM, (head + 1) * HEAD_DIM)
        value_lanes = slice(width + head * HEAD_DIM, width + (head + 1) * HEAD_DIM)
        scores = dot(kv_ref[:, lanes], q_ref[:, lanes], 1, 1) * scale
        scores = jnp.where(same, scores, FLOOR_SCORE)
        prob = jnp.exp(scores - log_ref[head : head + 1, :])
        grad_prob = dot(kv_ref[:, value_lanes], grad_ref[:, lanes], 1, 1)
        delta = jnp.sum(prob * grad_prob, axis=0, keepdims=True)
        grad_score = (prob * (grad_prob - delta)).astype(BF)
        grad_query = dot(kv_ref[:, lanes], grad_score, 0, 0) * scale
        dq_ref[head * HEAD_DIM : (head + 1) * HEAD_DIM, :] = grad_query.astype(BF)
        key_parts.append(dot(grad_score, q_ref[:, lanes]) * scale)
        value_parts.append(dot(prob.astype(BF), grad_ref[:, lanes]))
    dkv_ref[...] += jnp.concatenate(key_parts + value_parts, axis=1)


def query_block(count, keys):
    return min(count, 256) if keys <= 1024 else 128


def attend(queries, keyvals, query_clip, key_clip):
    count, width = queries.shape
    keys = keyvals.shape[0]
    heads = width // HEAD_DIM
    block = query_block(count, keys)
    return pl.pallas_call(
        functools.partial(attend_kernel, heads, HEAD_DIM ** (-0.5)),
        grid=(count // block,),
        in_specs=[
            pl.BlockSpec((block, width), lambda i: (i, 0)),
            pl.BlockSpec((keys, 2 * width), lambda i: (0, 0)),
            pl.BlockSpec((1, block), lambda i: (0, i)),
            pl.BlockSpec((keys, 1), lambda i: (0, 0)),
        ],
        out_specs=[
            pl.BlockSpec((width, block), lambda i: (0, i)),
            pl.BlockSpec((8, block), lambda i: (0, i)),
        ],
        out_shape=[
            jax.ShapeDtypeStruct((width, count), BF),
            jax.ShapeDtypeStruct((8, count), F32),
        ],
        compiler_params=pltpu.CompilerParams(vmem_limit_bytes=VMEM_LIMIT),
        name="attend",
    )(queries, keyvals, query_clip, key_clip)


def attend_back(queries, keyvals, grads, logs, query_clip, key_clip):
    count, width = queries.shape
    keys = keyvals.shape[0]
    heads = width // HEAD_DIM
    block = query_block(count, keys)
    return pl.pallas_call(
        functools.partial(attend_back_kernel, heads, HEAD_DIM ** (-0.5)),
        grid=(count // block,),
        in_specs=[
            pl.BlockSpec((block, width), lambda i: (i, 0)),
            pl.BlockSpec((keys, 2 * width), lambda i: (0, 0)),
            pl.BlockSpec((block, width), lambda i: (i, 0)),
            pl.BlockSpec((8, block), lambda i: (0, i)),
            pl.BlockSpec((1, block), lambda i: (0, i)),
            pl.BlockSpec((keys, 1), lambda i: (0, 0)),
        ],
        out_specs=[
            pl.BlockSpec((width, block), lambda i: (0, i)),
            pl.BlockSpec((keys, 2 * width), lambda i: (0, 0)),
        ],
        out_shape=[
            jax.ShapeDtypeStruct((width, count), BF),
            jax.ShapeDtypeStruct((keys, 2 * width), F32),
        ],
        compiler_params=pltpu.CompilerParams(vmem_limit_bytes=VMEM_LIMIT),
        name="attend_back",
    )(queries, keyvals, grads, logs, query_clip, key_clip)


def place_kernel(size, place_ref, *refs):
    pieces, out_ref = refs[:-1], refs[-1]
    index = 0
    for piece in pieces:
        for start in range(0, piece.shape[0], size):
            place = pl.multiple_of(place_ref[index] * size, size)
            out_ref[pl.ds(place, size), :] = piece[start : start + size, :]
            index += 1


def place_rows(pieces, places, size):
    columns = pieces[0].shape[1]
    return pl.pallas_call(
        functools.partial(place_kernel, size),
        in_specs=[pl.BlockSpec(memory_space=pltpu.SMEM)]
        + [pl.BlockSpec(memory_space=pltpu.VMEM)] * len(pieces),
        out_specs=pl.BlockSpec(memory_space=pltpu.VMEM),
        out_shape=jax.ShapeDtypeStruct((len(places) * size, columns), pieces[0].dtype),
        name="place_rows",
    )(jnp.stack(places), *pieces)


def ordered(refs, rank, lanes):
    blocks = [ref[:, lanes].astype(F32) for ref in refs]
    result = []
    for index in range(len(refs)):
        found = blocks[0]
        for bits in range(1, len(refs)):
            found = jnp.where(rank == index ^ bits, blocks[bits], found)
        result.append(found)
    return result


def finish_mlp_kernel(ranks, hidden_quarter, width, unit, rank_ref, *refs):
    parts = refs[:ranks]
    up_ref, down_ref, conv_ref = refs[ranks:]
    rank = rank_ref[0]
    ups = ordered(parts, rank, slice(0, hidden_quarter))
    pieces = []
    for group in range(hidden_quarter // unit):
        for block in ups:
            pieces.append(block[:, group * unit : (group + 1) * unit])
    up_ref[...] = jnp.concatenate(pieces, axis=1)
    size = parts[0].shape[0]
    downs = ordered(parts, rank, slice(hidden_quarter, hidden_quarter + width))
    for index in range(ranks):
        down_ref[index * size : (index + 1) * size, :] = downs[index]
    convs = ordered(parts, rank, slice(hidden_quarter + width, parts[0].shape[1]))
    total = convs[0]
    for block in convs[1:]:
        total = total + block
    conv_ref[...] = total[:, : conv_ref.shape[1]]


def finish_qkv_kernel(ranks, quarter, rank_ref, *refs):
    parts = refs[:ranks]
    qkv_ref, out_ref = refs[ranks:]
    rank = rank_ref[0]
    blocks = ordered(parts, rank, slice(0, 4 * quarter))
    pieces = []
    for part in range(3):
        for block in blocks:
            pieces.append(block[:, part * quarter : (part + 1) * quarter])
    qkv_ref[...] = jnp.concatenate(pieces, axis=1)
    out_ref[...] = jnp.concatenate([block[:, 3 * quarter :] for block in blocks], axis=1)


def finish(kernel, rank, parts, shapes, name):
    return pl.pallas_call(
        kernel,
        in_specs=[pl.BlockSpec(memory_space=pltpu.SMEM)]
        + [pl.BlockSpec(memory_space=pltpu.VMEM)] * len(parts),
        out_specs=[pl.BlockSpec(memory_space=pltpu.VMEM)] * len(shapes),
        out_shape=[jax.ShapeDtypeStruct(shape, F32) for shape in shapes],
        compiler_params=pltpu.CompilerParams(vmem_limit_bytes=VMEM_LIMIT),
        name=name,
    )(rank.reshape(1), *parts)


def shards_general(
    ranks,
    frame_size,
    inputs,
    clip_id,
    ln_gains,
    ln_biases,
    w_qkv,
    w_out,
    w_up,
    w_down,
    up_bias,
    down_bias,
    conv_first,
    conv_first_bias,
    conv_mid,
    conv_mid_bias,
    cotangent,
):
    lows = frame_size // ranks
    frames_dev = inputs.shape[1]
    patches = inputs.shape[2]
    width = inputs.shape[3]
    rows = frames_dev * patches
    hidden = up_bias.shape[0]
    quarter = width // ranks
    hidden_quarter = hidden // ranks
    row_shard = width // frame_size
    rank = lax.axis_index("seq")
    place = lax.axis_index("frame")
    high = place // lows
    low = place % lows

    def permute(array, target):
        pairs = []
        for seq in range(ranks):
            for hi in range(ranks):
                for lo in range(lows):
                    to_seq, to_hi, to_lo = target(seq, hi, lo)
                    pairs.append(
                        (
                            seq * frame_size + hi * lows + lo,
                            to_seq * frame_size + to_hi * lows + to_lo,
                        )
                    )
        return lax.ppermute(array, AXES, pairs)

    def across(array, bits):
        return permute(array, lambda seq, hi, lo: (seq ^ bits, hi, lo))

    def along_high(array, step):
        return permute(array, lambda seq, hi, lo: (seq, (hi + step) % ranks, lo))

    def along_low(array, step):
        return permute(array, lambda seq, hi, lo: (seq, hi, (lo + step) % lows))

    def to_planes(array):
        return permute(array, lambda seq, hi, lo: (RANK_OF[hi], PLANE_OF[seq], lo))

    def from_planes(array):
        return permute(
            array, lambda seq, hi, lo: (PLANE_OF.index(hi), RANK_OF.index(seq), lo)
        )

    def flip_high(array, bits):
        return permute(array, lambda seq, hi, lo: (seq, hi ^ bits, lo))

    def gather_tokens(block):
        far = across(block, 2)
        near = across(block, 1)
        both = across(far, 1)
        return jnp.concatenate([block, near, far, both], axis=0)

    def scatter_tokens(partial):
        blocks = partial.astype(BF).reshape(ranks, rows, partial.shape[1])
        arrived_far = across(blocks[3], 1)
        arrived_near = across(blocks[1], 1)
        far = partial[2 * rows : 3 * rows] + arrived_far.astype(F32)
        arrived = across(far.astype(BF), 2)
        return partial[:rows] + arrived_near.astype(F32) + arrived.astype(F32)

    half_rows = rows // 2

    def gather_plane(block):
        if lows != 2:
            own = gather_tokens(block)
            return jnp.concatenate(
                [own] + [along_low(own, step) for step in range(1, lows)], axis=0
            )
        far = across(block, 2)
        side = along_low(block, 1)
        near = across(block, 1)
        corner = jnp.concatenate(
            [along_low(far[:half_rows], 1), across(side[half_rows:], 2)], axis=0
        )
        return jnp.concatenate(
            [
                block,
                near,
                far,
                across(far, 1),
                side,
                across(side, 1),
                corner,
                across(corner, 1),
            ],
            axis=0,
        )

    def scatter_plane(partial):
        if lows != 2:
            count = ranks * rows
            own = partial[:count]
            for step in range(1, lows):
                piece = partial[step * count : (step + 1) * count].astype(BF)
                own = own + along_low(piece, -step).astype(F32)
            return scatter_tokens(own)
        blocks = [partial[index * rows : (index + 1) * rows] for index in range(2 * ranks)]
        sums = {}
        for index in (6, 4, 2, 0):
            sums[index] = blocks[index] + across(blocks[index + 1].astype(BF), 1).astype(F32)
        corner = sums[6].astype(BF)
        by_far = across(corner[:half_rows], 2).astype(F32)
        by_side = along_low(corner[half_rows:], 1).astype(F32)
        side = jnp.concatenate([sums[4][:half_rows] + by_far, sums[4][half_rows:]], axis=0)
        far = jnp.concatenate([sums[2][:half_rows], sums[2][half_rows:] + by_side], axis=0)
        return (
            sums[0]
            + across(far.astype(BF), 2).astype(F32)
            + along_low(side.astype(BF), 1).astype(F32)
        )

    places = [(high ^ bits) * lows + low for bits in (0, 2, 1, 3)] + [
        (high ^ bits) * lows + (low + 1) % lows for bits in (0, 2, 1, 3)
    ]

    def after(array, *others):
        return lax.optimization_barrier((array,) + others)[0]

    staged = lows == 2

    def gather_two(block):
        return jnp.concatenate([block, flip_high(block, 2)], axis=0) if staged else block

    def gather_four(two):
        return jnp.concatenate([two, flip_high(two, 1)], axis=0) if staged else two

    def gather_all(four):
        if not staged:
            return lax.all_gather(four, "frame", axis=0, tiled=True)
        return place_rows([four, along_low(four, 1)], places, four.shape[0] // ranks)

    def scatter_half(partials):
        if not staged:
            return jnp.concatenate([partial.astype(BF) for partial in partials], axis=1)
        columns = [partial.shape[1] for partial in partials]
        cuts = [sum(columns[:index]) for index in range(len(columns) + 1)]
        count = partials[0].shape[0] // frame_size
        splits = [
            partial.reshape(ranks, lows, count, partial.shape[1]) for partial in partials
        ]
        sent = jnp.concatenate(
            [lax.dynamic_index_in_dim(split.astype(BF), 1 - low, 1, False) for split in splits],
            axis=2,
        )
        arrived = along_low(sent, 1)
        return jnp.concatenate(
            [
                lax.dynamic_index_in_dim(split, low, 1, False)
                + arrived[:, :, cuts[index] : cuts[index + 1]].astype(F32)
                for index, split in enumerate(splits)
            ],
            axis=2,
        ).reshape(2, 2, count, cuts[-1])

    def scatter_rest(half):
        if not staged:
            return lax.psum_scatter(half, "frame", scatter_dimension=0, tiled=True)
        sent = lax.dynamic_index_in_dim(half, 1 - high % 2, 1, False).astype(BF)
        kept = lax.dynamic_index_in_dim(half, high % 2, 1, False)
        two = kept + flip_high(sent, 1).astype(F32)
        sent = lax.dynamic_index_in_dim(two, 1 - high // 2, 0, False).astype(BF)
        kept = lax.dynamic_index_in_dim(two, high // 2, 0, False)
        return (kept + flip_high(sent, 2).astype(F32)).astype(BF)

    def swap_ranks(blocks):
        split = blocks.reshape((2, 2) + blocks.shape[1:])
        kept = lax.dynamic_index_in_dim(split, rank // 2, 0, False)
        found = across(lax.dynamic_index_in_dim(split, 1 - rank // 2, 0, False), 2)
        own = lax.dynamic_index_in_dim(kept, rank % 2, 0, False)
        far = lax.dynamic_index_in_dim(found, rank % 2, 0, False)
        near = across(lax.dynamic_index_in_dim(kept, 1 - rank % 2, 0, False), 1)
        both = across(lax.dynamic_index_in_dim(found, 1 - rank % 2, 0, False), 1)
        return in_rank_order([own, near, far, both])

    def sum_everywhere(array):
        bits = 1
        while bits < ranks:
            array = array + across(array, bits)
            bits *= 2
        bits = 1
        while bits < frame_size:
            pairs = [
                (seq * frame_size + item, seq * frame_size + (item ^ bits))
                for seq in range(ranks)
                for item in range(frame_size)
            ]
            array = array + lax.ppermute(array, AXES, pairs)
            bits *= 2
        return array

    def in_rank_order(items):
        stacked = jnp.stack(items)
        return [
            lax.dynamic_index_in_dim(stacked, rank ^ index, 0, False) for index in range(ranks)
        ]

    def gather_ranks(block):
        far = across(block, 2)
        near = across(block, 1)
        both = across(far, 1)
        return [block, near, far, both]

    token_rows = inputs[0].reshape(rows, width)
    grad_rows = cotangent[0].reshape(frames_dev * CH, width)
    frame_count = clip_id.shape[1]
    clip_rows = jnp.pad(
        clip_id.astype(BF), ((0, 15), (0, width - frame_count))
    )
    moved = to_planes(jnp.concatenate([token_rows, grad_rows, clip_rows], axis=0))
    tokens = moved[:rows].astype(F32)
    grad_learned = moved[rows : rows + frames_dev * CH].astype(F32)
    clips = moved[rows + frames_dev * CH, :frame_count].astype(jnp.int32)

    own_qkv = jnp.concatenate(
        [
            lax.dynamic_slice_in_dim(w_qkv, part * width + rank * quarter, quarter, 1)
            for part in range(3)
        ],
        axis=1,
    )
    two_qkv = gather_two(own_qkv)
    unit = hidden // (frame_size * ranks)
    columns = jnp.arange(hidden_quarter, dtype=jnp.int32)
    wanted = (columns // unit) * (unit * ranks) + rank * unit + columns % unit
    choose = (jnp.arange(hidden, dtype=jnp.int32)[:, None] == wanted[None, :]).astype(BF)
    own_up = dot(w_up, choose).astype(BF)
    own_down = lax.dynamic_slice_in_dim(w_down, rank * unit, unit, 0)
    own_out = lax.dynamic_slice_in_dim(w_out, rank * quarter, quarter, 1)
    own_out = jnp.concatenate([own_out, conv_first], axis=1)
    two_out = gather_two(after(own_out, two_qkv))
    four_qkv = gather_four(two_qkv)
    two_up = gather_two(after(own_up, two_out))
    four_out = gather_four(after(two_out, four_qkv))
    qkv_quarter = gather_all(four_qkv)
    two_down = gather_two(after(own_down, two_up))
    four_up = gather_four(after(two_up, four_out))
    qkv_quarter = after(qkv_quarter, four_out, two_up)
    packed = gather_all(after(four_out, qkv_quarter))
    out_columns = packed[:, :quarter]
    full_conv = packed[:, quarter:]
    out_quarter = jnp.concatenate(
        swap_ranks(out_columns.reshape(ranks, quarter, quarter)), axis=1
    )
    up_bias_quarter = lax.dynamic_index_in_dim(
        up_bias.reshape(frame_size, ranks, unit), rank, 1, False
    ).reshape(1, hidden_quarter)

    frame_ids = jnp.arange(frame_count, dtype=jnp.int32)

    def clip_tokens(lo):
        blocks = []
        inverse = jnp.array([RANK_OF.index(item) for item in range(ranks)], jnp.int32)
        for bits in range(ranks):
            hi = lax.dynamic_index_in_dim(inverse, rank ^ bits, 0, False)
            for frame in range(frames_dev):
                blocks.append((hi * lows + lo) * frames_dev + frame)
        wanted_frames = jnp.stack(blocks)
        found = jnp.sum(
            jnp.where(wanted_frames[:, None] == frame_ids[None, :], clips[None, :], 0), axis=1
        )
        return jnp.broadcast_to(found[:, None], (found.shape[0], patches)).reshape(-1)

    query_clip = clip_tokens(low)
    key_clip = jnp.concatenate(
        [query_clip] + [clip_tokens((low - step) % lows) for step in range(1, lows)]
    )
    query_clip = query_clip[None, :]
    key_clip = key_clip[:, None]

    normed_one, inverse_one = norm_stats(tokens)
    own_count = ranks * rows
    all_one = gather_plane((normed_one * ln_gains[0] + ln_biases[0]).astype(BF))
    queries = dot(all_one[:own_count], qkv_quarter[:, :quarter]).astype(BF)
    keyvals = dot(all_one, qkv_quarter[:, quarter:]).astype(BF)
    queries = after(queries, packed, four_up, two_down)
    up_quarter = gather_all(after(four_up, packed))
    four_down = gather_four(two_down)
    attended, logs = attend(queries, keyvals, query_clip, key_clip)
    after_attention = tokens + scatter_tokens(dot(attended, out_quarter, 0, 0))
    after_attention = after(after_attention, four_down)
    down_quarter = gather_all(after(four_down, up_quarter))
    normed_two, inverse_two = norm_stats(after_attention)
    all_two = gather_tokens((normed_two * ln_gains[1] + ln_biases[1]).astype(BF))
    pre_act = dot(all_two, up_quarter) + up_bias_quarter
    act_low = gelu(pre_act).astype(BF)
    block_out = after_attention + scatter_tokens(dot(act_low, down_quarter)) + down_bias

    normed_three, inverse_three = norm_stats(block_out)
    normed_three_low = (normed_three * ln_gains[2] + ln_biases[2]).astype(BF)
    tap_rows = dot(normed_three_low, full_conv).reshape(frames_dev, GRID, GRID, 9 * CH)
    first = conv_grid(tap_rows) + conv_first_bias
    features = block_out.reshape(frames_dev, patches, width)

    def tail(first_arg, features_arg, mid_arg, mid_bias_arg):
        maps = token_maps(first_arg, mid_arg, mid_bias_arg).reshape(frames_dev, patches, CH)
        return pool_tokens(maps, features_arg)

    learned, tail_back = jax.vjp(tail, first, features, conv_mid, conv_mid_bias)
    grad_first, grad_pool, grad_mid, grad_mid_bias = tail_back(
        grad_learned.reshape(frames_dev, CH, width)
    )
    grad_first_low = grad_first.astype(BF)
    grad_first_bias = jnp.sum(grad_first_low.astype(F32), axis=(0, 1, 2))
    spread_unused, spread_back = jax.vjp(conv_grid, tap_rows)
    spread = spread_back(grad_first_low.astype(F32))[0].reshape(rows, 9 * CH).astype(BF)
    grad_conv = dot(normed_three_low, spread, 0, 0)
    grad_normed_three = dot(spread, full_conv, 1, 1)
    grad_block, grad_gain_three, grad_shift_three = norm_back(
        normed_three, inverse_three, ln_gains[2], grad_normed_three
    )
    grad_block = grad_block + grad_pool.reshape(rows, width)
    grad_mlp = grad_block.astype(BF)
    grad_down_bias = jnp.sum(grad_mlp.astype(F32), axis=0)

    all_mlp = gather_tokens(grad_mlp)
    grad_act = dot(all_mlp, down_quarter, 1, 1)
    gelu_unused, gelu_back = jax.vjp(gelu, pre_act)
    grad_pre = gelu_back(grad_act)[0].astype(BF)
    grad_up_bias = jnp.sum(grad_pre.astype(F32), axis=0)
    grad_normed_two = scatter_tokens(dot(grad_pre, up_quarter, 1, 1))
    grad_down = dot(act_low, all_mlp, 0, 0)
    grad_up = dot(all_two, grad_pre, 0, 0)
    mlp_half = scatter_half([grad_up, grad_down, grad_conv])
    grad_after, grad_gain_two, grad_shift_two = norm_back(
        normed_two, inverse_two, ln_gains[1], grad_normed_two
    )
    grad_after = grad_after + grad_block

    all_branch = gather_tokens(grad_after.astype(BF))
    grad_attended = dot(all_branch, out_quarter, 1, 1).astype(BF)
    grad_out = dot(attended, all_branch)
    grad_attended = after(grad_attended, mlp_half)
    mlp_share = scatter_rest(mlp_half)
    grad_queries, grad_keyvals = attend_back(
        queries, keyvals, grad_attended, logs, query_clip, key_clip
    )
    grad_queries = grad_queries.T
    grad_keyvals = grad_keyvals.astype(BF)
    grad_normed_own = dot(grad_keyvals, qkv_quarter[:, quarter:], 1, 1)
    grad_normed_own = jnp.concatenate(
        [
            grad_normed_own[:own_count] + dot(grad_queries, qkv_quarter[:, :quarter], 1, 1),
            grad_normed_own[own_count:],
        ],
        axis=0,
    )
    grad_normed_one = scatter_plane(grad_normed_own)
    grad_q = dot(all_one[:own_count], grad_queries, 0, 0)
    grad_kv = dot(all_one, grad_keyvals, 0, 0)
    grad_out_columns = jnp.concatenate(
        swap_ranks(grad_out.astype(BF).reshape(quarter, ranks, quarter).transpose(1, 0, 2)),
        axis=0,
    )
    qkv_share = scatter_rest(
        after(scatter_half([grad_q, grad_kv, grad_out_columns]), mlp_share)
    )
    grad_tokens, grad_gain_one, grad_shift_one = norm_back(
        normed_one, inverse_one, ln_gains[0], grad_normed_one
    )
    moved_back = from_planes(
        jnp.concatenate(
            [
                (grad_after + grad_tokens).astype(BF),
                learned.astype(BF).reshape(frames_dev * CH, width),
            ],
            axis=0,
        )
    ).astype(F32)
    grad_input = moved_back[:rows]
    learned = moved_back[rows:]

    sum_up, sum_down, sum_conv = finish(
        functools.partial(finish_mlp_kernel, ranks, hidden_quarter, width, unit),
        rank,
        gather_ranks(mlp_share),
        [(row_shard, hidden), (ranks * unit, width), (row_shard, 9 * CH)],
        "finish_mlp",
    )
    sum_qkv, sum_out = finish(
        functools.partial(finish_qkv_kernel, ranks, quarter),
        rank,
        gather_ranks(qkv_share),
        [(row_shard, 3 * width), (row_shard, width)],
        "finish_qkv",
    )

    conv_terms = jnp.concatenate(
        [grad_first_bias.reshape(-1), grad_mid.reshape(-1), grad_mid_bias.reshape(-1)]
    )
    conv_rows = -(-conv_terms.shape[0] // width)
    conv_terms = jnp.pad(conv_terms, (0, conv_rows * width - conv_terms.shape[0]))
    up_terms = jnp.where(
        jnp.arange(ranks, dtype=jnp.int32)[:, None] == rank,
        grad_up_bias.reshape(1, hidden_quarter),
        0.0,
    )
    early = sum_everywhere(
        jnp.concatenate(
            [
                jnp.stack(
                    [
                        grad_gain_one,
                        grad_gain_two,
                        grad_gain_three,
                        grad_shift_one,
                        grad_shift_two,
                        grad_shift_three,
                        grad_down_bias,
                    ]
                ),
                conv_terms.reshape(conv_rows, width),
                up_terms.reshape(-1, width),
            ],
            axis=0,
        )
    )
    sum_gains = early[0:3]
    sum_shifts = early[3:6]
    conv_sums = early[7 : 7 + conv_rows].reshape(-1)
    sum_up_bias = (
        early[7 + conv_rows :]
        .reshape(ranks, frame_size, unit)
        .transpose(1, 0, 2)
        .reshape(hidden)
    )
    mid_count = grad_mid.size
    sum_mid = conv_sums[CH : CH + mid_count].reshape(grad_mid.shape)
    sum_mid_bias = conv_sums[CH + mid_count : CH + mid_count + grad_mid_bias.size]
    return (
        learned.reshape(1, frames_dev, CH, width),
        grad_input.reshape(1, frames_dev, patches, width),
        sum_qkv,
        sum_out,
        sum_up,
        sum_down,
        sum_conv,
        sum_gains,
        sum_shifts,
        sum_up_bias,
        early[6],
        conv_sums[:CH],
        sum_mid,
        sum_mid_bias.reshape(grad_mid_bias.shape),
    )


PAD = 128


def run(kernel, name, scalars, arrays, outs, scratch=(), limit=16):
    vmem = pl.BlockSpec(memory_space=pltpu.VMEM)
    return pl.pallas_call(
        kernel,
        in_specs=[pl.BlockSpec(memory_space=pltpu.SMEM)] + [vmem] * len(arrays),
        out_specs=[vmem] * len(outs),
        out_shape=[jax.ShapeDtypeStruct(shape, kind) for shape, kind in outs],
        scratch_shapes=list(scratch),
        compiler_params=pltpu.CompilerParams(vmem_limit_bytes=limit * 1024 * 1024),
        name=name,
    )(scalars, *arrays)


def rows_at(start, size):
    return pl.ds(pl.multiple_of(start * size, size), size)


def stack_rows(refs):
    return jnp.concatenate([ref[...] for ref in refs], axis=0)


def exact(left, right, left_dim=1, right_dim=0):
    return lax.dot_general(
        left,
        right,
        (((left_dim,), (right_dim,)), ((), ())),
        precision=HIGHEST,
        preferred_element_type=F32,
    )


def column_sum(values):
    return jnp.sum(values, axis=0, keepdims=True)


def back_of_norm(values, gain, grad):
    normed, inverse = norm_stats(values)
    scaled = grad * gain
    mean_scaled = jnp.mean(scaled, axis=-1, keepdims=True)
    mean_cross = jnp.mean(scaled * normed, axis=-1, keepdims=True)
    result = inverse * (scaled - mean_scaled - normed * mean_cross)
    return result, column_sum(grad * normed), column_sum(grad)


def pack_kernel(unused_ref, grads_ref, clip_ref, pack_ref):
    more, width = grads_ref.shape
    rest = pack_ref.shape[0] - more
    pack_ref[:more, :] = grads_ref[...]
    clips = clip_ref[...].astype(F32)
    clips = jnp.concatenate([clips, jnp.zeros((1, PAD - clips.shape[1]), F32)], axis=1)
    pack_ref[more:, :] = jnp.zeros((rest, width), BF)
    pack_ref[more:, :PAD] = jnp.broadcast_to(clips, (rest, PAD)).astype(BF)


def select_kernel(ids_ref, qkv_ref, out_ref, own_ref):
    width = out_ref.shape[1]
    quarter = width // 4
    for rank in range(4):

        @pl.when(ids_ref[0] == rank)
        def _(rank=rank):
            pieces = [
                qkv_ref[:, part * width + rank * quarter : part * width + (rank + 1) * quarter]
                for part in range(3)
            ]
            pieces.append(out_ref[:, rank * quarter : (rank + 1) * quarter])
            own_ref[...] = jnp.concatenate(pieces, axis=1)


def prepare_kernel(ids_ref, up_ref, down_ref, conv_ref, own_ref, more_ref):
    size = own_ref.shape[0]
    unit = down_ref.shape[0] // 4
    quarter = 8 * unit
    for rank in range(4):

        @pl.when(ids_ref[0] == rank)
        def _(rank=rank):
            own_ref[:, :quarter] = jnp.concatenate(
                [
                    up_ref[:, (4 * group + rank) * unit : (4 * group + rank + 1) * unit]
                    for group in range(8)
                ],
                axis=1,
            )
            more_ref[...] = down_ref[rank * unit : (rank + 1) * unit, :]

    taps = conv_ref.shape[1]
    own_ref[:, quarter:] = jnp.concatenate(
        [conv_ref[...], jnp.zeros((size, PAD - taps), BF)], axis=1
    )


def norm_one_kernel(ids_ref, *refs):
    moved_ref, extra_ref, gains_ref, shifts_ref, low_ref, qclip_ref, kclip_ref = refs
    count = low_ref.shape[0]
    frames = count // (GRID * GRID)
    patches = GRID * GRID
    normed, unused = norm_stats(moved_ref[:count, :].astype(F32))
    low_ref[...] = (normed * gains_ref[0:1, :] + shifts_ref[0:1, :]).astype(BF)
    start = frames * CH
    clips = extra_ref[start : start + 16, :PAD].astype(F32)[0:1]
    lane = lax.broadcasted_iota(jnp.int32, (1, PAD), 1)
    rank, low = ids_ref[0], ids_ref[2]
    for side in range(2):
        for bits in range(4):
            for frame in range(frames):
                hi = sum(jnp.where(rank ^ bits == RANK_OF[item], item, 0) for item in range(4))
                wanted = (2 * hi + (low ^ side)) * frames + frame
                clip = jnp.sum(jnp.where(lane == wanted, clips, 0.0), axis=1, keepdims=True)
                first = ((4 * side + bits) * frames + frame) * patches
                kclip_ref[first : first + patches, :] = jnp.broadcast_to(clip, (patches, 1))
                if side == 0:
                    qclip_ref[:, first : first + patches] = jnp.broadcast_to(clip, (1, patches))


def pass_sum_kernel(unused_ref, even_ref, arrived_ref, out_ref):
    out_ref[...] = (even_ref[...] + arrived_ref[...].astype(F32)).astype(BF)


def add_kernel(unused_ref, left_ref, right_ref, out_ref):
    out_ref[...] = left_ref[...] + right_ref[...]


def pick_kernel(ids_ref, far_ref, side_ref, out_ref):
    @pl.when(lax.rem(ids_ref[0], 2) == 0)
    def _():
        out_ref[...] = far_ref[...]

    @pl.when(lax.rem(ids_ref[0], 2) == 1)
    def _():
        out_ref[...] = side_ref[...]


def pass_on_kernel(ids_ref, *refs):
    far_even_ref, side_even_ref, second_ref, third_ref, corner_ref, far_ref, side_ref = refs
    core = lax.rem(ids_ref[0], 2)
    corner = corner_ref[...].astype(F32)
    far = far_even_ref[...] + second_ref[...].astype(F32)
    side = side_even_ref[...] + third_ref[...].astype(F32)
    far_ref[...] = (far + jnp.where(core == 1, corner, 0.0)).astype(BF)
    side_ref[...] = (side + jnp.where(core == 0, corner, 0.0)).astype(BF)


def place_of(ids_ref, bits):
    return (2 * ids_ref[1] + ids_ref[2]) ^ bits


def project_kernel(quarter, ids_ref, *refs):
    tokens, blocks = refs[:8], refs[8:16]
    q_ref, kv_ref, w_ref = refs[16:19]
    out_refs, all_ref = refs[19:23], refs[23]
    size = blocks[0].shape[0]
    for bits in range(8):
        where = rows_at(place_of(ids_ref, bits), size)
        w_ref[where, :] = blocks[bits][:, : 3 * quarter]
        all_ref[where, :] = blocks[bits][:, 3 * quarter :]
    rank = ids_ref[0]
    for bits in range(4):
        out_refs[bits][...] = all_ref[rows_at(rank ^ bits, quarter), :]
    own = dot(stack_rows(tokens[:4]), w_ref[...]).astype(BF)
    q_ref[...] = own[:, :quarter]
    half = own.shape[0]
    kv_ref[:half, :] = own[:, quarter:]
    kv_ref[half:, :] = dot(stack_rows(tokens[4:]), w_ref[:, quarter:]).astype(BF)


def scores_of(kv_ref, q_ref, queries, lanes, same, scale):
    raw = dot(kv_ref[:, lanes], q_ref[queries, lanes], 1, 1) * scale
    return jnp.where(same, raw, FLOOR_SCORE)


def attend_wide_kernel(heads, scale, unused_ref, *refs):
    q_ref, kv_ref, qclip_ref, kclip_ref, mixed_ref, log_ref = refs
    width = heads * HEAD_DIM
    count = q_ref.shape[0] // 2

    def one(part, carry):
        queries = pl.ds(pl.multiple_of(part * count, count), count)
        same = kclip_ref[...] == qclip_ref[:, queries]
        for head in range(heads):
            lanes = slice(head * HEAD_DIM, (head + 1) * HEAD_DIM)
            values = slice(width + head * HEAD_DIM, width + (head + 1) * HEAD_DIM)
            scores = scores_of(kv_ref, q_ref, queries, lanes, same, scale)
            top = jnp.max(scores, axis=0, keepdims=True)
            shifted = jnp.exp(scores - top)
            total = jnp.sum(shifted, axis=0, keepdims=True)
            prob = (shifted * (1.0 / total)).astype(BF)
            mixed_ref[lanes, queries] = dot(kv_ref[:, values], prob, 0, 0).astype(BF)
            log_ref[head : head + 1, queries] = top + jnp.log(total)
        return carry

    lax.fori_loop(0, 2, one, 0)


def split_blocks(values, even_refs, odd_refs):
    rows = even_refs[0].shape[0]
    for part in range(len(odd_refs)):
        even_refs[part][...] = values[2 * part * rows : (2 * part + 1) * rows]
        odd_refs[part][...] = values[(2 * part + 1) * rows : (2 * part + 2) * rows].astype(BF)


def out_kernel(rank_ref, *refs):
    mixed_ref = refs[0]
    even_refs, odd_refs, w_ref = refs[5:7], refs[7:9], refs[9]
    blocks = [ref[...] for ref in refs[1:5]]
    rank = rank_ref[0]
    width = blocks[0].shape[0]
    for index in range(4):
        found = blocks[0]
        for bits in range(1, 4):
            found = jnp.where(rank == index ^ bits, blocks[bits], found)
        w_ref[:, index * width : (index + 1) * width] = found
    split_blocks(dot(mixed_ref[...], w_ref[...], 0, 0), even_refs, odd_refs)


def norm_two_kernel(unused_ref, *refs):
    moved_ref, even_ref, arrived_ref, far_ref, gains_ref, shifts_ref = refs[:6]
    sum_ref, low_ref = refs[6:]
    count = low_ref.shape[0]
    values = (
        moved_ref[:count, :].astype(F32)
        + even_ref[...]
        + arrived_ref[...].astype(F32)
        + far_ref[...].astype(F32)
    )
    sum_ref[...] = values
    normed, unused = norm_stats(values)
    low_ref[...] = (normed * gains_ref[1:2, :] + shifts_ref[1:2, :]).astype(BF)


def gelu_both(values):
    size = jnp.abs(values) * 0.7071067811865476
    ratio = 1.0 / (1.0 + 0.3275911 * size)
    bell = jnp.exp(-size * size)
    series = ratio * (
        0.254829592
        + ratio
        * (-0.284496736 + ratio * (1.421413741 + ratio * (-1.453152027 + ratio * 1.061405429)))
    )
    tail = 0.5 * series * bell
    below = jnp.where(values >= 0.0, 1.0 - tail, tail)
    return values * below, below + values * bell * 0.3989422804014327


def join_kernel(unused_ref, *refs):
    for index, ref in enumerate(refs[4:]):
        size = ref.shape[0] // 2
        ref[:size, :] = refs[2 * index][...]
        ref[size:, :] = refs[2 * index + 1][...]


def mlp_part(tokens, up_ref, down_ref, bias, act_ref, slope_ref, even_ref, odd_ref):
    pre = dot(stack_rows(tokens), up_ref[...]) + bias
    act, slope = gelu_both(pre)
    act = act.astype(BF)
    act_ref[...] = act
    slope_ref[...] = slope
    partial = dot(act, down_ref[...])
    count = even_ref.shape[0]
    even_ref[...] = partial[:count]
    odd_ref[...] = partial[count:].astype(BF)


def mlp_kernel(ids_ref, *refs):
    tokens = refs[:2]
    a_refs, b_refs, bias_ref = refs[2:4], refs[4:6], refs[6]
    up_ref, down_ref, conv_ref, own_bias_ref = refs[7:11]
    rank = ids_ref[0]
    size = a_refs[0].shape[0] // 4
    quarter = up_ref.shape[1]
    for ref, order in zip(a_refs, ((0, 4, 2, 6), (1, 5, 3, 7))):
        for index, bits in enumerate(order):
            where = rows_at(place_of(ids_ref, bits), size)
            rows = slice(index * size, (index + 1) * size)
            up_ref[where, :] = ref[rows, :quarter]
            conv_ref[where, :] = ref[rows, quarter:]
    for ref, order in zip(b_refs, ((0, 1, 4, 5), (2, 3, 6, 7))):
        for index, bits in enumerate(order):
            where = rows_at(place_of(ids_ref, bits), size)
            down_ref[where, :] = ref[index * size : (index + 1) * size, :]
    unit = quarter // 8
    bias = None
    for index in range(4):
        found = jnp.concatenate(
            [
                bias_ref[:, (4 * group + index) * unit : (4 * group + index + 1) * unit]
                for group in range(8)
            ],
            axis=1,
        )
        bias = found if bias is None else jnp.where(rank == index, found, bias)
    own_bias_ref[...] = bias
    mlp_part(tokens, up_ref, down_ref, bias, *refs[11:])


def mlp_more_kernel(unused_ref, *refs):
    up_ref, down_ref, bias_ref = refs[2:5]
    mlp_part(refs[:2], up_ref, down_ref, bias_ref[...], *refs[5:])


def grid_masks(count):
    row = lax.broadcasted_iota(jnp.int32, (count, PAD), 0)
    i = (row // GRID) % GRID
    j = row % GRID
    masks = []
    for tap in range(9):
        di, dj = tap // 3 - 1, tap % 3 - 1
        inside = (i + di >= 0) & (i + di < GRID) & (j + dj >= 0) & (j + dj < GRID)
        masks.append(inside.astype(F32))
    return masks


def collect_taps(taps, masks, first_lanes):
    count = taps.shape[0]
    total = None
    for tap in range(9):
        offset = (tap // 3 - 1) * GRID + tap % 3 - 1
        moved = pltpu.roll(taps, (PAD - tap * CH) % PAD, 1) if tap else taps
        moved = pltpu.roll(moved, (-offset) % count, 0) if offset else moved
        moved = moved * masks[tap]
        total = moved if total is None else total + moved
    return total * first_lanes


def spread_taps(values, masks):
    count = values.shape[0]
    total = None
    for tap in range(9):
        offset = (tap // 3 - 1) * GRID + tap % 3 - 1
        moved = pltpu.roll(values, tap * CH, 1) if tap else values
        moved = pltpu.roll(moved, offset % count, 0) if offset else moved
        moved = moved * masks[8 - tap]
        total = moved if total is None else total + moved
    return total


def store_rows(ref, start, values):
    for index in range(values.shape[1] // PAD):
        ref[start + index : start + index + 1, :] = values[:, index * PAD : (index + 1) * PAD]


def load_rows(ref, start, count):
    return jnp.concatenate(
        [ref[start + index : start + index + 1, :] for index in range(count)], axis=1
    )


def tail_kernel(vectors, unused_ref, *refs):
    sum_ref, even_ref, arrived_ref, far_ref, bias_ref, gains_ref, shifts_ref = refs[:7]
    conv_ref, first_bias_ref, mid_ref, mid_bias_ref, moved_ref = refs[7:12]
    learned_ref, low_ref, grad_ref, normed_ref, spread_ref, small_ref = refs[12:]
    count = low_ref.shape[0]
    frames = count // (GRID * GRID)
    patches = GRID * GRID
    value = (
        sum_ref[...]
        + even_ref[...]
        + arrived_ref[...].astype(F32)
        + far_ref[...].astype(F32)
        + bias_ref[...]
    )
    normed, inverse = norm_stats(value)
    gain = gains_ref[2:3, :]
    normed_low = (normed * gain + shifts_ref[2:3, :]).astype(BF)
    normed_ref[...] = normed_low
    masks = grid_masks(count)
    lane = lax.broadcasted_iota(jnp.int32, (count, PAD), 1)
    first_lanes = (lane < CH).astype(F32)
    first = collect_taps(dot(normed_low, conv_ref[...]), masks, first_lanes)
    hidden, slope = gelu_both(first + first_bias_ref[...])
    hidden = hidden * first_lanes
    hiddens, slopes = [hidden], [slope]
    maps = None
    for layer in range(3):
        pre = collect_taps(exact(hiddens[layer], mid_ref[layer]), masks, first_lanes)
        pre = pre + mid_bias_ref[layer : layer + 1, :]
        if layer < 2:
            hidden, slope = gelu_both(pre)
            hiddens.append(hidden * first_lanes)
            slopes.append(slope)
        else:
            maps = jax.nn.sigmoid(pre) * first_lanes
    frame_of_row = lax.broadcasted_iota(jnp.int32, (count, PAD), 0) // patches
    wide = None
    for frame in range(frames):
        moved = pltpu.roll(maps, frame * CH, 1) if frame else maps
        moved = moved * (frame_of_row == frame).astype(F32)
        wide = moved if wide is None else wide + moved
    cotangent = jnp.concatenate(
        [
            moved_ref[: frames * CH, :].astype(F32),
            jnp.zeros((PAD - frames * CH, value.shape[1]), F32),
        ],
        axis=0,
    )
    learned_ref[...] = exact(wide, value, 0, 0)[: frames * CH] * (1.0 / patches)
    pooled = exact(wide, cotangent) * (1.0 / patches)
    products = exact(value, cotangent, 1, 1) * (1.0 / patches)
    grad = None
    for frame in range(frames):
        moved = pltpu.roll(products, PAD - frame * CH, 1) if frame else products
        moved = moved * (frame_of_row == frame).astype(F32)
        grad = moved if grad is None else grad + moved
    grad = grad * maps * (1.0 - maps)
    small_ref[...] = jnp.zeros_like(small_ref)
    conv_start = 7 * vectors + 4 * vectors
    for layer in range(2, -1, -1):
        taps = spread_taps(grad, masks)
        weight = exact(hiddens[layer], taps, 0, 0)[:CH]
        small_ref[conv_start + layer * CH : conv_start + (layer + 1) * CH, :] = weight
        bias_row = conv_start + 3 * CH + 1 + layer
        small_ref[bias_row : bias_row + 1, :] = column_sum(grad)
        grad = exact(taps, mid_ref[layer], 1, 1) * slopes[layer]
    grad_low = grad.astype(BF).astype(F32)
    small_ref[conv_start + 3 * CH : conv_start + 3 * CH + 1, :] = column_sum(grad_low)
    spread = spread_taps(grad_low, masks).astype(BF)
    spread_ref[...] = spread
    grad_normed = dot(spread, conv_ref[...], 1, 1)
    scaled = grad_normed * gain
    mean_scaled = jnp.mean(scaled, axis=-1, keepdims=True)
    mean_cross = jnp.mean(scaled * normed, axis=-1, keepdims=True)
    grad_value = inverse * (scaled - mean_scaled - normed * mean_cross)
    grad_value = grad_value + pooled
    grad_ref[...] = grad_value
    low = grad_value.astype(BF)
    low_ref[...] = low
    store_rows(small_ref, 2 * vectors, column_sum(grad_normed * normed))
    store_rows(small_ref, 5 * vectors, column_sum(grad_normed))
    store_rows(small_ref, 6 * vectors, column_sum(low.astype(F32)))


def mlp_back_kernel(unused_ref, *refs):
    grads = refs[:2]
    slope_ref, up_ref, down_ref = refs[2:5]
    pre_ref, even_ref, odd_ref, bias_ref = refs[5:]
    grad_act = dot(stack_rows(grads), down_ref[...], 1, 1)
    grad_pre = (grad_act * slope_ref[...]).astype(BF)
    pre_ref[...] = grad_pre
    bias_ref[...] = column_sum(grad_pre.astype(F32))
    partial = dot(grad_pre, up_ref[...], 1, 1)
    count = even_ref.shape[0]
    even_ref[...] = partial[:count]
    odd_ref[...] = partial[count:].astype(BF)


def divide_rows(ids_ref, all_ref, refs):
    kept_ref, sent_ref, more_kept_ref, more_sent_ref = refs
    high, low = ids_ref[1], ids_ref[2]
    size = all_ref.shape[0] // 8
    columns = kept_ref.shape[1]
    for index in range(4):
        rows = slice(index * size, (index + 1) * size)
        kept_ref[rows, :] = all_ref[rows_at(2 * index + low, size), :columns]
        sent_ref[rows, :] = all_ref[rows_at(2 * index + 1 - low, size), :columns].astype(BF)
        hi = high ^ (2 * (index % 2))
        lo = low ^ (index // 2)
        more_kept_ref[rows, :] = all_ref[rows_at(2 * hi + lo, size), columns:]
        more_sent_ref[rows, :] = all_ref[rows_at(2 * (hi ^ 1) + lo, size), columns:].astype(BF)


def fold(values, count):
    size = values.shape[0] // count
    return jnp.concatenate(
        [values[index * size : (index + 1) * size] for index in range(count)], axis=1
    )


def unfold(values, count):
    lanes = values.shape[1] // count
    return jnp.concatenate(
        [values[:, index * lanes : (index + 1) * lanes] for index in range(count)], axis=0
    )


def rounded(values):
    return values.astype(BF).astype(F32)


def mlp_grads_kernel(ids_ref, *refs):
    tokens, grads = refs[:4], refs[4:8]
    act, pre = stack_rows(refs[8:10]), stack_rows(refs[10:12])
    normed_ref, spread_ref = refs[12:14]
    all_ref = refs[18]
    quarter = act.shape[1]
    width = tokens[0].shape[1]
    all_ref[:, :quarter] = dot(stack_rows(tokens), pre, 0, 0)
    all_ref[:, quarter : quarter + width] = dot(act, stack_rows(grads), 0, 0)
    all_ref[:, quarter + width :] = dot(normed_ref[...], spread_ref[...], 0, 0)
    divide_rows(ids_ref, all_ref, refs[14:18])


def norm_two_back_kernel(unused_ref, *refs):
    sum_ref, grad_ref, even_ref, arrived_ref, far_ref, gains_ref = refs[:6]
    total_ref, low_ref, rows_ref = refs[6:]
    grad_normed = even_ref[...] + arrived_ref[...].astype(F32) + far_ref[...].astype(F32)
    result, gain_row, shift_row = back_of_norm(sum_ref[...], gains_ref[1:2, :], grad_normed)
    total = result + grad_ref[...]
    total_ref[...] = total
    low_ref[...] = total.astype(BF)
    rows_ref[0:1, :] = gain_row
    rows_ref[1:2, :] = shift_row


def attend_back_part(heads, scale, first, branches, refs, prior_ref, own_ref, total_ref):
    out_ref, q_ref, kv_ref, log_ref, qclip_ref, kclip_ref = refs
    width = heads * HEAD_DIM
    count = own_ref.shape[0]
    queries = slice(first, first + count)
    grad_mixed = dot(stack_rows(branches), out_ref[...], 1, 1).astype(BF)
    same = kclip_ref[...] == qclip_ref[:, queries]
    query_parts, key_parts, value_parts = [], [], []
    for head in range(heads):
        lanes = slice(head * HEAD_DIM, (head + 1) * HEAD_DIM)
        values = slice(width + head * HEAD_DIM, width + (head + 1) * HEAD_DIM)
        scores = scores_of(kv_ref, q_ref, queries, lanes, same, scale)
        prob = jnp.exp(scores - log_ref[head : head + 1, queries])
        grad_prob = dot(kv_ref[:, values], grad_mixed[:, lanes], 1, 1)
        delta = jnp.sum(prob * grad_prob, axis=0, keepdims=True)
        grad_score = (prob * (grad_prob - delta)).astype(BF)
        query_parts.append(dot(kv_ref[:, lanes], grad_score, 0, 0) * scale)
        key_parts.append(dot(grad_score, q_ref[queries, lanes]) * scale)
        value_parts.append(dot(prob.astype(BF), grad_mixed[:, lanes]))
    own_ref[...] = jnp.concatenate(query_parts, axis=0).T.astype(BF)
    terms = jnp.concatenate(key_parts + value_parts, axis=1)
    total_ref[...] = terms if prior_ref is None else prior_ref[...] + terms


def attend_back_first_kernel(heads, scale, unused_ref, *refs):
    attend_back_part(heads, scale, 0, refs[:2], refs[2:8], None, refs[8], refs[9])


def attend_back_next_kernel(heads, scale, first, unused_ref, *refs):
    attend_back_part(heads, scale, first, refs[:1], refs[1:7], refs[7], refs[8], refs[9])


def attend_back_last_kernel(heads, scale, first, unused_ref, *refs):
    prior_ref, first_ref, next_ref, w_ref = refs[7:11]
    own_ref, other_ref = refs[11:13]
    even_refs, odd_refs = refs[13:17], refs[17:21]
    part_ref, total_ref = refs[21:]
    attend_back_part(heads, scale, first, refs[:1], refs[1:7], prior_ref, part_ref, total_ref)
    width = heads * HEAD_DIM
    count = own_ref.shape[0]
    middle = first_ref.shape[0]
    own_ref[:middle, :width] = first_ref[...]
    own_ref[middle:first, :width] = next_ref[...]
    own_ref[first:, :width] = part_ref[...]
    own_ref[:, width:] = total_ref[:count, :].astype(BF)
    other_ref[...] = total_ref[count:, :].astype(BF)
    own = dot(own_ref[...], w_ref[...], 1, 1)
    other = dot(other_ref[...], w_ref[:, width:], 1, 1)
    split_blocks(jnp.concatenate([own, other], axis=0), even_refs, odd_refs)


def qkv_grads_kernel(ids_ref, *refs):
    tokens, branches, mixes = refs[:8], refs[8:12], refs[12:16]
    own_ref, other_ref = refs[16:18]
    all_ref = refs[22]
    quarter = mixes[0].shape[0]
    full = dot(stack_rows(tokens[:4]), own_ref[...], 0, 0)
    more = dot(stack_rows(tokens[4:]), other_ref[...], 0, 0)
    all_ref[:, :quarter] = full[:, :quarter]
    all_ref[:, quarter : 3 * quarter] = full[:, quarter:] + more
    rank = ids_ref[0]
    branch = stack_rows(branches)
    wanted = branch[:, :quarter]
    for index in range(1, 4):
        wanted = jnp.where(
            rank == index, branch[:, index * quarter : (index + 1) * quarter], wanted
        )
    count = branches[0].shape[0]
    for bits in range(4):
        turned = jnp.concatenate(
            [wanted[(item ^ bits) * count : ((item ^ bits) + 1) * count] for item in range(4)],
            axis=0,
        )
        all_ref[rows_at(rank ^ bits, quarter), 3 * quarter :] = dot(mixes[bits][...], turned)
    divide_rows(ids_ref, all_ref, refs[18:22])


def half_rows(ids_ref, refs, outs):
    kept_ref, arrived_ref, more_kept_ref, more_arrived_ref = refs
    own_ref, sent_ref, more_own_ref, more_sent_ref = outs
    size = own_ref.shape[0] // 2
    high = ids_ref[1]
    for step in range(2):
        rows = slice(step * size, (step + 1) * size)
        where = rows_at(high ^ (2 * step), size)
        own_ref[rows, :] = kept_ref[where, :] + arrived_ref[where, :].astype(F32)
        where = rows_at(high ^ (2 * step + 1), size)
        sent_ref[rows, :] = (kept_ref[where, :] + arrived_ref[where, :].astype(F32)).astype(BF)
    more = more_kept_ref[...] + more_arrived_ref[...].astype(F32)
    more_own_ref[...] = more[: 2 * size]
    more_sent_ref[: 2 * size, :] = more[2 * size :].astype(BF)


def half_kernel(ids_ref, *refs):
    half_rows(ids_ref, refs[:4], refs[4:])


def half_sums_kernel(ids_ref, *refs):
    half_rows(ids_ref, refs[:4], (refs[6], refs[7], refs[8], refs[9]))
    sums = refs[4][...].astype(F32) + refs[5][...].astype(F32)
    refs[9][refs[8].shape[0] :, :] = fold(sums, 3).astype(BF)
    refs[10][...] = rounded(sums)


def fourth_rows(refs, own_ref, sent_ref):
    size = own_ref.shape[0]
    start = 0
    for kept_ref, arrived_ref in (refs[:2], refs[2:4]):
        columns = slice(start, start + kept_ref.shape[1])
        own_ref[:, columns] = kept_ref[:size, :] + arrived_ref[:size, :].astype(F32)
        sent_ref[:size, columns] = (
            kept_ref[size:, :] + arrived_ref[size : 2 * size, :].astype(F32)
        ).astype(BF)
        start += kept_ref.shape[1]


def fourth_kernel(unused_ref, *refs):
    fourth_rows(refs[:4], *refs[4:])


def fourth_sums_kernel(unused_ref, *refs):
    arrived_ref, sums_ref = refs[3], refs[4]
    own_ref, sent_ref, out_ref = refs[5:]
    fourth_rows(refs[:4], own_ref, sent_ref)
    sums = sums_ref[...] + unfold(arrived_ref[refs[2].shape[0] :, :].astype(F32), 3)
    sent_ref[own_ref.shape[0] :, :] = fold(sums, 6).astype(BF)
    out_ref[...] = rounded(sums)


def total_kernel(unused_ref, kept_ref, arrived_ref, out_ref):
    out_ref[...] = (kept_ref[...] + arrived_ref[...].astype(F32)).astype(BF)


def total_sums_kernel(unused_ref, kept_ref, arrived_ref, sums_ref, out_ref):
    size, columns = kept_ref.shape
    out_ref[:, :columns] = (kept_ref[...] + arrived_ref[:size, :].astype(F32)).astype(BF)
    out_ref[:, columns:] = (
        sums_ref[...] + unfold(arrived_ref[size:, :].astype(F32), 6)
    ).astype(BF)


def norm_one_back_kernel(vectors, rank_ref, *refs):
    moved_ref, grad_ref, even_ref, arrived_ref, far_ref, side_ref, gains_ref = refs[:7]
    learned_ref, small_ref, two_ref, up_ref, more_up_ref = refs[7:12]
    back_ref, rounded_ref, sums_ref = refs[12:]
    count = grad_ref.shape[0]
    grad_normed = (
        even_ref[...]
        + arrived_ref[...].astype(F32)
        + far_ref[...].astype(F32)
        + side_ref[...].astype(F32)
    )
    result, gain_row, shift_row = back_of_norm(
        moved_ref[:count, :].astype(F32), gains_ref[0:1, :], grad_normed
    )
    back_ref[:count, :] = (result + grad_ref[...]).astype(BF)
    back_ref[count:, :] = learned_ref[...].astype(BF)
    sums_ref[...] = small_ref[...]
    store_rows(sums_ref, 0, gain_row)
    store_rows(sums_ref, vectors, two_ref[0:1, :])
    store_rows(sums_ref, 3 * vectors, shift_row)
    store_rows(sums_ref, 4 * vectors, two_ref[1:2, :])
    for index in range(4):
        store_rows(
            sums_ref,
            (7 + index) * vectors,
            jnp.where(rank_ref[0] == index, up_ref[...] + more_up_ref[...], 0.0),
        )
    rounded_ref[...] = sums_ref[...].astype(BF)


def back_kernel(unused_ref, moved_ref, grad_ref, learned_ref):
    count = grad_ref.shape[0]
    grad_ref[...] = moved_ref[:count, :].astype(F32)
    learned_ref[...] = moved_ref[count:, :].astype(F32)


def finish_sums_kernel(vectors, quarter, rank_ref, *refs):
    parts, sums_ref = refs[:4], refs[-1]
    finish_qkv_kernel(4, quarter, rank_ref, *parts, *refs[4:6])
    total = None
    for block in ordered(parts, rank_ref[0], slice(4 * quarter, parts[0].shape[1])):
        total = block if total is None else total + block
    sums_ref[...] = total
    refs = refs[6:-1]
    gains_ref, shifts_ref, up_ref, down_ref, first_ref, mid_ref, mid_bias_ref = refs
    for index in range(3):
        gains_ref[index : index + 1, :] = load_rows(sums_ref, index * vectors, vectors)
        shifts_ref[index : index + 1, :] = load_rows(sums_ref, (3 + index) * vectors, vectors)
    down_ref[...] = load_rows(sums_ref, 6 * vectors, vectors)
    quarters = [load_rows(sums_ref, (7 + index) * vectors, vectors) for index in range(4)]
    unit = quarters[0].shape[1] // 8
    up_ref[...] = jnp.concatenate(
        [
            quarters[index][:, group * unit : (group + 1) * unit]
            for group in range(8)
            for index in range(4)
        ],
        axis=1,
    )
    start = 11 * vectors
    for layer in range(3):
        mid_ref[layer] = sums_ref[start + layer * CH : start + (layer + 1) * CH, : 9 * CH]
    start = start + 3 * CH
    first_ref[...] = sums_ref[start : start + 1, :CH]
    mid_bias_ref[...] = sums_ref[start + 1 : start + 4, :CH]


def shards_square(
    ranks,
    frame_size,
    inputs,
    clip_id,
    ln_gains,
    ln_biases,
    w_qkv,
    w_out,
    w_up,
    w_down,
    up_bias,
    down_bias,
    conv_first,
    conv_first_bias,
    conv_mid,
    conv_mid_bias,
    cotangent,
):
    lows = 2
    frames_dev = inputs.shape[1]
    patches = inputs.shape[2]
    width = inputs.shape[3]
    rows = frames_dev * patches
    learned_rows = frames_dev * CH
    hidden = up_bias.shape[0]
    quarter = width // ranks
    heads = quarter // HEAD_DIM
    hidden_quarter = hidden // ranks
    unit = hidden_quarter // frame_size
    size = width // frame_size
    vectors = width // PAD
    own_count = ranks * rows
    place = lax.axis_index("frame")
    ids = jnp.stack([lax.axis_index("seq"), place // lows, place % lows])

    def permute(array, target):
        pairs = []
        for seq in range(ranks):
            for hi in range(ranks):
                for lo in range(lows):
                    to_seq, to_hi, to_lo = target(seq, hi, lo)
                    pairs.append(
                        (
                            seq * frame_size + hi * lows + lo,
                            to_seq * frame_size + to_hi * lows + to_lo,
                        )
                    )
        return lax.ppermute(array, AXES, pairs)

    def flip(array, seq_bits, hi_bits=0, lo_bits=0):
        return permute(
            array, lambda seq, hi, lo: (seq ^ seq_bits, hi ^ hi_bits, lo ^ lo_bits)
        )

    def after(array, *others):
        return lax.optimization_barrier((array,) + others)[0]

    last = []

    def ordered_run(kernel, name, scalars, arrays, outs, scratch=()):
        if last:
            arrays = [after(arrays[0], last[0])] + list(arrays[1:])
        results = list(run(kernel, name, scalars, arrays, outs, scratch))
        last[:] = [results[-1]]
        return results

    def to_planes(array):
        return permute(array, lambda seq, hi, lo: (RANK_OF[hi], PLANE_OF[seq], lo))

    def from_planes(array):
        return permute(
            array, lambda seq, hi, lo: (PLANE_OF.index(hi), RANK_OF.index(seq), lo)
        )

    def gather_four(block):
        far = flip(block, 2)
        near = flip(block, 1)
        return [block, near, far, flip(far, 1)]

    def pass_sum(even, arrived, name):
        (result,) = ordered_run(
            pass_sum_kernel,
            name,
            ids,
            [even, arrived],
            [((rows, width), BF)],
        )
        return result

    def scatter_four(evens, odds, name):
        far = flip(pass_sum(evens[1], flip(odds[1], 1), name), 2)
        return flip(odds[0], 1), far

    def row_parts(blocks, first, second):
        return [
            ((blocks * size, columns), kind) for columns in (first, second) for kind in (F32, BF)
        ]

    def scatter_half(parts, sums, name):
        kept, sent, more_kept, more_sent = parts
        shapes = row_parts(2, kept.shape[1], more_kept.shape[1])
        arrays = [kept, flip(sent, 0, 0, 1), more_kept, flip(more_sent, 0, 1)]
        if sums is None:
            return ordered_run(half_kernel, name, ids, arrays, shapes), None
        shapes[3] = ((2 * size + small_rows // 3, more_kept.shape[1]), BF)
        arrays += [sums, flip(sums, 0, 1)]
        *parts, sums = ordered_run(
            half_sums_kernel, name, ids, arrays, shapes + [(sums.shape, F32)]
        )
        return parts, sums

    def scatter_fourth(parts, sums, name):
        kept, sent, more_kept, more_sent = parts
        columns = kept.shape[1] + more_kept.shape[1]
        arrays = [kept, flip(sent, 0, 1), more_kept, flip(more_sent, 0, 0, 1)]
        if sums is None:
            shapes = [((size, columns), F32), ((size, columns), BF)]
            return ordered_run(fourth_kernel, name, ids, arrays, shapes), None
        shapes = [((size, columns), F32), ((size + small_rows // 6, columns), BF)]
        *parts, sums = ordered_run(
            fourth_sums_kernel, name, ids, arrays + [sums], shapes + [(sums.shape, F32)]
        )
        return parts, sums

    def scatter_last(parts, sums, name):
        kept, sent = parts
        arrays = [kept, flip(sent, 0, 2)]
        if sums is None:
            return ordered_run(total_kernel, name, ids, arrays, [(kept.shape, BF)])[0]
        shape = (size, kept.shape[1] + PAD)
        return ordered_run(total_sums_kernel, name, ids, arrays + [sums], [(shape, BF)])[0]

    (own_pack,) = ordered_run(
        select_kernel, "select", ids, [w_qkv, w_out], [((size, width), BF)]
    )

    moved = to_planes(inputs.reshape(rows, width))
    (pack,) = ordered_run(
        pack_kernel,
        "pack",
        ids,
        [cotangent.reshape(learned_rows, width), clip_id],
        [((learned_rows + 16, width), BF)],
    )
    extra = to_planes(pack)
    pack_two = flip(own_pack, 0, 2)
    pack_one = flip(own_pack, 0, 1)
    pack_side = flip(own_pack, 0, 0, 1)
    pack_three = flip(pack_two, 0, 1)
    packs = [own_pack, pack_side]
    for item in (pack_one, pack_two, pack_three):
        packs += [item, flip(item, 0, 0, 1)]

    mid_pad = jnp.pad(conv_mid, ((0, 0), (0, PAD - CH), (0, PAD - 9 * CH)))
    mid_bias_pad = jnp.pad(conv_mid_bias, ((0, 0), (0, PAD - CH)))
    first_bias_pad = jnp.pad(conv_first_bias, (0, PAD - CH)).reshape(1, PAD)
    up_bias_row = up_bias.reshape(1, hidden)
    down_bias_row = down_bias.reshape(1, width)

    own_a, own_b = ordered_run(
        prepare_kernel,
        "prepare",
        ids,
        [
            after(w_up, mid_pad, mid_bias_pad, first_bias_pad, up_bias_row, down_bias_row),
            w_down,
            conv_first,
        ],
        [((size, hidden_quarter + PAD), BF), ((size, width), BF)],
    )

    low_norm, query_clip, key_clip = ordered_run(
        norm_one_kernel,
        "norm_one",
        ids,
        [moved, extra, ln_gains, ln_biases],
        [((rows, width), BF), ((1, own_count), F32), ((2 * own_count, 1), F32)],
    )
    low_norm = after(low_norm, pack_side, pack_one, pack_two)

    def join(pairs, name):
        flat = [item for pair in pairs for item in pair]
        outs = [((2 * pair[0].shape[0], pair[0].shape[1]), BF) for pair in pairs]
        return ordered_run(join_kernel, name, ids, flat, outs)

    far = flip(low_norm, 2)
    side = flip(low_norm, 0, 0, 1)
    near = flip(low_norm, 1)
    far_a, side_b = flip(own_a, 0, 2), flip(own_b, 0, 0, 1)
    (picked,) = ordered_run(
        pick_kernel,
        "pick",
        ids,
        [after(far, far_a, side_b, *packs[1:]), side],
        [((rows, width), BF)],
    )
    two_a, two_b = join(
        [(own_a, far_a), (own_b, side_b)], "join_two"
    )
    corner = permute(
        picked,
        lambda seq, hi, lo: (seq, hi, lo ^ 1) if seq % 2 == 0 else (seq ^ 2, hi, lo),
    )
    far_near = flip(far, 1)
    side_near = flip(side, 1)
    corner = after(corner, near, far_near, side_near)
    all_one = [near, far, far_near, side, side_near, corner, flip(corner, 1)]
    all_one = [low_norm] + all_one
    queries, keyvals, qkv_quarter, own_out, near_out, far_out, both_out = ordered_run(
        functools.partial(project_kernel, quarter),
        "project",
        ids,
        all_one + packs,
        [
            ((own_count, quarter), BF),
            ((2 * own_count, 2 * quarter), BF),
            ((width, 3 * quarter), BF),
        ]
        + [((quarter, quarter), BF)] * 4,
        [pltpu.VMEM((width, quarter), BF)],
    )
    out_blocks = [own_out, flip(near_out, 1), flip(far_out, 2), flip(both_out, 3)]
    scale = HEAD_DIM ** (-0.5)
    attended, logs = ordered_run(
        functools.partial(attend_wide_kernel, heads, scale),
        "attend",
        ids,
        [queries, keyvals, query_clip, key_clip],
        [((quarter, own_count), BF), ((8, own_count), F32)],
    )
    blocks_of = [((rows, width), F32)] * 2 + [((rows, width), BF)] * 2
    *parts, out_quarter = ordered_run(
        out_kernel,
        "out",
        ids,
        [attended] + out_blocks,
        blocks_of + [((quarter, width), BF)],
    )
    evens, odds = parts[:2], parts[2:]
    arrived, far = scatter_four(evens, odds, "out_pass")
    four_a, four_b = join(
        [(two_a, flip(two_a, 0, 1)), (two_b, flip(two_b, 0, 2))], "join_four"
    )
    after_attention, low_two = ordered_run(
        norm_two_kernel,
        "norm_two",
        ids,
        [moved, evens[0], arrived, far, ln_gains, ln_biases],
        [((rows, width), F32), ((rows, width), BF)],
    )
    near_two, far_two = flip(low_two, 1), flip(low_two, 2)
    pair = [
        ((2 * rows, hidden_quarter), BF),
        ((2 * rows, hidden_quarter), F32),
        ((rows, width), F32),
        ((rows, width), BF),
    ]
    up_full, down_full, conv_full, own_bias, act, slope, even, odd = ordered_run(
        mlp_kernel,
        "mlp",
        ids,
        [low_two, near_two]
        + [four_a, flip(four_a, 0, 0, 1), four_b, flip(four_b, 0, 1), up_bias_row],
        [
            ((width, hidden_quarter), BF),
            ((hidden_quarter, width), BF),
            ((width, PAD), BF),
            ((1, hidden_quarter), F32),
        ]
        + pair,
    )
    far_two = after(far_two, even)
    all_two = [low_two, near_two, far_two, flip(far_two, 1)]
    acts, slopes, evens, odds = [act], [slope], [even], [odd]
    for item, rest in zip(
        (acts, slopes, evens, odds),
        ordered_run(
            mlp_more_kernel, "mlp_more", ids, all_two[2:] + [up_full, down_full, own_bias], pair
        ),
    ):
        item.append(rest)
    arrived, far = scatter_four(evens, odds, "mlp_pass")

    small_rows = -(-(11 * vectors + 3 * CH + 4) // 8) * 8
    learned, low_mlp, grad_block, low_three, spread, small = ordered_run(
        functools.partial(tail_kernel, vectors),
        "tail",
        ids,
        [
            after_attention,
            evens[0],
            arrived,
            far,
            down_bias_row,
            ln_gains,
            ln_biases,
            conv_full,
            first_bias_pad,
            mid_pad,
            mid_bias_pad,
            extra,
        ],
        [
            ((learned_rows, width), F32),
            ((rows, width), BF),
            ((rows, width), F32),
            ((rows, width), BF),
            ((rows, PAD), BF),
            ((small_rows, PAD), F32),
        ],
    )

    near_mlp, far_mlp = flip(low_mlp, 1), flip(low_mlp, 2)
    pair = [
        ((2 * rows, hidden_quarter), BF),
        ((rows, width), F32),
        ((rows, width), BF),
        ((1, hidden_quarter), F32),
    ]
    pre, even, odd, bias = ordered_run(
        mlp_back_kernel,
        "mlp_back",
        ids,
        [low_mlp, near_mlp, slopes[0], up_full, down_full],
        pair,
    )
    far_mlp = after(far_mlp, even)
    all_mlp = [low_mlp, near_mlp, far_mlp, flip(far_mlp, 1)]
    pres, evens, odds, biases = [pre], [even], [odd], [bias]
    for item, rest in zip(
        (pres, evens, odds, biases),
        ordered_run(
            mlp_back_kernel,
            "mlp_back_more",
            ids,
            all_mlp[2:] + [slopes[1], up_full, down_full],
            pair,
        ),
    ):
        item.append(rest)
    arrived, far = scatter_four(evens, odds, "mlp_back_pass")
    columns = hidden_quarter + width + PAD
    mlp_parts = ordered_run(
        mlp_grads_kernel,
        "mlp_grads",
        ids,
        all_two + all_mlp + acts + pres + [low_three, spread],
        row_parts(4, hidden_quarter, width + PAD),
        [pltpu.VMEM((width, columns), F32)],
    )
    grad_after, low_branch, rows_two = ordered_run(
        norm_two_back_kernel,
        "norm_two_back",
        ids,
        [after_attention, grad_block, evens[0], arrived, far, ln_gains],
        [((rows, width), F32), ((rows, width), BF), ((2, width), F32)],
    )

    near_branch, far_branch = flip(low_branch, 1), flip(low_branch, 2)
    mixes = gather_four(after(attended, far_branch))
    common = [out_quarter, queries, keyvals, logs, query_clip, key_clip]
    total = ((2 * own_count, 2 * quarter), F32)
    grads_first, sums_first = ordered_run(
        functools.partial(attend_back_first_kernel, heads, scale),
        "attend_back",
        ids,
        [low_branch, near_branch] + common,
        [((2 * rows, quarter), BF), total],
    )
    far_branch = after(far_branch, sums_first)
    all_branch = [low_branch, near_branch, far_branch, flip(far_branch, 1)]
    grads_next, sums_next = ordered_run(
        functools.partial(attend_back_next_kernel, heads, scale, 2 * rows),
        "attend_back_next",
        ids,
        [far_branch] + common + [sums_first],
        [((rows, quarter), BF), total],
    )
    grads_own, grads_other, *parts = ordered_run(
        functools.partial(attend_back_last_kernel, heads, scale, 3 * rows),
        "attend_back_last",
        ids,
        all_branch[3:] + common + [sums_next, grads_first, grads_next, qkv_quarter],
        [((own_count, 3 * quarter), BF), ((own_count, 2 * quarter), BF)]
        + [((rows, width), F32)] * 4
        + [((rows, width), BF)] * 4,
        [
            pltpu.VMEM((rows, quarter), BF),
            pltpu.VMEM((2 * own_count, 2 * quarter), F32),
        ],
    )
    evens = parts[:4]
    arrived = [flip(item, 1) for item in parts[4:]]
    corner = permute(
        pass_sum(evens[3], arrived[3], "corner_pass"),
        lambda seq, hi, lo: (seq ^ 2, hi, lo) if seq % 2 == 0 else (seq, hi, lo ^ 1),
    )
    mlp_parts, unused = scatter_half(mlp_parts, None, "mlp_half")
    qkv_parts = ordered_run(
        qkv_grads_kernel,
        "qkv_grads",
        ids,
        all_one + all_branch + mixes + [grads_own, grads_other],
        row_parts(4, width // 2, width // 2),
        [pltpu.VMEM((width, width), F32)],
    )
    far, side = ordered_run(
        pass_on_kernel,
        "pass_on",
        ids,
        [evens[1], evens[2], arrived[1], arrived[2], corner],
        [((rows, width), BF), ((rows, width), BF)],
    )
    qkv_parts[1], qkv_parts[3] = after(qkv_parts[1], far), after(qkv_parts[3], far)
    far, side = flip(far, 2), flip(side, 0, 0, 1)
    mlp_parts, unused = scatter_fourth(mlp_parts, None, "mlp_fourth")
    moved_back, sums = ordered_run(
        functools.partial(norm_one_back_kernel, vectors),
        "norm_one_back",
        ids,
        [moved, grad_after, evens[0], arrived[0], far, side, ln_gains]
        + [learned, small, rows_two]
        + biases,
        [((rows + learned_rows, width), BF), ((small_rows, PAD), BF)],
        [pltpu.VMEM((small_rows, PAD), F32)],
    )

    qkv_parts, sums = scatter_half(qkv_parts, sums, "qkv_half")
    mlp_share = scatter_last(mlp_parts, None, "mlp_total")
    qkv_parts, sums = scatter_fourth(qkv_parts, sums, "qkv_fourth")
    mlp_share = after(mlp_share, sums)
    mlp_far, mlp_near = flip(mlp_share, 2), flip(mlp_share, 1)
    qkv_share = scatter_last(qkv_parts, sums, "qkv_total")
    qkv_far, qkv_near = flip(qkv_share, 2), flip(qkv_share, 1)
    sum_up, sum_down, sum_conv = ordered_run(
        functools.partial(finish_mlp_kernel, ranks, hidden_quarter, width, unit),
        "finish_mlp",
        ids,
        [mlp_share, mlp_near, mlp_far, flip(mlp_far, 1)],
        [((size, hidden), F32), ((ranks * unit, width), F32), ((size, 9 * CH), F32)],
    )
    grad_input, learned = ordered_run(
        back_kernel,
        "back",
        ids,
        [from_planes(moved_back)],
        [((rows, width), F32), ((learned_rows, width), F32)],
    )
    (
        sum_qkv,
        sum_out,
        sum_gains,
        sum_shifts,
        sum_up_bias,
        sum_down_bias,
        sum_first,
        sum_mid,
        sum_mid_bias,
    ) = ordered_run(
        functools.partial(finish_sums_kernel, vectors, quarter),
        "finish_qkv",
        ids,
        [qkv_share, qkv_near, qkv_far, flip(after(qkv_far, sum_down), 1)],
        [
            ((size, 3 * width), F32),
            ((size, width), F32),
            ((3, width), F32),
            ((3, width), F32),
            ((1, hidden), F32),
            ((1, width), F32),
            ((1, CH), F32),
            ((3, CH, 9 * CH), F32),
            ((3, CH), F32),
        ],
        [pltpu.VMEM((small_rows, PAD), F32)],
    )
    return (
        learned.reshape(1, frames_dev, CH, width),
        grad_input.reshape(1, frames_dev, patches, width),
        sum_qkv,
        sum_out,
        sum_up,
        sum_down,
        sum_conv,
        sum_gains,
        sum_shifts,
        sum_up_bias.reshape(hidden),
        sum_down_bias.reshape(width),
        sum_first.reshape(CH),
        sum_mid,
        sum_mid_bias,
    )


def solution(mesh):
    placed = (
        P("seq", "frame", None, None),
        P("seq", None),
        P(),
        P(),
        P("frame", None),
        P("frame", None),
        P("frame", None),
        P("frame", None),
        P(),
        P(),
        P("frame", None),
        P(),
        P(),
        P(),
        P("seq", "frame", None, None),
    )
    ranks, frame_size = mesh.shape["seq"], mesh.shape["frame"]
    body = shards_square if ranks == 4 and frame_size == 8 else shards_general
    return jax.shard_map(
        functools.partial(body, ranks, frame_size),
        mesh=mesh,
        in_specs=placed,
        out_specs=(
            P("seq", "frame", None, None),
            P("seq", "frame", None, None),
            P("frame", None),
            P("frame", None),
            P("frame", None),
            P("frame", None),
            P("frame", None),
            P(),
            P(),
            P(),
            P(),
            P(),
            P(),
            P(),
        ),
        check_vma=False,
    )
```
